32 devices in a mesh: fsdp: 8 (over z, y), seq: 4 (over x, core).
Axes of the slice: x: 2, y: 2, z: 4, core: 2. Of those that a mesh axis runs over, the one named last changes fastest.
Arguments:
- queries: bfloat16 [4096, 4096], P(('fsdp', 'seq')), may hold values from -6 to 6
- keys: bfloat16 [4096, 4096], P(('fsdp', 'seq')), may hold values from -6 to 6
- values: bfloat16 [4096, 4096], P(('fsdp', 'seq')), may hold values from -6 to 6
- cotangent: bfloat16 [4096, 4096], P(('fsdp', 'seq')), may hold values from -8 to 8
- out_weight: bfloat16 [4096, 4096], P('seq', 'fsdp'), may hold values from -0.09375 to 0.09375
- short_taps: float32 [3, 7, 4096], P(None, None, 'seq'), may hold values from -2 to 2
- long_taps: float32 [128, 256], P(None, 'seq'), may hold values from -0.5 to 0.5
- skip_gain: float32 [4096], P('seq'), may hold values from -1 to 1
Outputs:
- query_grad: bfloat16 [4096, 4096], P(('fsdp', 'seq'))
- key_grad: bfloat16 [4096, 4096], P(('fsdp', 'seq'))
- value_grad: bfloat16 [4096, 4096], P(('fsdp', 'seq'))
- weight_grad: float32 [4096, 4096], P('seq', 'fsdp')
- short_grad: float32 [3, 7, 4096], P(None, None, 'seq')
- long_grad: float32 [128, 256], P(None, 'seq')
- gain_grad: float32 [4096], P('seq')
The draws below stay inside these ranges and needn't reach their ends.
All inputs are finite; a program needn't handle non-finite values.
Results may differ from the reference program's by a relative error of at most 0.0075.
Values may be sent and summed in bfloat16 or wider, within the bound.
No kernel may reach another device: no remote copies, remote signals or barrier semaphores. Data moves between devices by JAX's collectives and lax.ppermute only.
A program may use at most 256 MiB of HBM per device.

```python
import jax
import jax.numpy as jnp
from jax import lax

D = 4096
C = 4096
SHORT = 7
LTAPS = 128
GROUP = 16
TOKENS = 4096
GROUPS = 256


def strengthened(values, key, source, target, shards_of, factor):
    def block_of(dim):
        return (jnp.arange(values.shape[dim]) // (values.shape[dim] // shards_of)).reshape((-1,) + (1,) * (values.ndim - 1 - dim))

    first = jax.random.permutation(key, shards_of)[block_of(target)]
    other_side = (block_of(target) + shards_of // 2) % shards_of
    return jnp.where((block_of(source) == first) | (block_of(source) == other_side), factor * values, values)


def level_of(stream_key, shape, cuts, low, top_value):
    def one(dim, blocks):
        draws = jax.random.uniform(jax.random.fold_in(jax.random.fold_in(stream_key, 6), dim), (blocks,), jnp.float32, low / len(cuts), top_value / len(cuts))
        return jnp.repeat(jnp.exp(draws), shape[dim] // blocks).reshape((-1,) + (1,) * (len(shape) - dim - 1))

    level = one(*cuts[0])
    for cut in cuts[1:]:
        level = level * one(*cut)
    return level


def noise(own_key, extent, width, limit, cuts=(), kind=jnp.bfloat16):
    gain = level_of(own_key, extent, cuts, -0.22, 0.18) if cuts else 1.0
    values = jax.random.normal(own_key, extent, jnp.float32) * width * gain
    return jnp.minimum(jnp.maximum(values, -limit), limit).astype(kind)


def bell_draw_with(own_key, dims, deviation, bound, cuts, heavy, kind=jnp.bfloat16):
    array = deviation * jax.random.normal(own_key, dims, jnp.float32)
    if cuts:
        array = array * level_of(own_key, dims, cuts, -0.22, 0.18)
    return jnp.clip(strengthened(array, jax.random.fold_in(own_key, 3), *heavy), -bound, bound).astype(kind)


def setup_inputs(seed: int = 0) -> dict:
    splits = jax.random.split(jax.random.key(seed), 9)
    queries = noise(splits[0], (TOKENS, C), 1.0, 6.0, ((0, 32),))
    keys = noise(splits[1], (TOKENS, C), 1.0, 6.0, ((0, 32),))
    values = noise(splits[2], (TOKENS, C), 1.0, 6.0, ((0, 32),))
    cotangent = bell_draw_with(splits[3], (TOKENS, D), 1.0, 8.0, ((0, 32),), (0, 1, 32, 2.75))
    out_weight = noise(splits[4], (C, D), C ** -0.5, 0.09375, ((0, 4), (1, 8)))
    short_taps = noise(splits[5], (3, SHORT, C), SHORT ** -0.5, 2.0, ((2, 4),), jnp.float32)
    long_taps = noise(splits[6], (LTAPS, GROUPS), LTAPS ** -0.5, 0.5, ((1, 4),), jnp.float32)
    skip_gain = jnp.clip(jax.random.uniform(splits[7], (C,), jnp.float32, -1.0, 1.0) * level_of(splits[7], (C,), ((0, 4),), -0.4, 0.0), -1.0, 1.0)
    return {"queries": queries, "keys": keys, "values": values, "cotangent": cotangent, "out_weight": out_weight, "short_taps": short_taps, "long_taps": long_taps, "skip_gain": skip_gain}


precise = lax.Precision.HIGHEST


def make_tables(taps):
    taps_count = taps.shape[0]
    lag_rows = jnp.arange(taps_count)[:, None] - jnp.arange(taps_count)[None, :]
    tap_ids = jnp.arange(taps_count)
    near_pick = (lag_rows[:, :, None] == tap_ids[None, None, :]).astype(jnp.float32)
    far_pick = ((lag_rows + taps_count)[:, :, None] == tap_ids[None, None, :]).astype(jnp.float32)
    near_taps = jnp.einsum("tsj,jg->gts", near_pick, taps, precision=precise)
    far_taps = jnp.einsum("tsj,jg->gts", far_pick, taps, precision=precise)
    return near_pick, far_pick, near_taps, far_taps


def to_blocks(field, block_len, group_count):
    row_count, col_count = field.shape
    return field.reshape(row_count // block_len, block_len, group_count, col_count // group_count)


def long_forward(product, edge_rows, tables):
    near_taps, far_taps = tables[2], tables[3]
    group_count, block_len = near_taps.shape[0], near_taps.shape[1]
    row_count, col_count = product.shape
    current = to_blocks(product, block_len, group_count)
    earlier = to_blocks(jnp.concatenate([edge_rows, product[:row_count - block_len]], 0), block_len, group_count)
    total = jnp.einsum("gts,bsgc->btgc", near_taps, current, precision=precise)
    total = total + jnp.einsum("gts,bsgc->btgc", far_taps, earlier, precision=precise)
    return total.reshape(row_count, col_count)


def long_backward(slope_grad, next_rows, product, edge_rows, tables):
    near_pick, far_pick, near_taps, far_taps = tables
    group_count, block_len = near_taps.shape[0], near_taps.shape[1]
    row_count, col_count = product.shape
    current_d = to_blocks(slope_grad, block_len, group_count)
    later_d = to_blocks(jnp.concatenate([slope_grad[block_len:], next_rows], 0), block_len, group_count)
    product_grad = jnp.einsum("gts,btgc->bsgc", near_taps, current_d, precision=precise)
    product_grad = product_grad + jnp.einsum("gts,btgc->bsgc", far_taps, later_d, precision=precise)
    current_z = to_blocks(product, block_len, group_count)
    earlier_z = to_blocks(jnp.concatenate([edge_rows, product[:row_count - block_len]], 0), block_len, group_count)
    gram_near = jnp.einsum("btgc,bsgc->gts", current_d, current_z, precision=precise)
    gram_far = jnp.einsum("btgc,bsgc->gts", current_d, earlier_z, precision=precise)
    taps_grad = jnp.einsum("tsj,gts->jg", near_pick, gram_near, precision=precise)
    taps_grad = taps_grad + jnp.einsum("tsj,gts->jg", far_pick, gram_far, precision=precise)
    return product_grad.reshape(row_count, col_count), taps_grad


def short_forward(inputs_f, edge_rows, taps):
    tap_count = taps.shape[1]
    row_count = inputs_f.shape[1]
    extended = jnp.concatenate([edge_rows, inputs_f], 1)
    result = jnp.zeros(inputs_f.shape, jnp.float32)
    for offset in range(tap_count):
        begin = tap_count - 1 - offset
        result = result + taps[:, offset, None, :] * extended[:, begin:begin + row_count]
    return result


def short_backward(feat_grad, next_rows, inputs_f, edge_rows, taps):
    tap_count = taps.shape[1]
    row_count = inputs_f.shape[1]
    later = jnp.concatenate([feat_grad, next_rows], 1)
    extended = jnp.concatenate([edge_rows, inputs_f], 1)
    inputs_grad = jnp.zeros(inputs_f.shape, jnp.float32)
    taps_list = []
    for offset in range(tap_count):
        inputs_grad = inputs_grad + taps[:, offset, None, :] * later[:, offset:offset + row_count]
        begin = tap_count - 1 - offset
        taps_list.append(jnp.sum(feat_grad * extended[:, begin:begin + row_count], axis=1))
    return inputs_grad, jnp.stack(taps_list, axis=1)


def reference(queries, keys, values, cotangent, out_weight, short_taps, long_taps, skip_gain):
    slab_cols = 256
    slab_count = C // slab_cols
    row_count = queries.shape[0]
    grad_scale = float(TOKENS) ** -0.5

    def one_slab(slab_index):
        first_col = slab_index * slab_cols
        inputs_f = jnp.stack([lax.dynamic_slice_in_dim(source, first_col, slab_cols, 1) for source in (queries, keys, values)]).astype(jnp.float32)
        taps_short = lax.dynamic_slice_in_dim(short_taps, first_col, slab_cols, 2)
        taps_long = lax.dynamic_slice_in_dim(long_taps, slab_index * (slab_cols // GROUP), slab_cols // GROUP, 1)
        skip_row = lax.dynamic_slice_in_dim(skip_gain, first_col, slab_cols, 0)
        weights = lax.dynamic_slice_in_dim(out_weight, first_col, slab_cols, 0)
        edge_in = jnp.zeros((3, SHORT - 1, slab_cols), jnp.float32)
        edge_prod = jnp.zeros((LTAPS, slab_cols), jnp.float32)
        tables = make_tables(taps_long)
        features = short_forward(inputs_f, edge_in, taps_short)
        product = features[1] * features[2]
        filtered = long_forward(product, edge_prod, tables) + skip_row * product
        mixed_out = (features[0] * filtered).astype(jnp.bfloat16)
        mixed_grad = lax.dot_general(cotangent, weights, (((1,), (1,)), ((), ())), preferred_element_type=jnp.float32)
        weight_part = lax.dot_general(mixed_out, cotangent, (((0,), (0,)), ((), ())), preferred_element_type=jnp.float32)
        query_feat = mixed_grad * filtered
        slope_grad = mixed_grad * features[0]
        next_slope = jnp.zeros((LTAPS, slab_cols), jnp.float32)
        product_core, long_part = long_backward(slope_grad, next_slope, product, edge_prod, tables)
        product_grad = product_core + skip_row * slope_grad
        gain_part = jnp.sum(slope_grad * product, axis=0)
        feat_grad = jnp.stack([query_feat, product_grad * features[2], product_grad * features[1]])
        next_feat = jnp.zeros((3, SHORT - 1, slab_cols), jnp.float32)
        inputs_grad, short_part = short_backward(feat_grad, next_feat, inputs_f, edge_in, taps_short)
        return (inputs_grad.astype(jnp.bfloat16), weight_part * grad_scale, short_part * grad_scale, long_part * grad_scale, gain_part * grad_scale)

    grads, weight_parts, short_parts, long_parts, gain_parts = lax.map(one_slab, jnp.arange(slab_count, dtype=jnp.int32))
    grads = jnp.transpose(grads, (1, 2, 0, 3)).reshape(3, row_count, C)
    weight_grad = weight_parts.reshape(C, D)
    short_grad = jnp.transpose(short_parts, (1, 2, 0, 3)).reshape(3, SHORT, C)
    long_grad = jnp.transpose(long_parts, (1, 0, 2)).reshape(LTAPS, C // GROUP)
    gain_grad = gain_parts.reshape(C)
    return (grads[0], grads[1], grads[2], weight_grad, short_grad, long_grad, gain_grad)
```

```python
import functools

import jax
import jax.numpy as jnp
from jax import lax
from jax.experimental import pallas as pl
from jax.experimental.pallas import tpu as pltpu
from jax.sharding import Mesh
from jax.sharding import PartitionSpec as P

SHORT = 7
LTAPS = 128
LANES = 128
PAD = 16
Z = 4
F32 = jnp.float32
BF16 = jnp.bfloat16


def params(mib):
    return pltpu.CompilerParams(vmem_limit_bytes=mib * 2**20)


def tables_kernel(fwd_ref, bwd_ref, tf_ref, tb_ref):
    for g in range(fwd_ref.shape[0]):
        rows = slice(g * LTAPS, (g + 1) * LTAPS)
        for src, dst in ((fwd_ref, tf_ref), (bwd_ref, tb_ref)):
            wide = jnp.broadcast_to(src[g : g + 1, :], (LTAPS, 2 * LTAPS))
            dst[rows, :] = pltpu.roll(wide, 0, 1, stride=1, stride_axis=0).astype(BF16)


def make_tables(long_taps):
    by_group = long_taps.T
    groups = by_group.shape[0]
    fwd = jnp.pad(by_group[:, ::-1], ((0, 0), (1, LTAPS - 1)))
    bwd = jnp.pad(by_group, ((0, 0), (0, LTAPS)))
    per = 8
    row_spec = pl.BlockSpec((per, 2 * LTAPS), lambda i: (i, 0))
    tab_spec = pl.BlockSpec((per * LTAPS, 2 * LTAPS), lambda i: (i, 0))
    shape = jax.ShapeDtypeStruct((groups * LTAPS, 2 * LTAPS), BF16)
    return pl.pallas_call(
        tables_kernel,
        grid=(groups // per,),
        in_specs=[row_spec, row_spec],
        out_specs=[tab_spec, tab_spec],
        out_shape=[shape, shape],
        compiler_params=params(32),
        name="tables",
    )(fwd, bwd)


def pick_groups(wide, col, rows, per):
    lane_group = lax.broadcasted_iota(jnp.int32, (rows, LANES), 1) // (LANES // per)
    cols = slice(col * LANES, (col + 1) * LANES)
    out = wide[0:rows, cols]
    for g in range(1, per):
        out = jnp.where(lane_group == g, wide[g * rows : (g + 1) * rows, cols], out)
    return out


def forward_kernel(x_ref, h_ref, taps_ref, skip_ref, tab_ref, mixed_ref, f_ref, filt_ref, xf, pf, pb, wide):
    blocks, _, rows, _ = x_ref.shape
    tokens = blocks * rows
    per = tab_ref.shape[0] // LTAPS
    xf[0, LTAPS : LTAPS + PAD] = h_ref[0:PAD].astype(F32)
    for i in (1, 2):
        begin = PAD + (i - 1) * (LTAPS + PAD)
        xf[i, 0 : LTAPS + PAD] = h_ref[begin : begin + LTAPS + PAD].astype(F32)
    for i in range(3):
        for b in range(blocks):
            begin = LTAPS + PAD + b * rows
            xf[i, begin : begin + rows] = x_ref[b, i].astype(F32)

    def feature(i, base):
        total = taps_ref[i, 0:1] * xf[i, PAD + base : PAD + base + LTAPS]
        for j in range(1, SHORT):
            total = total + taps_ref[i, j : j + 1] * xf[i, PAD + base - j : PAD + base - j + LTAPS]
        return total

    for n in range(tokens // LTAPS + 1):
        base = n * LTAPS
        own = slice(base - LTAPS, base)
        f1 = feature(1, base)
        f2 = feature(2, base)
        prod = f1 * f2
        pb[base : base + LTAPS] = prod.astype(BF16)
        if n:
            f_ref[1, own] = f1
            f_ref[2, own] = f2
            f_ref[0, own] = feature(0, base)
            pf[own] = prod
    skip = skip_ref[...]
    for b in range(0, tokens // LTAPS, 2):
        low = b * LTAPS
        windows = jnp.concatenate([pb[low : low + 2 * LTAPS], pb[low + LTAPS : low + 3 * LTAPS]], axis=1)
        wide[...] = jnp.dot(tab_ref[...], windows, preferred_element_type=F32)
        for n in range(2):
            own = slice(low + n * LTAPS, low + (n + 1) * LTAPS)
            filtered = pick_groups(wide, n, LTAPS, per) + skip * pf[own]
            filt_ref[own] = filtered
            mixed_ref[own] = (f_ref[0, own] * filtered).astype(BF16)


def forward(x, halo, short_taps, skip, table):
    blocks, _, rows, cols = x.shape
    tokens = blocks * rows
    tiles = cols // LANES
    tab_rows = table.shape[0] // tiles
    tok = pl.BlockSpec((tokens, LANES), lambda c: (0, c))
    return pl.pallas_call(
        forward_kernel,
        grid=(tiles,),
        in_specs=[
            pl.BlockSpec((blocks, 3, rows, LANES), lambda c: (0, 0, 0, c)),
            pl.BlockSpec((halo.shape[0], LANES), lambda c: (0, c)),
            pl.BlockSpec((3, SHORT, LANES), lambda c: (0, 0, c)),
            pl.BlockSpec((1, LANES), lambda c: (0, c)),
            pl.BlockSpec((tab_rows, 2 * LTAPS), lambda c: (c, 0)),
        ],
        out_specs=[tok, pl.BlockSpec((3, tokens, LANES), lambda c: (0, 0, c)), tok],
        out_shape=[
            jax.ShapeDtypeStruct((tokens, cols), BF16),
            jax.ShapeDtypeStruct((3, tokens, cols), F32),
            jax.ShapeDtypeStruct((tokens, cols), F32),
        ],
        scratch_shapes=[
            pltpu.VMEM((3, PAD + LTAPS + tokens, LANES), F32),
            pltpu.VMEM((tokens, LANES), F32),
            pltpu.VMEM((LTAPS + tokens, LANES), BF16),
            pltpu.VMEM((tab_rows, 2 * LTAPS), F32),
        ],
        compiler_params=params(48),
        name="forward",
    )(x, halo, short_taps, skip, table)


def sum_by_lag(gram):
    wide = gram.shape[1]
    parts = [gram[i : i + 8] for i in range(0, gram.shape[0], 8)]
    step = 8
    while len(parts) > 1:
        parts = [
            parts[k] + pltpu.roll(parts[k + 1], wide - step, 1) for k in range(0, len(parts), 2)
        ]
        step *= 2
    total = parts[0]
    row = lax.broadcasted_iota(jnp.int32, total.shape, 0)
    for bit in (1, 2, 4):
        total = jnp.where((row & bit) != 0, pltpu.roll(total, wide - bit, 1), total)
    return jnp.sum(total[:, :LTAPS], axis=0, keepdims=True)


def backward_kernel(
    mo_ref, mr_ref, f_ref, filt_ref, x_ref, n_ref, taps_ref, skip_ref, tab_ref,
    grad_ref, short_ref, long_ref, db, fg, wide, left, right,
):
    blocks, _, rows, _ = x_ref.shape
    tokens = blocks * rows
    per = tab_ref.shape[0] // LTAPS
    count = tokens // LTAPS
    skip = skip_ref[...]
    lane_group = lax.broadcasted_iota(jnp.int32, (1, LANES), 1) // (LANES // per)
    gain = jnp.zeros((8, LANES), F32)
    for b in range(count):
        own = slice(b * LTAPS, (b + 1) * LTAPS)
        mixed_grad = mo_ref[own] + mr_ref[own].astype(F32)
        slope = mixed_grad * f_ref[0, own]
        db[own] = slope.astype(BF16)
        fg[0, own] = mixed_grad * filt_ref[own]
        fg[1, own] = skip * slope
        prod = f_ref[1, own] * f_ref[2, own]
        gain = gain + jnp.sum((prod * slope).reshape(LTAPS // 8, 8, LANES), axis=0)
        prod_b = prod.astype(BF16)
        for g in range(per):
            keep = (lane_group == g).astype(F32).astype(BF16)
            left[g * LTAPS : (g + 1) * LTAPS, b * LANES : (b + 1) * LANES] = prod_b * keep
    db[tokens : tokens + LTAPS + PAD] = n_ref[0 : LTAPS + PAD]
    db[tokens + LTAPS + PAD :] = jnp.zeros((LTAPS - PAD, LANES), BF16)
    for b in range(count):
        right[:, b * LANES : (b + 1) * LANES] = db[b * LTAPS : (b + 2) * LTAPS]
    for b in range(0, count, 2):
        wide[...] = jnp.dot(
            tab_ref[...], right[:, b * LANES : (b + 2) * LANES], preferred_element_type=F32
        )
        for n in range(2):
            own = slice((b + n) * LTAPS, (b + n + 1) * LTAPS)
            grad = pick_groups(wide, n, LTAPS, per) + fg[1, own]
            fg[1, own] = grad * f_ref[2, own]
            fg[2, own] = grad * f_ref[1, own]
    few = jnp.concatenate([tab_ref[g * LTAPS : g * LTAPS + PAD] for g in range(per)], axis=0)
    edge = jnp.dot(few, db[tokens : tokens + 2 * LTAPS], preferred_element_type=F32)
    begin = LTAPS + PAD
    grad = pick_groups(edge, 0, PAD, per) + skip * n_ref[0:PAD].astype(F32)
    fg[1, tokens : tokens + PAD] = grad * n_ref[begin + PAD : begin + 2 * PAD].astype(F32)
    fg[2, tokens : tokens + PAD] = grad * n_ref[begin : begin + PAD].astype(F32)
    fg[0, tokens : tokens + PAD] = n_ref[begin + 2 * PAD : begin + 3 * PAD].astype(F32)
    for i in range(3):
        sums = [jnp.zeros((8, LANES), F32) for _ in range(SHORT)]
        for b in range(count):
            low = b * LTAPS
            inputs = x_ref[b, i].astype(F32)
            total = None
            for j in range(SHORT):
                later = fg[i, low + j : low + j + LTAPS]
                term = taps_ref[i, j : j + 1] * later
                total = term if total is None else total + term
                sums[j] = sums[j] + jnp.sum((later * inputs).reshape(LTAPS // 8, 8, LANES), axis=0)
            grad_ref[b, i] = total.astype(BF16)
        for j in range(SHORT):
            short_ref[i, j : j + 1] = jnp.sum(sums[j], axis=0, keepdims=True)
        short_ref[i, SHORT : SHORT + 1] = jnp.sum(gain, axis=0, keepdims=True)
    wide[...] = lax.dot_general(left[...], right[...], (((1,), (1,)), ((), ())), preferred_element_type=F32)
    for g in range(per):
        gram = wide[g * LTAPS : (g + 1) * LTAPS]
        long_ref[g : g + 1] = sum_by_lag(gram)


def backward(mixed_own, mixed_rest, feats, filt, x, later, short_taps, skip, table):
    blocks, _, rows, cols = x.shape
    tokens = blocks * rows
    tiles = cols // LANES
    tab_rows = table.shape[0] // tiles
    per = tab_rows // LTAPS
    tok = pl.BlockSpec((tokens, LANES), lambda c: (0, c))
    xs = pl.BlockSpec((blocks, 3, rows, LANES), lambda c: (0, 0, 0, c))
    return pl.pallas_call(
        backward_kernel,
        grid=(tiles,),
        in_specs=[
            tok,
            tok,
            pl.BlockSpec((3, tokens, LANES), lambda c: (0, 0, c)),
            tok,
            xs,
            pl.BlockSpec((later.shape[0], LANES), lambda c: (0, c)),
            pl.BlockSpec((3, SHORT, LANES), lambda c: (0, 0, c)),
            pl.BlockSpec((1, LANES), lambda c: (0, c)),
            pl.BlockSpec((tab_rows, 2 * LTAPS), lambda c: (c, 0)),
        ],
        out_specs=[
            xs,
            pl.BlockSpec((3, SHORT + 1, LANES), lambda c: (0, 0, c)),
            pl.BlockSpec((per, LTAPS), lambda c: (c, 0)),
        ],
        out_shape=[
            jax.ShapeDtypeStruct(x.shape, BF16),
            jax.ShapeDtypeStruct((3, SHORT + 1, cols), F32),
            jax.ShapeDtypeStruct((tiles * per, LTAPS), F32),
        ],
        scratch_shapes=[
            pltpu.VMEM((tokens + 2 * LTAPS, LANES), BF16),
            pltpu.VMEM((3, tokens + PAD, LANES), F32),
            pltpu.VMEM((tab_rows, 2 * LTAPS), F32),
            pltpu.VMEM((tab_rows, tokens), BF16),
            pltpu.VMEM((2 * LTAPS, tokens), BF16),
        ],
        compiler_params=params(48),
        name="backward",
    )(mixed_own, mixed_rest, feats, filt, x, later, short_taps, skip, table)


def along(block, axis, distance):
    size = lax.axis_size(axis)
    return lax.ppermute(block, axis, [(i, i + distance) for i in range(size) if 0 <= i + distance < size])


def around(block, axis, distance):
    size = lax.axis_size(axis)
    return lax.ppermute(block, axis, [(i, (i + distance) % size) for i in range(size)])


def body(queries, keys, values, cotangent, out_weight, short_taps, long_taps, skip_gain):
    rows, width = queries.shape
    col_part = out_weight.shape[1]
    seq, ys = lax.axis_size("seq"), lax.axis_size("y")
    cols = width // seq
    y = lax.axis_index("y")
    fsdp = ("z", "y")
    grad_scale = float(rows * seq * ys * Z) ** (-0.5)

    by_owner = jnp.stack([queries, keys, values]).reshape(3, rows, seq, cols).transpose(2, 0, 1, 3)
    x = lax.all_to_all(by_owner, "seq", split_axis=0, concat_axis=0, tiled=True)
    weights = lax.all_gather(out_weight, "z", axis=1, tiled=True)
    cot_parts = cotangent.reshape(rows, Z, ys, col_part)

    def cot_for(step):
        part = lax.dynamic_index_in_dim(cot_parts, (y + step) % ys, 2, keepdims=False)
        part = part.reshape(rows, Z * col_part)
        part = around(part, "y", step) if step else part
        return lax.all_gather(part, "seq", axis=0, tiled=True)

    cots = [cot_for(step) for step in range(ys)]
    fwd_table, bwd_table = make_tables(long_taps)
    skip = skip_gain.reshape(1, cols)

    tail = jnp.concatenate(
        [x[seq - 1, 0, rows - PAD :]]
        + [part for i in (1, 2) for part in (x[seq - 2, i, rows - PAD :], x[seq - 1, i])],
        axis=0,
    )
    halo = along(tail, fsdp, 1)
    mixed, feats, filt = forward(x, halo, short_taps, skip, fwd_table)

    weight_sum = lax.dot_general(mixed, cots[0], (((0,), (0,)), ((), ())), preferred_element_type=F32)
    for step in range(1, ys):
        weight_sum = weight_sum + lax.dot_general(
            around(mixed, "y", step), cots[step], (((0,), (0,)), ((), ())), preferred_element_type=F32
        )
    weight_part = lax.psum_scatter(weight_sum.astype(BF16), "z", scatter_dimension=1, tiled=True)

    mixed_grads = [
        lax.dot_general(cot, weights, (((1,), (1,)), ((), ())), preferred_element_type=F32) for cot in cots
    ]
    rest = [around(mixed_grads[step].astype(BF16), "y", -step) for step in range(1, ys)]
    mixed_rest = rest[0] if len(rest) == 1 else sum(part.astype(F32) for part in rest)
    mixed_own = mixed_grads[0]

    edge = LTAPS + PAD
    head = mixed_own[:edge] + mixed_rest[:edge].astype(F32)
    head = jnp.concatenate(
        [head * feats[0, :edge], feats[1, :PAD], feats[2, :PAD], head[:PAD] * filt[:PAD]], axis=0
    ).astype(BF16)
    later = along(head, fsdp, -1)
    grads, short_part, long_part = backward(
        mixed_own, mixed_rest, feats, filt, x, later, short_taps, skip, bwd_table
    )
    token_grads = lax.all_to_all(grads, "seq", split_axis=0, concat_axis=0, tiled=True)
    token_grads = token_grads.transpose(1, 2, 0, 3).reshape(3, rows, width)
    packed = jnp.concatenate([short_part.reshape(3 * (SHORT + 1), cols), long_part.reshape(-1, cols)], axis=0)
    packed = lax.psum(packed, fsdp) * grad_scale
    short_sum = packed[: 3 * (SHORT + 1)].reshape(3, SHORT + 1, cols)
    long_sum = packed[3 * (SHORT + 1) :].reshape(long_part.shape).T
    return (
        token_grads[0],
        token_grads[1],
        token_grads[2],
        weight_part.astype(F32) * grad_scale,
        short_sum[:, :SHORT],
        long_sum,
        short_sum[0, SHORT],
    )


def solution(mesh):
    fsdp, seq = mesh.shape["fsdp"], mesh.shape["seq"]
    split = Mesh(mesh.devices.reshape(Z, fsdp // Z, seq), ("z", "y", "seq"))
    tokens = P(("z", "y", "seq"), None)
    specs = (P("seq", ("z", "y")), P(None, None, "seq"), P(None, "seq"), P("seq"))
    return jax.shard_map(
        body,
        mesh=split,
        in_specs=(tokens,) * 4 + specs,
        out_specs=(tokens,) * 3 + specs,
        check_vma=False,
    )
```

```python
import functools

import jax
import jax.numpy as jnp
from jax import lax
from jax.experimental import pallas as pl
from jax.experimental.pallas import tpu as pltpu
from jax.sharding import Mesh
from jax.sharding import PartitionSpec as P

SHORT = 7
LTAPS = 128
LANES = 128
PAD = 16
Z = 4
F32 = jnp.float32
BF16 = jnp.bfloat16


def params(mib):
    return pltpu.CompilerParams(vmem_limit_bytes=mib * 2**20)


def tables_kernel(fwd_ref, bwd_ref, tf_ref, tb_ref):
    for g in range(fwd_ref.shape[0]):
        rows = slice(g * LTAPS, (g + 1) * LTAPS)
        for src, dst in ((fwd_ref, tf_ref), (bwd_ref, tb_ref)):
            wide = jnp.broadcast_to(src[g : g + 1, :], (LTAPS, 2 * LTAPS))
            dst[rows, :] = pltpu.roll(wide, 0, 1, stride=1, stride_axis=0).astype(BF16)


def make_tables(long_taps):
    by_group = long_taps.T
    groups = by_group.shape[0]
    fwd = jnp.pad(by_group[:, ::-1], ((0, 0), (1, LTAPS - 1)))
    bwd = jnp.pad(by_group, ((0, 0), (0, LTAPS)))
    per = 8
    row_spec = pl.BlockSpec((per, 2 * LTAPS), lambda i: (i, 0))
    tab_spec = pl.BlockSpec((per * LTAPS, 2 * LTAPS), lambda i: (i, 0))
    shape = jax.ShapeDtypeStruct((groups * LTAPS, 2 * LTAPS), BF16)
    return pl.pallas_call(
        tables_kernel,
        grid=(groups // per,),
        in_specs=[row_spec, row_spec],
        out_specs=[tab_spec, tab_spec],
        out_shape=[shape, shape],
        compiler_params=params(32),
        name="tables",
    )(fwd, bwd)


def pick_groups(wide, col, rows, per):
    lane_group = lax.broadcasted_iota(jnp.int32, (rows, LANES), 1) // (LANES // per)
    cols = slice(col * LANES, (col + 1) * LANES)
    out = wide[0:rows, cols]
    for g in range(1, per):
        out = jnp.where(lane_group == g, wide[g * rows : (g + 1) * rows, cols], out)
    return out


def forward_kernel(x_ref, h_ref, taps_ref, skip_ref, tab_ref, mixed_ref, f_ref, filt_ref, xf, pf, pb, wide):
    blocks, _, rows, _ = x_ref.shape
    tokens = blocks * rows
    per = tab_ref.shape[0] // LTAPS
    xf[0, LTAPS : LTAPS + PAD] = h_ref[0:PAD].astype(F32)
    for i in (1, 2):
        begin = PAD + (i - 1) * (LTAPS + PAD)
        xf[i, 0 : LTAPS + PAD] = h_ref[begin : begin + LTAPS + PAD].astype(F32)
    for i in range(3):
        for b in range(blocks):
            begin = LTAPS + PAD + b * rows
            xf[i, begin : begin + rows] = x_ref[b, i].astype(F32)

    def feature(i, base):
        total = taps_ref[i, 0:1] * xf[i, PAD + base : PAD + base + LTAPS]
        for j in range(1, SHORT):
            total = total + taps_ref[i, j : j + 1] * xf[i, PAD + base - j : PAD + base - j + LTAPS]
        return total

    for n in range(tokens // LTAPS + 1):
        base = n * LTAPS
        own = slice(base - LTAPS, base)
        f1 = feature(1, base)
        f2 = feature(2, base)
        prod = f1 * f2
        pb[base : base + LTAPS] = prod.astype(BF16)
        if n:
            f_ref[1, own] = f1
            f_ref[2, own] = f2
            f_ref[0, own] = feature(0, base)
            pf[own] = prod
    skip = skip_ref[...]
    for b in range(0, tokens // LTAPS, 2):
        low = b * LTAPS
        windows = jnp.concatenate([pb[low : low + 2 * LTAPS], pb[low + LTAPS : low + 3 * LTAPS]], axis=1)
        wide[...] = jnp.dot(tab_ref[...], windows, preferred_element_type=F32)
        for n in range(2):
            own = slice(low + n * LTAPS, low + (n + 1) * LTAPS)
            filtered = pick_groups(wide, n, LTAPS, per) + skip * pf[own]
            filt_ref[own] = filtered
            mixed_ref[own] = (f_ref[0, own] * filtered).astype(BF16)


def forward(x, halo, short_taps, skip, table):
    blocks, _, rows, cols = x.shape
    tokens = blocks * rows
    tiles = cols // LANES
    tab_rows = table.shape[0] // tiles
    tok = pl.BlockSpec((tokens, LANES), lambda c: (0, c))
    return pl.pallas_call(
        forward_kernel,
        grid=(tiles,),
        in_specs=[
            pl.BlockSpec((blocks, 3, rows, LANES), lambda c: (0, 0, 0, c)),
            pl.BlockSpec((halo.shape[0], LANES), lambda c: (0, c)),
            pl.BlockSpec((3, SHORT, LANES), lambda c: (0, 0, c)),
            pl.BlockSpec((1, LANES), lambda c: (0, c)),
            pl.BlockSpec((tab_rows, 2 * LTAPS), lambda c: (c, 0)),
        ],
        out_specs=[tok, pl.BlockSpec((3, tokens, LANES), lambda c: (0, 0, c)), tok],
        out_shape=[
            jax.ShapeDtypeStruct((tokens, cols), BF16),
            jax.ShapeDtypeStruct((3, tokens, cols), F32),
            jax.ShapeDtypeStruct((tokens, cols), F32),
        ],
        scratch_shapes=[
            pltpu.VMEM((3, PAD + LTAPS + tokens, LANES), F32),
            pltpu.VMEM((tokens, LANES), F32),
            pltpu.VMEM((LTAPS + tokens, LANES), BF16),
            pltpu.VMEM((tab_rows, 2 * LTAPS), F32),
        ],
        compiler_params=params(48),
        name="forward",
    )(x, halo, short_taps, skip, table)


def sum_by_lag(gram):
    wide = gram.shape[1]
    parts = [gram[i : i + 8] for i in range(0, gram.shape[0], 8)]
    step = 8
    while len(parts) > 1:
        parts = [
            parts[k] + pltpu.roll(parts[k + 1], wide - step, 1) for k in range(0, len(parts), 2)
        ]
        step *= 2
    total = parts[0]
    row = lax.broadcasted_iota(jnp.int32, total.shape, 0)
    for bit in (1, 2, 4):
        total = jnp.where((row & bit) != 0, pltpu.roll(total, wide - bit, 1), total)
    return jnp.sum(total[:, :LTAPS], axis=0, keepdims=True)


def backward_kernel(
    mo_ref, mr_ref, f_ref, filt_ref, x_ref, n_ref, taps_ref, skip_ref, tab_ref,
    grad_ref, short_ref, long_ref, db, fg, wide, left, right,
):
    blocks, _, rows, _ = x_ref.shape
    tokens = blocks * rows
    per = tab_ref.shape[0] // LTAPS
    count = tokens // LTAPS
    skip = skip_ref[...]
    lane_group = lax.broadcasted_iota(jnp.int32, (1, LANES), 1) // (LANES // per)
    gain = jnp.zeros((8, LANES), F32)
    for b in range(count):
        own = slice(b * LTAPS, (b + 1) * LTAPS)
        mixed_grad = mo_ref[own] + mr_ref[own].astype(F32)
        slope = mixed_grad * f_ref[0, own]
        db[own] = slope.astype(BF16)
        fg[0, own] = mixed_grad * filt_ref[own]
        fg[1, own] = skip * slope
        prod = f_ref[1, own] * f_ref[2, own]
        gain = gain + jnp.sum((prod * slope).reshape(LTAPS // 8, 8, LANES), axis=0)
        prod_b = prod.astype(BF16)
        for g in range(per):
            keep = (lane_group == g).astype(F32).astype(BF16)
            left[g * LTAPS : (g + 1) * LTAPS, b * LANES : (b + 1) * LANES] = prod_b * keep
    db[tokens : tokens + LTAPS + PAD] = n_ref[0 : LTAPS + PAD]
    db[tokens + LTAPS + PAD :] = jnp.zeros((LTAPS - PAD, LANES), BF16)
    for b in range(count):
        right[:, b * LANES : (b + 1) * LANES] = db[b * LTAPS : (b + 2) * LTAPS]
    for b in range(0, count, 2):
        wide[...] = jnp.dot(
            tab_ref[...], right[:, b * LANES : (b + 2) * LANES], preferred_element_type=F32
        )
        for n in range(2):
            own = slice((b + n) * LTAPS, (b + n + 1) * LTAPS)
            grad = pick_groups(wide, n, LTAPS, per) + fg[1, own]
            fg[1, own] = grad * f_ref[2, own]
            fg[2, own] = grad * f_ref[1, own]
    few = jnp.concatenate([tab_ref[g * LTAPS : g * LTAPS + PAD] for g in range(per)], axis=0)
    edge = jnp.dot(few, db[tokens : tokens + 2 * LTAPS], preferred_element_type=F32)
    begin = LTAPS + PAD
    grad = pick_groups(edge, 0, PAD, per) + skip * n_ref[0:PAD].astype(F32)
    fg[1, tokens : tokens + PAD] = grad * n_ref[begin + PAD : begin + 2 * PAD].astype(F32)
    fg[2, tokens : tokens + PAD] = grad * n_ref[begin : begin + PAD].astype(F32)
    fg[0, tokens : tokens + PAD] = n_ref[begin + 2 * PAD : begin + 3 * PAD].astype(F32)
    for i in range(3):
        sums = [jnp.zeros((8, LANES), F32) for _ in range(SHORT)]
        for b in range(count):
            low = b * LTAPS
            inputs = x_ref[b, i].astype(F32)
            total = None
            for j in range(SHORT):
                later = fg[i, low + j : low + j + LTAPS]
                term = taps_ref[i, j : j + 1] * later
                total = term if total is None else total + term
                sums[j] = sums[j] + jnp.sum((later * inputs).reshape(LTAPS // 8, 8, LANES), axis=0)
            grad_ref[b, i] = total.astype(BF16)
        for j in range(SHORT):
            short_ref[i, j : j + 1] = jnp.sum(sums[j], axis=0, keepdims=True)
        short_ref[i, SHORT : SHORT + 1] = jnp.sum(gain, axis=0, keepdims=True)
    wide[...] = lax.dot_general(left[...], right[...], (((1,), (1,)), ((), ())), preferred_element_type=F32)
    for g in range(per):
        gram = wide[g * LTAPS : (g + 1) * LTAPS]
        long_ref[g : g + 1] = sum_by_lag(gram)


def backward(mixed_own, mixed_rest, feats, filt, x, later, short_taps, skip, table):
    blocks, _, rows, cols = x.shape
    tokens = blocks * rows
    tiles = cols // LANES
    tab_rows = table.shape[0] // tiles
    per = tab_rows // LTAPS
    tok = pl.BlockSpec((tokens, LANES), lambda c: (0, c))
    xs = pl.BlockSpec((blocks, 3, rows, LANES), lambda c: (0, 0, 0, c))
    return pl.pallas_call(
        backward_kernel,
        grid=(tiles,),
        in_specs=[
            tok,
            tok,
            pl.BlockSpec((3, tokens, LANES), lambda c: (0, 0, c)),
            tok,
            xs,
            pl.BlockSpec((later.shape[0], LANES), lambda c: (0, c)),
            pl.BlockSpec((3, SHORT, LANES), lambda c: (0, 0, c)),
            pl.BlockSpec((1, LANES), lambda c: (0, c)),
            pl.BlockSpec((tab_rows, 2 * LTAPS), lambda c: (c, 0)),
        ],
        out_specs=[
            xs,
            pl.BlockSpec((3, SHORT + 1, LANES), lambda c: (0, 0, c)),
            pl.BlockSpec((per, LTAPS), lambda c: (c, 0)),
        ],
        out_shape=[
            jax.ShapeDtypeStruct(x.shape, BF16),
            jax.ShapeDtypeStruct((3, SHORT + 1, cols), F32),
            jax.ShapeDtypeStruct((tiles * per, LTAPS), F32),
        ],
        scratch_shapes=[
            pltpu.VMEM((tokens + 2 * LTAPS, LANES), BF16),
            pltpu.VMEM((3, tokens + PAD, LANES), F32),
            pltpu.VMEM((tab_rows, 2 * LTAPS), F32),
            pltpu.VMEM((tab_rows, tokens), BF16),
            pltpu.VMEM((2 * LTAPS, tokens), BF16),
        ],
        compiler_params=params(48),
        name="backward",
    )(mixed_own, mixed_rest, feats, filt, x, later, short_taps, skip, table)


def pack_kernel(q_ref, k_ref, v_ref, out_ref):
    for i, ref in enumerate((q_ref, k_ref, v_ref)):
        out_ref[0, i] = ref[...]


def pack(arrays, seq, chunks, chunk):
    rows, width = arrays[0].shape
    cols = width // seq // chunks
    source = pl.BlockSpec((rows, cols), lambda s: (0, s * chunks + chunk))
    return pl.pallas_call(
        pack_kernel,
        grid=(seq,),
        in_specs=[source] * 3,
        out_specs=pl.BlockSpec((1, 3, rows, cols), lambda s: (s, 0, 0, 0)),
        out_shape=jax.ShapeDtypeStruct((seq, 3, rows, cols), BF16),
        compiler_params=params(32),
        name="pack",
    )(*arrays)


def unpack_kernel(*refs):
    parts, outs = refs[:-3], refs[-3:]
    cols = parts[0].shape[3]
    for n, part in enumerate(parts):
        for i, out in enumerate(outs):
            out[:, n * cols : (n + 1) * cols] = part[0, i]


def unpack(parts):
    seq, _, rows, cols = parts[0].shape
    wide = cols * len(parts)
    shape = jax.ShapeDtypeStruct((rows, seq * wide), BF16)
    return pl.pallas_call(
        unpack_kernel,
        grid=(seq,),
        in_specs=[pl.BlockSpec((1, 3, rows, cols), lambda s: (s, 0, 0, 0))] * len(parts),
        out_specs=[pl.BlockSpec((rows, wide), lambda s: (0, s))] * 3,
        out_shape=[shape] * 3,
        compiler_params=params(32),
        name="unpack",
    )(*parts)


def along(block, axis, distance):
    size = lax.axis_size(axis)
    return lax.ppermute(block, axis, [(i, i + distance) for i in range(size) if 0 <= i + distance < size])


def around(block, axis, distance):
    size = lax.axis_size(axis)
    return lax.ppermute(block, axis, [(i, (i + distance) % size) for i in range(size)])


def across(block, axis, bit):
    return lax.ppermute(block, axis, [(i, i ^ bit) for i in range(lax.axis_size(axis))])


def bits_of(axis):
    size = lax.axis_size(axis)
    return [1 << n for n in range(size.bit_length() - 1)]


def sum_over(value, axes):
    for axis in axes:
        for bit in bits_of(axis):
            value = value + across(value, axis, bit)
    return value


def gather_cotangent(cotangent, col_part):
    rows = cotangent.shape[0]
    ys, y, s = lax.axis_size("y"), lax.axis_index("y"), lax.axis_index("seq")
    parts = cotangent.reshape(rows, Z, ys, col_part)
    held = []
    for step in range(ys):
        part = lax.dynamic_index_in_dim(parts, (y + step) % ys, 2, keepdims=False).reshape(rows, Z * col_part)
        held.append(around(part, "y", step) if step else part)
    held = jnp.stack(held)[:, None]
    for bit in reversed(bits_of("seq")):
        other = across(held, "seq", bit)
        upper = (s & bit) != 0
        low, high = jnp.where(upper, other, held), jnp.where(upper, held, other)
        held = jnp.stack([low, high], axis=2).reshape(ys, 2 * held.shape[1], rows, Z * col_part)
    return held.reshape(ys, held.shape[1] * rows, Z * col_part)


def contract(a, b, dim):
    return lax.dot_general(a, b, (((dim,), (dim,)), ((), ())), preferred_element_type=F32)


def body(queries, keys, values, cotangent, out_weight, short_taps, long_taps, skip_gain):
    rows, width = queries.shape
    col_part = out_weight.shape[1]
    seq, ys = lax.axis_size("seq"), lax.axis_size("y")
    cols = width // seq
    chunks = 2 if cols % (2 * LANES) == 0 else 1
    part = cols // chunks
    groups = long_taps.shape[1]
    fsdp = ("z", "y")
    grad_scale = float(rows * seq * ys * Z) ** (-0.5)
    edge = LTAPS + PAD

    weights = [
        lax.all_gather(out_weight[h * part : (h + 1) * part], "z", axis=1, tiled=True) for h in range(chunks)
    ]
    xs = [
        lax.all_to_all(
            pack((queries, keys, values), seq, chunks, h), "seq", split_axis=0, concat_axis=0, tiled=True
        )
        for h in range(chunks)
    ]
    cots = gather_cotangent(cotangent, col_part)
    fwd_table, bwd_table = make_tables(long_taps)
    skip = skip_gain.reshape(1, cols)

    mixers = []
    for h in range(chunks):
        x = xs[h]
        own = slice(h * part, (h + 1) * part)
        tab = slice(h * groups // chunks * LTAPS, (h + 1) * groups // chunks * LTAPS)
        tail = jnp.concatenate(
            [x[seq - 1, 0, rows - PAD :]]
            + [piece for i in (1, 2) for piece in (x[seq - 2, i, rows - PAD :], x[seq - 1, i])],
            axis=0,
        )
        halo = along(tail, fsdp, 1)
        taps, gain, table = short_taps[:, :, own], skip[:, own], bwd_table[tab]
        mixed, feats, filt = forward(x, halo, taps, gain, fwd_table[tab])
        mixers.append((x, mixed, feats, filt, taps, gain, table))

    weight_parts, grads, short_parts, long_parts = [], [], [], []
    for h in range(chunks):
        x, mixed, feats, filt, taps, gain, table = mixers[h]
        weight_sum = contract(mixed, cots[0], 0)
        for step in range(1, ys):
            weight_sum = weight_sum + contract(around(mixed, "y", step), cots[step], 0)
        weight_sum = (weight_sum * grad_scale).astype(BF16)
        weight_parts.append(lax.psum_scatter(weight_sum, "z", scatter_dimension=1, tiled=True))

        rest = [
            around(contract(cots[step], weights[h], 1).astype(BF16), "y", -step) for step in range(1, ys)
        ]
        mixed_rest = rest[0] if len(rest) == 1 else sum(piece.astype(F32) for piece in rest)
        mixed_own = contract(cots[0], weights[h], 1)
        head = mixed_own[:edge] + mixed_rest[:edge].astype(F32)
        head = jnp.concatenate(
            [head * feats[0, :edge], feats[1, :PAD], feats[2, :PAD], head[:PAD] * filt[:PAD]], axis=0
        ).astype(BF16)
        later = along(head, fsdp, -1)
        grad, short_part, long_part = backward(mixed_own, mixed_rest, feats, filt, x, later, taps, gain, table)
        grads.append(lax.all_to_all(grad, "seq", split_axis=0, concat_axis=0, tiled=True))
        short_parts.append(short_part)
        long_parts.append(long_part)

    query_grad, key_grad, value_grad = unpack(grads)
    packed = jnp.concatenate(
        [
            jnp.concatenate(short_parts, axis=2).reshape(3 * (SHORT + 1), cols),
            jnp.concatenate(long_parts, axis=0).reshape(-1, cols),
        ],
        axis=0,
    )
    packed = sum_over(packed, ("y", "z")) * grad_scale
    short_sum = packed[: 3 * (SHORT + 1)].reshape(3, SHORT + 1, cols)
    long_sum = packed[3 * (SHORT + 1) :].reshape(groups, LTAPS).T
    return (
        query_grad,
        key_grad,
        value_grad,
        jnp.concatenate(weight_parts, axis=0).astype(F32),
        short_sum[:, :SHORT],
        long_sum,
        short_sum[0, SHORT],
    )


def solution(mesh):
    fsdp, seq = mesh.shape["fsdp"], mesh.shape["seq"]
    split = Mesh(mesh.devices.reshape(Z, fsdp // Z, seq), ("z", "y", "seq"))
    tokens = P(("z", "y", "seq"), None)
    specs = (P("seq", ("z", "y")), P(None, None, "seq"), P(None, "seq"), P("seq"))
    return jax.shard_map(
        body,
        mesh=split,
        in_specs=(tokens,) * 4 + specs,
        out_specs=(tokens,) * 3 + specs,
        check_vma=False,
    )
```

```python
import functools

import jax
import jax.numpy as jnp
from jax import lax
from jax.experimental import pallas as pl
from jax.experimental.pallas import tpu as pltpu
from jax.sharding import Mesh
from jax.sharding import PartitionSpec as P

SHORT = 7
LTAPS = 128
LANES = 128
PAD = 16
Z = 4
F32 = jnp.float32
BF16 = jnp.bfloat16


def params(mib):
    return pltpu.CompilerParams(vmem_limit_bytes=mib * 2**20)


def cost(flops, nbytes):
    return pl.CostEstimate(flops=flops, bytes_accessed=nbytes, transcendentals=0)


def tables_kernel(fwd_ref, bwd_ref, tf_ref, tb_ref):
    for g in range(fwd_ref.shape[0]):
        rows = slice(g * LTAPS, (g + 1) * LTAPS)
        for src, dst in ((fwd_ref, tf_ref), (bwd_ref, tb_ref)):
            wide = jnp.broadcast_to(src[g : g + 1, :], (LTAPS, 2 * LTAPS))
            dst[rows, :] = pltpu.roll(wide, 0, 1, stride=1, stride_axis=0).astype(BF16)


def make_tables(long_taps):
    by_group = long_taps.T
    groups = by_group.shape[0]
    fwd = jnp.pad(by_group[:, ::-1], ((0, 0), (1, LTAPS - 1)))
    bwd = jnp.pad(by_group, ((0, 0), (0, LTAPS)))
    per = 8
    row_spec = pl.BlockSpec((per, 2 * LTAPS), lambda i: (i, 0))
    tab_spec = pl.BlockSpec((per * LTAPS, 2 * LTAPS), lambda i: (i, 0))
    shape = jax.ShapeDtypeStruct((groups * LTAPS, 2 * LTAPS), BF16)
    return pl.pallas_call(
        tables_kernel,
        grid=(groups // per,),
        in_specs=[row_spec, row_spec],
        out_specs=[tab_spec, tab_spec],
        out_shape=[shape, shape],
        compiler_params=params(32),
        name="tables",
    )(fwd, bwd)


def pick_groups(wide, col, rows, per):
    lane_group = lax.broadcasted_iota(jnp.int32, (rows, LANES), 1) // (LANES // per)
    cols = slice(col * LANES, (col + 1) * LANES)
    out = wide[0:rows, cols]
    for g in range(1, per):
        out = jnp.where(lane_group == g, wide[g * rows : (g + 1) * rows, cols], out)
    return out


def forward_kernel(place_ref, x_ref, h_ref, taps_ref, skip_ref, tab_ref, mixed_ref, f_ref, filt_ref, xf, pf, pb, wide):
    blocks, _, rows, _ = x_ref.shape
    tokens = blocks * rows
    per = tab_ref.shape[0] // LTAPS
    xf[0, LTAPS : LTAPS + PAD] = h_ref[0:PAD].astype(F32)
    for i in (1, 2):
        begin = PAD + (i - 1) * (LTAPS + PAD)
        xf[i, 0 : LTAPS + PAD] = h_ref[begin : begin + LTAPS + PAD].astype(F32)
    for i in range(3):
        for b in range(blocks):
            begin = LTAPS + PAD + b * rows
            xf[i, begin : begin + rows] = x_ref[b, i].astype(F32)

    def feature(i, base):
        total = taps_ref[i, 0:1] * xf[i, PAD + base : PAD + base + LTAPS]
        for j in range(1, SHORT):
            total = total + taps_ref[i, j : j + 1] * xf[i, PAD + base - j : PAD + base - j + LTAPS]
        return total

    for n in range(tokens // LTAPS + 1):
        base = n * LTAPS
        own = slice(base - LTAPS, base)
        f1 = feature(1, base)
        f2 = feature(2, base)
        prod = f1 * f2
        pb[base : base + LTAPS] = prod.astype(BF16)
        if n:
            f_ref[1, own] = f1
            f_ref[2, own] = f2
            f_ref[0, own] = feature(0, base)
            pf[own] = prod
    skip = skip_ref[...]
    for b in range(0, tokens // LTAPS, 2):
        low = b * LTAPS
        windows = jnp.concatenate([pb[low : low + 2 * LTAPS], pb[low + LTAPS : low + 3 * LTAPS]], axis=1)
        wide[...] = jnp.dot(tab_ref[...], windows, preferred_element_type=F32)
        for n in range(2):
            own = slice(low + n * LTAPS, low + (n + 1) * LTAPS)
            filtered = pick_groups(wide, n, LTAPS, per) + skip * pf[own]
            filt_ref[own] = filtered
            mixed = f_ref[0, own] * filtered
            there = pl.multiple_of(place_ref[b + n] * LTAPS, LTAPS)
            mixed_ref[:, pl.ds(there, LTAPS)] = mixed.T.astype(BF16)


def forward(x, halo, short_taps, skip, table, place, chunk):
    blocks, _, rows, cols = x.shape
    tokens = blocks * rows
    tiles = cols // LANES
    first = chunk * tiles
    tab_rows = table.shape[0] * LANES // skip.shape[1]
    return pl.pallas_call(
        forward_kernel,
        grid_spec=pltpu.PrefetchScalarGridSpec(
            num_scalar_prefetch=1,
            grid=(tiles,),
            in_specs=[
                pl.BlockSpec((blocks, 3, rows, LANES), lambda c, _: (0, 0, 0, c)),
                pl.BlockSpec((halo.shape[0], LANES), lambda c, _: (0, c)),
                pl.BlockSpec((3, SHORT, LANES), lambda c, _: (0, 0, first + c)),
                pl.BlockSpec((1, LANES), lambda c, _: (0, first + c)),
                pl.BlockSpec((tab_rows, 2 * LTAPS), lambda c, _: (first + c, 0)),
            ],
            out_specs=[
                pl.BlockSpec((LANES, tokens), lambda c, _: (c, 0)),
                pl.BlockSpec((3, tokens, LANES), lambda c, _: (0, 0, c)),
                pl.BlockSpec((tokens, LANES), lambda c, _: (0, c)),
            ],
            scratch_shapes=[
                pltpu.VMEM((3, PAD + LTAPS + tokens, LANES), F32),
                pltpu.VMEM((tokens, LANES), F32),
                pltpu.VMEM((LTAPS + tokens, LANES), BF16),
                pltpu.VMEM((tab_rows, 2 * LTAPS), F32),
            ],
        ),
        out_shape=[
            jax.ShapeDtypeStruct((cols, tokens), BF16),
            jax.ShapeDtypeStruct((3, tokens, cols), F32),
            jax.ShapeDtypeStruct((tokens, cols), F32),
        ],
        compiler_params=params(48),
        cost_estimate=cost(4 * LTAPS * tokens * tab_rows, 24 * tokens * cols),
        name="forward",
    )(place, x, halo, short_taps, skip, table)


def sum_by_lag(gram):
    wide = gram.shape[1]
    parts = [gram[i : i + 8] for i in range(0, gram.shape[0], 8)]
    step = 8
    while len(parts) > 1:
        parts = [
            parts[k] + pltpu.roll(parts[k + 1], wide - step, 1) for k in range(0, len(parts), 2)
        ]
        step *= 2
    total = parts[0]
    row = lax.broadcasted_iota(jnp.int32, total.shape, 0)
    for bit in (1, 2, 4):
        total = jnp.where((row & bit) != 0, pltpu.roll(total, wide - bit, 1), total)
    return jnp.sum(total[:, :LTAPS], axis=0, keepdims=True)


def backward_kernel(
    mo_ref, mr_ref, f_ref, filt_ref, x_ref, n_ref, taps_ref, skip_ref, tab_ref,
    grad_ref, short_ref, long_ref, db, fg, wide, left, right,
):
    blocks, _, rows, _ = x_ref.shape
    tokens = blocks * rows
    per = tab_ref.shape[0] // LTAPS
    count = tokens // LTAPS
    skip = skip_ref[...]
    lane_group = lax.broadcasted_iota(jnp.int32, (1, LANES), 1) // (LANES // per)
    gain = jnp.zeros((8, LANES), F32)
    for b in range(count):
        own = slice(b * LTAPS, (b + 1) * LTAPS)
        mixed_grad = mo_ref[own] + mr_ref[own].astype(F32)
        slope = mixed_grad * f_ref[0, own]
        db[own] = slope.astype(BF16)
        fg[0, own] = mixed_grad * filt_ref[own]
        fg[1, own] = skip * slope
        prod = f_ref[1, own] * f_ref[2, own]
        gain = gain + jnp.sum((prod * slope).reshape(LTAPS // 8, 8, LANES), axis=0)
        prod_b = prod.astype(BF16)
        for g in range(per):
            keep = (lane_group == g).astype(F32).astype(BF16)
            left[g * LTAPS : (g + 1) * LTAPS, b * LANES : (b + 1) * LANES] = prod_b * keep
    db[tokens : tokens + LTAPS + PAD] = n_ref[0 : LTAPS + PAD]
    db[tokens + LTAPS + PAD :] = jnp.zeros((LTAPS - PAD, LANES), BF16)
    for b in range(count):
        right[:, b * LANES : (b + 1) * LANES] = db[b * LTAPS : (b + 2) * LTAPS]
    for b in range(0, count, 2):
        wide[...] = jnp.dot(
            tab_ref[...], right[:, b * LANES : (b + 2) * LANES], preferred_element_type=F32
        )
        for n in range(2):
            own = slice((b + n) * LTAPS, (b + n + 1) * LTAPS)
            grad = pick_groups(wide, n, LTAPS, per) + fg[1, own]
            fg[1, own] = grad * f_ref[2, own]
            fg[2, own] = grad * f_ref[1, own]
    few = jnp.concatenate([tab_ref[g * LTAPS : g * LTAPS + PAD] for g in range(per)], axis=0)
    edge = jnp.dot(few, db[tokens : tokens + 2 * LTAPS], preferred_element_type=F32)
    begin = LTAPS + PAD
    grad = pick_groups(edge, 0, PAD, per) + skip * n_ref[0:PAD].astype(F32)
    fg[1, tokens : tokens + PAD] = grad * n_ref[begin + PAD : begin + 2 * PAD].astype(F32)
    fg[2, tokens : tokens + PAD] = grad * n_ref[begin : begin + PAD].astype(F32)
    fg[0, tokens : tokens + PAD] = n_ref[begin + 2 * PAD : begin + 3 * PAD].astype(F32)
    for i in range(3):
        sums = [jnp.zeros((8, LANES), F32) for _ in range(SHORT)]
        for b in range(count):
            low = b * LTAPS
            inputs = x_ref[b, i].astype(F32)
            total = None
            for j in range(SHORT):
                later = fg[i, low + j : low + j + LTAPS]
                term = taps_ref[i, j : j + 1] * later
                total = term if total is None else total + term
                sums[j] = sums[j] + jnp.sum((later * inputs).reshape(LTAPS // 8, 8, LANES), axis=0)
            grad_ref[b, i] = total.astype(BF16)
        for j in range(SHORT):
            short_ref[i, j : j + 1] = jnp.sum(sums[j], axis=0, keepdims=True)
        short_ref[i, SHORT : SHORT + 1] = jnp.sum(gain, axis=0, keepdims=True)
    wide[...] = lax.dot_general(left[...], right[...], (((1,), (1,)), ((), ())), preferred_element_type=F32)
    for g in range(per):
        gram = wide[g * LTAPS : (g + 1) * LTAPS]
        long_ref[g : g + 1] = sum_by_lag(gram)


def backward(mixed_own, mixed_rest, feats, filt, x, later, short_taps, skip, table, chunk):
    blocks, _, rows, cols = x.shape
    tokens = blocks * rows
    tiles = cols // LANES
    first = chunk * tiles
    tab_rows = table.shape[0] * LANES // skip.shape[1]
    per = tab_rows // LTAPS
    tok = pl.BlockSpec((tokens, LANES), lambda c: (0, c))
    xs = pl.BlockSpec((blocks, 3, rows, LANES), lambda c: (0, 0, 0, c))
    return pl.pallas_call(
        backward_kernel,
        grid=(tiles,),
        in_specs=[
            tok,
            tok,
            pl.BlockSpec((3, tokens, LANES), lambda c: (0, 0, c)),
            tok,
            xs,
            pl.BlockSpec((later.shape[0], LANES), lambda c: (0, c)),
            pl.BlockSpec((3, SHORT, LANES), lambda c: (0, 0, first + c)),
            pl.BlockSpec((1, LANES), lambda c: (0, first + c)),
            pl.BlockSpec((tab_rows, 2 * LTAPS), lambda c: (first + c, 0)),
        ],
        out_specs=[
            xs,
            pl.BlockSpec((3, SHORT + 1, LANES), lambda c: (0, 0, c)),
            pl.BlockSpec((per, LTAPS), lambda c: (c, 0)),
        ],
        out_shape=[
            jax.ShapeDtypeStruct(x.shape, BF16),
            jax.ShapeDtypeStruct((3, SHORT + 1, cols), F32),
            jax.ShapeDtypeStruct((tiles * per, LTAPS), F32),
        ],
        scratch_shapes=[
            pltpu.VMEM((tokens + 2 * LTAPS, LANES), BF16),
            pltpu.VMEM((3, tokens + PAD, LANES), F32),
            pltpu.VMEM((tab_rows, 2 * LTAPS), F32),
            pltpu.VMEM((tab_rows, tokens), BF16),
            pltpu.VMEM((2 * LTAPS, tokens), BF16),
        ],
        compiler_params=params(48),
        cost_estimate=cost(8 * LTAPS * tokens * tab_rows, 36 * tokens * cols),
        name="backward",
    )(mixed_own, mixed_rest, feats, filt, x, later, short_taps, skip, table)


def pack_kernel(q_ref, k_ref, v_ref, out_ref):
    for i, ref in enumerate((q_ref, k_ref, v_ref)):
        out_ref[0, i] = ref[...]


def pack(arrays, seq, chunks, chunk):
    rows, width = arrays[0].shape
    cols = width // seq // chunks
    source = pl.BlockSpec((rows, cols), lambda s: (0, s * chunks + chunk))
    return pl.pallas_call(
        pack_kernel,
        grid=(seq,),
        in_specs=[source] * 3,
        out_specs=pl.BlockSpec((1, 3, rows, cols), lambda s: (s, 0, 0, 0)),
        out_shape=jax.ShapeDtypeStruct((seq, 3, rows, cols), BF16),
        compiler_params=params(32),
        name="pack",
    )(*arrays)


def unpack_kernel(*refs):
    parts, outs = refs[:-3], refs[-3:]
    cols = parts[0].shape[3]
    for n, part in enumerate(parts):
        for i, out in enumerate(outs):
            out[:, n * cols : (n + 1) * cols] = part[0, i]


def unpack(parts):
    seq, _, rows, cols = parts[0].shape
    wide = cols * len(parts)
    shape = jax.ShapeDtypeStruct((rows, seq * wide), BF16)
    return pl.pallas_call(
        unpack_kernel,
        grid=(seq,),
        in_specs=[pl.BlockSpec((1, 3, rows, cols), lambda s: (s, 0, 0, 0))] * len(parts),
        out_specs=[pl.BlockSpec((rows, wide), lambda s: (0, s))] * 3,
        out_shape=[shape] * 3,
        compiler_params=params(32),
        name="unpack",
    )(*parts)


def along(block, axis, distance):
    size = lax.axis_size(axis)
    return lax.ppermute(block, axis, [(i, i + distance) for i in range(size) if 0 <= i + distance < size])


def around(block, axis, distance):
    size = lax.axis_size(axis)
    return lax.ppermute(block, axis, [(i, (i + distance) % size) for i in range(size)])


def across(block, axis, bit):
    return lax.ppermute(block, axis, [(i, i ^ bit) for i in range(lax.axis_size(axis))])


def bits_of(axis):
    size = lax.axis_size(axis)
    return [1 << n for n in range(size.bit_length() - 1)]


def sum_over(value, axes):
    for axis in axes:
        for bit in bits_of(axis):
            value = value + across(value, axis, bit)
    return value


def split_kernel(y_ref, *refs):
    count = len(refs) // 2
    for n in range(count):
        refs[count + n][...] = refs[n][...]


def split_cotangent(cotangent, y, ys, col_part):
    rows, width = cotangent.shape

    def source(step):
        return pl.BlockSpec((rows, col_part), lambda z, y_ref: (0, z * ys + (y_ref[0] + step) % ys))

    return pl.pallas_call(
        split_kernel,
        grid_spec=pltpu.PrefetchScalarGridSpec(
            num_scalar_prefetch=1,
            grid=(Z,),
            in_specs=[source(step) for step in range(ys)],
            out_specs=[pl.BlockSpec((rows, col_part), lambda z, _: (0, z))] * ys,
        ),
        out_shape=[jax.ShapeDtypeStruct((rows, width // ys), BF16)] * ys,
        compiler_params=params(32),
        name="split",
    )(y.reshape(1), *([cotangent] * ys))


def join_kernel(axis, count, *refs):
    out = refs[-1]
    for n in range(count):
        size = refs[n].shape[axis]
        here = slice(n * size, (n + 1) * size)
        if axis == 0:
            out[here] = refs[n][...]
        else:
            out[:, here] = refs[n][...]


def join(parts, axis, after=()):
    shape = list(parts[0].shape)
    tile = shape[-1] // Z
    block = pl.BlockSpec((*shape[:-1], tile), lambda i: (0, 0, 0, i))
    shape[axis] *= len(parts)
    return pl.pallas_call(
        functools.partial(join_kernel, axis, len(parts)),
        grid=(Z,),
        in_specs=[block] * len(parts) + [pl.BlockSpec(memory_space=pl.ANY)] * len(after),
        out_specs=pl.BlockSpec((*shape[:-1], tile), lambda i: (0, 0, 0, i)),
        out_shape=jax.ShapeDtypeStruct(tuple(shape), BF16),
        compiler_params=params(32),
        name="join",
    )(*parts, *after)


def gather_cotangent(cotangent, col_part, after):
    ys, y = lax.axis_size("y"), lax.axis_index("y")
    held = split_cotangent(cotangent, y, ys, col_part)
    held = [around(part, "y", step) if step else part for step, part in enumerate(held)]
    held = join([part[None, None] for part in held], 0, after)
    bits = bits_of("seq")
    for bit in reversed(bits[1:]):
        held = join([held, across(held, "seq", bit)], 1)
    return held, across(held, "seq", bits[0])


def mixed_grad_kernel(place_ref, a_ref, b_ref, w_ref, out_ref, found):
    _, count, rows, _ = a_ref.shape
    tokens = count * rows
    for n, ref in enumerate((a_ref, b_ref)):
        found[n * tokens : (n + 1) * tokens] = contract(ref[0].reshape(tokens, -1), w_ref[...], 1)
    for block in range(2 * count):
        there = pl.multiple_of(place_ref[block] * rows, rows)
        out_ref[block * rows : (block + 1) * rows] = found[pl.ds(there, rows)].astype(out_ref.dtype)


def mixed_grad(cots, weights, place, step, part, chunk, dtype):
    _, count, rows, width = cots[0].shape
    tokens = 2 * count * rows
    tile = min(part, 2 * LANES)
    piece = pl.BlockSpec((1, count, rows, width), lambda i, _: (step, 0, 0, 0))
    return pl.pallas_call(
        mixed_grad_kernel,
        grid_spec=pltpu.PrefetchScalarGridSpec(
            num_scalar_prefetch=1,
            grid=(part // tile,),
            in_specs=[piece, piece, pl.BlockSpec((tile, width), lambda i, _: (chunk * (part // tile) + i, 0))],
            out_specs=pl.BlockSpec((tokens, tile), lambda i, _: (0, i)),
            scratch_shapes=[pltpu.VMEM((tokens, tile), F32)],
        ),
        out_shape=jax.ShapeDtypeStruct((tokens, part), dtype),
        compiler_params=params(48),
        cost_estimate=cost(2 * tokens * width * part, 2 * (tokens + part) * width + 4 * tokens * part),
        name="mixed_grad",
    )(place, *cots, weights)


def weight_grad_kernel(scale, chunks, a_ref, b_ref, *refs):
    mixed, out = refs[:-1], refs[-1]
    steps, count, rows, tile = a_ref.shape
    tokens = count * rows
    part = mixed[0].shape[0]
    for h in range(chunks):
        total = None
        for step in range(steps):
            for n, ref in enumerate((a_ref, b_ref)):
                left = mixed[step * chunks + h][:, n * tokens : (n + 1) * tokens]
                term = jnp.dot(left, ref[step].reshape(tokens, tile), preferred_element_type=F32)
                total = term if total is None else total + term
        out[h * part : (h + 1) * part] = (total * scale).astype(BF16)


def weight_grad(cots, mixed, chunks, scale):
    steps, count, rows, width = cots[0].shape
    part, tokens = mixed[0].shape
    tile = width // Z
    piece = pl.BlockSpec((steps, count, rows, tile), lambda i: (0, 0, 0, i))
    return pl.pallas_call(
        functools.partial(weight_grad_kernel, scale, chunks),
        grid=(Z,),
        in_specs=[piece, piece] + [pl.BlockSpec((part, tokens), lambda i: (0, 0))] * len(mixed),
        out_specs=pl.BlockSpec((part * chunks, tile), lambda i: (0, i)),
        out_shape=jax.ShapeDtypeStruct((part * chunks, width), BF16),
        compiler_params=params(48),
        cost_estimate=cost(
            2 * part * chunks * steps * tokens * width, 2 * (steps * tokens + part * chunks) * width
        ),
        name="weight_grad",
    )(*cots, *mixed)


def tail_kernel(x_ref, before_ref, out_ref):
    rows = x_ref.shape[2]
    out_ref[0:PAD] = x_ref[0, 0, rows - PAD :]
    for i in (1, 2):
        begin = PAD + (i - 1) * (PAD + rows)
        out_ref[begin : begin + PAD] = before_ref[0, i, rows - PAD :]
        out_ref[begin + PAD : begin + PAD + rows] = x_ref[0, i]


def tail_of(x):
    seq, _, rows, cols = x.shape

    def block(s):
        return pl.BlockSpec((1, 3, rows, cols), lambda i: (s, 0, 0, 0))

    out_rows = PAD + 2 * (PAD + rows)
    return pl.pallas_call(
        tail_kernel,
        grid=(1,),
        in_specs=[block(seq - 1), block(seq - 2)],
        out_specs=pl.BlockSpec((out_rows, cols), lambda i: (0, 0)),
        out_shape=jax.ShapeDtypeStruct((out_rows, cols), BF16),
        compiler_params=params(32),
        name="tail",
    )(x, x)


def head_kernel(mo_ref, mr_ref, f_ref, filt_ref, out_ref):
    edge = LTAPS + PAD
    mixed = mo_ref[...] + mr_ref[...].astype(F32)
    out_ref[0:edge] = (mixed * f_ref[0]).astype(BF16)
    out_ref[edge : edge + PAD] = f_ref[1, 0:PAD].astype(BF16)
    out_ref[edge + PAD : edge + 2 * PAD] = f_ref[2, 0:PAD].astype(BF16)
    out_ref[edge + 2 * PAD :] = (mixed[0:PAD] * filt_ref[0:PAD]).astype(BF16)


def head_of(mixed_own, mixed_rest, feats, filt):
    edge, cols = LTAPS + PAD, filt.shape[1]
    first = pl.BlockSpec((edge, cols), lambda i: (0, 0))
    return pl.pallas_call(
        head_kernel,
        grid=(1,),
        in_specs=[first, first, pl.BlockSpec((3, edge, cols), lambda i: (0, 0, 0)), first],
        out_specs=pl.BlockSpec((edge + 3 * PAD, cols), lambda i: (0, 0)),
        out_shape=jax.ShapeDtypeStruct((edge + 3 * PAD, cols), BF16),
        compiler_params=params(32),
        name="head",
    )(mixed_own, mixed_rest, feats, filt)


def contract(a, b, dim):
    return lax.dot_general(a, b, (((dim,), (dim,)), ((), ())), preferred_element_type=F32)


def places(seq):
    bits = bits_of("seq")
    source = lax.iota(jnp.int32, seq) ^ lax.axis_index("seq")
    return sum(((source >> n) & 1) << (len(bits) - 1 - n) for n in range(len(bits)))


def body(queries, keys, values, cotangent, out_weight, short_taps, long_taps, skip_gain):
    rows, width = queries.shape
    col_part = out_weight.shape[1]
    seq, ys = lax.axis_size("seq"), lax.axis_size("y")
    cols = width // seq
    chunks = 2 if cols % (2 * LANES) == 0 else 1
    part = cols // chunks
    groups = long_taps.shape[1]
    fsdp = ("z", "y")
    grad_scale = float(rows * seq * ys * Z) ** (-0.5)

    weights = lax.all_gather(out_weight, "z", axis=1, tiled=True)
    xs = [
        lax.all_to_all(
            pack((queries, keys, values), seq, chunks, h), "seq", split_axis=0, concat_axis=0, tiled=True
        )
        for h in range(chunks)
    ]
    cots = gather_cotangent(cotangent, col_part, xs[-1:])
    fwd_table, bwd_table = make_tables(long_taps)
    skip = skip_gain.reshape(1, cols)
    place = places(seq)

    mixers = []
    for h in range(chunks):
        halo = along(tail_of(xs[h]), fsdp, 1)
        mixers.append(forward(xs[h], halo, short_taps, skip, fwd_table, place, h))

    mixed_all = [
        around(mixers[h][0], "y", step) if step else mixers[h][0] for step in range(ys) for h in range(chunks)
    ]
    weight_sum = weight_grad(cots, mixed_all, chunks, grad_scale)
    weight_part = lax.psum_scatter(weight_sum, "z", scatter_dimension=1, tiled=True)

    grads, short_parts, long_parts = [], [], []
    for h in range(chunks):
        _, feats, filt = mixers[h]
        rest = [
            around(mixed_grad(cots, weights, place, step, part, h, BF16), "y", -step) for step in range(1, ys)
        ]
        mixed_rest = rest[0] if len(rest) == 1 else sum(piece.astype(F32) for piece in rest)
        mixed_own = mixed_grad(cots, weights, place, 0, part, h, F32)
        later = along(head_of(mixed_own, mixed_rest, feats, filt), fsdp, -1)
        grad, short_part, long_part = backward(
            mixed_own, mixed_rest, feats, filt, xs[h], later, short_taps, skip, bwd_table, h
        )
        grads.append(lax.all_to_all(grad, "seq", split_axis=0, concat_axis=0, tiled=True))
        short_parts.append(short_part)
        long_parts.append(long_part)

    query_grad, key_grad, value_grad = unpack(grads)
    packed = jnp.concatenate(
        [
            jnp.concatenate(short_parts, axis=2).reshape(3 * (SHORT + 1), cols),
            jnp.concatenate(long_parts, axis=0).reshape(-1, cols),
        ],
        axis=0,
    )
    packed = sum_over(packed, ("y", "z")) * grad_scale
    short_sum = packed[: 3 * (SHORT + 1)].reshape(3, SHORT + 1, cols)
    long_sum = packed[3 * (SHORT + 1) :].reshape(groups, LTAPS).T
    return (
        query_grad,
        key_grad,
        value_grad,
        weight_part.astype(F32),
        short_sum[:, :SHORT],
        long_sum,
        short_sum[0, SHORT],
    )


def solution(mesh):
    fsdp, seq = mesh.shape["fsdp"], mesh.shape["seq"]
    split = Mesh(mesh.devices.reshape(Z, fsdp // Z, seq), ("z", "y", "seq"))
    tokens = P(("z", "y", "seq"), None)
    specs = (P("seq", ("z", "y")), P(None, None, "seq"), P(None, "seq"), P("seq"))
    return jax.shard_map(
        body,
        mesh=split,
        in_specs=(tokens,) * 4 + specs,
        out_specs=(tokens,) * 3 + specs,
        check_vma=False,
    )
```

```python
import functools

import jax
import jax.numpy as jnp
from jax import lax
from jax.experimental import pallas as pl
from jax.experimental.pallas import tpu as pltpu
from jax.sharding import Mesh
from jax.sharding import PartitionSpec as P

SHORT = 7
LTAPS = 128
LANES = 128
PAD = 16
Z = 4
F32 = jnp.float32
BF16 = jnp.bfloat16


def params(mib):
    return pltpu.CompilerParams(vmem_limit_bytes=mib * 2**20)


def cost(flops, nbytes):
    return pl.CostEstimate(flops=flops, bytes_accessed=nbytes, transcendentals=0)


def tables_kernel(fwd_ref, bwd_ref, tf_ref, tb_ref):
    for g in range(fwd_ref.shape[0]):
        rows = slice(g * LTAPS, (g + 1) * LTAPS)
        for src, dst in ((fwd_ref, tf_ref), (bwd_ref, tb_ref)):
            wide = jnp.broadcast_to(src[g : g + 1, :], (LTAPS, 2 * LTAPS))
            dst[rows, :] = pltpu.roll(wide, 0, 1, stride=1, stride_axis=0).astype(BF16)


def make_tables(long_taps):
    by_group = long_taps.T
    groups = by_group.shape[0]
    fwd = jnp.pad(by_group[:, ::-1], ((0, 0), (1, LTAPS - 1)))
    bwd = jnp.pad(by_group, ((0, 0), (0, LTAPS)))
    per = 8
    row_spec = pl.BlockSpec((per, 2 * LTAPS), lambda i: (i, 0))
    tab_spec = pl.BlockSpec((per * LTAPS, 2 * LTAPS), lambda i: (i, 0))
    shape = jax.ShapeDtypeStruct((groups * LTAPS, 2 * LTAPS), BF16)
    return pl.pallas_call(
        tables_kernel,
        grid=(groups // per,),
        in_specs=[row_spec, row_spec],
        out_specs=[tab_spec, tab_spec],
        out_shape=[shape, shape],
        compiler_params=params(32),
        name="tables",
    )(fwd, bwd)


def pick_groups(wide, col, rows, per):
    lane_group = lax.broadcasted_iota(jnp.int32, (rows, LANES), 1) // (LANES // per)
    cols = slice(col * LANES, (col + 1) * LANES)
    out = wide[0:rows, cols]
    for g in range(1, per):
        out = jnp.where(lane_group == g, wide[g * rows : (g + 1) * rows, cols], out)
    return out


def forward_kernel(place_ref, x_ref, h_ref, taps_ref, skip_ref, tab_ref, mixed_ref, f_ref, filt_ref, xf, pf, pb, wide):
    blocks, _, rows, _ = x_ref.shape
    tokens = blocks * rows
    per = tab_ref.shape[0] // LTAPS
    xf[0, LTAPS : LTAPS + PAD] = h_ref[0:PAD].astype(F32)
    for i in (1, 2):
        begin = PAD + (i - 1) * (LTAPS + PAD)
        xf[i, 0 : LTAPS + PAD] = h_ref[begin : begin + LTAPS + PAD].astype(F32)
    for i in range(3):
        for b in range(blocks):
            begin = LTAPS + PAD + b * rows
            xf[i, begin : begin + rows] = x_ref[b, i].astype(F32)

    def feature(i, base):
        total = taps_ref[i, 0:1] * xf[i, PAD + base : PAD + base + LTAPS]
        for j in range(1, SHORT):
            total = total + taps_ref[i, j : j + 1] * xf[i, PAD + base - j : PAD + base - j + LTAPS]
        return total

    for n in range(tokens // LTAPS + 1):
        base = n * LTAPS
        own = slice(base - LTAPS, base)
        f1 = feature(1, base)
        f2 = feature(2, base)
        prod = f1 * f2
        pb[base : base + LTAPS] = prod.astype(BF16)
        if n:
            f_ref[1, own] = f1
            f_ref[2, own] = f2
            f_ref[0, own] = feature(0, base)
            pf[own] = prod
    skip = skip_ref[...]
    for b in range(0, tokens // LTAPS, 2):
        low = b * LTAPS
        windows = jnp.concatenate([pb[low : low + 2 * LTAPS], pb[low + LTAPS : low + 3 * LTAPS]], axis=1)
        wide[...] = jnp.dot(tab_ref[...], windows, preferred_element_type=F32)
        for n in range(2):
            own = slice(low + n * LTAPS, low + (n + 1) * LTAPS)
            filtered = pick_groups(wide, n, LTAPS, per) + skip * pf[own]
            filt_ref[own] = filtered
            mixed = f_ref[0, own] * filtered
            there = pl.multiple_of(place_ref[b + n] * LTAPS, LTAPS)
            mixed_ref[:, pl.ds(there, LTAPS)] = mixed.T.astype(BF16)


def forward(x, halo, short_taps, skip, table, place, chunk):
    blocks, _, rows, cols = x.shape
    tokens = blocks * rows
    tiles = cols // LANES
    first = chunk * tiles
    tab_rows = table.shape[0] * LANES // skip.shape[1]
    return pl.pallas_call(
        forward_kernel,
        grid_spec=pltpu.PrefetchScalarGridSpec(
            num_scalar_prefetch=1,
            grid=(tiles,),
            in_specs=[
                pl.BlockSpec((blocks, 3, rows, LANES), lambda c, _: (0, 0, 0, c)),
                pl.BlockSpec((halo.shape[0], LANES), lambda c, _: (0, c)),
                pl.BlockSpec((3, SHORT, LANES), lambda c, _: (0, 0, first + c)),
                pl.BlockSpec((1, LANES), lambda c, _: (0, first + c)),
                pl.BlockSpec((tab_rows, 2 * LTAPS), lambda c, _: (first + c, 0)),
            ],
            out_specs=[
                pl.BlockSpec((LANES, tokens), lambda c, _: (c, 0)),
                pl.BlockSpec((3, tokens, LANES), lambda c, _: (0, 0, c)),
                pl.BlockSpec((tokens, LANES), lambda c, _: (0, c)),
            ],
            scratch_shapes=[
                pltpu.VMEM((3, PAD + LTAPS + tokens, LANES), F32),
                pltpu.VMEM((tokens, LANES), F32),
                pltpu.VMEM((LTAPS + tokens, LANES), BF16),
                pltpu.VMEM((tab_rows, 2 * LTAPS), F32),
            ],
        ),
        out_shape=[
            jax.ShapeDtypeStruct((cols, tokens), BF16),
            jax.ShapeDtypeStruct((3, tokens, cols), F32),
            jax.ShapeDtypeStruct((tokens, cols), F32),
        ],
        compiler_params=params(48),
        cost_estimate=cost(4 * LTAPS * tokens * tab_rows, 24 * tokens * cols),
        name="forward",
    )(place, x, halo, short_taps, skip, table)


def sum_by_lag(gram):
    wide = gram.shape[1]
    parts = [gram[i : i + 8] for i in range(0, gram.shape[0], 8)]
    step = 8
    while len(parts) > 1:
        parts = [
            parts[k] + pltpu.roll(parts[k + 1], wide - step, 1) for k in range(0, len(parts), 2)
        ]
        step *= 2
    total = parts[0]
    row = lax.broadcasted_iota(jnp.int32, total.shape, 0)
    for bit in (1, 2, 4):
        total = jnp.where((row & bit) != 0, pltpu.roll(total, wide - bit, 1), total)
    return jnp.sum(total[:, :LTAPS], axis=0, keepdims=True)


def backward_kernel(
    mo_ref, mr_ref, f_ref, filt_ref, x_ref, n_ref, taps_ref, skip_ref, tab_ref,
    grad_ref, short_ref, long_ref, db, fg, wide, left, right,
):
    blocks, _, rows, _ = x_ref.shape
    tokens = blocks * rows
    per = tab_ref.shape[0] // LTAPS
    count = tokens // LTAPS
    skip = skip_ref[...]
    lane_group = lax.broadcasted_iota(jnp.int32, (1, LANES), 1) // (LANES // per)
    gain = jnp.zeros((8, LANES), F32)
    for b in range(count):
        own = slice(b * LTAPS, (b + 1) * LTAPS)
        mixed_grad = mo_ref[own] + mr_ref[own].astype(F32)
        slope = mixed_grad * f_ref[0, own]
        db[own] = slope.astype(BF16)
        fg[0, own] = mixed_grad * filt_ref[own]
        fg[1, own] = skip * slope
        prod = f_ref[1, own] * f_ref[2, own]
        gain = gain + jnp.sum((prod * slope).reshape(LTAPS // 8, 8, LANES), axis=0)
        prod_b = prod.astype(BF16)
        for g in range(per):
            keep = (lane_group == g).astype(F32).astype(BF16)
            left[g * LTAPS : (g + 1) * LTAPS, b * LANES : (b + 1) * LANES] = prod_b * keep
    db[tokens : tokens + LTAPS + PAD] = n_ref[0 : LTAPS + PAD]
    db[tokens + LTAPS + PAD :] = jnp.zeros((LTAPS - PAD, LANES), BF16)
    for b in range(count):
        right[:, b * LANES : (b + 1) * LANES] = db[b * LTAPS : (b + 2) * LTAPS]
    for b in range(0, count, 2):
        wide[...] = jnp.dot(
            tab_ref[...], right[:, b * LANES : (b + 2) * LANES], preferred_element_type=F32
        )
        for n in range(2):
            own = slice((b + n) * LTAPS, (b + n + 1) * LTAPS)
            grad = pick_groups(wide, n, LTAPS, per) + fg[1, own]
            fg[1, own] = grad * f_ref[2, own]
            fg[2, own] = grad * f_ref[1, own]
    few = jnp.concatenate([tab_ref[g * LTAPS : g * LTAPS + PAD] for g in range(per)], axis=0)
    edge = jnp.dot(few, db[tokens : tokens + 2 * LTAPS], preferred_element_type=F32)
    begin = LTAPS + PAD
    grad = pick_groups(edge, 0, PAD, per) + skip * n_ref[0:PAD].astype(F32)
    fg[1, tokens : tokens + PAD] = grad * n_ref[begin + PAD : begin + 2 * PAD].astype(F32)
    fg[2, tokens : tokens + PAD] = grad * n_ref[begin : begin + PAD].astype(F32)
    fg[0, tokens : tokens + PAD] = n_ref[begin + 2 * PAD : begin + 3 * PAD].astype(F32)
    for i in range(3):
        sums = [jnp.zeros((8, LANES), F32) for _ in range(SHORT)]
        for b in range(count):
            low = b * LTAPS
            inputs = x_ref[b, i].astype(F32)
            total = None
            for j in range(SHORT):
                later = fg[i, low + j : low + j + LTAPS]
                term = taps_ref[i, j : j + 1] * later
                total = term if total is None else total + term
                sums[j] = sums[j] + jnp.sum((later * inputs).reshape(LTAPS // 8, 8, LANES), axis=0)
            grad_ref[b, i] = total.astype(BF16)
        for j in range(SHORT):
            short_ref[i, j : j + 1] = jnp.sum(sums[j], axis=0, keepdims=True)
        short_ref[i, SHORT : SHORT + 1] = jnp.sum(gain, axis=0, keepdims=True)
    wide[...] = lax.dot_general(left[...], right[...], (((1,), (1,)), ((), ())), preferred_element_type=F32)
    for g in range(per):
        gram = wide[g * LTAPS : (g + 1) * LTAPS]
        long_ref[g : g + 1] = sum_by_lag(gram)


def backward(mixed_own, mixed_rest, feats, filt, x, later, short_taps, skip, table, chunk):
    blocks, _, rows, cols = x.shape
    tokens = blocks * rows
    tiles = cols // LANES
    first = chunk * tiles
    tab_rows = table.shape[0] * LANES // skip.shape[1]
    per = tab_rows // LTAPS
    tok = pl.BlockSpec((tokens, LANES), lambda c: (0, c))
    xs = pl.BlockSpec((blocks, 3, rows, LANES), lambda c: (0, 0, 0, c))
    return pl.pallas_call(
        backward_kernel,
        grid=(tiles,),
        in_specs=[
            tok,
            tok,
            pl.BlockSpec((3, tokens, LANES), lambda c: (0, 0, c)),
            tok,
            xs,
            pl.BlockSpec((later.shape[0], LANES), lambda c: (0, c)),
            pl.BlockSpec((3, SHORT, LANES), lambda c: (0, 0, first + c)),
            pl.BlockSpec((1, LANES), lambda c: (0, first + c)),
            pl.BlockSpec((tab_rows, 2 * LTAPS), lambda c: (first + c, 0)),
        ],
        out_specs=[
            xs,
            pl.BlockSpec((3, SHORT + 1, LANES), lambda c: (0, 0, c)),
            pl.BlockSpec((per, LTAPS), lambda c: (c, 0)),
        ],
        out_shape=[
            jax.ShapeDtypeStruct(x.shape, BF16),
            jax.ShapeDtypeStruct((3, SHORT + 1, cols), F32),
            jax.ShapeDtypeStruct((tiles * per, LTAPS), F32),
        ],
        scratch_shapes=[
            pltpu.VMEM((tokens + 2 * LTAPS, LANES), BF16),
            pltpu.VMEM((3, tokens + PAD, LANES), F32),
            pltpu.VMEM((tab_rows, 2 * LTAPS), F32),
            pltpu.VMEM((tab_rows, tokens), BF16),
            pltpu.VMEM((2 * LTAPS, tokens), BF16),
        ],
        compiler_params=params(48),
        cost_estimate=cost(8 * LTAPS * tokens * tab_rows, 36 * tokens * cols),
        name="backward",
    )(mixed_own, mixed_rest, feats, filt, x, later, short_taps, skip, table)


def pack_kernel(*refs):
    out_ref = refs[-1]
    for i, ref in enumerate(refs[:3]):
        out_ref[0, i] = ref[...]


def pack(arrays, seq, chunks, chunk, after=()):
    rows, width = arrays[0].shape
    cols = width // seq // chunks
    source = pl.BlockSpec((rows, cols), lambda s: (0, s * chunks + chunk))
    return pl.pallas_call(
        pack_kernel,
        grid=(seq,),
        in_specs=[source] * 3 + [pl.BlockSpec(memory_space=pl.ANY)] * len(after),
        out_specs=pl.BlockSpec((1, 3, rows, cols), lambda s: (s, 0, 0, 0)),
        out_shape=jax.ShapeDtypeStruct((seq, 3, rows, cols), BF16),
        compiler_params=params(32),
        name="pack",
    )(*arrays, *after)


def unpack_kernel(*refs):
    parts, outs = refs[:-3], refs[-3:]
    cols = parts[0].shape[3]
    for n, part in enumerate(parts):
        for i, out in enumerate(outs):
            out[:, n * cols : (n + 1) * cols] = part[0, i]


def unpack(parts):
    seq, _, rows, cols = parts[0].shape
    wide = cols * len(parts)
    shape = jax.ShapeDtypeStruct((rows, seq * wide), BF16)
    return pl.pallas_call(
        unpack_kernel,
        grid=(seq,),
        in_specs=[pl.BlockSpec((1, 3, rows, cols), lambda s: (s, 0, 0, 0))] * len(parts),
        out_specs=[pl.BlockSpec((rows, wide), lambda s: (0, s))] * 3,
        out_shape=[shape] * 3,
        compiler_params=params(32),
        name="unpack",
    )(*parts)


def along(block, axis, distance):
    size = lax.axis_size(axis)
    return lax.ppermute(block, axis, [(i, i + distance) for i in range(size) if 0 <= i + distance < size])


def around(block, axis, distance):
    size = lax.axis_size(axis)
    return lax.ppermute(block, axis, [(i, (i + distance) % size) for i in range(size)])


def across(block, axis, bit):
    return lax.ppermute(block, axis, [(i, i ^ bit) for i in range(lax.axis_size(axis))])


def bits_of(axis):
    size = lax.axis_size(axis)
    return [1 << n for n in range(size.bit_length() - 1)]


def sum_over(value, axes):
    for axis in axes:
        for bit in bits_of(axis):
            value = value + across(value, axis, bit)
    return value


def split_kernel(y_ref, *refs):
    count = len(refs) // 2
    for n in range(count):
        refs[count + n][...] = refs[n][...]


def split_cotangent(cotangent, y, ys, col_part):
    rows, width = cotangent.shape

    def source(step):
        return pl.BlockSpec((rows, col_part), lambda z, y_ref: (0, z * ys + (y_ref[0] + step) % ys))

    return pl.pallas_call(
        split_kernel,
        grid_spec=pltpu.PrefetchScalarGridSpec(
            num_scalar_prefetch=1,
            grid=(Z,),
            in_specs=[source(step) for step in range(ys)],
            out_specs=[pl.BlockSpec((rows, col_part), lambda z, _: (0, z))] * ys,
        ),
        out_shape=[jax.ShapeDtypeStruct((rows, width // ys), BF16)] * ys,
        compiler_params=params(32),
        name="split",
    )(y.reshape(1), *([cotangent] * ys))


def join_kernel(axis, count, *refs):
    out = refs[-1]
    for n in range(count):
        size = refs[n].shape[axis]
        here = slice(n * size, (n + 1) * size)
        if axis == 0:
            out[here] = refs[n][...]
        else:
            out[:, here] = refs[n][...]


def join(parts, axis, after=()):
    shape = list(parts[0].shape)
    tile = shape[-1] // Z
    block = pl.BlockSpec((*shape[:-1], tile), lambda i: (0, 0, 0, i))
    shape[axis] *= len(parts)
    return pl.pallas_call(
        functools.partial(join_kernel, axis, len(parts)),
        grid=(Z,),
        in_specs=[block] * len(parts) + [pl.BlockSpec(memory_space=pl.ANY)] * len(after),
        out_specs=pl.BlockSpec((*shape[:-1], tile), lambda i: (0, 0, 0, i)),
        out_shape=jax.ShapeDtypeStruct(tuple(shape), BF16),
        compiler_params=params(32),
        name="join",
    )(*parts, *after)


def gather_cotangent(cotangent, col_part, after):
    ys, y = lax.axis_size("y"), lax.axis_index("y")
    held = split_cotangent(cotangent, y, ys, col_part)
    held = [around(part, "y", step) if step else part for step, part in enumerate(held)]
    held = join([part[None, None] for part in held], 0, after)
    bits = bits_of("seq")
    for bit in reversed(bits[1:]):
        held = join([held, across(held, "seq", bit)], 1)
    return held, across(held, "seq", bits[0])


def mixed_grad_kernel(chunks, place_ref, a_ref, b_ref, w_ref, *refs):
    outs, found = refs[:-1], refs[-1]
    steps, count, rows, _ = a_ref.shape
    tokens = count * rows
    tiles = pl.num_programs(0) // chunks
    weights = w_ref[...]
    for n, ref in enumerate((a_ref, b_ref)):
        part = contract(ref[...].reshape(steps * tokens, -1), weights, 1)
        for step in range(steps):
            begin = (2 * step + n) * tokens
            found[begin : begin + tokens] = part[step * tokens : (step + 1) * tokens]
    for h in range(chunks):

        @pl.when(pl.program_id(0) // tiles == h)
        def _():
            for step in range(steps):
                out = outs[h * steps + step]
                for block in range(2 * count):
                    there = pl.multiple_of(2 * step * tokens + place_ref[block] * rows, rows)
                    out[block * rows : (block + 1) * rows] = found[pl.ds(there, rows)].astype(out.dtype)


def mixed_grad(cots, weights, place, chunks):
    steps, count, rows, width = cots[0].shape
    tokens = 2 * count * rows
    part = weights.shape[0] // chunks
    tile = min(part, 2 * LANES)
    tiles = part // tile
    piece = pl.BlockSpec((steps, count, rows, width), lambda i, _: (0, 0, 0, 0))

    def out_spec(h):
        return pl.BlockSpec((tokens, tile), lambda i, _: (0, jnp.clip(i - h * tiles, 0, tiles - 1)))

    outs = pl.pallas_call(
        functools.partial(mixed_grad_kernel, chunks),
        grid_spec=pltpu.PrefetchScalarGridSpec(
            num_scalar_prefetch=1,
            grid=(chunks * tiles,),
            in_specs=[piece, piece, pl.BlockSpec((tile, width), lambda i, _: (i, 0))],
            out_specs=[out_spec(h) for h in range(chunks) for _ in range(steps)],
            scratch_shapes=[pltpu.VMEM((steps * tokens, tile), F32)],
        ),
        out_shape=[
            jax.ShapeDtypeStruct((tokens, part), BF16 if step else F32) for _ in range(chunks) for step in range(steps)
        ],
        compiler_params=params(56),
        cost_estimate=cost(
            2 * steps * tokens * width * part * chunks, 2 * (steps * tokens + part * chunks) * width
        ),
        name="mixed_grad",
    )(place, *cots, weights)
    return [outs[h * steps : (h + 1) * steps] for h in range(chunks)]


def weight_grad_kernel(scale, chunks, a_ref, b_ref, *refs):
    mixed, out = refs[:-1], refs[-1]
    steps, count, rows, tile = a_ref.shape
    tokens = count * rows
    part = mixed[0].shape[0]
    for h in range(chunks):
        total = None
        for step in range(steps):
            for n, ref in enumerate((a_ref, b_ref)):
                left = mixed[step * chunks + h][:, n * tokens : (n + 1) * tokens]
                term = jnp.dot(left, ref[step].reshape(tokens, tile), preferred_element_type=F32)
                total = term if total is None else total + term
        out[h * part : (h + 1) * part] = (total * scale).astype(BF16)


def weight_grad(cots, mixed, chunks, scale):
    steps, count, rows, width = cots[0].shape
    part, tokens = mixed[0].shape
    tile = width // Z
    piece = pl.BlockSpec((steps, count, rows, tile), lambda i: (0, 0, 0, i))
    return pl.pallas_call(
        functools.partial(weight_grad_kernel, scale, chunks),
        grid=(Z,),
        in_specs=[piece, piece] + [pl.BlockSpec((part, tokens), lambda i: (0, 0))] * len(mixed),
        out_specs=pl.BlockSpec((part * chunks, tile), lambda i: (0, i)),
        out_shape=jax.ShapeDtypeStruct((part * chunks, width), BF16),
        compiler_params=params(48),
        cost_estimate=cost(
            2 * part * chunks * steps * tokens * width, 2 * (steps * tokens + part * chunks) * width
        ),
        name="weight_grad",
    )(*cots, *mixed)


def tail_kernel(x_ref, before_ref, out_ref):
    rows = x_ref.shape[2]
    out_ref[0:PAD] = x_ref[0, 0, rows - PAD :]
    for i in (1, 2):
        begin = PAD + (i - 1) * (PAD + rows)
        out_ref[begin : begin + PAD] = before_ref[0, i, rows - PAD :]
        out_ref[begin + PAD : begin + PAD + rows] = x_ref[0, i]


def tail_of(x):
    seq, _, rows, cols = x.shape

    def block(s):
        return pl.BlockSpec((1, 3, rows, cols), lambda i: (s, 0, 0, 0))

    out_rows = PAD + 2 * (PAD + rows)
    return pl.pallas_call(
        tail_kernel,
        grid=(1,),
        in_specs=[block(seq - 1), block(seq - 2)],
        out_specs=pl.BlockSpec((out_rows, cols), lambda i: (0, 0)),
        out_shape=jax.ShapeDtypeStruct((out_rows, cols), BF16),
        compiler_params=params(32),
        name="tail",
    )(x, x)


def head_kernel(mo_ref, mr_ref, f_ref, filt_ref, out_ref):
    edge = LTAPS + PAD
    mixed = mo_ref[...] + mr_ref[...].astype(F32)
    out_ref[0:edge] = (mixed * f_ref[0]).astype(BF16)
    out_ref[edge : edge + PAD] = f_ref[1, 0:PAD].astype(BF16)
    out_ref[edge + PAD : edge + 2 * PAD] = f_ref[2, 0:PAD].astype(BF16)
    out_ref[edge + 2 * PAD :] = (mixed[0:PAD] * filt_ref[0:PAD]).astype(BF16)


def head_of(mixed_own, mixed_rest, feats, filt):
    edge, cols = LTAPS + PAD, filt.shape[1]
    first = pl.BlockSpec((edge, cols), lambda i: (0, 0))
    return pl.pallas_call(
        head_kernel,
        grid=(1,),
        in_specs=[first, first, pl.BlockSpec((3, edge, cols), lambda i: (0, 0, 0)), first],
        out_specs=pl.BlockSpec((edge + 3 * PAD, cols), lambda i: (0, 0)),
        out_shape=jax.ShapeDtypeStruct((edge + 3 * PAD, cols), BF16),
        compiler_params=params(32),
        name="head",
    )(mixed_own, mixed_rest, feats, filt)


def contract(a, b, dim):
    return lax.dot_general(a, b, (((dim,), (dim,)), ((), ())), preferred_element_type=F32)


def places(seq):
    bits = bits_of("seq")
    source = lax.iota(jnp.int32, seq) ^ lax.axis_index("seq")
    return sum(((source >> n) & 1) << (len(bits) - 1 - n) for n in range(len(bits)))


def body(queries, keys, values, cotangent, out_weight, short_taps, long_taps, skip_gain):
    rows, width = queries.shape
    col_part = out_weight.shape[1]
    seq, ys = lax.axis_size("seq"), lax.axis_size("y")
    cols = width // seq
    chunks = 2 if cols % (2 * LANES) == 0 else 1
    part = cols // chunks
    groups = long_taps.shape[1]
    fsdp = ("z", "y")
    grad_scale = float(rows * seq * ys * Z) ** (-0.5)

    weights = lax.all_gather(out_weight, "z", axis=1, tiled=True)
    fwd_table, bwd_table = make_tables(long_taps)
    xs = []
    for h in range(chunks):
        packed = pack((queries, keys, values), seq, chunks, h, (fwd_table, xs[-1]) if h else ())
        xs.append(lax.all_to_all(packed, "seq", split_axis=0, concat_axis=0, tiled=True))
    cots = gather_cotangent(cotangent, col_part, xs[-1:])
    skip = skip_gain.reshape(1, cols)
    place = places(seq)

    mixers = []
    for h in range(chunks):
        halo = along(tail_of(xs[h]), fsdp, 1)
        mixers.append(forward(xs[h], halo, short_taps, skip, fwd_table, place, h))

    mixed_all = [
        around(mixers[h][0], "y", step) if step else mixers[h][0] for step in range(ys) for h in range(chunks)
    ]
    weight_sum = weight_grad(cots, mixed_all, chunks, grad_scale)
    weight_part = lax.psum_scatter(weight_sum, "z", scatter_dimension=1, tiled=True)

    partial_grads = mixed_grad(cots, weights, place, chunks)
    grads, short_parts, long_parts = [], [], []
    for h in range(chunks):
        _, feats, filt = mixers[h]
        rest = [around(partial_grads[h][step], "y", -step) for step in range(1, ys)]
        mixed_rest = rest[0] if len(rest) == 1 else sum(piece.astype(F32) for piece in rest)
        mixed_own = partial_grads[h][0]
        later = along(head_of(mixed_own, mixed_rest, feats, filt), fsdp, -1)
        grad, short_part, long_part = backward(
            mixed_own, mixed_rest, feats, filt, xs[h], later, short_taps, skip, bwd_table, h
        )
        grads.append(lax.all_to_all(grad, "seq", split_axis=0, concat_axis=0, tiled=True))
        short_parts.append(short_part)
        long_parts.append(long_part)

    query_grad, key_grad, value_grad = unpack(grads)
    packed = jnp.concatenate(
        [
            jnp.concatenate(short_parts, axis=2).reshape(3 * (SHORT + 1), cols),
            jnp.concatenate(long_parts, axis=0).reshape(-1, cols),
        ],
        axis=0,
    )
    packed = sum_over(packed, ("y", "z")) * grad_scale
    short_sum = packed[: 3 * (SHORT + 1)].reshape(3, SHORT + 1, cols)
    long_sum = packed[3 * (SHORT + 1) :].reshape(groups, LTAPS).T
    return (
        query_grad,
        key_grad,
        value_grad,
        weight_part.astype(F32),
        short_sum[:, :SHORT],
        long_sum,
        short_sum[0, SHORT],
    )


def solution(mesh):
    fsdp, seq = mesh.shape["fsdp"], mesh.shape["seq"]
    split = Mesh(mesh.devices.reshape(Z, fsdp // Z, seq), ("z", "y", "seq"))
    tokens = P(("z", "y", "seq"), None)
    specs = (P("seq", ("z", "y")), P(None, None, "seq"), P(None, "seq"), P("seq"))
    return jax.shard_map(
        body,
        mesh=split,
        in_specs=(tokens,) * 4 + specs,
        out_specs=(tokens,) * 3 + specs,
        check_vma=False,
    )
```

```python
import functools

import jax
import jax.numpy as jnp
from jax import lax
from jax.experimental import pallas as pl
from jax.experimental.pallas import tpu as pltpu
from jax.sharding import Mesh
from jax.sharding import PartitionSpec as P

SHORT = 7
LTAPS = 128
LANES = 128
PAD = 16
Z = 4
F32 = jnp.float32
BF16 = jnp.bfloat16


def params(mib):
    return pltpu.CompilerParams(vmem_limit_bytes=mib * 2**20)


def cost(flops, nbytes):
    return pl.CostEstimate(flops=flops, bytes_accessed=nbytes, transcendentals=0)


def tables_kernel(fwd_ref, bwd_ref, tf_ref, tb_ref):
    for g in range(fwd_ref.shape[0]):
        rows = slice(g * LTAPS, (g + 1) * LTAPS)
        for src, dst in ((fwd_ref, tf_ref), (bwd_ref, tb_ref)):
            wide = jnp.broadcast_to(src[g : g + 1, :], (LTAPS, 2 * LTAPS))
            dst[rows, :] = pltpu.roll(wide, 0, 1, stride=1, stride_axis=0).astype(BF16)


def make_tables(long_taps):
    by_group = long_taps.T
    groups = by_group.shape[0]
    fwd = jnp.pad(by_group[:, ::-1], ((0, 0), (1, LTAPS - 1)))
    bwd = jnp.pad(by_group, ((0, 0), (0, LTAPS)))
    per = 8
    row_spec = pl.BlockSpec((per, 2 * LTAPS), lambda i: (i, 0))
    tab_spec = pl.BlockSpec((per * LTAPS, 2 * LTAPS), lambda i: (i, 0))
    shape = jax.ShapeDtypeStruct((groups * LTAPS, 2 * LTAPS), BF16)
    return pl.pallas_call(
        tables_kernel,
        grid=(groups // per,),
        in_specs=[row_spec, row_spec],
        out_specs=[tab_spec, tab_spec],
        out_shape=[shape, shape],
        compiler_params=params(32),
        name="tables",
    )(fwd, bwd)


def pick_groups(wide, col, rows, per):
    lane_group = lax.broadcasted_iota(jnp.int32, (rows, LANES), 1) // (LANES // per)
    cols = slice(col * LANES, (col + 1) * LANES)
    out = wide[0:rows, cols]
    for g in range(1, per):
        out = jnp.where(lane_group == g, wide[g * rows : (g + 1) * rows, cols], out)
    return out


def forward_kernel(place_ref, x_ref, h_ref, taps_ref, skip_ref, tab_ref, mixed_ref, f_ref, filt_ref, xf, pf, pb, wide):
    blocks, _, rows, _ = x_ref.shape
    tokens = blocks * rows
    per = tab_ref.shape[0] // LTAPS
    xf[0, LTAPS : LTAPS + PAD] = h_ref[0:PAD].astype(F32)
    for i in (1, 2):
        begin = PAD + (i - 1) * (LTAPS + PAD)
        xf[i, 0 : LTAPS + PAD] = h_ref[begin : begin + LTAPS + PAD].astype(F32)
    for i in range(3):
        for b in range(blocks):
            begin = LTAPS + PAD + b * rows
            xf[i, begin : begin + rows] = x_ref[b, i].astype(F32)

    def feature(i, base):
        total = taps_ref[i, 0:1] * xf[i, PAD + base : PAD + base + LTAPS]
        for j in range(1, SHORT):
            total = total + taps_ref[i, j : j + 1] * xf[i, PAD + base - j : PAD + base - j + LTAPS]
        return total

    for n in range(tokens // LTAPS + 1):
        base = n * LTAPS
        own = slice(base - LTAPS, base)
        f1 = feature(1, base)
        f2 = feature(2, base)
        prod = f1 * f2
        pb[base : base + LTAPS] = prod.astype(BF16)
        if n:
            f_ref[1, own] = f1
            f_ref[2, own] = f2
            f_ref[0, own] = feature(0, base)
            pf[own] = prod
    skip = skip_ref[...]
    for b in range(0, tokens // LTAPS, 2):
        low = b * LTAPS
        windows = jnp.concatenate([pb[low : low + 2 * LTAPS], pb[low + LTAPS : low + 3 * LTAPS]], axis=1)
        wide[...] = jnp.dot(tab_ref[...], windows, preferred_element_type=F32)
        for n in range(2):
            own = slice(low + n * LTAPS, low + (n + 1) * LTAPS)
            filtered = pick_groups(wide, n, LTAPS, per) + skip * pf[own]
            filt_ref[own] = filtered
            mixed = f_ref[0, own] * filtered
            there = pl.multiple_of(place_ref[b + n] * LTAPS, LTAPS)
            mixed_ref[:, pl.ds(there, LTAPS)] = mixed.T.astype(BF16)


def forward(x, halo, short_taps, skip, table, place, chunk, chunks):
    blocks, _, rows, cols = x.shape
    cols //= chunks
    tokens = blocks * rows
    tiles = cols // LANES
    first = chunk * tiles
    tab_rows = table.shape[0] * LANES // skip.shape[1]
    return pl.pallas_call(
        forward_kernel,
        grid_spec=pltpu.PrefetchScalarGridSpec(
            num_scalar_prefetch=1,
            grid=(tiles,),
            in_specs=[
                pl.BlockSpec((blocks, 3, rows, LANES), lambda c, _: (0, 0, 0, first + c)),
                pl.BlockSpec((halo.shape[0], LANES), lambda c, _: (0, first + c)),
                pl.BlockSpec((3, SHORT, LANES), lambda c, _: (0, 0, first + c)),
                pl.BlockSpec((1, LANES), lambda c, _: (0, first + c)),
                pl.BlockSpec((tab_rows, 2 * LTAPS), lambda c, _: (first + c, 0)),
            ],
            out_specs=[
                pl.BlockSpec((LANES, tokens), lambda c, _: (c, 0)),
                pl.BlockSpec((3, tokens, LANES), lambda c, _: (0, 0, c)),
                pl.BlockSpec((tokens, LANES), lambda c, _: (0, c)),
            ],
            scratch_shapes=[
                pltpu.VMEM((3, PAD + LTAPS + tokens, LANES), F32),
                pltpu.VMEM((tokens, LANES), F32),
                pltpu.VMEM((LTAPS + tokens, LANES), BF16),
                pltpu.VMEM((tab_rows, 2 * LTAPS), F32),
            ],
        ),
        out_shape=[
            jax.ShapeDtypeStruct((cols, tokens), BF16),
            jax.ShapeDtypeStruct((3, tokens, cols), F32),
            jax.ShapeDtypeStruct((tokens, cols), F32),
        ],
        compiler_params=params(48),
        cost_estimate=cost(4 * LTAPS * tokens * tab_rows, 24 * tokens * cols),
        name="forward",
    )(place, x, halo, short_taps, skip, table)


def sum_by_lag(gram):
    wide = gram.shape[1]
    parts = [gram[i : i + 8] for i in range(0, gram.shape[0], 8)]
    step = 8
    while len(parts) > 1:
        parts = [
            parts[k] + pltpu.roll(parts[k + 1], wide - step, 1) for k in range(0, len(parts), 2)
        ]
        step *= 2
    total = parts[0]
    row = lax.broadcasted_iota(jnp.int32, total.shape, 0)
    for bit in (1, 2, 4):
        total = jnp.where((row & bit) != 0, pltpu.roll(total, wide - bit, 1), total)
    return jnp.sum(total[:, :LTAPS], axis=0, keepdims=True)


def backward_kernel(
    mo_ref, mr_ref, f_ref, filt_ref, x_ref, n_ref, taps_ref, skip_ref, tab_ref,
    grad_ref, short_ref, long_ref, db, fg, wide, left, right,
):
    blocks, _, rows, _ = x_ref.shape
    tokens = blocks * rows
    per = tab_ref.shape[0] // LTAPS
    count = tokens // LTAPS
    skip = skip_ref[...]
    lane_group = lax.broadcasted_iota(jnp.int32, (1, LANES), 1) // (LANES // per)
    gain = jnp.zeros((8, LANES), F32)
    for b in range(count):
        own = slice(b * LTAPS, (b + 1) * LTAPS)
        mixed_grad = mo_ref[own] + mr_ref[own].astype(F32)
        slope = mixed_grad * f_ref[0, own]
        db[own] = slope.astype(BF16)
        fg[0, own] = mixed_grad * filt_ref[own]
        fg[1, own] = skip * slope
        prod = f_ref[1, own] * f_ref[2, own]
        gain = gain + jnp.sum((prod * slope).reshape(LTAPS // 8, 8, LANES), axis=0)
        prod_b = prod.astype(BF16)
        for g in range(per):
            keep = (lane_group == g).astype(F32).astype(BF16)
            left[g * LTAPS : (g + 1) * LTAPS, b * LANES : (b + 1) * LANES] = prod_b * keep
    db[tokens : tokens + LTAPS + PAD] = n_ref[0 : LTAPS + PAD]
    db[tokens + LTAPS + PAD :] = jnp.zeros((LTAPS - PAD, LANES), BF16)
    for b in range(count):
        right[:, b * LANES : (b + 1) * LANES] = db[b * LTAPS : (b + 2) * LTAPS]
    for b in range(0, count, 2):
        wide[...] = jnp.dot(
            tab_ref[...], right[:, b * LANES : (b + 2) * LANES], preferred_element_type=F32
        )
        for n in range(2):
            own = slice((b + n) * LTAPS, (b + n + 1) * LTAPS)
            grad = pick_groups(wide, n, LTAPS, per) + fg[1, own]
            fg[1, own] = grad * f_ref[2, own]
            fg[2, own] = grad * f_ref[1, own]
    few = jnp.concatenate([tab_ref[g * LTAPS : g * LTAPS + PAD] for g in range(per)], axis=0)
    edge = jnp.dot(few, db[tokens : tokens + 2 * LTAPS], preferred_element_type=F32)
    begin = LTAPS + PAD
    grad = pick_groups(edge, 0, PAD, per) + skip * n_ref[0:PAD].astype(F32)
    fg[1, tokens : tokens + PAD] = grad * n_ref[begin + PAD : begin + 2 * PAD].astype(F32)
    fg[2, tokens : tokens + PAD] = grad * n_ref[begin : begin + PAD].astype(F32)
    fg[0, tokens : tokens + PAD] = n_ref[begin + 2 * PAD : begin + 3 * PAD].astype(F32)
    for i in range(3):
        sums = [jnp.zeros((8, LANES), F32) for _ in range(SHORT)]
        for b in range(count):
            low = b * LTAPS
            inputs = x_ref[b, i].astype(F32)
            total = None
            for j in range(SHORT):
                later = fg[i, low + j : low + j + LTAPS]
                term = taps_ref[i, j : j + 1] * later
                total = term if total is None else total + term
                sums[j] = sums[j] + jnp.sum((later * inputs).reshape(LTAPS // 8, 8, LANES), axis=0)
            grad_ref[b, i] = total.astype(BF16)
        for j in range(SHORT):
            short_ref[i, j : j + 1] = jnp.sum(sums[j], axis=0, keepdims=True)
        short_ref[i, SHORT : SHORT + 1] = jnp.sum(gain, axis=0, keepdims=True)
    wide[...] = lax.dot_general(left[...], right[...], (((1,), (1,)), ((), ())), preferred_element_type=F32)
    for g in range(per):
        gram = wide[g * LTAPS : (g + 1) * LTAPS]
        long_ref[g : g + 1] = sum_by_lag(gram)


def backward(mixed_own, mixed_rest, feats, filt, x, later, short_taps, skip, table, chunk, chunks):
    blocks, _, rows, cols = x.shape
    cols //= chunks
    tokens = blocks * rows
    tiles = cols // LANES
    first = chunk * tiles
    tab_rows = table.shape[0] * LANES // skip.shape[1]
    per = tab_rows // LTAPS
    tok = pl.BlockSpec((tokens, LANES), lambda c: (0, first + c))
    return pl.pallas_call(
        backward_kernel,
        grid=(tiles,),
        in_specs=[
            tok,
            tok,
            pl.BlockSpec((3, tokens, LANES), lambda c: (0, 0, c)),
            pl.BlockSpec((tokens, LANES), lambda c: (0, c)),
            pl.BlockSpec((blocks, 3, rows, LANES), lambda c: (0, 0, 0, first + c)),
            pl.BlockSpec((later.shape[0], LANES), lambda c: (0, first + c)),
            pl.BlockSpec((3, SHORT, LANES), lambda c: (0, 0, first + c)),
            pl.BlockSpec((1, LANES), lambda c: (0, first + c)),
            pl.BlockSpec((tab_rows, 2 * LTAPS), lambda c: (first + c, 0)),
        ],
        out_specs=[
            pl.BlockSpec((blocks, 3, rows, LANES), lambda c: (0, 0, 0, c)),
            pl.BlockSpec((3, SHORT + 1, LANES), lambda c: (0, 0, c)),
            pl.BlockSpec((per, LTAPS), lambda c: (c, 0)),
        ],
        out_shape=[
            jax.ShapeDtypeStruct((blocks, 3, rows, cols), BF16),
            jax.ShapeDtypeStruct((3, SHORT + 1, cols), F32),
            jax.ShapeDtypeStruct((tiles * per, LTAPS), F32),
        ],
        scratch_shapes=[
            pltpu.VMEM((tokens + 2 * LTAPS, LANES), BF16),
            pltpu.VMEM((3, tokens + PAD, LANES), F32),
            pltpu.VMEM((tab_rows, 2 * LTAPS), F32),
            pltpu.VMEM((tab_rows, tokens), BF16),
            pltpu.VMEM((2 * LTAPS, tokens), BF16),
        ],
        compiler_params=params(48),
        cost_estimate=cost(8 * LTAPS * tokens * tab_rows, 36 * tokens * cols),
        name="backward",
    )(mixed_own, mixed_rest, feats, filt, x, later, short_taps, skip, table)


def pack_kernel(*refs):
    out_ref = refs[-1]
    for i, ref in enumerate(refs[:3]):
        out_ref[0, i] = ref[...]


def pack(arrays, seq):
    rows, width = arrays[0].shape
    cols = width // seq
    return pl.pallas_call(
        pack_kernel,
        grid=(seq,),
        in_specs=[pl.BlockSpec((rows, cols), lambda s: (0, s))] * 3,
        out_specs=pl.BlockSpec((1, 3, rows, cols), lambda s: (s, 0, 0, 0)),
        out_shape=jax.ShapeDtypeStruct((seq, 3, rows, cols), BF16),
        compiler_params=params(32),
        name="pack",
    )(*arrays)


def unpack_kernel(*refs):
    parts, outs = refs[:-3], refs[-3:]
    cols = parts[0].shape[3]
    for n, part in enumerate(parts):
        for i, out in enumerate(outs):
            out[:, n * cols : (n + 1) * cols] = part[0, i]


def unpack(parts):
    seq, _, rows, cols = parts[0].shape
    wide = cols * len(parts)
    shape = jax.ShapeDtypeStruct((rows, seq * wide), BF16)
    return pl.pallas_call(
        unpack_kernel,
        grid=(seq,),
        in_specs=[pl.BlockSpec((1, 3, rows, cols), lambda s: (s, 0, 0, 0))] * len(parts),
        out_specs=[pl.BlockSpec((rows, wide), lambda s: (0, s))] * 3,
        out_shape=[shape] * 3,
        compiler_params=params(32),
        name="unpack",
    )(*parts)


def along(block, axis, distance):
    size = lax.axis_size(axis)
    return lax.ppermute(block, axis, [(i, i + distance) for i in range(size) if 0 <= i + distance < size])


def around(block, axis, distance):
    size = lax.axis_size(axis)
    return lax.ppermute(block, axis, [(i, (i + distance) % size) for i in range(size)])


def across(block, axis, bit):
    return lax.ppermute(block, axis, [(i, i ^ bit) for i in range(lax.axis_size(axis))])


def bits_of(axis):
    size = lax.axis_size(axis)
    return [1 << n for n in range(size.bit_length() - 1)]


def sum_over(value, axes):
    for axis in axes:
        for bit in bits_of(axis):
            value = value + across(value, axis, bit)
    return value


def split_kernel(y_ref, *refs):
    count = (len(refs) - 1) // 2
    for n in range(count):
        refs[count + 1 + n][...] = refs[n][...]


def split_cotangent(cotangent, y, ys, col_part, after):
    rows, width = cotangent.shape

    def source(step):
        return pl.BlockSpec((rows, col_part), lambda z, y_ref: (0, z * ys + (y_ref[0] + step) % ys))

    return pl.pallas_call(
        split_kernel,
        grid_spec=pltpu.PrefetchScalarGridSpec(
            num_scalar_prefetch=1,
            grid=(Z,),
            in_specs=[source(step) for step in range(ys)] + [pl.BlockSpec(memory_space=pl.ANY)],
            out_specs=[pl.BlockSpec((rows, col_part), lambda z, _: (0, z))] * ys,
        ),
        out_shape=[jax.ShapeDtypeStruct((rows, width // ys), BF16)] * ys,
        compiler_params=params(32),
        name="split",
    )(y.reshape(1), *([cotangent] * ys), after)


def join_kernel(axis, count, *refs):
    out = refs[-1]
    for n in range(count):
        size = refs[n].shape[axis]
        here = slice(n * size, (n + 1) * size)
        if axis == 0:
            out[here] = refs[n][...]
        else:
            out[:, here] = refs[n][...]


def join(parts, axis, after=()):
    shape = list(parts[0].shape)
    tile = shape[-1] // Z
    block = pl.BlockSpec((*shape[:-1], tile), lambda i: (0, 0, 0, i))
    shape[axis] *= len(parts)
    return pl.pallas_call(
        functools.partial(join_kernel, axis, len(parts)),
        grid=(Z,),
        in_specs=[block] * len(parts) + [pl.BlockSpec(memory_space=pl.ANY)] * len(after),
        out_specs=pl.BlockSpec((*shape[:-1], tile), lambda i: (0, 0, 0, i)),
        out_shape=jax.ShapeDtypeStruct(tuple(shape), BF16),
        compiler_params=params(32),
        name="join",
    )(*parts, *after)


def gather_cotangent(cotangent, col_part, after_first, after):
    ys, y = lax.axis_size("y"), lax.axis_index("y")
    held = split_cotangent(cotangent, y, ys, col_part, after_first)
    held = [around(part, "y", step) if step else part for step, part in enumerate(held)]
    held = join([part[None, None] for part in held], 0, after)
    bits = bits_of("seq")
    for bit in reversed(bits[1:]):
        held = join([held, across(held, "seq", bit)], 1)
    return held, across(held, "seq", bits[0])


def mixed_grad_kernel(place_ref, a_ref, b_ref, w_ref, _, out_ref, found):
    _, count, rows, _ = a_ref.shape
    tokens = count * rows
    pieces = jnp.concatenate([ref[...].reshape(tokens, -1) for ref in (a_ref, b_ref)], axis=0)
    found[...] = contract(pieces, w_ref[...], 1)
    for block in range(2 * count):
        there = pl.multiple_of(place_ref[block] * rows, rows)
        out_ref[block * rows : (block + 1) * rows] = found[pl.ds(there, rows)].astype(out_ref.dtype)


def mixed_grad(cots, weights, place, step, dtype, after):
    _, count, rows, width = cots[0].shape
    tokens = 2 * count * rows
    cols = weights.shape[0]
    tile = min(cols, 2 * LANES)
    piece = pl.BlockSpec((1, count, rows, width), lambda i, _: (step, 0, 0, 0))
    return pl.pallas_call(
        mixed_grad_kernel,
        grid_spec=pltpu.PrefetchScalarGridSpec(
            num_scalar_prefetch=1,
            grid=(cols // tile,),
            in_specs=[
                piece,
                piece,
                pl.BlockSpec((tile, width), lambda i, _: (i, 0)),
                pl.BlockSpec(memory_space=pl.ANY),
            ],
            out_specs=pl.BlockSpec((tokens, tile), lambda i, _: (0, i)),
            scratch_shapes=[pltpu.VMEM((tokens, tile), F32)],
        ),
        out_shape=jax.ShapeDtypeStruct((tokens, cols), dtype),
        compiler_params=params(56),
        cost_estimate=cost(2 * tokens * width * cols, 2 * (tokens + cols) * width),
        name="mixed_grad",
    )(place, *cots, weights, after)


def weight_grad_kernel(scale, chunks, a_ref, b_ref, *refs):
    mixed, out = refs[:-2], refs[-1]
    steps, count, rows, tile = a_ref.shape
    tokens = count * rows
    part = mixed[0].shape[0]
    for h in range(chunks):
        total = None
        for step in range(steps):
            for n, ref in enumerate((a_ref, b_ref)):
                left = mixed[step * chunks + h][:, n * tokens : (n + 1) * tokens]
                term = jnp.dot(left, ref[step].reshape(tokens, tile), preferred_element_type=F32)
                total = term if total is None else total + term
        out[h * part : (h + 1) * part] = (total * scale).astype(BF16)


def weight_grad(cots, mixed, chunks, scale, after):
    steps, count, rows, width = cots[0].shape
    part, tokens = mixed[0].shape
    tile = width // Z
    piece = pl.BlockSpec((steps, count, rows, tile), lambda i: (0, 0, 0, i))
    return pl.pallas_call(
        functools.partial(weight_grad_kernel, scale, chunks),
        grid=(Z,),
        in_specs=[piece, piece] + [pl.BlockSpec((part, tokens), lambda i: (0, 0))] * len(mixed)
        + [pl.BlockSpec(memory_space=pl.ANY)],
        out_specs=pl.BlockSpec((part * chunks, tile), lambda i: (0, i)),
        out_shape=jax.ShapeDtypeStruct((part * chunks, width), BF16),
        compiler_params=params(48),
        cost_estimate=cost(
            2 * part * chunks * steps * tokens * width, 2 * (steps * tokens + part * chunks) * width
        ),
        name="weight_grad",
    )(*cots, *mixed, after)


def tail_kernel(x_ref, before_ref, out_ref):
    rows = x_ref.shape[2]
    out_ref[0:PAD] = x_ref[0, 0, rows - PAD :]
    for i in (1, 2):
        begin = PAD + (i - 1) * (PAD + rows)
        out_ref[begin : begin + PAD] = before_ref[0, i, rows - PAD :]
        out_ref[begin + PAD : begin + PAD + rows] = x_ref[0, i]


def tail_of(x):
    seq, _, rows, cols = x.shape

    def block(s):
        return pl.BlockSpec((1, 3, rows, cols), lambda i: (s, 0, 0, 0))

    out_rows = PAD + 2 * (PAD + rows)
    return pl.pallas_call(
        tail_kernel,
        grid=(1,),
        in_specs=[block(seq - 1), block(seq - 2)],
        out_specs=pl.BlockSpec((out_rows, cols), lambda i: (0, 0)),
        out_shape=jax.ShapeDtypeStruct((out_rows, cols), BF16),
        compiler_params=params(32),
        name="tail",
    )(x, x)


def head_kernel(mo_ref, mr_ref, *refs):
    out_ref = refs[-1]
    chunks = len(refs) // 2
    edge = LTAPS + PAD
    part = out_ref.shape[1] // chunks
    for h in range(chunks):
        own = slice(h * part, (h + 1) * part)
        f_ref, filt_ref = refs[2 * h : 2 * h + 2]
        mixed = mo_ref[:, own] + mr_ref[:, own].astype(F32)
        out_ref[0:edge, own] = (mixed * f_ref[0]).astype(BF16)
        out_ref[edge : edge + PAD, own] = f_ref[1, 0:PAD].astype(BF16)
        out_ref[edge + PAD : edge + 2 * PAD, own] = f_ref[2, 0:PAD].astype(BF16)
        out_ref[edge + 2 * PAD :, own] = (mixed[0:PAD] * filt_ref[0:PAD]).astype(BF16)


def head_of(mixed_own, mixed_rest, mixers):
    edge, cols = LTAPS + PAD, mixed_own.shape[1]
    part = cols // len(mixers)
    whole = pl.BlockSpec((edge, cols), lambda i: (0, 0))
    feat_specs = [
        pl.BlockSpec((3, edge, part), lambda i: (0, 0, 0)),
        pl.BlockSpec((edge, part), lambda i: (0, 0)),
    ]
    return pl.pallas_call(
        head_kernel,
        grid=(1,),
        in_specs=[whole, whole] + feat_specs * len(mixers),
        out_specs=pl.BlockSpec((edge + 3 * PAD, cols), lambda i: (0, 0)),
        out_shape=jax.ShapeDtypeStruct((edge + 3 * PAD, cols), BF16),
        compiler_params=params(32),
        name="head",
    )(mixed_own, mixed_rest, *[array for mixer in mixers for array in mixer[1:]])


def contract(a, b, dim):
    return lax.dot_general(a, b, (((dim,), (dim,)), ((), ())), preferred_element_type=F32)


def places(seq):
    bits = bits_of("seq")
    source = lax.iota(jnp.int32, seq) ^ lax.axis_index("seq")
    return sum(((source >> n) & 1) << (len(bits) - 1 - n) for n in range(len(bits)))


def body(queries, keys, values, cotangent, out_weight, short_taps, long_taps, skip_gain):
    rows, width = queries.shape
    col_part = out_weight.shape[1]
    seq, ys = lax.axis_size("seq"), lax.axis_size("y")
    cols = width // seq
    chunks = 2 if cols % (2 * LANES) == 0 else 1
    groups = long_taps.shape[1]
    fsdp = ("z", "y")
    grad_scale = float(rows * seq * ys * Z) ** (-0.5)

    weights = lax.all_gather(out_weight, "z", axis=1, tiled=True)
    fwd_table, bwd_table = make_tables(long_taps)
    skip = skip_gain.reshape(1, cols)
    place = places(seq)
    by_owner = pack((queries, keys, values), seq)
    x = lax.all_to_all(by_owner, "seq", split_axis=0, concat_axis=0, tiled=True)
    halo = along(tail_of(x), fsdp, 1)
    cots = gather_cotangent(cotangent, col_part, by_owner, [halo])
    mixers = [forward(x, halo, short_taps, skip, fwd_table, place, h, chunks) for h in range(chunks)]

    parts = []
    for step in range(1, ys):
        parts.append(mixed_grad(cots, weights, place, step, BF16, parts[-1] if parts else place))
    rest = [around(parts[step - 1], "y", -step) for step in range(1, ys)]
    mixed_rest = rest[0] if len(rest) == 1 else sum(piece.astype(F32) for piece in rest)

    mixed_all = [
        around(mixers[h][0], "y", step) if step else mixers[h][0] for step in range(ys) for h in range(chunks)
    ]
    weight_sum = weight_grad(cots, mixed_all, chunks, grad_scale, parts[-1])
    weight_part = lax.psum_scatter(weight_sum, "z", scatter_dimension=1, tiled=True)

    mixed_own = mixed_grad(cots, weights, place, 0, F32, weight_sum)
    later = along(head_of(mixed_own, mixed_rest, mixers), fsdp, -1)
    grads, short_parts, long_parts = [], [], []
    for h in range(chunks):
        _, feats, filt = mixers[h]
        grad, short_part, long_part = backward(
            mixed_own, mixed_rest, feats, filt, x, later, short_taps, skip, bwd_table, h, chunks
        )
        grads.append(lax.all_to_all(grad, "seq", split_axis=0, concat_axis=0, tiled=True))
        short_parts.append(short_part)
        long_parts.append(long_part)

    query_grad, key_grad, value_grad = unpack(grads)
    packed = jnp.concatenate(
        [
            jnp.concatenate(short_parts, axis=2).reshape(3 * (SHORT + 1), cols),
            jnp.concatenate(long_parts, axis=0).reshape(-1, cols),
        ],
        axis=0,
    )
    packed = sum_over(packed, ("y", "z")) * grad_scale
    short_sum = packed[: 3 * (SHORT + 1)].reshape(3, SHORT + 1, cols)
    long_sum = packed[3 * (SHORT + 1) :].reshape(groups, LTAPS).T
    return (
        query_grad,
        key_grad,
        value_grad,
        weight_part.astype(F32),
        short_sum[:, :SHORT],
        long_sum,
        short_sum[0, SHORT],
    )


def solution(mesh):
    fsdp, seq = mesh.shape["fsdp"], mesh.shape["seq"]
    split = Mesh(mesh.devices.reshape(Z, fsdp // Z, seq), ("z", "y", "seq"))
    tokens = P(("z", "y", "seq"), None)
    specs = (P("seq", ("z", "y")), P(None, None, "seq"), P(None, "seq"), P("seq"))
    return jax.shard_map(
        body,
        mesh=split,
        in_specs=(tokens,) * 4 + specs,
        out_specs=(tokens,) * 3 + specs,
        check_vma=False,
    )
```

```python
import functools

import jax
import jax.numpy as jnp
from jax import lax
from jax.experimental import pallas as pl
from jax.experimental.pallas import tpu as pltpu
from jax.sharding import Mesh
from jax.sharding import PartitionSpec as P

SHORT = 7
LTAPS = 128
LANES = 128
PAD = 16
Z = 4
F32 = jnp.float32
BF16 = jnp.bfloat16


def params():
    return pltpu.CompilerParams(vmem_limit_bytes=60 * 2**20)


def tables_kernel(fwd_ref, bwd_ref, tf_ref, tb_ref):
    for g in range(fwd_ref.shape[0]):
        rows = slice(g * LTAPS, (g + 1) * LTAPS)
        for src, dst in ((fwd_ref, tf_ref), (bwd_ref, tb_ref)):
            wide = jnp.broadcast_to(src[g : g + 1, :], (LTAPS, 2 * LTAPS))
            dst[rows, :] = pltpu.roll(wide, 0, 1, stride=1, stride_axis=0).astype(BF16)


def make_tables(long_taps):
    by_group = long_taps.T
    groups = by_group.shape[0]
    fwd = jnp.pad(by_group[:, ::-1], ((0, 0), (1, LTAPS - 1)))
    bwd = jnp.pad(by_group, ((0, 0), (0, LTAPS)))
    per = 8
    row_spec = pl.BlockSpec((per, 2 * LTAPS), lambda i: (i, 0))
    tab_spec = pl.BlockSpec((per * LTAPS, 2 * LTAPS), lambda i: (i, 0))
    shape = jax.ShapeDtypeStruct((groups * LTAPS, 2 * LTAPS), BF16)
    return pl.pallas_call(
        tables_kernel,
        grid=(groups // per,),
        in_specs=[row_spec, row_spec],
        out_specs=[tab_spec, tab_spec],
        out_shape=[shape, shape],
        compiler_params=params(),
        name="tables",
    )(fwd, bwd)


def pick_groups(wide, col, rows, per):
    lane_group = lax.broadcasted_iota(jnp.int32, (rows, LANES), 1) // (LANES // per)
    cols = slice(col * LANES, (col + 1) * LANES)
    out = wide[0:rows, cols]
    for g in range(1, per):
        out = jnp.where(lane_group == g, wide[g * rows : (g + 1) * rows, cols], out)
    return out


def forward_kernel(place_ref, x_ref, h_ref, taps_ref, skip_ref, tab_ref, mixed_ref, f_ref, filt_ref, xf, pf, pb, wide):
    blocks, _, rows, _ = x_ref.shape
    tokens = blocks * rows
    per = tab_ref.shape[0] // LTAPS
    xf[0, LTAPS : LTAPS + PAD] = h_ref[0:PAD].astype(F32)
    for i in (1, 2):
        begin = PAD + (i - 1) * (LTAPS + PAD)
        xf[i, 0 : LTAPS + PAD] = h_ref[begin : begin + LTAPS + PAD].astype(F32)
    for i in range(3):
        for b in range(blocks):
            begin = LTAPS + PAD + b * rows
            xf[i, begin : begin + rows] = x_ref[b, i].astype(F32)

    def feature(i, base):
        total = taps_ref[i, 0:1] * xf[i, PAD + base : PAD + base + LTAPS]
        for j in range(1, SHORT):
            total = total + taps_ref[i, j : j + 1] * xf[i, PAD + base - j : PAD + base - j + LTAPS]
        return total

    for n in range(tokens // LTAPS + 1):
        base = n * LTAPS
        own = slice(base - LTAPS, base)
        f1 = feature(1, base)
        f2 = feature(2, base)
        prod = f1 * f2
        pb[base : base + LTAPS] = prod.astype(BF16)
        if n:
            f_ref[1, own] = f1
            f_ref[2, own] = f2
            f_ref[0, own] = feature(0, base)
            pf[own] = prod
    skip = skip_ref[...]
    for b in range(0, tokens // LTAPS, 2):
        low = b * LTAPS
        windows = jnp.concatenate([pb[low : low + 2 * LTAPS], pb[low + LTAPS : low + 3 * LTAPS]], axis=1)
        wide[...] = jnp.dot(tab_ref[...], windows, preferred_element_type=F32)
        for n in range(2):
            own = slice(low + n * LTAPS, low + (n + 1) * LTAPS)
            filtered = pick_groups(wide, n, LTAPS, per) + skip * pf[own]
            filt_ref[own] = filtered
            mixed = f_ref[0, own] * filtered
            there = pl.multiple_of(place_ref[b + n] * LTAPS, LTAPS)
            mixed_ref[:, pl.ds(there, LTAPS)] = mixed.T.astype(BF16)


def forward(x, halo, short_taps, skip, table, place, chunk, chunks):
    blocks, _, rows, cols = x.shape
    cols //= chunks
    tokens = blocks * rows
    tiles = cols // LANES
    first = chunk * tiles
    tab_rows = table.shape[0] * LANES // skip.shape[1]
    return pl.pallas_call(
        forward_kernel,
        grid_spec=pltpu.PrefetchScalarGridSpec(
            num_scalar_prefetch=1,
            grid=(tiles,),
            in_specs=[
                pl.BlockSpec((blocks, 3, rows, LANES), lambda c, _: (0, 0, 0, first + c)),
                pl.BlockSpec((halo.shape[0], LANES), lambda c, _: (0, first + c)),
                pl.BlockSpec((3, SHORT, LANES), lambda c, _: (0, 0, first + c)),
                pl.BlockSpec((1, LANES), lambda c, _: (0, first + c)),
                pl.BlockSpec((tab_rows, 2 * LTAPS), lambda c, _: (first + c, 0)),
            ],
            out_specs=[
                pl.BlockSpec((LANES, tokens), lambda c, _: (c, 0)),
                pl.BlockSpec((3, tokens, LANES), lambda c, _: (0, 0, c)),
                pl.BlockSpec((tokens, LANES), lambda c, _: (0, c)),
            ],
            scratch_shapes=[
                pltpu.VMEM((3, PAD + LTAPS + tokens, LANES), F32),
                pltpu.VMEM((tokens, LANES), F32),
                pltpu.VMEM((LTAPS + tokens, LANES), BF16),
                pltpu.VMEM((tab_rows, 2 * LTAPS), F32),
            ],
        ),
        out_shape=[
            jax.ShapeDtypeStruct((cols, tokens), BF16),
            jax.ShapeDtypeStruct((3, tokens, cols), F32),
            jax.ShapeDtypeStruct((tokens, cols), F32),
        ],
        compiler_params=params(),
        name="forward",
    )(place, x, halo, short_taps, skip, table)


def sum_by_lag(gram):
    wide = gram.shape[1]
    parts = [gram[i : i + 8] for i in range(0, gram.shape[0], 8)]
    step = 8
    while len(parts) > 1:
        parts = [
            parts[k] + pltpu.roll(parts[k + 1], wide - step, 1) for k in range(0, len(parts), 2)
        ]
        step *= 2
    total = parts[0]
    row = lax.broadcasted_iota(jnp.int32, total.shape, 0)
    for bit in (1, 2, 4):
        total = jnp.where((row & bit) != 0, pltpu.roll(total, wide - bit, 1), total)
    return jnp.sum(total[:, :LTAPS], axis=0, keepdims=True)


def backward_kernel(
    mo_ref, mr_ref, f_ref, filt_ref, x_ref, n_ref, taps_ref, skip_ref, tab_ref,
    grad_ref, short_ref, long_ref, db, fg, wide, left, right,
):
    blocks, _, rows, _ = x_ref.shape
    tokens = blocks * rows
    per = tab_ref.shape[0] // LTAPS
    count = tokens // LTAPS
    skip = skip_ref[...]
    lane_group = lax.broadcasted_iota(jnp.int32, (1, LANES), 1) // (LANES // per)
    gain = jnp.zeros((8, LANES), F32)
    for b in range(count):
        own = slice(b * LTAPS, (b + 1) * LTAPS)
        mixed_grad = mo_ref[own] + mr_ref[own].astype(F32)
        slope = mixed_grad * f_ref[0, own]
        db[own] = slope.astype(BF16)
        fg[0, own] = mixed_grad * filt_ref[own]
        fg[1, own] = skip * slope
        prod = f_ref[1, own] * f_ref[2, own]
        gain = gain + jnp.sum((prod * slope).reshape(LTAPS // 8, 8, LANES), axis=0)
        prod_b = prod.astype(BF16)
        for g in range(per):
            keep = (lane_group == g).astype(F32).astype(BF16)
            left[g * LTAPS : (g + 1) * LTAPS, b * LANES : (b + 1) * LANES] = prod_b * keep
    db[tokens : tokens + LTAPS + PAD] = n_ref[0 : LTAPS + PAD]
    db[tokens + LTAPS + PAD :] = jnp.zeros((LTAPS - PAD, LANES), BF16)
    for b in range(count):
        right[:, b * LANES : (b + 1) * LANES] = db[b * LTAPS : (b + 2) * LTAPS]
    for b in range(0, count, 2):
        wide[...] = jnp.dot(
            tab_ref[...], right[:, b * LANES : (b + 2) * LANES], preferred_element_type=F32
        )
        for n in range(2):
            own = slice((b + n) * LTAPS, (b + n + 1) * LTAPS)
            grad = pick_groups(wide, n, LTAPS, per) + fg[1, own]
            fg[1, own] = grad * f_ref[2, own]
            fg[2, own] = grad * f_ref[1, own]
    few = jnp.concatenate([tab_ref[g * LTAPS : g * LTAPS + PAD] for g in range(per)], axis=0)
    edge = jnp.dot(few, db[tokens : tokens + 2 * LTAPS], preferred_element_type=F32)
    begin = LTAPS + PAD
    grad = pick_groups(edge, 0, PAD, per) + skip * n_ref[0:PAD].astype(F32)
    fg[1, tokens : tokens + PAD] = grad * n_ref[begin + PAD : begin + 2 * PAD].astype(F32)
    fg[2, tokens : tokens + PAD] = grad * n_ref[begin : begin + PAD].astype(F32)
    fg[0, tokens : tokens + PAD] = n_ref[begin + 2 * PAD : begin + 3 * PAD].astype(F32)
    for i in range(3):
        sums = [jnp.zeros((8, LANES), F32) for _ in range(SHORT)]
        for b in range(count):
            low = b * LTAPS
            inputs = x_ref[b, i].astype(F32)
            total = None
            for j in range(SHORT):
                later = fg[i, low + j : low + j + LTAPS]
                term = taps_ref[i, j : j + 1] * later
                total = term if total is None else total + term
                sums[j] = sums[j] + jnp.sum((later * inputs).reshape(LTAPS // 8, 8, LANES), axis=0)
            grad_ref[b, i] = total.astype(BF16)
        for j in range(SHORT):
            short_ref[i, j : j + 1] = jnp.sum(sums[j], axis=0, keepdims=True)
        short_ref[i, SHORT : SHORT + 1] = jnp.sum(gain, axis=0, keepdims=True)
    wide[...] = lax.dot_general(left[...], right[...], (((1,), (1,)), ((), ())), preferred_element_type=F32)
    for g in range(per):
        gram = wide[g * LTAPS : (g + 1) * LTAPS]
        long_ref[g : g + 1] = sum_by_lag(gram)


def backward(mixed_own, mixed_rest, feats, filt, x, later, short_taps, skip, table, chunk, chunks):
    blocks, _, rows, cols = x.shape
    cols //= chunks
    tokens = blocks * rows
    tiles = cols // LANES
    first = chunk * tiles
    tab_rows = table.shape[0] * LANES // skip.shape[1]
    per = tab_rows // LTAPS
    tok = pl.BlockSpec((tokens, LANES), lambda c: (0, first + c))
    return pl.pallas_call(
        backward_kernel,
        grid=(tiles,),
        in_specs=[
            tok,
            tok,
            pl.BlockSpec((3, tokens, LANES), lambda c: (0, 0, c)),
            pl.BlockSpec((tokens, LANES), lambda c: (0, c)),
            pl.BlockSpec((blocks, 3, rows, LANES), lambda c: (0, 0, 0, first + c)),
            pl.BlockSpec((later.shape[0], LANES), lambda c: (0, first + c)),
            pl.BlockSpec((3, SHORT, LANES), lambda c: (0, 0, first + c)),
            pl.BlockSpec((1, LANES), lambda c: (0, first + c)),
            pl.BlockSpec((tab_rows, 2 * LTAPS), lambda c: (first + c, 0)),
        ],
        out_specs=[
            pl.BlockSpec((blocks, 3, rows, LANES), lambda c: (0, 0, 0, c)),
            pl.BlockSpec((3, SHORT + 1, LANES), lambda c: (0, 0, c)),
            pl.BlockSpec((per, LTAPS), lambda c: (c, 0)),
        ],
        out_shape=[
            jax.ShapeDtypeStruct((blocks, 3, rows, cols), BF16),
            jax.ShapeDtypeStruct((3, SHORT + 1, cols), F32),
            jax.ShapeDtypeStruct((tiles * per, LTAPS), F32),
        ],
        scratch_shapes=[
            pltpu.VMEM((tokens + 2 * LTAPS, LANES), BF16),
            pltpu.VMEM((3, tokens + PAD, LANES), F32),
            pltpu.VMEM((tab_rows, 2 * LTAPS), F32),
            pltpu.VMEM((tab_rows, tokens), BF16),
            pltpu.VMEM((2 * LTAPS, tokens), BF16),
        ],
        compiler_params=params(),
        name="backward",
    )(mixed_own, mixed_rest, feats, filt, x, later, short_taps, skip, table)


def pack_kernel(*refs):
    out_ref = refs[-1]
    for i, ref in enumerate(refs[:3]):
        out_ref[0, i] = ref[...]


def pack(arrays, seq):
    rows, width = arrays[0].shape
    cols = width // seq
    return pl.pallas_call(
        pack_kernel,
        grid=(seq,),
        in_specs=[pl.BlockSpec((rows, cols), lambda s: (0, s))] * 3,
        out_specs=pl.BlockSpec((1, 3, rows, cols), lambda s: (s, 0, 0, 0)),
        out_shape=jax.ShapeDtypeStruct((seq, 3, rows, cols), BF16),
        compiler_params=params(),
        name="pack",
    )(*arrays)


def unpack_kernel(*refs):
    parts, outs = refs[:-3], refs[-3:]
    cols = parts[0].shape[3]
    for n, part in enumerate(parts):
        for i, out in enumerate(outs):
            out[:, n * cols : (n + 1) * cols] = part[0, i]


def unpack(parts):
    seq, _, rows, cols = parts[0].shape
    wide = cols * len(parts)
    shape = jax.ShapeDtypeStruct((rows, seq * wide), BF16)
    return pl.pallas_call(
        unpack_kernel,
        grid=(seq,),
        in_specs=[pl.BlockSpec((1, 3, rows, cols), lambda s: (s, 0, 0, 0))] * len(parts),
        out_specs=[pl.BlockSpec((rows, wide), lambda s: (0, s))] * 3,
        out_shape=[shape] * 3,
        compiler_params=params(),
        name="unpack",
    )(*parts)


def along(block, axis, distance):
    size = lax.axis_size(axis)
    return lax.ppermute(block, axis, [(i, i + distance) for i in range(size) if 0 <= i + distance < size])


def around(block, axis, distance):
    size = lax.axis_size(axis)
    return lax.ppermute(block, axis, [(i, (i + distance) % size) for i in range(size)])


def across(block, axis, bit):
    return lax.ppermute(block, axis, [(i, i ^ bit) for i in range(lax.axis_size(axis))])


def bits_of(axis):
    size = lax.axis_size(axis)
    return [1 << n for n in range(size.bit_length() - 1)]


def sum_over(value, axes):
    for axis in axes:
        for bit in bits_of(axis):
            value = value + across(value, axis, bit)
    return value


def split_kernel(y_ref, *refs):
    count = (len(refs) - 1) // 2
    for n in range(count):
        refs[count + 1 + n][...] = refs[n][...]


def split_cotangent(cotangent, y, ys, col_part, after):
    rows, width = cotangent.shape

    def source(step):
        return pl.BlockSpec((rows, col_part), lambda z, y_ref: (0, z * ys + (y_ref[0] + step) % ys))

    return pl.pallas_call(
        split_kernel,
        grid_spec=pltpu.PrefetchScalarGridSpec(
            num_scalar_prefetch=1,
            grid=(Z,),
            in_specs=[source(step) for step in range(ys)] + [pl.BlockSpec(memory_space=pl.ANY)],
            out_specs=[pl.BlockSpec((rows, col_part), lambda z, _: (0, z))] * ys,
        ),
        out_shape=[jax.ShapeDtypeStruct((rows, width // ys), BF16)] * ys,
        compiler_params=params(),
        name="split",
    )(y.reshape(1), *([cotangent] * ys), after)


def join_kernel(axis, count, *refs):
    out = refs[-1]
    for n in range(count):
        size = refs[n].shape[axis]
        here = slice(n * size, (n + 1) * size)
        if axis == 0:
            out[here] = refs[n][...]
        else:
            out[:, here] = refs[n][...]


def join(parts, axis, after=()):
    shape = list(parts[0].shape)
    tile = shape[-1] // Z
    block = pl.BlockSpec((*shape[:-1], tile), lambda i: (0, 0, 0, i))
    shape[axis] *= len(parts)
    return pl.pallas_call(
        functools.partial(join_kernel, axis, len(parts)),
        grid=(Z,),
        in_specs=[block] * len(parts) + [pl.BlockSpec(memory_space=pl.ANY)] * len(after),
        out_specs=pl.BlockSpec((*shape[:-1], tile), lambda i: (0, 0, 0, i)),
        out_shape=jax.ShapeDtypeStruct(tuple(shape), BF16),
        compiler_params=params(),
        name="join",
    )(*parts, *after)


def own_cotangent(cotangent, col_part, after):
    ys, y = lax.axis_size("y"), lax.axis_index("y")
    held = split_cotangent(cotangent, y, ys, col_part, after)
    held = [around(part, "y", step) if step else part for step, part in enumerate(held)]
    return join([part[None, None] for part in held], 0)


def gather_cotangent(held, after):
    bits = bits_of("seq")
    for bit in reversed(bits[1:]):
        held = join([held, across(held, "seq", bit)], 1, after)
    return held, across(held, "seq", bits[0])


def mixed_grad_kernel(place_ref, a_ref, b_ref, w_ref, _, out_ref, head_ref, found):
    _, count, rows, _ = a_ref.shape
    tokens = count * rows
    pieces = jnp.concatenate([ref[...].reshape(tokens, -1) for ref in (a_ref, b_ref)], axis=0)
    found[...] = contract(pieces, w_ref[...], 1)
    for block in range(2 * count):
        there = pl.multiple_of(place_ref[block] * rows, rows)
        out_ref[block * rows : (block + 1) * rows] = found[pl.ds(there, rows)].astype(out_ref.dtype)
    head_ref[...] = out_ref[0 : LTAPS + PAD]


def mixed_grad(cots, weights, place, step, dtype, after):
    _, count, rows, width = cots[0].shape
    tokens = 2 * count * rows
    cols = weights.shape[0]
    tile = min(cols, 2 * LANES)
    piece = pl.BlockSpec((1, count, rows, width), lambda i, _: (step, 0, 0, 0))
    return pl.pallas_call(
        mixed_grad_kernel,
        grid_spec=pltpu.PrefetchScalarGridSpec(
            num_scalar_prefetch=1,
            grid=(cols // tile,),
            in_specs=[
                piece,
                piece,
                pl.BlockSpec((tile, width), lambda i, _: (i, 0)),
                pl.BlockSpec(memory_space=pl.ANY),
            ],
            out_specs=[
                pl.BlockSpec((tokens, tile), lambda i, _: (0, i)),
                pl.BlockSpec((LTAPS + PAD, tile), lambda i, _: (0, i)),
            ],
            scratch_shapes=[pltpu.VMEM((tokens, tile), F32)],
        ),
        out_shape=[
            jax.ShapeDtypeStruct((tokens, cols), dtype),
            jax.ShapeDtypeStruct((LTAPS + PAD, cols), dtype),
        ],
        compiler_params=params(),
        name="mixed_grad",
    )(place, *cots, weights, after)


def weight_grad_kernel(scale, chunks, a_ref, b_ref, *refs):
    mixed, out = refs[:-2], refs[-1]
    steps, count, rows, tile = a_ref.shape
    tokens = count * rows
    part = mixed[0].shape[0]
    for h in range(chunks):
        total = None
        for step in range(steps):
            for n, ref in enumerate((a_ref, b_ref)):
                left = mixed[step * chunks + h][:, n * tokens : (n + 1) * tokens]
                term = jnp.dot(left, ref[step].reshape(tokens, tile), preferred_element_type=F32)
                total = term if total is None else total + term
        out[h * part : (h + 1) * part] = (total * scale).astype(BF16)


def weight_grad(cots, mixed, chunks, scale, after):
    steps, count, rows, width = cots[0].shape
    part, tokens = mixed[0].shape
    tile = width // Z
    piece = pl.BlockSpec((steps, count, rows, tile), lambda i: (0, 0, 0, i))
    return pl.pallas_call(
        functools.partial(weight_grad_kernel, scale, chunks),
        grid=(Z,),
        in_specs=[piece, piece] + [pl.BlockSpec((part, tokens), lambda i: (0, 0))] * len(mixed)
        + [pl.BlockSpec(memory_space=pl.ANY)],
        out_specs=pl.BlockSpec((part * chunks, tile), lambda i: (0, i)),
        out_shape=jax.ShapeDtypeStruct((part * chunks, width), BF16),
        compiler_params=params(),
        name="weight_grad",
    )(*cots, *mixed, after)


def tail_kernel(x_ref, before_ref, *refs):
    out_ref = refs[-1]
    rows = x_ref.shape[2]
    out_ref[0:PAD] = x_ref[0, 0, rows - PAD :]
    for i in (1, 2):
        begin = PAD + (i - 1) * (PAD + rows)
        out_ref[begin : begin + PAD] = before_ref[0, i, rows - PAD :]
        out_ref[begin + PAD : begin + PAD + rows] = x_ref[0, i]


def tail_of(x, after):
    seq, _, rows, cols = x.shape

    def block(s):
        return pl.BlockSpec((1, 3, rows, cols), lambda i: (s, 0, 0, 0))

    out_rows = PAD + 2 * (PAD + rows)
    return pl.pallas_call(
        tail_kernel,
        grid=(1,),
        in_specs=[block(seq - 1), block(seq - 2)] + [pl.BlockSpec(memory_space=pl.ANY)] * len(after),
        out_specs=pl.BlockSpec((out_rows, cols), lambda i: (0, 0)),
        out_shape=jax.ShapeDtypeStruct((out_rows, cols), BF16),
        compiler_params=params(),
        name="tail",
    )(x, x, *after)


def head_kernel(mo_ref, mr_ref, *refs):
    out_ref = refs[-1]
    chunks = len(refs) // 2
    edge = LTAPS + PAD
    part = out_ref.shape[1] // chunks
    for h in range(chunks):
        own = slice(h * part, (h + 1) * part)
        f_ref, filt_ref = refs[2 * h : 2 * h + 2]
        mixed = mo_ref[:, own] + mr_ref[:, own].astype(F32)
        out_ref[0:edge, own] = (mixed * f_ref[0]).astype(BF16)
        out_ref[edge : edge + PAD, own] = f_ref[1, 0:PAD].astype(BF16)
        out_ref[edge + PAD : edge + 2 * PAD, own] = f_ref[2, 0:PAD].astype(BF16)
        out_ref[edge + 2 * PAD :, own] = (mixed[0:PAD] * filt_ref[0:PAD]).astype(BF16)


def head_of(mixed_own, mixed_rest, mixers):
    edge, cols = LTAPS + PAD, mixed_own.shape[1]
    part = cols // len(mixers)
    whole = pl.BlockSpec((edge, cols), lambda i: (0, 0))
    feat_specs = [
        pl.BlockSpec((3, edge, part), lambda i: (0, 0, 0)),
        pl.BlockSpec((edge, part), lambda i: (0, 0)),
    ]
    return pl.pallas_call(
        head_kernel,
        grid=(1,),
        in_specs=[whole, whole] + feat_specs * len(mixers),
        out_specs=pl.BlockSpec((edge + 3 * PAD, cols), lambda i: (0, 0)),
        out_shape=jax.ShapeDtypeStruct((edge + 3 * PAD, cols), BF16),
        compiler_params=params(),
        name="head",
    )(mixed_own, mixed_rest, *[array for mixer in mixers for array in mixer[1:]])


def contract(a, b, dim):
    return lax.dot_general(a, b, (((dim,), (dim,)), ((), ())), preferred_element_type=F32)


def places(seq):
    bits = bits_of("seq")
    source = lax.iota(jnp.int32, seq) ^ lax.axis_index("seq")
    return sum(((source >> n) & 1) << (len(bits) - 1 - n) for n in range(len(bits)))


def body(queries, keys, values, cotangent, out_weight, short_taps, long_taps, skip_gain):
    rows, width = queries.shape
    col_part = out_weight.shape[1]
    seq, ys = lax.axis_size("seq"), lax.axis_size("y")
    cols = width // seq
    chunks = 2 if cols % (2 * LANES) == 0 else 1
    groups = long_taps.shape[1]
    fsdp = ("z", "y")
    grad_scale = float(rows * seq * ys * Z) ** (-0.5)

    weights = lax.all_gather(out_weight, "z", axis=1, tiled=True)
    fwd_table, bwd_table = make_tables(long_taps)
    skip = skip_gain.reshape(1, cols)
    place = places(seq)
    by_owner = pack((queries, keys, values), seq)
    x = lax.all_to_all(by_owner, "seq", split_axis=0, concat_axis=0, tiled=True)
    held = own_cotangent(cotangent, col_part, by_owner)
    halo = along(tail_of(x, [fwd_table, held]), fsdp, 1)
    mixers = [forward(x, halo, short_taps, skip, fwd_table, place, h, chunks) for h in range(chunks)]
    cots = gather_cotangent(held, [mixer[0] for mixer in mixers])

    parts, heads = [], []
    for step in range(1, ys):
        part, head = mixed_grad(cots, weights, place, step, BF16, parts[-1] if parts else place)
        parts.append(part)
        heads.append(around(head, "y", -step))
    mixed_own, own_head = mixed_grad(cots, weights, place, 0, F32, parts[-1])
    rest = [around(parts[step - 1], "y", -step) for step in range(1, ys)]
    mixed_rest = rest[0] if len(rest) == 1 else sum(piece.astype(F32) for piece in rest)
    head_rest = heads[0] if len(heads) == 1 else sum(piece.astype(F32) for piece in heads)
    head = head_of(own_head, head_rest, mixers)
    later = along(head, fsdp, -1)

    mixed_all = [
        around(mixers[h][0], "y", step) if step else mixers[h][0] for step in range(ys) for h in range(chunks)
    ]
    weight_sum = weight_grad(cots, mixed_all, chunks, grad_scale, head)
    weight_part = lax.psum_scatter(weight_sum, "z", scatter_dimension=1, tiled=True)

    grads, short_parts, long_parts = [], [], []
    for h in range(chunks):
        _, feats, filt = mixers[h]
        grad, short_part, long_part = backward(
            mixed_own, mixed_rest, feats, filt, x, later, short_taps, skip, bwd_table, h, chunks
        )
        grads.append(lax.all_to_all(grad, "seq", split_axis=0, concat_axis=0, tiled=True))
        short_parts.append(short_part)
        long_parts.append(long_part)

    query_grad, key_grad, value_grad = unpack(grads)
    packed = jnp.concatenate(
        [
            jnp.concatenate(short_parts, axis=2).reshape(3 * (SHORT + 1), cols),
            jnp.concatenate(long_parts, axis=0).reshape(-1, cols),
        ],
        axis=0,
    )
    packed = sum_over(packed, ("y", "z")) * grad_scale
    short_sum = packed[: 3 * (SHORT + 1)].reshape(3, SHORT + 1, cols)
    long_sum = packed[3 * (SHORT + 1) :].reshape(groups, LTAPS).T
    return (
        query_grad,
        key_grad,
        value_grad,
        weight_part.astype(F32),
        short_sum[:, :SHORT],
        long_sum,
        short_sum[0, SHORT],
    )


def solution(mesh):
    fsdp, seq = mesh.shape["fsdp"], mesh.shape["seq"]
    split = Mesh(mesh.devices.reshape(Z, fsdp // Z, seq), ("z", "y", "seq"))
    tokens = P(("z", "y", "seq"), None)
    specs = (P("seq", ("z", "y")), P(None, None, "seq"), P(None, "seq"), P("seq"))
    return jax.shard_map(
        body,
        mesh=split,
        in_specs=(tokens,) * 4 + specs,
        out_specs=(tokens,) * 3 + specs,
        check_vma=False,
    )
```

```python
import functools

import jax
import jax.numpy as jnp
from jax import lax
from jax.experimental import pallas as pl
from jax.experimental.pallas import tpu as pltpu
from jax.sharding import Mesh
from jax.sharding import PartitionSpec as P

SHORT = 7
LTAPS = 128
LANES = 128
PAD = 16
Z = 4
F32 = jnp.float32
BF16 = jnp.bfloat16


def params():
    return pltpu.CompilerParams(vmem_limit_bytes=60 * 2**20)


def tables_kernel(fwd_ref, bwd_ref, tf_ref, tb_ref):
    for g in range(fwd_ref.shape[0]):
        rows = slice(g * LTAPS, (g + 1) * LTAPS)
        for src, dst in ((fwd_ref, tf_ref), (bwd_ref, tb_ref)):
            wide = jnp.broadcast_to(src[g : g + 1, :], (LTAPS, 2 * LTAPS))
            dst[rows, :] = pltpu.roll(wide, 0, 1, stride=1, stride_axis=0).astype(BF16)


def make_tables(long_taps):
    by_group = long_taps.T
    groups = by_group.shape[0]
    fwd = jnp.pad(by_group[:, ::-1], ((0, 0), (1, LTAPS - 1)))
    bwd = jnp.pad(by_group, ((0, 0), (0, LTAPS)))
    per = 8
    row_spec = pl.BlockSpec((per, 2 * LTAPS), lambda i: (i, 0))
    tab_spec = pl.BlockSpec((per * LTAPS, 2 * LTAPS), lambda i: (i, 0))
    shape = jax.ShapeDtypeStruct((groups * LTAPS, 2 * LTAPS), BF16)
    return pl.pallas_call(
        tables_kernel,
        grid=(groups // per,),
        in_specs=[row_spec, row_spec],
        out_specs=[tab_spec, tab_spec],
        out_shape=[shape, shape],
        compiler_params=params(),
        name="tables",
    )(fwd, bwd)


def pick_groups(wide, col, rows, per):
    lane_group = lax.broadcasted_iota(jnp.int32, (rows, LANES), 1) // (LANES // per)
    cols = slice(col * LANES, (col + 1) * LANES)
    out = wide[0:rows, cols]
    for g in range(1, per):
        out = jnp.where(lane_group == g, wide[g * rows : (g + 1) * rows, cols], out)
    return out


def features_of(taps_ref, row, xf, i, begin):
    total = taps_ref[row, 0:1] * xf[i, PAD + begin : PAD + begin + LTAPS]
    for j in range(1, SHORT):
        total = total + taps_ref[row, j : j + 1] * xf[i, PAD + begin - j : PAD + begin - j + LTAPS]
    return total


def forward_kernel(
    place_ref, x_ref, h_ref, taps_ref, skip_ref, tab_ref, _, mixed_ref, f_ref, filt_ref, xf, pf, pb, wide
):
    blocks, _, rows, _ = x_ref.shape
    tokens = blocks * rows
    per = tab_ref.shape[0] // LTAPS
    for i in range(3):
        xf[i, 0:PAD] = h_ref[i * PAD : (i + 1) * PAD].astype(F32)
        for b in range(blocks):
            begin = PAD + b * rows
            xf[i, begin : begin + rows] = x_ref[b, i].astype(F32)
    pb[0:LTAPS] = h_ref[3 * PAD : 3 * PAD + LTAPS]
    for begin in range(0, tokens, LTAPS):
        own = slice(begin, begin + LTAPS)
        f1 = features_of(taps_ref, 1, xf, 1, begin)
        f2 = features_of(taps_ref, 2, xf, 2, begin)
        prod = f1 * f2
        f_ref[1, own] = f1
        f_ref[2, own] = f2
        f_ref[0, own] = features_of(taps_ref, 0, xf, 0, begin)
        pf[own] = prod
        pb[LTAPS + begin : 2 * LTAPS + begin] = prod.astype(BF16)
    skip = skip_ref[...]
    for b in range(0, tokens // LTAPS, 2):
        low = b * LTAPS
        windows = jnp.concatenate([pb[low : low + 2 * LTAPS], pb[low + LTAPS : low + 3 * LTAPS]], axis=1)
        wide[...] = jnp.dot(tab_ref[...], windows, preferred_element_type=F32)
        for n in range(2):
            own = slice(low + n * LTAPS, low + (n + 1) * LTAPS)
            filtered = pick_groups(wide, n, LTAPS, per) + skip * pf[own]
            filt_ref[own] = filtered
            mixed = f_ref[0, own] * filtered
            there = pl.multiple_of(place_ref[b + n] * LTAPS, LTAPS)
            mixed_ref[:, pl.ds(there, LTAPS)] = mixed.T.astype(BF16)


def forward(x, halo, short_taps, skip, table, place, chunk, chunks, after):
    blocks, _, rows, cols = x.shape
    cols //= chunks
    tokens = blocks * rows
    tiles = cols // LANES
    first = chunk * tiles
    tab_rows = table.shape[0] * LANES // skip.shape[1]
    return pl.pallas_call(
        forward_kernel,
        grid_spec=pltpu.PrefetchScalarGridSpec(
            num_scalar_prefetch=1,
            grid=(tiles,),
            in_specs=[
                pl.BlockSpec((blocks, 3, rows, LANES), lambda c, _: (0, 0, 0, first + c)),
                pl.BlockSpec((halo.shape[0], LANES), lambda c, _: (0, first + c)),
                pl.BlockSpec((3, SHORT, LANES), lambda c, _: (0, 0, first + c)),
                pl.BlockSpec((1, LANES), lambda c, _: (0, first + c)),
                pl.BlockSpec((tab_rows, 2 * LTAPS), lambda c, _: (first + c, 0)),
                pl.BlockSpec(memory_space=pl.ANY),
            ],
            out_specs=[
                pl.BlockSpec((LANES, tokens), lambda c, _: (c, 0)),
                pl.BlockSpec((3, tokens, LANES), lambda c, _: (0, 0, c)),
                pl.BlockSpec((tokens, LANES), lambda c, _: (0, c)),
            ],
            scratch_shapes=[
                pltpu.VMEM((3, PAD + tokens, LANES), F32),
                pltpu.VMEM((tokens, LANES), F32),
                pltpu.VMEM((LTAPS + tokens, LANES), BF16),
                pltpu.VMEM((tab_rows, 2 * LTAPS), F32),
            ],
        ),
        out_shape=[
            jax.ShapeDtypeStruct((cols, tokens), BF16),
            jax.ShapeDtypeStruct((3, tokens, cols), F32),
            jax.ShapeDtypeStruct((tokens, cols), F32),
        ],
        compiler_params=params(),
        name="forward",
    )(place, x, halo, short_taps, skip, table, after)


def sum_by_lag(gram):
    wide = gram.shape[1]
    parts = [gram[i : i + 8] for i in range(0, gram.shape[0], 8)]
    step = 8
    while len(parts) > 1:
        parts = [
            parts[k] + pltpu.roll(parts[k + 1], wide - step, 1) for k in range(0, len(parts), 2)
        ]
        step *= 2
    total = parts[0]
    row = lax.broadcasted_iota(jnp.int32, total.shape, 0)
    for bit in (1, 2, 4):
        total = jnp.where((row & bit) != 0, pltpu.roll(total, wide - bit, 1), total)
    return jnp.sum(total[:, :LTAPS], axis=0, keepdims=True)


def backward_kernel(
    mo_ref, mr_ref, f_ref, filt_ref, x_ref, n_ref, taps_ref, skip_ref, tab_ref,
    grad_ref, short_ref, long_ref, db, fg, wide, left, right,
):
    blocks, _, rows, _ = x_ref.shape
    tokens = blocks * rows
    per = tab_ref.shape[0] // LTAPS
    count = tokens // LTAPS
    skip = skip_ref[...]
    lane_group = lax.broadcasted_iota(jnp.int32, (1, LANES), 1) // (LANES // per)
    gain = jnp.zeros((8, LANES), F32)
    for b in range(count):
        own = slice(b * LTAPS, (b + 1) * LTAPS)
        mixed_grad = mo_ref[own] + mr_ref[own].astype(F32)
        slope = mixed_grad * f_ref[0, own]
        db[own] = slope.astype(BF16)
        fg[0, own] = mixed_grad * filt_ref[own]
        fg[1, own] = skip * slope
        prod = f_ref[1, own] * f_ref[2, own]
        gain = gain + jnp.sum((prod * slope).reshape(LTAPS // 8, 8, LANES), axis=0)
        prod_b = prod.astype(BF16)
        for g in range(per):
            keep = (lane_group == g).astype(F32).astype(BF16)
            left[g * LTAPS : (g + 1) * LTAPS, b * LANES : (b + 1) * LANES] = prod_b * keep
    db[tokens : tokens + LTAPS + PAD] = n_ref[0 : LTAPS + PAD]
    db[tokens + LTAPS + PAD :] = jnp.zeros((LTAPS - PAD, LANES), BF16)
    for b in range(count):
        right[:, b * LANES : (b + 1) * LANES] = db[b * LTAPS : (b + 2) * LTAPS]
    for b in range(0, count, 2):
        wide[...] = jnp.dot(
            tab_ref[...], right[:, b * LANES : (b + 2) * LANES], preferred_element_type=F32
        )
        for n in range(2):
            own = slice((b + n) * LTAPS, (b + n + 1) * LTAPS)
            grad = pick_groups(wide, n, LTAPS, per) + fg[1, own]
            fg[1, own] = grad * f_ref[2, own]
            fg[2, own] = grad * f_ref[1, own]
    few = jnp.concatenate([tab_ref[g * LTAPS : g * LTAPS + PAD] for g in range(per)], axis=0)
    edge = jnp.dot(few, db[tokens : tokens + 2 * LTAPS], preferred_element_type=F32)
    begin = LTAPS + PAD
    grad = pick_groups(edge, 0, PAD, per) + skip * n_ref[0:PAD].astype(F32)
    fg[1, tokens : tokens + PAD] = grad * n_ref[begin + PAD : begin + 2 * PAD].astype(F32)
    fg[2, tokens : tokens + PAD] = grad * n_ref[begin : begin + PAD].astype(F32)
    fg[0, tokens : tokens + PAD] = n_ref[begin + 2 * PAD : begin + 3 * PAD].astype(F32)
    for i in range(3):
        sums = [jnp.zeros((8, LANES), F32) for _ in range(SHORT)]
        for b in range(count):
            low = b * LTAPS
            inputs = x_ref[b, i].astype(F32)
            total = None
            for j in range(SHORT):
                later = fg[i, low + j : low + j + LTAPS]
                term = taps_ref[i, j : j + 1] * later
                total = term if total is None else total + term
                sums[j] = sums[j] + jnp.sum((later * inputs).reshape(LTAPS // 8, 8, LANES), axis=0)
            grad_ref[b, i] = total.astype(BF16)
        for j in range(SHORT):
            short_ref[i, j : j + 1] = jnp.sum(sums[j], axis=0, keepdims=True)
        short_ref[i, SHORT : SHORT + 1] = jnp.sum(gain, axis=0, keepdims=True)
    wide[...] = lax.dot_general(left[...], right[...], (((1,), (1,)), ((), ())), preferred_element_type=F32)
    for g in range(per):
        gram = wide[g * LTAPS : (g + 1) * LTAPS]
        long_ref[g : g + 1] = sum_by_lag(gram)


def backward(mixed_own, mixed_rest, feats, filt, x, later, short_taps, skip, table, chunk, chunks):
    blocks, _, rows, cols = x.shape
    cols //= chunks
    tokens = blocks * rows
    tiles = cols // LANES
    first = chunk * tiles
    tab_rows = table.shape[0] * LANES // skip.shape[1]
    per = tab_rows // LTAPS
    tok = pl.BlockSpec((tokens, LANES), lambda c: (0, first + c))
    return pl.pallas_call(
        backward_kernel,
        grid=(tiles,),
        in_specs=[
            tok,
            tok,
            pl.BlockSpec((3, tokens, LANES), lambda c: (0, 0, c)),
            pl.BlockSpec((tokens, LANES), lambda c: (0, c)),
            pl.BlockSpec((blocks, 3, rows, LANES), lambda c: (0, 0, 0, first + c)),
            pl.BlockSpec((later.shape[0], LANES), lambda c: (0, first + c)),
            pl.BlockSpec((3, SHORT, LANES), lambda c: (0, 0, first + c)),
            pl.BlockSpec((1, LANES), lambda c: (0, first + c)),
            pl.BlockSpec((tab_rows, 2 * LTAPS), lambda c: (first + c, 0)),
        ],
        out_specs=[
            pl.BlockSpec((blocks, 3, rows, LANES), lambda c: (0, 0, 0, c)),
            pl.BlockSpec((3, SHORT + 1, LANES), lambda c: (0, 0, c)),
            pl.BlockSpec((per, LTAPS), lambda c: (c, 0)),
        ],
        out_shape=[
            jax.ShapeDtypeStruct((blocks, 3, rows, cols), BF16),
            jax.ShapeDtypeStruct((3, SHORT + 1, cols), F32),
            jax.ShapeDtypeStruct((tiles * per, LTAPS), F32),
        ],
        scratch_shapes=[
            pltpu.VMEM((tokens + 2 * LTAPS, LANES), BF16),
            pltpu.VMEM((3, tokens + PAD, LANES), F32),
            pltpu.VMEM((tab_rows, 2 * LTAPS), F32),
            pltpu.VMEM((tab_rows, tokens), BF16),
            pltpu.VMEM((2 * LTAPS, tokens), BF16),
        ],
        compiler_params=params(),
        name="backward",
    )(mixed_own, mixed_rest, feats, filt, x, later, short_taps, skip, table)


def pack_kernel(*refs):
    out_ref = refs[-1]
    for i, ref in enumerate(refs[:3]):
        out_ref[0, i] = ref[...]


def pack(arrays, seq):
    rows, width = arrays[0].shape
    cols = width // seq
    return pl.pallas_call(
        pack_kernel,
        grid=(seq,),
        in_specs=[pl.BlockSpec((rows, cols), lambda s: (0, s))] * 3,
        out_specs=pl.BlockSpec((1, 3, rows, cols), lambda s: (s, 0, 0, 0)),
        out_shape=jax.ShapeDtypeStruct((seq, 3, rows, cols), BF16),
        compiler_params=params(),
        name="pack",
    )(*arrays)


def unpack_kernel(*refs):
    parts, outs = refs[:-3], refs[-3:]
    cols = parts[0].shape[3]
    for n, part in enumerate(parts):
        for i, out in enumerate(outs):
            out[:, n * cols : (n + 1) * cols] = part[0, i]


def unpack(parts):
    seq, _, rows, cols = parts[0].shape
    wide = cols * len(parts)
    shape = jax.ShapeDtypeStruct((rows, seq * wide), BF16)
    return pl.pallas_call(
        unpack_kernel,
        grid=(seq,),
        in_specs=[pl.BlockSpec((1, 3, rows, cols), lambda s: (s, 0, 0, 0))] * len(parts),
        out_specs=[pl.BlockSpec((rows, wide), lambda s: (0, s))] * 3,
        out_shape=[shape] * 3,
        compiler_params=params(),
        name="unpack",
    )(*parts)


def along(block, axis, distance):
    size = lax.axis_size(axis)
    return lax.ppermute(block, axis, [(i, i + distance) for i in range(size) if 0 <= i + distance < size])


def around(block, axis, distance):
    size = lax.axis_size(axis)
    return lax.ppermute(block, axis, [(i, (i + distance) % size) for i in range(size)])


def across(block, axis, bit):
    return lax.ppermute(block, axis, [(i, i ^ bit) for i in range(lax.axis_size(axis))])


def bits_of(axis):
    size = lax.axis_size(axis)
    return [1 << n for n in range(size.bit_length() - 1)]


def sum_over(value, axes):
    for axis in axes:
        for bit in bits_of(axis):
            value = value + across(value, axis, bit)
    return value


def split_kernel(y_ref, *refs):
    count = (len(refs) - 1) // 2
    for n in range(count):
        refs[count + 1 + n][...] = refs[n][...]


def split_cotangent(cotangent, y, ys, col_part, after):
    rows, width = cotangent.shape

    def source(step):
        return pl.BlockSpec((rows, col_part), lambda z, y_ref: (0, z * ys + (y_ref[0] + step) % ys))

    return pl.pallas_call(
        split_kernel,
        grid_spec=pltpu.PrefetchScalarGridSpec(
            num_scalar_prefetch=1,
            grid=(Z,),
            in_specs=[source(step) for step in range(ys)] + [pl.BlockSpec(memory_space=pl.ANY)],
            out_specs=[pl.BlockSpec((rows, col_part), lambda z, _: (0, z))] * ys,
        ),
        out_shape=[jax.ShapeDtypeStruct((rows, width // ys), BF16)] * ys,
        compiler_params=params(),
        name="split",
    )(y.reshape(1), *([cotangent] * ys), after)


def join_kernel(axis, count, *refs):
    out = refs[-1]
    for n in range(count):
        size = refs[n].shape[axis]
        here = slice(n * size, (n + 1) * size)
        if axis == 0:
            out[here] = refs[n][...]
        else:
            out[:, here] = refs[n][...]


def join(parts, axis, after=()):
    shape = list(parts[0].shape)
    tile = shape[-1] // Z
    block = pl.BlockSpec((*shape[:-1], tile), lambda i: (0, 0, 0, i))
    shape[axis] *= len(parts)
    return pl.pallas_call(
        functools.partial(join_kernel, axis, len(parts)),
        grid=(Z,),
        in_specs=[block] * len(parts) + [pl.BlockSpec(memory_space=pl.ANY)] * len(after),
        out_specs=pl.BlockSpec((*shape[:-1], tile), lambda i: (0, 0, 0, i)),
        out_shape=jax.ShapeDtypeStruct(tuple(shape), BF16),
        compiler_params=params(),
        name="join",
    )(*parts, *after)


def own_cotangent(cotangent, col_part, after):
    ys, y = lax.axis_size("y"), lax.axis_index("y")
    held = split_cotangent(cotangent, y, ys, col_part, after)
    held = [around(part, "y", step) if step else part for step, part in enumerate(held)]
    return join([part[None, None] for part in held], 0)


def gather_cotangent(held, after):
    bits = bits_of("seq")
    for bit in reversed(bits[1:]):
        held = join([held, across(held, "seq", bit)], 1, after)
    return held, across(held, "seq", bits[0])


def mixed_grad_kernel(place_ref, a_ref, b_ref, w_ref, _, out_ref, head_ref, found):
    _, count, rows, _ = a_ref.shape
    tokens = count * rows
    pieces = jnp.concatenate([ref[...].reshape(tokens, -1) for ref in (a_ref, b_ref)], axis=0)
    found[...] = contract(pieces, w_ref[...], 1)
    for block in range(2 * count):
        there = pl.multiple_of(place_ref[block] * rows, rows)
        out_ref[block * rows : (block + 1) * rows] = found[pl.ds(there, rows)].astype(out_ref.dtype)
    head_ref[...] = out_ref[0 : LTAPS + PAD]


def mixed_grad(cots, weights, place, step, dtype, after):
    _, count, rows, width = cots[0].shape
    tokens = 2 * count * rows
    cols = weights.shape[0]
    tile = min(cols, 2 * LANES)
    piece = pl.BlockSpec((1, count, rows, width), lambda i, _: (step, 0, 0, 0))
    return pl.pallas_call(
        mixed_grad_kernel,
        grid_spec=pltpu.PrefetchScalarGridSpec(
            num_scalar_prefetch=1,
            grid=(cols // tile,),
            in_specs=[
                piece,
                piece,
                pl.BlockSpec((tile, width), lambda i, _: (i, 0)),
                pl.BlockSpec(memory_space=pl.ANY),
            ],
            out_specs=[
                pl.BlockSpec((tokens, tile), lambda i, _: (0, i)),
                pl.BlockSpec((LTAPS + PAD, tile), lambda i, _: (0, i)),
            ],
            scratch_shapes=[pltpu.VMEM((tokens, tile), F32)],
        ),
        out_shape=[
            jax.ShapeDtypeStruct((tokens, cols), dtype),
            jax.ShapeDtypeStruct((LTAPS + PAD, cols), dtype),
        ],
        compiler_params=params(),
        name="mixed_grad",
    )(place, *cots, weights, after)


def weight_grad_kernel(scale, a_ref, b_ref, *refs):
    steps, count, rows, tile = a_ref.shape
    tokens = count * rows
    mixed, out = refs[:steps], refs[-1]
    total = None
    for step in range(steps):
        for n, ref in enumerate((a_ref, b_ref)):
            left = mixed[step][:, n * tokens : (n + 1) * tokens]
            term = jnp.dot(left, ref[step].reshape(tokens, tile), preferred_element_type=F32)
            total = term if total is None else total + term
    out[...] = (total * scale).astype(BF16)


def weight_grad(cots, mixed, chunk, chunks, scale, target, after):
    steps, count, rows, width = cots[0].shape
    part, tokens = mixed[0].shape
    tile = width // Z
    piece = pl.BlockSpec((steps, count, rows, tile), lambda i: (0, 0, 0, i))
    extra = [after] + ([] if target is None else [target])
    return pl.pallas_call(
        functools.partial(weight_grad_kernel, scale),
        grid=(Z,),
        in_specs=[piece, piece]
        + [pl.BlockSpec((part, tokens), lambda i: (0, 0))] * len(mixed)
        + [pl.BlockSpec(memory_space=pl.ANY)] * len(extra),
        out_specs=pl.BlockSpec((part, tile), lambda i: (chunk, i)),
        out_shape=jax.ShapeDtypeStruct((part * chunks, width), BF16),
        input_output_aliases={} if target is None else {3 + len(mixed): 0},
        compiler_params=params(),
        name="weight_grad",
    )(*cots, *mixed, *extra)


def tail_kernel(x_ref, before_ref, taps_ref, *refs):
    out_ref, xf = refs[-2:]
    rows = x_ref.shape[2]
    for i in range(3):
        out_ref[i * PAD : (i + 1) * PAD] = x_ref[0, i, rows - PAD :]
    for i in (1, 2):
        xf[i - 1, 0:PAD] = before_ref[0, i, rows - PAD :].astype(F32)
        xf[i - 1, PAD:] = x_ref[0, i].astype(F32)
    prod = features_of(taps_ref, 1, xf, 0, 0) * features_of(taps_ref, 2, xf, 1, 0)
    out_ref[3 * PAD :] = prod.astype(BF16)


def tail_of(x, short_taps, after):
    seq, _, rows, cols = x.shape

    def block(s):
        return pl.BlockSpec((1, 3, rows, LANES), lambda c: (s, 0, 0, c))

    out_rows = 3 * PAD + rows
    return pl.pallas_call(
        tail_kernel,
        grid=(cols // LANES,),
        in_specs=[block(seq - 1), block(seq - 2), pl.BlockSpec((3, SHORT, LANES), lambda c: (0, 0, c))]
        + [pl.BlockSpec(memory_space=pl.ANY)] * len(after),
        out_specs=pl.BlockSpec((out_rows, LANES), lambda c: (0, c)),
        out_shape=jax.ShapeDtypeStruct((out_rows, cols), BF16),
        scratch_shapes=[pltpu.VMEM((2, PAD + rows, LANES), F32)],
        compiler_params=params(),
        name="tail",
    )(x, x, short_taps, *after)


def head_kernel(mo_ref, mr_ref, *refs):
    out_ref = refs[-1]
    chunks = len(refs) // 2
    edge = LTAPS + PAD
    part = out_ref.shape[1] // chunks
    for h in range(chunks):
        own = slice(h * part, (h + 1) * part)
        f_ref, filt_ref = refs[2 * h : 2 * h + 2]
        mixed = mo_ref[:, own] + mr_ref[:, own].astype(F32)
        out_ref[0:edge, own] = (mixed * f_ref[0]).astype(BF16)
        out_ref[edge : edge + PAD, own] = f_ref[1, 0:PAD].astype(BF16)
        out_ref[edge + PAD : edge + 2 * PAD, own] = f_ref[2, 0:PAD].astype(BF16)
        out_ref[edge + 2 * PAD :, own] = (mixed[0:PAD] * filt_ref[0:PAD]).astype(BF16)


def head_of(mixed_own, mixed_rest, mixers):
    edge, cols = LTAPS + PAD, mixed_own.shape[1]
    part = cols // len(mixers)
    whole = pl.BlockSpec((edge, cols), lambda i: (0, 0))
    feat_specs = [
        pl.BlockSpec((3, edge, part), lambda i: (0, 0, 0)),
        pl.BlockSpec((edge, part), lambda i: (0, 0)),
    ]
    return pl.pallas_call(
        head_kernel,
        grid=(1,),
        in_specs=[whole, whole] + feat_specs * len(mixers),
        out_specs=pl.BlockSpec((edge + 3 * PAD, cols), lambda i: (0, 0)),
        out_shape=jax.ShapeDtypeStruct((edge + 3 * PAD, cols), BF16),
        compiler_params=params(),
        name="head",
    )(mixed_own, mixed_rest, *[array for mixer in mixers for array in mixer[1:]])


def contract(a, b, dim):
    return lax.dot_general(a, b, (((dim,), (dim,)), ((), ())), preferred_element_type=F32)


def places(seq):
    bits = bits_of("seq")
    source = lax.iota(jnp.int32, seq) ^ lax.axis_index("seq")
    return sum(((source >> n) & 1) << (len(bits) - 1 - n) for n in range(len(bits)))


def body(queries, keys, values, cotangent, out_weight, short_taps, long_taps, skip_gain):
    rows, width = queries.shape
    col_part = out_weight.shape[1]
    seq, ys = lax.axis_size("seq"), lax.axis_size("y")
    cols = width // seq
    chunks = 2 if cols % (2 * LANES) == 0 else 1
    groups = long_taps.shape[1]
    fsdp = ("z", "y")
    grad_scale = float(rows * seq * ys * Z) ** (-0.5)

    weights = lax.all_gather(out_weight, "z", axis=1, tiled=True)
    fwd_table, bwd_table = make_tables(long_taps)
    skip = skip_gain.reshape(1, cols)
    place = places(seq)
    by_owner = pack((queries, keys, values), seq)
    x = lax.all_to_all(by_owner, "seq", split_axis=0, concat_axis=0, tiled=True)
    held = own_cotangent(cotangent, col_part, by_owner)
    halo = along(tail_of(x, short_taps, [fwd_table, held]), fsdp, 1)
    mixers = [forward(x, halo, short_taps, skip, fwd_table, place, 0, chunks, held)]
    cots = gather_cotangent(held, [mixers[0][0]])
    for h in range(1, chunks):
        mixers.append(forward(x, halo, short_taps, skip, fwd_table, place, h, chunks, cots[0]))

    parts, heads = [], []
    for step in range(1, ys):
        part, head = mixed_grad(cots, weights, place, step, BF16, parts[-1] if parts else place)
        parts.append(part)
        heads.append(around(head, "y", -step))
    mixed_own, own_head = mixed_grad(cots, weights, place, 0, F32, parts[-1])
    rest = [around(parts[step - 1], "y", -step) for step in range(1, ys)]
    mixed_rest = rest[0] if len(rest) == 1 else sum(piece.astype(F32) for piece in rest)
    head_rest = heads[0] if len(heads) == 1 else sum(piece.astype(F32) for piece in heads)
    head = head_of(own_head, head_rest, mixers)
    later = along(head, fsdp, -1)

    weight_sum = None
    for h in range(chunks):
        mixed_all = [around(mixers[h][0], "y", step) if step else mixers[h][0] for step in range(ys)]
        after = later if h == chunks - 1 else mixed_own
        weight_sum = weight_grad(cots, mixed_all, h, chunks, grad_scale, weight_sum, after)
    weight_part = lax.psum_scatter(weight_sum, "z", scatter_dimension=1, tiled=True)

    grads, short_parts, long_parts = [], [], []
    for h in range(chunks):
        _, feats, filt = mixers[h]
        grad, short_part, long_part = backward(
            mixed_own, mixed_rest, feats, filt, x, later, short_taps, skip, bwd_table, h, chunks
        )
        grads.append(lax.all_to_all(grad, "seq", split_axis=0, concat_axis=0, tiled=True))
        short_parts.append(short_part)
        long_parts.append(long_part)

    query_grad, key_grad, value_grad = unpack(grads)
    packed = jnp.concatenate(
        [
            jnp.concatenate(short_parts, axis=2).reshape(3 * (SHORT + 1), cols),
            jnp.concatenate(long_parts, axis=0).reshape(-1, cols),
        ],
        axis=0,
    )
    packed = sum_over(packed, ("y", "z")) * grad_scale
    short_sum = packed[: 3 * (SHORT + 1)].reshape(3, SHORT + 1, cols)
    long_sum = packed[3 * (SHORT + 1) :].reshape(groups, LTAPS).T
    return (
        query_grad,
        key_grad,
        value_grad,
        weight_part.astype(F32),
        short_sum[:, :SHORT],
        long_sum,
        short_sum[0, SHORT],
    )


def solution(mesh):
    fsdp, seq = mesh.shape["fsdp"], mesh.shape["seq"]
    split = Mesh(mesh.devices.reshape(Z, fsdp // Z, seq), ("z", "y", "seq"))
    tokens = P(("z", "y", "seq"), None)
    specs = (P("seq", ("z", "y")), P(None, None, "seq"), P(None, "seq"), P("seq"))
    return jax.shard_map(
        body,
        mesh=split,
        in_specs=(tokens,) * 4 + specs,
        out_specs=(tokens,) * 3 + specs,
        check_vma=False,
    )
```

```python
import functools

import jax
import jax.numpy as jnp
from jax import lax
from jax.experimental import pallas as pl
from jax.experimental.pallas import tpu as pltpu
from jax.sharding import Mesh
from jax.sharding import PartitionSpec as P

SHORT = 7
LTAPS = 128
LANES = 128
PAD = 16
Z = 4
F32 = jnp.float32
BF16 = jnp.bfloat16


def params():
    return pltpu.CompilerParams(vmem_limit_bytes=60 * 2**20)


def tables_kernel(fwd_ref, bwd_ref, tf_ref, tb_ref):
    for g in range(fwd_ref.shape[0]):
        rows = slice(g * LTAPS, (g + 1) * LTAPS)
        for src, dst in ((fwd_ref, tf_ref), (bwd_ref, tb_ref)):
            wide = jnp.broadcast_to(src[g : g + 1, :], (LTAPS, 2 * LTAPS))
            dst[rows, :] = pltpu.roll(wide, 0, 1, stride=1, stride_axis=0).astype(BF16)


def make_tables(long_taps):
    by_group = long_taps.T
    groups = by_group.shape[0]
    fwd = jnp.pad(by_group[:, ::-1], ((0, 0), (1, LTAPS - 1)))
    bwd = jnp.pad(by_group, ((0, 0), (0, LTAPS)))
    per = 8
    row_spec = pl.BlockSpec((per, 2 * LTAPS), lambda i: (i, 0))
    tab_spec = pl.BlockSpec((per * LTAPS, 2 * LTAPS), lambda i: (i, 0))
    shape = jax.ShapeDtypeStruct((groups * LTAPS, 2 * LTAPS), BF16)
    return pl.pallas_call(
        tables_kernel,
        grid=(groups // per,),
        in_specs=[row_spec, row_spec],
        out_specs=[tab_spec, tab_spec],
        out_shape=[shape, shape],
        compiler_params=params(),
        name="tables",
    )(fwd, bwd)


def pick_groups(wide, col, rows, per):
    lane_group = lax.broadcasted_iota(jnp.int32, (rows, LANES), 1) // (LANES // per)
    cols = slice(col * LANES, (col + 1) * LANES)
    out = wide[0:rows, cols]
    for g in range(1, per):
        out = jnp.where(lane_group == g, wide[g * rows : (g + 1) * rows, cols], out)
    return out


def features_of(taps_ref, row, xf, i, begin):
    total = taps_ref[row, 0:1] * xf[i, PAD + begin : PAD + begin + LTAPS]
    for j in range(1, SHORT):
        total = total + taps_ref[row, j : j + 1] * xf[i, PAD + begin - j : PAD + begin - j + LTAPS]
    return total


def forward_kernel(
    place_ref, x_ref, h_ref, taps_ref, skip_ref, tab_ref, _, mixed_ref, f_ref, filt_ref, xf, pf, pb, wide
):
    blocks, _, rows, _ = x_ref.shape
    tokens = blocks * rows
    per = tab_ref.shape[0] // LTAPS
    for i in range(3):
        xf[i, 0:PAD] = h_ref[i * PAD : (i + 1) * PAD].astype(F32)
        for b in range(blocks):
            begin = PAD + b * rows
            xf[i, begin : begin + rows] = x_ref[b, i].astype(F32)
    pb[0:LTAPS] = h_ref[3 * PAD : 3 * PAD + LTAPS]
    for begin in range(0, tokens, LTAPS):
        own = slice(begin, begin + LTAPS)
        f1 = features_of(taps_ref, 1, xf, 1, begin)
        f2 = features_of(taps_ref, 2, xf, 2, begin)
        prod = f1 * f2
        f_ref[1, own] = f1
        f_ref[2, own] = f2
        f_ref[0, own] = features_of(taps_ref, 0, xf, 0, begin)
        pf[own] = prod
        pb[LTAPS + begin : 2 * LTAPS + begin] = prod.astype(BF16)
    skip = skip_ref[...]
    for b in range(0, tokens // LTAPS, 2):
        low = b * LTAPS
        windows = jnp.concatenate([pb[low : low + 2 * LTAPS], pb[low + LTAPS : low + 3 * LTAPS]], axis=1)
        wide[...] = jnp.dot(tab_ref[...], windows, preferred_element_type=F32)
        for n in range(2):
            own = slice(low + n * LTAPS, low + (n + 1) * LTAPS)
            filtered = pick_groups(wide, n, LTAPS, per) + skip * pf[own]
            filt_ref[own] = filtered
            mixed = f_ref[0, own] * filtered
            there = pl.multiple_of(place_ref[b + n] * LTAPS, LTAPS)
            mixed_ref[:, pl.ds(there, LTAPS)] = mixed.T.astype(BF16)


def forward(x, halo, short_taps, skip, table, place, chunk, chunks, after):
    blocks, _, rows, cols = x.shape
    cols //= chunks
    tokens = blocks * rows
    tiles = cols // LANES
    first = chunk * tiles
    tab_rows = table.shape[0] * LANES // skip.shape[1]
    return pl.pallas_call(
        forward_kernel,
        grid_spec=pltpu.PrefetchScalarGridSpec(
            num_scalar_prefetch=1,
            grid=(tiles,),
            in_specs=[
                pl.BlockSpec((blocks, 3, rows, LANES), lambda c, _: (0, 0, 0, first + c)),
                pl.BlockSpec((halo.shape[0], LANES), lambda c, _: (0, first + c)),
                pl.BlockSpec((3, SHORT, LANES), lambda c, _: (0, 0, first + c)),
                pl.BlockSpec((1, LANES), lambda c, _: (0, first + c)),
                pl.BlockSpec((tab_rows, 2 * LTAPS), lambda c, _: (first + c, 0)),
                pl.BlockSpec(memory_space=pl.ANY),
            ],
            out_specs=[
                pl.BlockSpec((LANES, tokens), lambda c, _: (c, 0)),
                pl.BlockSpec((3, tokens, LANES), lambda c, _: (0, 0, c)),
                pl.BlockSpec((tokens, LANES), lambda c, _: (0, c)),
            ],
            scratch_shapes=[
                pltpu.VMEM((3, PAD + tokens, LANES), F32),
                pltpu.VMEM((tokens, LANES), F32),
                pltpu.VMEM((LTAPS + tokens, LANES), BF16),
                pltpu.VMEM((tab_rows, 2 * LTAPS), F32),
            ],
        ),
        out_shape=[
            jax.ShapeDtypeStruct((cols, tokens), BF16),
            jax.ShapeDtypeStruct((3, tokens, cols), F32),
            jax.ShapeDtypeStruct((tokens, cols), F32),
        ],
        compiler_params=params(),
        name="forward",
    )(place, x, halo, short_taps, skip, table, after)


def sum_by_lag(gram):
    wide = gram.shape[1]
    parts = [gram[i : i + 8] for i in range(0, gram.shape[0], 8)]
    step = 8
    while len(parts) > 1:
        parts = [
            parts[k] + pltpu.roll(parts[k + 1], wide - step, 1) for k in range(0, len(parts), 2)
        ]
        step *= 2
    total = parts[0]
    row = lax.broadcasted_iota(jnp.int32, total.shape, 0)
    for bit in (1, 2, 4):
        total = jnp.where((row & bit) != 0, pltpu.roll(total, wide - bit, 1), total)
    return jnp.sum(total[:, :LTAPS], axis=0, keepdims=True)


def backward_kernel(
    mo_ref, mr_ref, f_ref, filt_ref, x_ref, n_ref, taps_ref, skip_ref, tab_ref,
    grad_ref, short_ref, long_ref, db, fg, wide, left, right,
):
    blocks, _, rows, _ = x_ref.shape
    tokens = blocks * rows
    per = tab_ref.shape[0] // LTAPS
    count = tokens // LTAPS
    skip = skip_ref[...]
    lane_group = lax.broadcasted_iota(jnp.int32, (1, LANES), 1) // (LANES // per)
    gain = jnp.zeros((8, LANES), F32)
    for b in range(count):
        own = slice(b * LTAPS, (b + 1) * LTAPS)
        mixed_grad = mo_ref[own] + mr_ref[own].astype(F32)
        slope = mixed_grad * f_ref[0, own]
        db[own] = slope.astype(BF16)
        fg[0, own] = mixed_grad * filt_ref[own]
        fg[1, own] = skip * slope
        prod = f_ref[1, own] * f_ref[2, own]
        gain = gain + jnp.sum((prod * slope).reshape(LTAPS // 8, 8, LANES), axis=0)
        prod_b = prod.astype(BF16)
        for g in range(per):
            keep = (lane_group == g).astype(F32).astype(BF16)
            left[g * LTAPS : (g + 1) * LTAPS, b * LANES : (b + 1) * LANES] = prod_b * keep
    db[tokens : tokens + LTAPS + PAD] = n_ref[0 : LTAPS + PAD]
    db[tokens + LTAPS + PAD :] = jnp.zeros((LTAPS - PAD, LANES), BF16)
    for b in range(count):
        right[:, b * LANES : (b + 1) * LANES] = db[b * LTAPS : (b + 2) * LTAPS]
    for b in range(0, count, 2):
        wide[...] = jnp.dot(
            tab_ref[...], right[:, b * LANES : (b + 2) * LANES], preferred_element_type=F32
        )
        for n in range(2):
            own = slice((b + n) * LTAPS, (b + n + 1) * LTAPS)
            grad = pick_groups(wide, n, LTAPS, per) + fg[1, own]
            fg[1, own] = grad * f_ref[2, own]
            fg[2, own] = grad * f_ref[1, own]
    few = jnp.concatenate([tab_ref[g * LTAPS : g * LTAPS + PAD] for g in range(per)], axis=0)
    edge = jnp.dot(few, db[tokens : tokens + 2 * LTAPS], preferred_element_type=F32)
    begin = LTAPS + PAD
    grad = pick_groups(edge, 0, PAD, per) + skip * n_ref[0:PAD].astype(F32)
    fg[1, tokens : tokens + PAD] = grad * n_ref[begin + PAD : begin + 2 * PAD].astype(F32)
    fg[2, tokens : tokens + PAD] = grad * n_ref[begin : begin + PAD].astype(F32)
    fg[0, tokens : tokens + PAD] = n_ref[begin + 2 * PAD : begin + 3 * PAD].astype(F32)
    for i in range(3):
        sums = [jnp.zeros((8, LANES), F32) for _ in range(SHORT)]
        for b in range(count):
            low = b * LTAPS
            inputs = x_ref[b, i].astype(F32)
            total = None
            for j in range(SHORT):
                later = fg[i, low + j : low + j + LTAPS]
                term = taps_ref[i, j : j + 1] * later
                total = term if total is None else total + term
                sums[j] = sums[j] + jnp.sum((later * inputs).reshape(LTAPS // 8, 8, LANES), axis=0)
            grad_ref[b, i] = total.astype(BF16)
        for j in range(SHORT):
            short_ref[i, j : j + 1] = jnp.sum(sums[j], axis=0, keepdims=True)
        short_ref[i, SHORT : SHORT + 1] = jnp.sum(gain, axis=0, keepdims=True)
    wide[...] = lax.dot_general(left[...], right[...], (((1,), (1,)), ((), ())), preferred_element_type=F32)
    for g in range(per):
        gram = wide[g * LTAPS : (g + 1) * LTAPS]
        long_ref[g : g + 1] = sum_by_lag(gram)


def backward(mixed_own, mixed_rest, feats, filt, x, later, short_taps, skip, table, chunk, chunks):
    blocks, _, rows, cols = x.shape
    cols //= chunks
    tokens = blocks * rows
    tiles = cols // LANES
    first = chunk * tiles
    tab_rows = table.shape[0] * LANES // skip.shape[1]
    per = tab_rows // LTAPS
    tok = pl.BlockSpec((tokens, LANES), lambda c: (0, first + c))
    return pl.pallas_call(
        backward_kernel,
        grid=(tiles,),
        in_specs=[
            tok,
            tok,
            pl.BlockSpec((3, tokens, LANES), lambda c: (0, 0, c)),
            pl.BlockSpec((tokens, LANES), lambda c: (0, c)),
            pl.BlockSpec((blocks, 3, rows, LANES), lambda c: (0, 0, 0, first + c)),
            pl.BlockSpec((later.shape[0], LANES), lambda c: (0, first + c)),
            pl.BlockSpec((3, SHORT, LANES), lambda c: (0, 0, first + c)),
            pl.BlockSpec((1, LANES), lambda c: (0, first + c)),
            pl.BlockSpec((tab_rows, 2 * LTAPS), lambda c: (first + c, 0)),
        ],
        out_specs=[
            pl.BlockSpec((blocks, 3, rows, LANES), lambda c: (0, 0, 0, c)),
            pl.BlockSpec((3, SHORT + 1, LANES), lambda c: (0, 0, c)),
            pl.BlockSpec((per, LTAPS), lambda c: (c, 0)),
        ],
        out_shape=[
            jax.ShapeDtypeStruct((blocks, 3, rows, cols), BF16),
            jax.ShapeDtypeStruct((3, SHORT + 1, cols), F32),
            jax.ShapeDtypeStruct((tiles * per, LTAPS), F32),
        ],
        scratch_shapes=[
            pltpu.VMEM((tokens + 2 * LTAPS, LANES), BF16),
            pltpu.VMEM((3, tokens + PAD, LANES), F32),
            pltpu.VMEM((tab_rows, 2 * LTAPS), F32),
            pltpu.VMEM((tab_rows, tokens), BF16),
            pltpu.VMEM((2 * LTAPS, tokens), BF16),
        ],
        compiler_params=params(),
        name="backward",
    )(mixed_own, mixed_rest, feats, filt, x, later, short_taps, skip, table)


def pack_kernel(*refs):
    out_ref = refs[-1]
    for i, ref in enumerate(refs[:3]):
        out_ref[0, i] = ref[...]


def pack(arrays, seq):
    rows, width = arrays[0].shape
    cols = width // seq
    return pl.pallas_call(
        pack_kernel,
        grid=(seq,),
        in_specs=[pl.BlockSpec((rows, cols), lambda s: (0, s))] * 3,
        out_specs=pl.BlockSpec((1, 3, rows, cols), lambda s: (s, 0, 0, 0)),
        out_shape=jax.ShapeDtypeStruct((seq, 3, rows, cols), BF16),
        compiler_params=params(),
        name="pack",
    )(*arrays)


def unpack_kernel(*refs):
    parts, outs = refs[:-3], refs[-3:]
    cols = parts[0].shape[3]
    for n, part in enumerate(parts):
        for i, out in enumerate(outs):
            out[:, n * cols : (n + 1) * cols] = part[0, i]


def unpack(parts):
    seq, _, rows, cols = parts[0].shape
    wide = cols * len(parts)
    shape = jax.ShapeDtypeStruct((rows, seq * wide), BF16)
    return pl.pallas_call(
        unpack_kernel,
        grid=(seq,),
        in_specs=[pl.BlockSpec((1, 3, rows, cols), lambda s: (s, 0, 0, 0))] * len(parts),
        out_specs=[pl.BlockSpec((rows, wide), lambda s: (0, s))] * 3,
        out_shape=[shape] * 3,
        compiler_params=params(),
        name="unpack",
    )(*parts)


def along(block, axis, distance):
    size = lax.axis_size(axis)
    return lax.ppermute(block, axis, [(i, i + distance) for i in range(size) if 0 <= i + distance < size])


def around(block, axis, distance):
    size = lax.axis_size(axis)
    return lax.ppermute(block, axis, [(i, (i + distance) % size) for i in range(size)])


def across(block, axis, bit):
    return lax.ppermute(block, axis, [(i, i ^ bit) for i in range(lax.axis_size(axis))])


def bits_of(axis):
    size = lax.axis_size(axis)
    return [1 << n for n in range(size.bit_length() - 1)]


def sum_over(value, axes):
    for axis in axes:
        for bit in bits_of(axis):
            value = value + across(value, axis, bit)
    return value


def split_kernel(y_ref, *refs):
    count = (len(refs) - 1) // 2
    for n in range(count):
        refs[count + 1 + n][...] = refs[n][...]


def split_cotangent(cotangent, y, ys, col_part, after):
    rows, width = cotangent.shape

    def source(step):
        return pl.BlockSpec((rows, col_part), lambda z, y_ref: (0, z * ys + (y_ref[0] + step) % ys))

    return pl.pallas_call(
        split_kernel,
        grid_spec=pltpu.PrefetchScalarGridSpec(
            num_scalar_prefetch=1,
            grid=(Z,),
            in_specs=[source(step) for step in range(ys)] + [pl.BlockSpec(memory_space=pl.ANY)],
            out_specs=[pl.BlockSpec((rows, col_part), lambda z, _: (0, z))] * ys,
        ),
        out_shape=[jax.ShapeDtypeStruct((rows, width // ys), BF16)] * ys,
        compiler_params=params(),
        name="split",
    )(y.reshape(1), *([cotangent] * ys), after)


def join_kernel(axis, count, *refs):
    out = refs[-1]
    for n in range(count):
        size = refs[n].shape[axis]
        here = slice(n * size, (n + 1) * size)
        if axis == 0:
            out[here] = refs[n][...]
        else:
            out[:, here] = refs[n][...]


def join(parts, axis, after=()):
    shape = list(parts[0].shape)
    tile = shape[-1] // Z
    block = pl.BlockSpec((*shape[:-1], tile), lambda i: (0, 0, 0, i))
    shape[axis] *= len(parts)
    return pl.pallas_call(
        functools.partial(join_kernel, axis, len(parts)),
        grid=(Z,),
        in_specs=[block] * len(parts) + [pl.BlockSpec(memory_space=pl.ANY)] * len(after),
        out_specs=pl.BlockSpec((*shape[:-1], tile), lambda i: (0, 0, 0, i)),
        out_shape=jax.ShapeDtypeStruct(tuple(shape), BF16),
        compiler_params=params(),
        name="join",
    )(*parts, *after)


def own_cotangent(cotangent, col_part, after):
    ys, y = lax.axis_size("y"), lax.axis_index("y")
    held = split_cotangent(cotangent, y, ys, col_part, after)
    held = [around(part, "y", step) if step else part for step, part in enumerate(held)]
    return join([part[None, None] for part in held], 0)


def gather_cotangent(held, after):
    bits = bits_of("seq")
    for bit in reversed(bits[1:]):
        held = join([held, across(held, "seq", bit)], 1, after)
    return held, across(held, "seq", bits[0])


def mixed_grad_kernel(place_ref, a_ref, b_ref, w_ref, _, out_ref, head_ref, found):
    _, count, rows, _ = a_ref.shape
    tokens = count * rows
    pieces = jnp.concatenate([ref[...].reshape(tokens, -1) for ref in (a_ref, b_ref)], axis=0)
    found[...] = contract(pieces, w_ref[...], 1)
    for block in range(2 * count):
        there = pl.multiple_of(place_ref[block] * rows, rows)
        out_ref[block * rows : (block + 1) * rows] = found[pl.ds(there, rows)].astype(out_ref.dtype)
    head_ref[...] = out_ref[0 : LTAPS + PAD]


def mixed_grad(cots, weights, place, step, dtype, after):
    _, count, rows, width = cots[0].shape
    tokens = 2 * count * rows
    cols = weights.shape[0]
    tile = min(cols, 2 * LANES)
    piece = pl.BlockSpec((1, count, rows, width), lambda i, _: (step, 0, 0, 0))
    return pl.pallas_call(
        mixed_grad_kernel,
        grid_spec=pltpu.PrefetchScalarGridSpec(
            num_scalar_prefetch=1,
            grid=(cols // tile,),
            in_specs=[
                piece,
                piece,
                pl.BlockSpec((tile, width), lambda i, _: (i, 0)),
                pl.BlockSpec(memory_space=pl.ANY),
            ],
            out_specs=[
                pl.BlockSpec((tokens, tile), lambda i, _: (0, i)),
                pl.BlockSpec((LTAPS + PAD, tile), lambda i, _: (0, i)),
            ],
            scratch_shapes=[pltpu.VMEM((tokens, tile), F32)],
        ),
        out_shape=[
            jax.ShapeDtypeStruct((tokens, cols), dtype),
            jax.ShapeDtypeStruct((LTAPS + PAD, cols), dtype),
        ],
        compiler_params=params(),
        name="mixed_grad",
    )(place, *cots, weights, after)


def weight_grad_kernel(scale, a_ref, b_ref, *refs):
    steps, count, rows, tile = a_ref.shape
    tokens = count * rows
    mixed, out = refs[:steps], refs[-1]
    total = None
    for step in range(steps):
        for n, ref in enumerate((a_ref, b_ref)):
            left = mixed[step][:, n * tokens : (n + 1) * tokens]
            term = jnp.dot(left, ref[step].reshape(tokens, tile), preferred_element_type=F32)
            total = term if total is None else total + term
    out[...] = (total * scale).astype(BF16)


def weight_grad(cots, mixed, chunk, chunks, scale, target, after):
    steps, count, rows, width = cots[0].shape
    part, tokens = mixed[0].shape
    tile = width // Z
    piece = pl.BlockSpec((steps, count, rows, tile), lambda i: (0, 0, 0, i))
    extra = [*after] + ([] if target is None else [target])
    return pl.pallas_call(
        functools.partial(weight_grad_kernel, scale),
        grid=(Z,),
        in_specs=[piece, piece]
        + [pl.BlockSpec((part, tokens), lambda i: (0, 0))] * len(mixed)
        + [pl.BlockSpec(memory_space=pl.ANY)] * len(extra),
        out_specs=pl.BlockSpec((part, tile), lambda i: (chunk, i)),
        out_shape=jax.ShapeDtypeStruct((part * chunks, width), BF16),
        input_output_aliases={} if target is None else {2 + len(mixed) + len(after): 0},
        compiler_params=params(),
        name="weight_grad",
    )(*cots, *mixed, *extra)


def tail_kernel(x_ref, before_ref, taps_ref, *refs):
    out_ref, xf = refs[-2:]
    rows = x_ref.shape[2]
    for i in range(3):
        out_ref[i * PAD : (i + 1) * PAD] = x_ref[0, i, rows - PAD :]
    for tile in range(x_ref.shape[3] // LANES):
        cols = slice(tile * LANES, (tile + 1) * LANES)
        taps = taps_ref[:, :, cols]
        prod = None
        for i in (1, 2):
            xf[tile, i - 1, 0:PAD] = before_ref[0, i, :, cols].astype(F32)
            xf[tile, i - 1, PAD:] = x_ref[0, i, :, cols].astype(F32)
            feature = taps[i, 0:1] * xf[tile, i - 1, PAD : PAD + rows]
            for j in range(1, SHORT):
                feature = feature + taps[i, j : j + 1] * xf[tile, i - 1, PAD - j : PAD - j + rows]
            prod = feature if prod is None else prod * feature
        out_ref[3 * PAD :, cols] = prod.astype(BF16)


def tail_of(x, short_taps, after):
    seq, _, rows, cols = x.shape
    wide = min(cols, 4 * LANES)
    out_rows = 3 * PAD + rows
    return pl.pallas_call(
        tail_kernel,
        grid=(cols // wide,),
        in_specs=[
            pl.BlockSpec((1, 3, rows, wide), lambda c: (seq - 1, 0, 0, c)),
            pl.BlockSpec((1, 3, PAD, wide), lambda c: (seq - 2, 0, rows // PAD - 1, c)),
            pl.BlockSpec((3, SHORT, wide), lambda c: (0, 0, c)),
        ]
        + [pl.BlockSpec(memory_space=pl.ANY)] * len(after),
        out_specs=pl.BlockSpec((out_rows, wide), lambda c: (0, c)),
        out_shape=jax.ShapeDtypeStruct((out_rows, cols), BF16),
        scratch_shapes=[pltpu.VMEM((wide // LANES, 2, PAD + rows, LANES), F32)],
        compiler_params=params(),
        name="tail",
    )(x, x, short_taps, *after)


def head_kernel(mo_ref, mr_ref, *refs):
    out_ref = refs[-1]
    chunks = len(refs) // 2
    edge = LTAPS + PAD
    part = out_ref.shape[1] // chunks
    for h in range(chunks):
        own = slice(h * part, (h + 1) * part)
        f_ref, filt_ref = refs[2 * h : 2 * h + 2]
        mixed = mo_ref[:, own] + mr_ref[:, own].astype(F32)
        out_ref[0:edge, own] = (mixed * f_ref[0]).astype(BF16)
        out_ref[edge : edge + PAD, own] = f_ref[1, 0:PAD].astype(BF16)
        out_ref[edge + PAD : edge + 2 * PAD, own] = f_ref[2, 0:PAD].astype(BF16)
        out_ref[edge + 2 * PAD :, own] = (mixed[0:PAD] * filt_ref[0:PAD]).astype(BF16)


def head_of(mixed_own, mixed_rest, mixers):
    edge, cols = LTAPS + PAD, mixed_own.shape[1]
    part = cols // len(mixers)
    whole = pl.BlockSpec((edge, cols), lambda i: (0, 0))
    feat_specs = [
        pl.BlockSpec((3, edge, part), lambda i: (0, 0, 0)),
        pl.BlockSpec((edge, part), lambda i: (0, 0)),
    ]
    return pl.pallas_call(
        head_kernel,
        grid=(1,),
        in_specs=[whole, whole] + feat_specs * len(mixers),
        out_specs=pl.BlockSpec((edge + 3 * PAD, cols), lambda i: (0, 0)),
        out_shape=jax.ShapeDtypeStruct((edge + 3 * PAD, cols), BF16),
        compiler_params=params(),
        name="head",
    )(mixed_own, mixed_rest, *[array for mixer in mixers for array in mixer[1:]])


def contract(a, b, dim):
    return lax.dot_general(a, b, (((dim,), (dim,)), ((), ())), preferred_element_type=F32)


def places(seq):
    bits = bits_of("seq")
    source = lax.iota(jnp.int32, seq) ^ lax.axis_index("seq")
    return sum(((source >> n) & 1) << (len(bits) - 1 - n) for n in range(len(bits)))


def body(queries, keys, values, cotangent, out_weight, short_taps, long_taps, skip_gain):
    rows, width = queries.shape
    col_part = out_weight.shape[1]
    seq, ys = lax.axis_size("seq"), lax.axis_size("y")
    cols = width // seq
    chunks = 2 if cols % (2 * LANES) == 0 else 1
    groups = long_taps.shape[1]
    fsdp = ("z", "y")
    grad_scale = float(rows * seq * ys * Z) ** (-0.5)

    weights = lax.all_gather(out_weight, "z", axis=1, tiled=True)
    fwd_table, bwd_table = make_tables(long_taps)
    skip = skip_gain.reshape(1, cols)
    place = places(seq)
    by_owner = pack((queries, keys, values), seq)
    x = lax.all_to_all(by_owner, "seq", split_axis=0, concat_axis=0, tiled=True)
    held = own_cotangent(cotangent, col_part, by_owner)
    halo = along(tail_of(x, short_taps, [fwd_table, held]), fsdp, 1)
    cots = gather_cotangent(held, [])
    mixers = [
        forward(x, halo, short_taps, skip, fwd_table, place, h, chunks, cots[1]) for h in range(chunks)
    ]

    parts, heads = [], []
    for step in range(1, ys):
        part, head = mixed_grad(cots, weights, place, step, BF16, parts[-1] if parts else place)
        parts.append(part)
        heads.append(around(head, "y", -step))
    mixed_own, own_head = mixed_grad(cots, weights, place, 0, F32, parts[-1])
    rest = [around(parts[step - 1], "y", -step) for step in range(1, ys)]
    mixed_rest = rest[0] if len(rest) == 1 else sum(piece.astype(F32) for piece in rest)
    head_rest = heads[0] if len(heads) == 1 else sum(piece.astype(F32) for piece in heads)
    head = head_of(own_head, head_rest, mixers)
    later = along(head, fsdp, -1)

    weight_sum = None
    for h in range(chunks):
        mixed_all = [around(mixers[h][0], "y", step) if step else mixers[h][0] for step in range(ys)]
        after = [later, *rest] if h == chunks - 1 else [mixed_own]
        weight_sum = weight_grad(cots, mixed_all, h, chunks, grad_scale, weight_sum, after)
    weight_part = lax.psum_scatter(weight_sum, "z", scatter_dimension=1, tiled=True)

    grads, short_parts, long_parts = [], [], []
    for h in range(chunks):
        _, feats, filt = mixers[h]
        grad, short_part, long_part = backward(
            mixed_own, mixed_rest, feats, filt, x, later, short_taps, skip, bwd_table, h, chunks
        )
        grads.append(lax.all_to_all(grad, "seq", split_axis=0, concat_axis=0, tiled=True))
        short_parts.append(short_part)
        long_parts.append(long_part)

    query_grad, key_grad, value_grad = unpack(grads)
    packed = jnp.concatenate(
        [
            jnp.concatenate(short_parts, axis=2).reshape(3 * (SHORT + 1), cols),
            jnp.concatenate(long_parts, axis=0).reshape(-1, cols),
        ],
        axis=0,
    )
    packed = sum_over(packed, ("y", "z")) * grad_scale
    short_sum = packed[: 3 * (SHORT + 1)].reshape(3, SHORT + 1, cols)
    long_sum = packed[3 * (SHORT + 1) :].reshape(groups, LTAPS).T
    return (
        query_grad,
        key_grad,
        value_grad,
        weight_part.astype(F32),
        short_sum[:, :SHORT],
        long_sum,
        short_sum[0, SHORT],
    )


def solution(mesh):
    fsdp, seq = mesh.shape["fsdp"], mesh.shape["seq"]
    split = Mesh(mesh.devices.reshape(Z, fsdp // Z, seq), ("z", "y", "seq"))
    tokens = P(("z", "y", "seq"), None)
    specs = (P("seq", ("z", "y")), P(None, None, "seq"), P(None, "seq"), P("seq"))
    return jax.shard_map(
        body,
        mesh=split,
        in_specs=(tokens,) * 4 + specs,
        out_specs=(tokens,) * 3 + specs,
        check_vma=False,
    )
```

```python
import functools

import jax
import jax.numpy as jnp
from jax import lax
from jax.experimental import pallas as pl
from jax.experimental.pallas import tpu as pltpu
from jax.sharding import Mesh
from jax.sharding import PartitionSpec as P

SHORT = 7
LTAPS = 128
LANES = 128
PAD = 16
Z = 4
F32 = jnp.float32
BF16 = jnp.bfloat16


def params():
    return pltpu.CompilerParams(vmem_limit_bytes=60 * 2**20)


def tables_kernel(fwd_ref, bwd_ref, tf_ref, tb_ref):
    for g in range(fwd_ref.shape[0]):
        rows = slice(g * LTAPS, (g + 1) * LTAPS)
        for src, dst in ((fwd_ref, tf_ref), (bwd_ref, tb_ref)):
            wide = jnp.broadcast_to(src[g : g + 1, :], (LTAPS, 2 * LTAPS))
            dst[rows, :] = pltpu.roll(wide, 0, 1, stride=1, stride_axis=0).astype(BF16)


def make_tables(long_taps):
    by_group = long_taps.T
    groups = by_group.shape[0]
    fwd = jnp.pad(by_group[:, ::-1], ((0, 0), (1, LTAPS - 1)))
    bwd = jnp.pad(by_group, ((0, 0), (0, LTAPS)))
    per = 8
    row_spec = pl.BlockSpec((per, 2 * LTAPS), lambda i: (i, 0))
    tab_spec = pl.BlockSpec((per * LTAPS, 2 * LTAPS), lambda i: (i, 0))
    shape = jax.ShapeDtypeStruct((groups * LTAPS, 2 * LTAPS), BF16)
    return pl.pallas_call(
        tables_kernel,
        grid=(groups // per,),
        in_specs=[row_spec, row_spec],
        out_specs=[tab_spec, tab_spec],
        out_shape=[shape, shape],
        compiler_params=params(),
        name="tables",
    )(fwd, bwd)


def pick_groups(wide, col, rows, per):
    lane_group = lax.broadcasted_iota(jnp.int32, (rows, LANES), 1) // (LANES // per)
    cols = slice(col * LANES, (col + 1) * LANES)
    out = wide[0:rows, cols]
    for g in range(1, per):
        out = jnp.where(lane_group == g, wide[g * rows : (g + 1) * rows, cols], out)
    return out


def features_of(taps_ref, row, xf, i, begin):
    total = taps_ref[row, 0:1] * xf[i, PAD + begin : PAD + begin + LTAPS]
    for j in range(1, SHORT):
        total = total + taps_ref[row, j : j + 1] * xf[i, PAD + begin - j : PAD + begin - j + LTAPS]
    return total


def forward_kernel(
    place_ref, x_ref, h_ref, taps_ref, skip_ref, tab_ref, _, mixed_ref, f_ref, filt_ref, xf, pf, pb, wide
):
    blocks, _, rows, _ = x_ref.shape
    tokens = blocks * rows
    per = tab_ref.shape[0] // LTAPS
    for i in range(3):
        xf[i, 0:PAD] = h_ref[i * PAD : (i + 1) * PAD].astype(F32)
        for b in range(blocks):
            begin = PAD + b * rows
            xf[i, begin : begin + rows] = x_ref[b, i].astype(F32)
    pb[0:LTAPS] = h_ref[3 * PAD : 3 * PAD + LTAPS]
    for begin in range(0, tokens, LTAPS):
        own = slice(begin, begin + LTAPS)
        f1 = features_of(taps_ref, 1, xf, 1, begin)
        f2 = features_of(taps_ref, 2, xf, 2, begin)
        prod = f1 * f2
        f_ref[1, own] = f1
        f_ref[2, own] = f2
        f_ref[0, own] = features_of(taps_ref, 0, xf, 0, begin)
        pf[own] = prod
        pb[LTAPS + begin : 2 * LTAPS + begin] = prod.astype(BF16)
    skip = skip_ref[...]
    for b in range(0, tokens // LTAPS, 2):
        low = b * LTAPS
        windows = jnp.concatenate([pb[low : low + 2 * LTAPS], pb[low + LTAPS : low + 3 * LTAPS]], axis=1)
        wide[...] = jnp.dot(tab_ref[...], windows, preferred_element_type=F32)
        for n in range(2):
            own = slice(low + n * LTAPS, low + (n + 1) * LTAPS)
            filtered = pick_groups(wide, n, LTAPS, per) + skip * pf[own]
            filt_ref[own] = filtered
            mixed = f_ref[0, own] * filtered
            there = pl.multiple_of(place_ref[b + n] * LTAPS, LTAPS)
            mixed_ref[:, pl.ds(there, LTAPS)] = mixed.T.astype(BF16)


def forward(x, halo, short_taps, skip, table, place, chunk, chunks, after):
    blocks, _, rows, cols = x.shape
    cols //= chunks
    tokens = blocks * rows
    tiles = cols // LANES
    first = chunk * tiles
    tab_rows = table.shape[0] * LANES // skip.shape[1]
    return pl.pallas_call(
        forward_kernel,
        grid_spec=pltpu.PrefetchScalarGridSpec(
            num_scalar_prefetch=1,
            grid=(tiles,),
            in_specs=[
                pl.BlockSpec((blocks, 3, rows, LANES), lambda c, _: (0, 0, 0, first + c)),
                pl.BlockSpec((halo.shape[0], LANES), lambda c, _: (0, first + c)),
                pl.BlockSpec((3, SHORT, LANES), lambda c, _: (0, 0, first + c)),
                pl.BlockSpec((1, LANES), lambda c, _: (0, first + c)),
                pl.BlockSpec((tab_rows, 2 * LTAPS), lambda c, _: (first + c, 0)),
                pl.BlockSpec(memory_space=pl.ANY),
            ],
            out_specs=[
                pl.BlockSpec((LANES, tokens), lambda c, _: (c, 0)),
                pl.BlockSpec((3, tokens, LANES), lambda c, _: (0, 0, c)),
                pl.BlockSpec((tokens, LANES), lambda c, _: (0, c)),
            ],
            scratch_shapes=[
                pltpu.VMEM((3, PAD + tokens, LANES), F32),
                pltpu.VMEM((tokens, LANES), F32),
                pltpu.VMEM((LTAPS + tokens, LANES), BF16),
                pltpu.VMEM((tab_rows, 2 * LTAPS), F32),
            ],
        ),
        out_shape=[
            jax.ShapeDtypeStruct((cols, tokens), BF16),
            jax.ShapeDtypeStruct((3, tokens, cols), F32),
            jax.ShapeDtypeStruct((tokens, cols), F32),
        ],
        compiler_params=params(),
        name="forward",
    )(place, x, halo, short_taps, skip, table, after)


def sum_by_lag(gram):
    wide = gram.shape[1]
    parts = [gram[i : i + 8] for i in range(0, gram.shape[0], 8)]
    step = 8
    while len(parts) > 1:
        parts = [
            parts[k] + pltpu.roll(parts[k + 1], wide - step, 1) for k in range(0, len(parts), 2)
        ]
        step *= 2
    total = parts[0]
    row = lax.broadcasted_iota(jnp.int32, total.shape, 0)
    for bit in (1, 2, 4):
        total = jnp.where((row & bit) != 0, pltpu.roll(total, wide - bit, 1), total)
    return jnp.sum(total[:, :LTAPS], axis=0, keepdims=True)


def backward_kernel(
    mo_ref, mr_ref, f_ref, filt_ref, x_ref, n_ref, taps_ref, skip_ref, tab_ref,
    grad_ref, short_ref, long_ref, db, fg, wide, left, right,
):
    blocks, _, rows, _ = x_ref.shape
    tokens = blocks * rows
    per = tab_ref.shape[0] // LTAPS
    count = tokens // LTAPS
    skip = skip_ref[...]
    lane_group = lax.broadcasted_iota(jnp.int32, (1, LANES), 1) // (LANES // per)
    gain = jnp.zeros((8, LANES), F32)
    for b in range(count):
        own = slice(b * LTAPS, (b + 1) * LTAPS)
        mixed_grad = mo_ref[own] + mr_ref[own].astype(F32)
        slope = mixed_grad * f_ref[0, own]
        db[own] = slope.astype(BF16)
        fg[0, own] = mixed_grad * filt_ref[own]
        fg[1, own] = skip * slope
        prod = f_ref[1, own] * f_ref[2, own]
        gain = gain + jnp.sum((prod * slope).reshape(LTAPS // 8, 8, LANES), axis=0)
        prod_b = prod.astype(BF16)
        for g in range(per):
            keep = (lane_group == g).astype(F32).astype(BF16)
            left[g * LTAPS : (g + 1) * LTAPS, b * LANES : (b + 1) * LANES] = prod_b * keep
    db[tokens : tokens + LTAPS + PAD] = n_ref[0 : LTAPS + PAD]
    db[tokens + LTAPS + PAD :] = jnp.zeros((LTAPS - PAD, LANES), BF16)
    for b in range(count):
        right[:, b * LANES : (b + 1) * LANES] = db[b * LTAPS : (b + 2) * LTAPS]
    for b in range(0, count, 2):
        wide[...] = jnp.dot(
            tab_ref[...], right[:, b * LANES : (b + 2) * LANES], preferred_element_type=F32
        )
        for n in range(2):
            own = slice((b + n) * LTAPS, (b + n + 1) * LTAPS)
            grad = pick_groups(wide, n, LTAPS, per) + fg[1, own]
            fg[1, own] = grad * f_ref[2, own]
            fg[2, own] = grad * f_ref[1, own]
    few = jnp.concatenate([tab_ref[g * LTAPS : g * LTAPS + PAD] for g in range(per)], axis=0)
    edge = jnp.dot(few, db[tokens : tokens + 2 * LTAPS], preferred_element_type=F32)
    begin = LTAPS + PAD
    grad = pick_groups(edge, 0, PAD, per) + skip * n_ref[0:PAD].astype(F32)
    fg[1, tokens : tokens + PAD] = grad * n_ref[begin + PAD : begin + 2 * PAD].astype(F32)
    fg[2, tokens : tokens + PAD] = grad * n_ref[begin : begin + PAD].astype(F32)
    fg[0, tokens : tokens + PAD] = n_ref[begin + 2 * PAD : begin + 3 * PAD].astype(F32)
    for i in range(3):
        sums = [jnp.zeros((8, LANES), F32) for _ in range(SHORT)]
        for b in range(count):
            low = b * LTAPS
            inputs = x_ref[b, i].astype(F32)
            total = None
            for j in range(SHORT):
                later = fg[i, low + j : low + j + LTAPS]
                term = taps_ref[i, j : j + 1] * later
                total = term if total is None else total + term
                sums[j] = sums[j] + jnp.sum((later * inputs).reshape(LTAPS // 8, 8, LANES), axis=0)
            grad_ref[b, i] = total.astype(BF16)
        for j in range(SHORT):
            short_ref[i, j : j + 1] = jnp.sum(sums[j], axis=0, keepdims=True)
        short_ref[i, SHORT : SHORT + 1] = jnp.sum(gain, axis=0, keepdims=True)
    wide[...] = lax.dot_general(left[...], right[...], (((1,), (1,)), ((), ())), preferred_element_type=F32)
    for g in range(per):
        gram = wide[g * LTAPS : (g + 1) * LTAPS]
        long_ref[g : g + 1] = sum_by_lag(gram)


def backward(mixed_own, mixed_rest, feats, filt, x, later, short_taps, skip, table, chunk, chunks):
    blocks, _, rows, cols = x.shape
    cols //= chunks
    tokens = blocks * rows
    tiles = cols // LANES
    first = chunk * tiles
    tab_rows = table.shape[0] * LANES // skip.shape[1]
    per = tab_rows // LTAPS
    tok = pl.BlockSpec((tokens, LANES), lambda c: (0, first + c))
    return pl.pallas_call(
        backward_kernel,
        grid=(tiles,),
        in_specs=[
            tok,
            tok,
            pl.BlockSpec((3, tokens, LANES), lambda c: (0, 0, c)),
            pl.BlockSpec((tokens, LANES), lambda c: (0, c)),
            pl.BlockSpec((blocks, 3, rows, LANES), lambda c: (0, 0, 0, first + c)),
            pl.BlockSpec((later.shape[0], LANES), lambda c: (0, first + c)),
            pl.BlockSpec((3, SHORT, LANES), lambda c: (0, 0, first + c)),
            pl.BlockSpec((1, LANES), lambda c: (0, first + c)),
            pl.BlockSpec((tab_rows, 2 * LTAPS), lambda c: (first + c, 0)),
        ],
        out_specs=[
            pl.BlockSpec((blocks, 3, rows, LANES), lambda c: (0, 0, 0, c)),
            pl.BlockSpec((3, SHORT + 1, LANES), lambda c: (0, 0, c)),
            pl.BlockSpec((per, LTAPS), lambda c: (c, 0)),
        ],
        out_shape=[
            jax.ShapeDtypeStruct((blocks, 3, rows, cols), BF16),
            jax.ShapeDtypeStruct((3, SHORT + 1, cols), F32),
            jax.ShapeDtypeStruct((tiles * per, LTAPS), F32),
        ],
        scratch_shapes=[
            pltpu.VMEM((tokens + 2 * LTAPS, LANES), BF16),
            pltpu.VMEM((3, tokens + PAD, LANES), F32),
            pltpu.VMEM((tab_rows, 2 * LTAPS), F32),
            pltpu.VMEM((tab_rows, tokens), BF16),
            pltpu.VMEM((2 * LTAPS, tokens), BF16),
        ],
        compiler_params=params(),
        name="backward",
    )(mixed_own, mixed_rest, feats, filt, x, later, short_taps, skip, table)


def pack_kernel(*refs):
    out_ref = refs[-1]
    for i, ref in enumerate(refs[:3]):
        out_ref[0, i] = ref[...]


def pack(arrays, seq):
    rows, width = arrays[0].shape
    cols = width // seq
    return pl.pallas_call(
        pack_kernel,
        grid=(seq,),
        in_specs=[pl.BlockSpec((rows, cols), lambda s: (0, s))] * 3,
        out_specs=pl.BlockSpec((1, 3, rows, cols), lambda s: (s, 0, 0, 0)),
        out_shape=jax.ShapeDtypeStruct((seq, 3, rows, cols), BF16),
        compiler_params=params(),
        name="pack",
    )(*arrays)


def unpack_kernel(*refs):
    parts, outs = refs[:-3], refs[-3:]
    cols = parts[0].shape[3]
    for n, part in enumerate(parts):
        for i, out in enumerate(outs):
            out[:, n * cols : (n + 1) * cols] = part[0, i]


def unpack(parts):
    seq, _, rows, cols = parts[0].shape
    wide = cols * len(parts)
    shape = jax.ShapeDtypeStruct((rows, seq * wide), BF16)
    return pl.pallas_call(
        unpack_kernel,
        grid=(seq,),
        in_specs=[pl.BlockSpec((1, 3, rows, cols), lambda s: (s, 0, 0, 0))] * len(parts),
        out_specs=[pl.BlockSpec((rows, wide), lambda s: (0, s))] * 3,
        out_shape=[shape] * 3,
        compiler_params=params(),
        name="unpack",
    )(*parts)


def along(block, axis, distance):
    size = lax.axis_size(axis)
    return lax.ppermute(block, axis, [(i, i + distance) for i in range(size) if 0 <= i + distance < size])


def around(block, axis, distance):
    size = lax.axis_size(axis)
    return lax.ppermute(block, axis, [(i, (i + distance) % size) for i in range(size)])


def across(block, axis, bit):
    return lax.ppermute(block, axis, [(i, i ^ bit) for i in range(lax.axis_size(axis))])


def bits_of(axis):
    size = lax.axis_size(axis)
    return [1 << n for n in range(size.bit_length() - 1)]


def sum_over(value, axes):
    for axis in axes:
        for bit in bits_of(axis):
            value = value + across(value, axis, bit)
    return value


def split_kernel(y_ref, *refs):
    count = (len(refs) - 1) // 2
    for n in range(count):
        refs[count + 1 + n][...] = refs[n][...]


def split_cotangent(cotangent, y, ys, col_part, after):
    rows, width = cotangent.shape

    def source(step):
        return pl.BlockSpec((rows, col_part), lambda z, y_ref: (0, z * ys + (y_ref[0] + step) % ys))

    return pl.pallas_call(
        split_kernel,
        grid_spec=pltpu.PrefetchScalarGridSpec(
            num_scalar_prefetch=1,
            grid=(Z,),
            in_specs=[source(step) for step in range(ys)] + [pl.BlockSpec(memory_space=pl.ANY)],
            out_specs=[pl.BlockSpec((rows, col_part), lambda z, _: (0, z))] * ys,
        ),
        out_shape=[jax.ShapeDtypeStruct((rows, width // ys), BF16)] * ys,
        compiler_params=params(),
        name="split",
    )(y.reshape(1), *([cotangent] * ys), after)


def join_kernel(axis, count, *refs):
    out = refs[-1]
    for n in range(count):
        size = refs[n].shape[axis]
        here = slice(n * size, (n + 1) * size)
        if axis == 0:
            out[here] = refs[n][...]
        else:
            out[:, here] = refs[n][...]


def join(parts, axis, after=()):
    shape = list(parts[0].shape)
    tile = shape[-1] // Z
    block = pl.BlockSpec((*shape[:-1], tile), lambda i: (0, 0, 0, i))
    shape[axis] *= len(parts)
    return pl.pallas_call(
        functools.partial(join_kernel, axis, len(parts)),
        grid=(Z,),
        in_specs=[block] * len(parts) + [pl.BlockSpec(memory_space=pl.ANY)] * len(after),
        out_specs=pl.BlockSpec((*shape[:-1], tile), lambda i: (0, 0, 0, i)),
        out_shape=jax.ShapeDtypeStruct(tuple(shape), BF16),
        compiler_params=params(),
        name="join",
    )(*parts, *after)


def own_cotangent(cotangent, col_part, after):
    ys, y = lax.axis_size("y"), lax.axis_index("y")
    held = split_cotangent(cotangent, y, ys, col_part, after)
    held = [around(part, "y", step) if step else part for step, part in enumerate(held)]
    return join([part[None, None] for part in held], 0)


def gather_cotangent(held, after):
    bits = bits_of("seq")
    for bit in reversed(bits[1:]):
        held = join([held, across(held, "seq", bit)], 1, after)
    return held, across(held, "seq", bits[0])


def mixed_grad_kernel(place_ref, a_ref, b_ref, w_ref, _, out_ref, head_ref, found):
    _, count, rows, _ = a_ref.shape
    tokens = count * rows
    pieces = jnp.concatenate([ref[...].reshape(tokens, -1) for ref in (a_ref, b_ref)], axis=0)
    found[...] = contract(pieces, w_ref[...], 1)
    for block in range(2 * count):
        there = pl.multiple_of(place_ref[block] * rows, rows)
        out_ref[block * rows : (block + 1) * rows] = found[pl.ds(there, rows)].astype(out_ref.dtype)
    head_ref[...] = out_ref[0 : LTAPS + PAD]


def mixed_grad(cots, weights, place, step, dtype, after):
    _, count, rows, width = cots[0].shape
    tokens = 2 * count * rows
    cols = weights.shape[0]
    tile = min(cols, 2 * LANES)
    piece = pl.BlockSpec((1, count, rows, width), lambda i, _: (step, 0, 0, 0))
    return pl.pallas_call(
        mixed_grad_kernel,
        grid_spec=pltpu.PrefetchScalarGridSpec(
            num_scalar_prefetch=1,
            grid=(cols // tile,),
            in_specs=[
                piece,
                piece,
                pl.BlockSpec((tile, width), lambda i, _: (i, 0)),
                pl.BlockSpec(memory_space=pl.ANY),
            ],
            out_specs=[
                pl.BlockSpec((tokens, tile), lambda i, _: (0, i)),
                pl.BlockSpec((LTAPS + PAD, tile), lambda i, _: (0, i)),
            ],
            scratch_shapes=[pltpu.VMEM((tokens, tile), F32)],
        ),
        out_shape=[
            jax.ShapeDtypeStruct((tokens, cols), dtype),
            jax.ShapeDtypeStruct((LTAPS + PAD, cols), dtype),
        ],
        compiler_params=params(),
        name="mixed_grad",
    )(place, *cots, weights, after)


def weight_grad_kernel(scale, a_ref, b_ref, *refs):
    steps, count, rows, tile = a_ref.shape
    tokens = count * rows
    mixed, out = refs[:steps], refs[-1]
    total = None
    for step in range(steps):
        for n, ref in enumerate((a_ref, b_ref)):
            left = mixed[step][:, n * tokens : (n + 1) * tokens]
            term = jnp.dot(left, ref[step].reshape(tokens, tile), preferred_element_type=F32)
            total = term if total is None else total + term
    out[...] = (total * scale).astype(BF16)


def weight_grad(cots, mixed, chunk, chunks, scale, target, after):
    steps, count, rows, width = cots[0].shape
    part, tokens = mixed[0].shape
    tile = width // Z
    piece = pl.BlockSpec((steps, count, rows, tile), lambda i: (0, 0, 0, i))
    extra = [*after] + ([] if target is None else [target])
    return pl.pallas_call(
        functools.partial(weight_grad_kernel, scale),
        grid=(Z,),
        in_specs=[piece, piece]
        + [pl.BlockSpec((part, tokens), lambda i: (0, 0))] * len(mixed)
        + [pl.BlockSpec(memory_space=pl.ANY)] * len(extra),
        out_specs=pl.BlockSpec((part, tile), lambda i: (chunk, i)),
        out_shape=jax.ShapeDtypeStruct((part * chunks, width), BF16),
        input_output_aliases={} if target is None else {2 + len(mixed) + len(after): 0},
        compiler_params=params(),
        name="weight_grad",
    )(*cots, *mixed, *extra)


def tail_kernel(x_ref, before_ref, taps_ref, *refs):
    out_ref, xf = refs[-2:]
    rows = x_ref.shape[2]
    for i in range(3):
        out_ref[i * PAD : (i + 1) * PAD] = x_ref[0, i, rows - PAD :]
    for tile in range(x_ref.shape[3] // LANES):
        cols = slice(tile * LANES, (tile + 1) * LANES)
        taps = taps_ref[:, :, cols]
        prod = None
        for i in (1, 2):
            xf[tile, i - 1, 0:PAD] = before_ref[0, i, :, cols].astype(F32)
            xf[tile, i - 1, PAD:] = x_ref[0, i, :, cols].astype(F32)
            feature = taps[i, 0:1] * xf[tile, i - 1, PAD : PAD + rows]
            for j in range(1, SHORT):
                feature = feature + taps[i, j : j + 1] * xf[tile, i - 1, PAD - j : PAD - j + rows]
            prod = feature if prod is None else prod * feature
        out_ref[3 * PAD :, cols] = prod.astype(BF16)


def tail_of(x, short_taps, after):
    seq, _, rows, cols = x.shape
    wide = min(cols, 4 * LANES)
    out_rows = 3 * PAD + rows
    return pl.pallas_call(
        tail_kernel,
        grid=(cols // wide,),
        in_specs=[
            pl.BlockSpec((1, 3, rows, wide), lambda c: (seq - 1, 0, 0, c)),
            pl.BlockSpec((1, 3, PAD, wide), lambda c: (seq - 2, 0, rows // PAD - 1, c)),
            pl.BlockSpec((3, SHORT, wide), lambda c: (0, 0, c)),
        ]
        + [pl.BlockSpec(memory_space=pl.ANY)] * len(after),
        out_specs=pl.BlockSpec((out_rows, wide), lambda c: (0, c)),
        out_shape=jax.ShapeDtypeStruct((out_rows, cols), BF16),
        scratch_shapes=[pltpu.VMEM((wide // LANES, 2, PAD + rows, LANES), F32)],
        compiler_params=params(),
        name="tail",
    )(x, x, short_taps, *after)


def head_kernel(mo_ref, mr_ref, *refs):
    out_ref = refs[-1]
    chunks = len(refs) // 2
    edge = LTAPS + PAD
    part = out_ref.shape[1] // chunks
    for h in range(chunks):
        own = slice(h * part, (h + 1) * part)
        f_ref, filt_ref = refs[2 * h : 2 * h + 2]
        mixed = mo_ref[:, own] + mr_ref[:, own].astype(F32)
        out_ref[0:edge, own] = (mixed * f_ref[0]).astype(BF16)
        out_ref[edge : edge + PAD, own] = f_ref[1, 0:PAD].astype(BF16)
        out_ref[edge + PAD : edge + 2 * PAD, own] = f_ref[2, 0:PAD].astype(BF16)
        out_ref[edge + 2 * PAD :, own] = (mixed[0:PAD] * filt_ref[0:PAD]).astype(BF16)


def head_of(mixed_own, mixed_rest, mixers):
    edge, cols = LTAPS + PAD, mixed_own.shape[1]
    part = cols // len(mixers)
    whole = pl.BlockSpec((edge, cols), lambda i: (0, 0))
    feat_specs = [
        pl.BlockSpec((3, edge, part), lambda i: (0, 0, 0)),
        pl.BlockSpec((edge, part), lambda i: (0, 0)),
    ]
    return pl.pallas_call(
        head_kernel,
        grid=(1,),
        in_specs=[whole, whole] + feat_specs * len(mixers),
        out_specs=pl.BlockSpec((edge + 3 * PAD, cols), lambda i: (0, 0)),
        out_shape=jax.ShapeDtypeStruct((edge + 3 * PAD, cols), BF16),
        compiler_params=params(),
        name="head",
    )(mixed_own, mixed_rest, *[array for mixer in mixers for array in mixer[1:]])


def contract(a, b, dim):
    return lax.dot_general(a, b, (((dim,), (dim,)), ((), ())), preferred_element_type=F32)


def places(seq):
    bits = bits_of("seq")
    source = lax.iota(jnp.int32, seq) ^ lax.axis_index("seq")
    return sum(((source >> n) & 1) << (len(bits) - 1 - n) for n in range(len(bits)))


def body(queries, keys, values, cotangent, out_weight, short_taps, long_taps, skip_gain):
    rows, width = queries.shape
    col_part = out_weight.shape[1]
    seq, ys = lax.axis_size("seq"), lax.axis_size("y")
    cols = width // seq
    chunks = 2 if cols % (2 * LANES) == 0 else 1
    groups = long_taps.shape[1]
    fsdp = ("z", "y")
    grad_scale = float(rows * seq * ys * Z) ** (-0.5)

    weights = lax.all_gather(out_weight, "z", axis=1, tiled=True)
    fwd_table, bwd_table = make_tables(long_taps)
    skip = skip_gain.reshape(1, cols)
    place = places(seq)
    by_owner = pack((queries, keys, values), seq)
    x = lax.all_to_all(by_owner, "seq", split_axis=0, concat_axis=0, tiled=True)
    held = own_cotangent(cotangent, col_part, by_owner)
    tail = tail_of(x, short_taps, [fwd_table, held])
    halo = along(tail, fsdp, 1)
    cots = gather_cotangent(held, [tail])
    mixers = [forward(x, halo, short_taps, skip, fwd_table, place, 0, chunks, cots[1])]

    parts, heads = [], []
    for step in range(1, ys):
        part, head = mixed_grad(cots, weights, place, step, BF16, parts[-1] if parts else mixers[0][0])
        parts.append(part)
        heads.append(around(head, "y", -step))
    for h in range(1, chunks):
        mixers.append(forward(x, halo, short_taps, skip, fwd_table, place, h, chunks, parts[-1]))
    mixed_own, own_head = mixed_grad(cots, weights, place, 0, F32, parts[-1])
    rest = [around(parts[step - 1], "y", -step) for step in range(1, ys)]
    mixed_rest = rest[0] if len(rest) == 1 else sum(piece.astype(F32) for piece in rest)
    head_rest = heads[0] if len(heads) == 1 else sum(piece.astype(F32) for piece in heads)
    head = head_of(own_head, head_rest, mixers)
    later = along(head, fsdp, -1)

    weight_sum = None
    for h in range(chunks):
        mixed_all = [around(mixers[h][0], "y", step) if step else mixers[h][0] for step in range(ys)]
        after = [later, *rest] if h == chunks - 1 else [mixed_own]
        weight_sum = weight_grad(cots, mixed_all, h, chunks, grad_scale, weight_sum, after)
    weight_part = lax.psum_scatter(weight_sum, "z", scatter_dimension=1, tiled=True)

    grads, short_parts, long_parts = [], [], []
    for h in range(chunks):
        _, feats, filt = mixers[h]
        grad, short_part, long_part = backward(
            mixed_own, mixed_rest, feats, filt, x, later, short_taps, skip, bwd_table, h, chunks
        )
        grads.append(lax.all_to_all(grad, "seq", split_axis=0, concat_axis=0, tiled=True))
        short_parts.append(short_part)
        long_parts.append(long_part)

    query_grad, key_grad, value_grad = unpack(grads)
    packed = jnp.concatenate(
        [
            jnp.concatenate(short_parts, axis=2).reshape(3 * (SHORT + 1), cols),
            jnp.concatenate(long_parts, axis=0).reshape(-1, cols),
        ],
        axis=0,
    )
    packed = sum_over(packed, ("y", "z")) * grad_scale
    short_sum = packed[: 3 * (SHORT + 1)].reshape(3, SHORT + 1, cols)
    long_sum = packed[3 * (SHORT + 1) :].reshape(groups, LTAPS).T
    return (
        query_grad,
        key_grad,
        value_grad,
        weight_part.astype(F32),
        short_sum[:, :SHORT],
        long_sum,
        short_sum[0, SHORT],
    )


def solution(mesh):
    fsdp, seq = mesh.shape["fsdp"], mesh.shape["seq"]
    split = Mesh(mesh.devices.reshape(Z, fsdp // Z, seq), ("z", "y", "seq"))
    tokens = P(("z", "y", "seq"), None)
    specs = (P("seq", ("z", "y")), P(None, None, "seq"), P(None, "seq"), P("seq"))
    return jax.shard_map(
        body,
        mesh=split,
        in_specs=(tokens,) * 4 + specs,
        out_specs=(tokens,) * 3 + specs,
        check_vma=False,
    )
```

```python
import functools

import jax
import jax.numpy as jnp
from jax import lax
from jax.experimental import pallas as pl
from jax.experimental.pallas import tpu as pltpu
from jax.sharding import Mesh
from jax.sharding import PartitionSpec as P

SHORT = 7
LTAPS = 128
LANES = 128
PAD = 16
Z = 4
F32 = jnp.float32
BF16 = jnp.bfloat16


def params():
    return pltpu.CompilerParams(vmem_limit_bytes=60 * 2**20)


def tables_kernel(fwd_ref, bwd_ref, tf_ref, tb_ref):
    for g in range(fwd_ref.shape[0]):
        rows = slice(g * LTAPS, (g + 1) * LTAPS)
        for src, dst in ((fwd_ref, tf_ref), (bwd_ref, tb_ref)):
            wide = jnp.broadcast_to(src[g : g + 1, :], (LTAPS, 2 * LTAPS))
            dst[rows, :] = pltpu.roll(wide, 0, 1, stride=1, stride_axis=0).astype(BF16)


def make_tables(long_taps):
    by_group = long_taps.T
    groups = by_group.shape[0]
    fwd = jnp.pad(by_group[:, ::-1], ((0, 0), (1, LTAPS - 1)))
    bwd = jnp.pad(by_group, ((0, 0), (0, LTAPS)))
    per = 8
    row_spec = pl.BlockSpec((per, 2 * LTAPS), lambda i: (i, 0))
    tab_spec = pl.BlockSpec((per * LTAPS, 2 * LTAPS), lambda i: (i, 0))
    shape = jax.ShapeDtypeStruct((groups * LTAPS, 2 * LTAPS), BF16)
    return pl.pallas_call(
        tables_kernel,
        grid=(groups // per,),
        in_specs=[row_spec, row_spec],
        out_specs=[tab_spec, tab_spec],
        out_shape=[shape, shape],
        compiler_params=params(),
        name="tables",
    )(fwd, bwd)


def pick_groups(wide, col, rows, per):
    lane_group = lax.broadcasted_iota(jnp.int32, (rows, LANES), 1) // (LANES // per)
    cols = slice(col * LANES, (col + 1) * LANES)
    out = wide[0:rows, cols]
    for g in range(1, per):
        out = jnp.where(lane_group == g, wide[g * rows : (g + 1) * rows, cols], out)
    return out


def features_of(taps_ref, row, xf, i, begin):
    total = taps_ref[row, 0:1] * xf[i, PAD + begin : PAD + begin + LTAPS]
    for j in range(1, SHORT):
        total = total + taps_ref[row, j : j + 1] * xf[i, PAD + begin - j : PAD + begin - j + LTAPS]
    return total


def forward_kernel(
    place_ref, x_ref, h_ref, taps_ref, skip_ref, tab_ref, _, mixed_ref, f_ref, filt_ref, xf, pf, pb, wide
):
    blocks, _, rows, _ = x_ref.shape
    tokens = blocks * rows
    per = tab_ref.shape[0] // LTAPS
    for i in range(3):
        xf[i, 0:PAD] = h_ref[i * PAD : (i + 1) * PAD].astype(F32)
        for b in range(blocks):
            begin = PAD + b * rows
            xf[i, begin : begin + rows] = x_ref[b, i].astype(F32)
    pb[0:LTAPS] = h_ref[3 * PAD : 3 * PAD + LTAPS]
    for begin in range(0, tokens, LTAPS):
        own = slice(begin, begin + LTAPS)
        f1 = features_of(taps_ref, 1, xf, 1, begin)
        f2 = features_of(taps_ref, 2, xf, 2, begin)
        prod = f1 * f2
        f_ref[1, own] = f1
        f_ref[2, own] = f2
        f_ref[0, own] = features_of(taps_ref, 0, xf, 0, begin)
        pf[own] = prod
        pb[LTAPS + begin : 2 * LTAPS + begin] = prod.astype(BF16)
    skip = skip_ref[...]
    for b in range(0, tokens // LTAPS, 2):
        low = b * LTAPS
        windows = jnp.concatenate([pb[low : low + 2 * LTAPS], pb[low + LTAPS : low + 3 * LTAPS]], axis=1)
        wide[...] = jnp.dot(tab_ref[...], windows, preferred_element_type=F32)
        for n in range(2):
            own = slice(low + n * LTAPS, low + (n + 1) * LTAPS)
            filtered = pick_groups(wide, n, LTAPS, per) + skip * pf[own]
            filt_ref[own] = filtered
            mixed = f_ref[0, own] * filtered
            there = pl.multiple_of(place_ref[b + n] * LTAPS, LTAPS)
            mixed_ref[:, pl.ds(there, LTAPS)] = mixed.T.astype(BF16)


def forward(x, halo, short_taps, skip, table, place, chunk, chunks, after):
    blocks, _, rows, cols = x.shape
    cols //= chunks
    tokens = blocks * rows
    tiles = cols // LANES
    first = chunk * tiles
    tab_rows = table.shape[0] * LANES // skip.shape[1]
    return pl.pallas_call(
        forward_kernel,
        grid_spec=pltpu.PrefetchScalarGridSpec(
            num_scalar_prefetch=1,
            grid=(tiles,),
            in_specs=[
                pl.BlockSpec((blocks, 3, rows, LANES), lambda c, _: (0, 0, 0, first + c)),
                pl.BlockSpec((halo.shape[0], LANES), lambda c, _: (0, first + c)),
                pl.BlockSpec((3, SHORT, LANES), lambda c, _: (0, 0, first + c)),
                pl.BlockSpec((1, LANES), lambda c, _: (0, first + c)),
                pl.BlockSpec((tab_rows, 2 * LTAPS), lambda c, _: (first + c, 0)),
                pl.BlockSpec(memory_space=pl.ANY),
            ],
            out_specs=[
                pl.BlockSpec((LANES, tokens), lambda c, _: (c, 0)),
                pl.BlockSpec((3, tokens, LANES), lambda c, _: (0, 0, c)),
                pl.BlockSpec((tokens, LANES), lambda c, _: (0, c)),
            ],
            scratch_shapes=[
                pltpu.VMEM((3, PAD + tokens, LANES), F32),
                pltpu.VMEM((tokens, LANES), F32),
                pltpu.VMEM((LTAPS + tokens, LANES), BF16),
                pltpu.VMEM((tab_rows, 2 * LTAPS), F32),
            ],
        ),
        out_shape=[
            jax.ShapeDtypeStruct((cols, tokens), BF16),
            jax.ShapeDtypeStruct((3, tokens, cols), F32),
            jax.ShapeDtypeStruct((tokens, cols), F32),
        ],
        compiler_params=params(),
        name="forward",
    )(place, x, halo, short_taps, skip, table, after)


def sum_by_lag(gram):
    wide = gram.shape[1]
    parts = [gram[i : i + 8] for i in range(0, gram.shape[0], 8)]
    step = 8
    while len(parts) > 1:
        parts = [
            parts[k] + pltpu.roll(parts[k + 1], wide - step, 1) for k in range(0, len(parts), 2)
        ]
        step *= 2
    total = parts[0]
    row = lax.broadcasted_iota(jnp.int32, total.shape, 0)
    for bit in (1, 2, 4):
        total = jnp.where((row & bit) != 0, pltpu.roll(total, wide - bit, 1), total)
    return jnp.sum(total[:, :LTAPS], axis=0, keepdims=True)


def backward_kernel(
    mo_ref, mr_ref, f_ref, filt_ref, x_ref, n_ref, taps_ref, skip_ref, tab_ref,
    grad_ref, short_ref, long_ref, db, fg, wide, left, right,
):
    blocks, _, rows, _ = x_ref.shape
    tokens = blocks * rows
    per = tab_ref.shape[0] // LTAPS
    count = tokens // LTAPS
    skip = skip_ref[...]
    lane_group = lax.broadcasted_iota(jnp.int32, (1, LANES), 1) // (LANES // per)
    gain = jnp.zeros((8, LANES), F32)
    for b in range(count):
        own = slice(b * LTAPS, (b + 1) * LTAPS)
        mixed_grad = mo_ref[own] + mr_ref[own].astype(F32)
        slope = mixed_grad * f_ref[0, own]
        db[own] = slope.astype(BF16)
        fg[0, own] = mixed_grad * filt_ref[own]
        fg[1, own] = skip * slope
        prod = f_ref[1, own] * f_ref[2, own]
        gain = gain + jnp.sum((prod * slope).reshape(LTAPS // 8, 8, LANES), axis=0)
        prod_b = prod.astype(BF16)
        for g in range(per):
            keep = (lane_group == g).astype(F32).astype(BF16)
            left[g * LTAPS : (g + 1) * LTAPS, b * LANES : (b + 1) * LANES] = prod_b * keep
    db[tokens : tokens + LTAPS + PAD] = n_ref[0 : LTAPS + PAD]
    db[tokens + LTAPS + PAD :] = jnp.zeros((LTAPS - PAD, LANES), BF16)
    for b in range(count):
        right[:, b * LANES : (b + 1) * LANES] = db[b * LTAPS : (b + 2) * LTAPS]
    for b in range(0, count, 2):
        wide[...] = jnp.dot(
            tab_ref[...], right[:, b * LANES : (b + 2) * LANES], preferred_element_type=F32
        )
        for n in range(2):
            own = slice((b + n) * LTAPS, (b + n + 1) * LTAPS)
            grad = pick_groups(wide, n, LTAPS, per) + fg[1, own]
            fg[1, own] = grad * f_ref[2, own]
            fg[2, own] = grad * f_ref[1, own]
    few = jnp.concatenate([tab_ref[g * LTAPS : g * LTAPS + PAD] for g in range(per)], axis=0)
    edge = jnp.dot(few, db[tokens : tokens + 2 * LTAPS], preferred_element_type=F32)
    begin = LTAPS + PAD
    grad = pick_groups(edge, 0, PAD, per) + skip * n_ref[0:PAD].astype(F32)
    fg[1, tokens : tokens + PAD] = grad * n_ref[begin + PAD : begin + 2 * PAD].astype(F32)
    fg[2, tokens : tokens + PAD] = grad * n_ref[begin : begin + PAD].astype(F32)
    fg[0, tokens : tokens + PAD] = n_ref[begin + 2 * PAD : begin + 3 * PAD].astype(F32)
    for i in range(3):
        sums = [jnp.zeros((8, LANES), F32) for _ in range(SHORT)]
        for b in range(count):
            low = b * LTAPS
            inputs = x_ref[b, i].astype(F32)
            total = None
            for j in range(SHORT):
                later = fg[i, low + j : low + j + LTAPS]
                term = taps_ref[i, j : j + 1] * later
                total = term if total is None else total + term
                sums[j] = sums[j] + jnp.sum((later * inputs).reshape(LTAPS // 8, 8, LANES), axis=0)
            grad_ref[b, i] = total.astype(BF16)
        for j in range(SHORT):
            short_ref[i, j : j + 1] = jnp.sum(sums[j], axis=0, keepdims=True)
        short_ref[i, SHORT : SHORT + 1] = jnp.sum(gain, axis=0, keepdims=True)
    wide[...] = lax.dot_general(left[...], right[...], (((1,), (1,)), ((), ())), preferred_element_type=F32)
    for g in range(per):
        gram = wide[g * LTAPS : (g + 1) * LTAPS]
        long_ref[g : g + 1] = sum_by_lag(gram)


def backward(mixed_own, mixed_rest, feats, filt, x, later, short_taps, skip, table, chunk, chunks):
    blocks, _, rows, cols = x.shape
    cols //= chunks
    tokens = blocks * rows
    tiles = cols // LANES
    first = chunk * tiles
    tab_rows = table.shape[0] * LANES // skip.shape[1]
    per = tab_rows // LTAPS
    tok = pl.BlockSpec((tokens, LANES), lambda c: (0, first + c))
    return pl.pallas_call(
        backward_kernel,
        grid=(tiles,),
        in_specs=[
            tok,
            tok,
            pl.BlockSpec((3, tokens, LANES), lambda c: (0, 0, c)),
            pl.BlockSpec((tokens, LANES), lambda c: (0, c)),
            pl.BlockSpec((blocks, 3, rows, LANES), lambda c: (0, 0, 0, first + c)),
            pl.BlockSpec((later.shape[0], LANES), lambda c: (0, first + c)),
            pl.BlockSpec((3, SHORT, LANES), lambda c: (0, 0, first + c)),
            pl.BlockSpec((1, LANES), lambda c: (0, first + c)),
            pl.BlockSpec((tab_rows, 2 * LTAPS), lambda c: (first + c, 0)),
        ],
        out_specs=[
            pl.BlockSpec((blocks, 3, rows, LANES), lambda c: (0, 0, 0, c)),
            pl.BlockSpec((3, SHORT + 1, LANES), lambda c: (0, 0, c)),
            pl.BlockSpec((per, LTAPS), lambda c: (c, 0)),
        ],
        out_shape=[
            jax.ShapeDtypeStruct((blocks, 3, rows, cols), BF16),
            jax.ShapeDtypeStruct((3, SHORT + 1, cols), F32),
            jax.ShapeDtypeStruct((tiles * per, LTAPS), F32),
        ],
        scratch_shapes=[
            pltpu.VMEM((tokens + 2 * LTAPS, LANES), BF16),
            pltpu.VMEM((3, tokens + PAD, LANES), F32),
            pltpu.VMEM((tab_rows, 2 * LTAPS), F32),
            pltpu.VMEM((tab_rows, tokens), BF16),
            pltpu.VMEM((2 * LTAPS, tokens), BF16),
        ],
        compiler_params=params(),
        name="backward",
    )(mixed_own, mixed_rest, feats, filt, x, later, short_taps, skip, table)


def pack_kernel(*refs):
    out_ref = refs[-1]
    for i, ref in enumerate(refs[:3]):
        out_ref[0, i] = ref[...]


def pack(arrays, seq):
    rows, width = arrays[0].shape
    cols = width // seq
    return pl.pallas_call(
        pack_kernel,
        grid=(seq,),
        in_specs=[pl.BlockSpec((rows, cols), lambda s: (0, s))] * 3,
        out_specs=pl.BlockSpec((1, 3, rows, cols), lambda s: (s, 0, 0, 0)),
        out_shape=jax.ShapeDtypeStruct((seq, 3, rows, cols), BF16),
        compiler_params=params(),
        name="pack",
    )(*arrays)


def unpack_kernel(*refs):
    parts, outs = refs[:-3], refs[-3:]
    cols = parts[0].shape[3]
    for n, part in enumerate(parts):
        for i, out in enumerate(outs):
            out[:, n * cols : (n + 1) * cols] = part[0, i]


def unpack(parts):
    seq, _, rows, cols = parts[0].shape
    wide = cols * len(parts)
    shape = jax.ShapeDtypeStruct((rows, seq * wide), BF16)
    return pl.pallas_call(
        unpack_kernel,
        grid=(seq,),
        in_specs=[pl.BlockSpec((1, 3, rows, cols), lambda s: (s, 0, 0, 0))] * len(parts),
        out_specs=[pl.BlockSpec((rows, wide), lambda s: (0, s))] * 3,
        out_shape=[shape] * 3,
        compiler_params=params(),
        name="unpack",
    )(*parts)


def along(block, axis, distance):
    size = lax.axis_size(axis)
    return lax.ppermute(block, axis, [(i, i + distance) for i in range(size) if 0 <= i + distance < size])


def around(block, axis, distance):
    size = lax.axis_size(axis)
    return lax.ppermute(block, axis, [(i, (i + distance) % size) for i in range(size)])


def across(block, axis, bit):
    return lax.ppermute(block, axis, [(i, i ^ bit) for i in range(lax.axis_size(axis))])


def bits_of(axis):
    size = lax.axis_size(axis)
    return [1 << n for n in range(size.bit_length() - 1)]


def sum_over(value, axes):
    for axis in axes:
        for bit in bits_of(axis):
            value = value + across(value, axis, bit)
    return value


def split_kernel(y_ref, *refs):
    count = (len(refs) - 1) // 2
    for n in range(count):
        refs[count + 1 + n][...] = refs[n][...]


def split_cotangent(cotangent, y, ys, col_part, after):
    rows, width = cotangent.shape

    def source(step):
        return pl.BlockSpec((rows, col_part), lambda z, y_ref: (0, z * ys + (y_ref[0] + step) % ys))

    return pl.pallas_call(
        split_kernel,
        grid_spec=pltpu.PrefetchScalarGridSpec(
            num_scalar_prefetch=1,
            grid=(Z,),
            in_specs=[source(step) for step in range(ys)] + [pl.BlockSpec(memory_space=pl.ANY)],
            out_specs=[pl.BlockSpec((rows, col_part), lambda z, _: (0, z))] * ys,
        ),
        out_shape=[jax.ShapeDtypeStruct((rows, width // ys), BF16)] * ys,
        compiler_params=params(),
        name="split",
    )(y.reshape(1), *([cotangent] * ys), after)


def join_kernel(axis, count, *refs):
    out = refs[-1]
    for n in range(count):
        size = refs[n].shape[axis]
        here = slice(n * size, (n + 1) * size)
        if axis == 0:
            out[here] = refs[n][...]
        else:
            out[:, here] = refs[n][...]


def join(parts, axis, after=()):
    shape = list(parts[0].shape)
    tile = shape[-1] // Z
    block = pl.BlockSpec((*shape[:-1], tile), lambda i: (0, 0, 0, i))
    shape[axis] *= len(parts)
    return pl.pallas_call(
        functools.partial(join_kernel, axis, len(parts)),
        grid=(Z,),
        in_specs=[block] * len(parts) + [pl.BlockSpec(memory_space=pl.ANY)] * len(after),
        out_specs=pl.BlockSpec((*shape[:-1], tile), lambda i: (0, 0, 0, i)),
        out_shape=jax.ShapeDtypeStruct(tuple(shape), BF16),
        compiler_params=params(),
        name="join",
    )(*parts, *after)


def own_cotangent(cotangent, col_part, after):
    ys, y = lax.axis_size("y"), lax.axis_index("y")
    held = split_cotangent(cotangent, y, ys, col_part, after)
    held = [around(part, "y", step) if step else part for step, part in enumerate(held)]
    return join([part[None, None] for part in held], 0)


def gather_cotangent(held, after):
    bits = bits_of("seq")
    for bit in reversed(bits[1:]):
        held = join([held, across(held, "seq", bit)], 1, after)
    return held, across(held, "seq", bits[0])


def mixed_grad_kernel(place_ref, a_ref, b_ref, w_ref, _, out_ref, head_ref, *refs):
    found = refs[-1]
    _, count, rows, _ = a_ref.shape
    tokens = count * rows
    pieces = jnp.concatenate([ref[...].reshape(tokens, -1) for ref in (a_ref, b_ref)], axis=0)
    found[...] = contract(pieces, w_ref[...], 1)
    for block in range(2 * count):
        there = pl.multiple_of(place_ref[block] * rows, rows)
        out_ref[block * rows : (block + 1) * rows] = found[pl.ds(there, rows)].astype(out_ref.dtype)
    head_ref[...] = out_ref[0 : LTAPS + PAD]


def mixed_grad(cots, weights, place, step, dtype, after, passed=False):
    _, count, rows, width = cots[0].shape
    tokens = 2 * count * rows
    cols = weights.shape[0]
    tile = min(cols, 2 * LANES)
    piece = pl.BlockSpec((1, count, rows, width), lambda i, _: (step, 0, 0, 0))
    return pl.pallas_call(
        mixed_grad_kernel,
        grid_spec=pltpu.PrefetchScalarGridSpec(
            num_scalar_prefetch=1,
            grid=(cols // tile,),
            in_specs=[
                piece,
                piece,
                pl.BlockSpec((tile, width), lambda i, _: (i, 0)),
                pl.BlockSpec(memory_space=pl.ANY),
            ],
            out_specs=[
                pl.BlockSpec((tokens, tile), lambda i, _: (0, i)),
                pl.BlockSpec((LTAPS + PAD, tile), lambda i, _: (0, i)),
            ]
            + [pl.BlockSpec(memory_space=pl.ANY)] * passed,
            scratch_shapes=[pltpu.VMEM((tokens, tile), F32)],
        ),
        input_output_aliases={4: 2} if passed else {},
        out_shape=[
            jax.ShapeDtypeStruct((tokens, cols), dtype),
            jax.ShapeDtypeStruct((LTAPS + PAD, cols), dtype),
        ]
        + [jax.ShapeDtypeStruct(after.shape, after.dtype)] * passed,
        compiler_params=params(),
        name="mixed_grad",
    )(place, *cots, weights, after)


def weight_grad_kernel(scale, a_ref, b_ref, *refs):
    steps, count, rows, tile = a_ref.shape
    tokens = count * rows
    mixed, out = refs[:steps], refs[-1]
    total = None
    for step in range(steps):
        for n, ref in enumerate((a_ref, b_ref)):
            left = mixed[step][:, n * tokens : (n + 1) * tokens]
            term = jnp.dot(left, ref[step].reshape(tokens, tile), preferred_element_type=F32)
            total = term if total is None else total + term
    out[...] = (total * scale).astype(BF16)


def weight_grad(cots, mixed, chunk, chunks, scale, target, after):
    steps, count, rows, width = cots[0].shape
    part, tokens = mixed[0].shape
    tile = width // Z
    piece = pl.BlockSpec((steps, count, rows, tile), lambda i: (0, 0, 0, i))
    extra = [*after] + ([] if target is None else [target])
    return pl.pallas_call(
        functools.partial(weight_grad_kernel, scale),
        grid=(Z,),
        in_specs=[piece, piece]
        + [pl.BlockSpec((part, tokens), lambda i: (0, 0))] * len(mixed)
        + [pl.BlockSpec(memory_space=pl.ANY)] * len(extra),
        out_specs=pl.BlockSpec((part, tile), lambda i: (chunk, i)),
        out_shape=jax.ShapeDtypeStruct((part * chunks, width), BF16),
        input_output_aliases={} if target is None else {2 + len(mixed) + len(after): 0},
        compiler_params=params(),
        name="weight_grad",
    )(*cots, *mixed, *extra)


def tail_kernel(x_ref, before_ref, taps_ref, *refs):
    out_ref, xf = refs[-2:]
    rows = x_ref.shape[2]
    for i in range(3):
        out_ref[i * PAD : (i + 1) * PAD] = x_ref[0, i, rows - PAD :]
    for tile in range(x_ref.shape[3] // LANES):
        cols = slice(tile * LANES, (tile + 1) * LANES)
        taps = taps_ref[:, :, cols]
        prod = None
        for i in (1, 2):
            xf[tile, i - 1, 0:PAD] = before_ref[0, i, :, cols].astype(F32)
            xf[tile, i - 1, PAD:] = x_ref[0, i, :, cols].astype(F32)
            feature = taps[i, 0:1] * xf[tile, i - 1, PAD : PAD + rows]
            for j in range(1, SHORT):
                feature = feature + taps[i, j : j + 1] * xf[tile, i - 1, PAD - j : PAD - j + rows]
            prod = feature if prod is None else prod * feature
        out_ref[3 * PAD :, cols] = prod.astype(BF16)


def tail_of(x, short_taps, after):
    seq, _, rows, cols = x.shape
    wide = min(cols, 4 * LANES)
    out_rows = 3 * PAD + rows
    return pl.pallas_call(
        tail_kernel,
        grid=(cols // wide,),
        in_specs=[
            pl.BlockSpec((1, 3, rows, wide), lambda c: (seq - 1, 0, 0, c)),
            pl.BlockSpec((1, 3, PAD, wide), lambda c: (seq - 2, 0, rows // PAD - 1, c)),
            pl.BlockSpec((3, SHORT, wide), lambda c: (0, 0, c)),
        ]
        + [pl.BlockSpec(memory_space=pl.ANY)] * len(after),
        out_specs=pl.BlockSpec((out_rows, wide), lambda c: (0, c)),
        out_shape=jax.ShapeDtypeStruct((out_rows, cols), BF16),
        scratch_shapes=[pltpu.VMEM((wide // LANES, 2, PAD + rows, LANES), F32)],
        compiler_params=params(),
        name="tail",
    )(x, x, short_taps, *after)


def head_kernel(mo_ref, mr_ref, *refs):
    out_ref = refs[-1]
    chunks = len(refs) // 2
    edge = LTAPS + PAD
    part = out_ref.shape[1] // chunks
    for h in range(chunks):
        own = slice(h * part, (h + 1) * part)
        f_ref, filt_ref = refs[2 * h : 2 * h + 2]
        mixed = mo_ref[:, own] + mr_ref[:, own].astype(F32)
        out_ref[0:edge, own] = (mixed * f_ref[0]).astype(BF16)
        out_ref[edge : edge + PAD, own] = f_ref[1, 0:PAD].astype(BF16)
        out_ref[edge + PAD : edge + 2 * PAD, own] = f_ref[2, 0:PAD].astype(BF16)
        out_ref[edge + 2 * PAD :, own] = (mixed[0:PAD] * filt_ref[0:PAD]).astype(BF16)


def head_of(mixed_own, mixed_rest, mixers):
    edge, cols = LTAPS + PAD, mixed_own.shape[1]
    part = cols // len(mixers)
    whole = pl.BlockSpec((edge, cols), lambda i: (0, 0))
    feat_specs = [
        pl.BlockSpec((3, edge, part), lambda i: (0, 0, 0)),
        pl.BlockSpec((edge, part), lambda i: (0, 0)),
    ]
    return pl.pallas_call(
        head_kernel,
        grid=(1,),
        in_specs=[whole, whole] + feat_specs * len(mixers),
        out_specs=pl.BlockSpec((edge + 3 * PAD, cols), lambda i: (0, 0)),
        out_shape=jax.ShapeDtypeStruct((edge + 3 * PAD, cols), BF16),
        compiler_params=params(),
        name="head",
    )(mixed_own, mixed_rest, *[array for mixer in mixers for array in mixer[1:]])


def contract(a, b, dim):
    return lax.dot_general(a, b, (((dim,), (dim,)), ((), ())), preferred_element_type=F32)


def places(seq):
    bits = bits_of("seq")
    source = lax.iota(jnp.int32, seq) ^ lax.axis_index("seq")
    return sum(((source >> n) & 1) << (len(bits) - 1 - n) for n in range(len(bits)))


def body(queries, keys, values, cotangent, out_weight, short_taps, long_taps, skip_gain):
    rows, width = queries.shape
    col_part = out_weight.shape[1]
    seq, ys = lax.axis_size("seq"), lax.axis_size("y")
    cols = width // seq
    chunks = 2 if cols % (2 * LANES) == 0 else 1
    groups = long_taps.shape[1]
    fsdp = ("z", "y")
    grad_scale = float(rows * seq * ys * Z) ** (-0.5)

    weights = lax.all_gather(out_weight, "z", axis=1, tiled=True)
    fwd_table, bwd_table = make_tables(long_taps)
    skip = skip_gain.reshape(1, cols)
    place = places(seq)
    by_owner = pack((queries, keys, values), seq)
    x = lax.all_to_all(by_owner, "seq", split_axis=0, concat_axis=0, tiled=True)
    held = own_cotangent(cotangent, col_part, by_owner)
    tail = tail_of(x, short_taps, [fwd_table, held])
    halo = along(tail, fsdp, 1)
    cots = gather_cotangent(held, [halo])
    mixers = []
    for h in range(chunks):
        after = mixers[-1][0] if mixers else cots[0]
        mixers.append(forward(x, halo, short_taps, skip, fwd_table, place, h, chunks, after))

    parts, heads = [], []
    for step in range(1, ys):
        part, head = mixed_grad(cots, weights, place, step, BF16, parts[-1] if parts else mixers[-1][0])
        parts.append(part)
        heads.append(around(head, "y", -step))
    mixed_own, own_head, parts[-1] = mixed_grad(cots, weights, place, 0, F32, parts[-1], True)
    rest = [around(parts[step - 1], "y", -step) for step in range(1, ys)]
    mixed_rest = rest[0] if len(rest) == 1 else sum(piece.astype(F32) for piece in rest)
    head_rest = heads[0] if len(heads) == 1 else sum(piece.astype(F32) for piece in heads)
    head = head_of(own_head, head_rest, mixers)
    later = along(head, fsdp, -1)

    weight_sum = None
    for h in range(chunks):
        mixed_all = [around(mixers[h][0], "y", step) if step else mixers[h][0] for step in range(ys)]
        after = [later] if h == chunks - 1 else [head]
        weight_sum = weight_grad(cots, mixed_all, h, chunks, grad_scale, weight_sum, after)
    weight_part = lax.psum_scatter(weight_sum, "z", scatter_dimension=1, tiled=True)

    grads, short_parts, long_parts = [], [], []
    for h in range(chunks):
        _, feats, filt = mixers[h]
        grad, short_part, long_part = backward(
            mixed_own, mixed_rest, feats, filt, x, later, short_taps, skip, bwd_table, h, chunks
        )
        grads.append(lax.all_to_all(grad, "seq", split_axis=0, concat_axis=0, tiled=True))
        short_parts.append(short_part)
        long_parts.append(long_part)

    query_grad, key_grad, value_grad = unpack(grads)
    packed = jnp.concatenate(
        [
            jnp.concatenate(short_parts, axis=2).reshape(3 * (SHORT + 1), cols),
            jnp.concatenate(long_parts, axis=0).reshape(-1, cols),
        ],
        axis=0,
    )
    packed = sum_over(packed, ("y", "z")) * grad_scale
    short_sum = packed[: 3 * (SHORT + 1)].reshape(3, SHORT + 1, cols)
    long_sum = packed[3 * (SHORT + 1) :].reshape(groups, LTAPS).T
    return (
        query_grad,
        key_grad,
        value_grad,
        weight_part.astype(F32),
        short_sum[:, :SHORT],
        long_sum,
        short_sum[0, SHORT],
    )


def solution(mesh):
    fsdp, seq = mesh.shape["fsdp"], mesh.shape["seq"]
    split = Mesh(mesh.devices.reshape(Z, fsdp // Z, seq), ("z", "y", "seq"))
    tokens = P(("z", "y", "seq"), None)
    specs = (P("seq", ("z", "y")), P(None, None, "seq"), P(None, "seq"), P("seq"))
    return jax.shard_map(
        body,
        mesh=split,
        in_specs=(tokens,) * 4 + specs,
        out_specs=(tokens,) * 3 + specs,
        check_vma=False,
    )
```

```python
import functools

import jax
import jax.numpy as jnp
from jax import lax
from jax.experimental import pallas as pl
from jax.experimental.pallas import tpu as pltpu
from jax.sharding import Mesh
from jax.sharding import PartitionSpec as P

SHORT = 7
LTAPS = 128
LANES = 128
PAD = 16
Z = 4
F32 = jnp.float32
BF16 = jnp.bfloat16


def params():
    return pltpu.CompilerParams(vmem_limit_bytes=60 * 2**20)


def tables_kernel(fwd_ref, bwd_ref, tf_ref, tb_ref):
    for g in range(fwd_ref.shape[0]):
        rows = slice(g * LTAPS, (g + 1) * LTAPS)
        for src, dst in ((fwd_ref, tf_ref), (bwd_ref, tb_ref)):
            wide = jnp.broadcast_to(src[g : g + 1, :], (LTAPS, 2 * LTAPS))
            dst[rows, :] = pltpu.roll(wide, 0, 1, stride=1, stride_axis=0).astype(BF16)


def make_tables(long_taps):
    by_group = long_taps.T
    groups = by_group.shape[0]
    fwd = jnp.pad(by_group[:, ::-1], ((0, 0), (1, LTAPS - 1)))
    bwd = jnp.pad(by_group, ((0, 0), (0, LTAPS)))
    per = 8
    row_spec = pl.BlockSpec((per, 2 * LTAPS), lambda i: (i, 0))
    tab_spec = pl.BlockSpec((per * LTAPS, 2 * LTAPS), lambda i: (i, 0))
    shape = jax.ShapeDtypeStruct((groups * LTAPS, 2 * LTAPS), BF16)
    return pl.pallas_call(
        tables_kernel,
        grid=(groups // per,),
        in_specs=[row_spec, row_spec],
        out_specs=[tab_spec, tab_spec],
        out_shape=[shape, shape],
        compiler_params=params(),
        name="tables",
    )(fwd, bwd)


def pick_groups(wide, col, rows, per):
    lane_group = lax.broadcasted_iota(jnp.int32, (rows, LANES), 1) // (LANES // per)
    cols = slice(col * LANES, (col + 1) * LANES)
    out = wide[0:rows, cols]
    for g in range(1, per):
        out = jnp.where(lane_group == g, wide[g * rows : (g + 1) * rows, cols], out)
    return out


def features_of(taps_ref, row, xf, i, begin):
    total = taps_ref[row, 0:1] * xf[i, PAD + begin : PAD + begin + LTAPS]
    for j in range(1, SHORT):
        total = total + taps_ref[row, j : j + 1] * xf[i, PAD + begin - j : PAD + begin - j + LTAPS]
    return total


def forward_kernel(
    place_ref, x_ref, h_ref, taps_ref, skip_ref, tab_ref, _, mixed_ref, f_ref, filt_ref, xf, pf, pb, wide
):
    blocks, _, rows, _ = x_ref.shape
    tokens = blocks * rows
    per = tab_ref.shape[0] // LTAPS
    for i in range(3):
        xf[i, 0:PAD] = h_ref[i * PAD : (i + 1) * PAD].astype(F32)
        for b in range(blocks):
            begin = PAD + b * rows
            xf[i, begin : begin + rows] = x_ref[b, i].astype(F32)
    pb[0:LTAPS] = h_ref[3 * PAD : 3 * PAD + LTAPS]
    for begin in range(0, tokens, LTAPS):
        own = slice(begin, begin + LTAPS)
        f1 = features_of(taps_ref, 1, xf, 1, begin)
        f2 = features_of(taps_ref, 2, xf, 2, begin)
        prod = f1 * f2
        f_ref[1, own] = f1
        f_ref[2, own] = f2
        f_ref[0, own] = features_of(taps_ref, 0, xf, 0, begin)
        pf[own] = prod
        pb[LTAPS + begin : 2 * LTAPS + begin] = prod.astype(BF16)
    skip = skip_ref[...]
    for b in range(0, tokens // LTAPS, 2):
        low = b * LTAPS
        windows = jnp.concatenate([pb[low : low + 2 * LTAPS], pb[low + LTAPS : low + 3 * LTAPS]], axis=1)
        wide[...] = jnp.dot(tab_ref[...], windows, preferred_element_type=F32)
        for n in range(2):
            own = slice(low + n * LTAPS, low + (n + 1) * LTAPS)
            filtered = pick_groups(wide, n, LTAPS, per) + skip * pf[own]
            filt_ref[own] = filtered
            mixed = f_ref[0, own] * filtered
            there = pl.multiple_of(place_ref[b + n] * LTAPS, LTAPS)
            mixed_ref[:, pl.ds(there, LTAPS)] = mixed.T.astype(BF16)


def forward(x, halo, short_taps, skip, table, place, chunk, chunks, after):
    blocks, _, rows, cols = x.shape
    cols //= chunks
    tokens = blocks * rows
    tiles = cols // LANES
    first = chunk * tiles
    tab_rows = table.shape[0] * LANES // skip.shape[1]
    return pl.pallas_call(
        forward_kernel,
        grid_spec=pltpu.PrefetchScalarGridSpec(
            num_scalar_prefetch=1,
            grid=(tiles,),
            in_specs=[
                pl.BlockSpec((blocks, 3, rows, LANES), lambda c, _: (0, 0, 0, first + c)),
                pl.BlockSpec((halo.shape[0], LANES), lambda c, _: (0, first + c)),
                pl.BlockSpec((3, SHORT, LANES), lambda c, _: (0, 0, first + c)),
                pl.BlockSpec((1, LANES), lambda c, _: (0, first + c)),
                pl.BlockSpec((tab_rows, 2 * LTAPS), lambda c, _: (first + c, 0)),
                pl.BlockSpec(memory_space=pl.ANY),
            ],
            out_specs=[
                pl.BlockSpec((LANES, tokens), lambda c, _: (c, 0)),
                pl.BlockSpec((3, tokens, LANES), lambda c, _: (0, 0, c)),
                pl.BlockSpec((tokens, LANES), lambda c, _: (0, c)),
            ],
            scratch_shapes=[
                pltpu.VMEM((3, PAD + tokens, LANES), F32),
                pltpu.VMEM((tokens, LANES), F32),
                pltpu.VMEM((LTAPS + tokens, LANES), BF16),
                pltpu.VMEM((tab_rows, 2 * LTAPS), F32),
            ],
        ),
        out_shape=[
            jax.ShapeDtypeStruct((cols, tokens), BF16),
            jax.ShapeDtypeStruct((3, tokens, cols), F32),
            jax.ShapeDtypeStruct((tokens, cols), F32),
        ],
        compiler_params=params(),
        name="forward",
    )(place, x, halo, short_taps, skip, table, after)


def sum_by_lag(gram):
    wide = gram.shape[1]
    parts = [gram[i : i + 8] for i in range(0, gram.shape[0], 8)]
    step = 8
    while len(parts) > 1:
        parts = [
            parts[k] + pltpu.roll(parts[k + 1], wide - step, 1) for k in range(0, len(parts), 2)
        ]
        step *= 2
    total = parts[0]
    row = lax.broadcasted_iota(jnp.int32, total.shape, 0)
    for bit in (1, 2, 4):
        total = jnp.where((row & bit) != 0, pltpu.roll(total, wide - bit, 1), total)
    return jnp.sum(total[:, :LTAPS], axis=0, keepdims=True)


def backward_kernel(
    mo_ref, mr_ref, f_ref, filt_ref, x_ref, n_ref, taps_ref, skip_ref, tab_ref,
    grad_ref, short_ref, long_ref, db, fg, wide, left, right,
):
    blocks, _, rows, _ = x_ref.shape
    tokens = blocks * rows
    per = tab_ref.shape[0] // LTAPS
    count = tokens // LTAPS
    skip = skip_ref[...]
    lane_group = lax.broadcasted_iota(jnp.int32, (1, LANES), 1) // (LANES // per)
    gain = jnp.zeros((8, LANES), F32)
    for b in range(count):
        own = slice(b * LTAPS, (b + 1) * LTAPS)
        mixed_grad = mo_ref[own] + mr_ref[own].astype(F32)
        slope = mixed_grad * f_ref[0, own]
        db[own] = slope.astype(BF16)
        fg[0, own] = mixed_grad * filt_ref[own]
        fg[1, own] = skip * slope
        prod = f_ref[1, own] * f_ref[2, own]
        gain = gain + jnp.sum((prod * slope).reshape(LTAPS // 8, 8, LANES), axis=0)
        prod_b = prod.astype(BF16)
        for g in range(per):
            keep = (lane_group == g).astype(F32).astype(BF16)
            left[g * LTAPS : (g + 1) * LTAPS, b * LANES : (b + 1) * LANES] = prod_b * keep
    db[tokens : tokens + LTAPS + PAD] = n_ref[0 : LTAPS + PAD]
    db[tokens + LTAPS + PAD :] = jnp.zeros((LTAPS - PAD, LANES), BF16)
    for b in range(count):
        right[:, b * LANES : (b + 1) * LANES] = db[b * LTAPS : (b + 2) * LTAPS]
    for b in range(0, count, 2):
        wide[...] = jnp.dot(
            tab_ref[...], right[:, b * LANES : (b + 2) * LANES], preferred_element_type=F32
        )
        for n in range(2):
            own = slice((b + n) * LTAPS, (b + n + 1) * LTAPS)
            grad = pick_groups(wide, n, LTAPS, per) + fg[1, own]
            fg[1, own] = grad * f_ref[2, own]
            fg[2, own] = grad * f_ref[1, own]
    few = jnp.concatenate([tab_ref[g * LTAPS : g * LTAPS + PAD] for g in range(per)], axis=0)
    edge = jnp.dot(few, db[tokens : tokens + 2 * LTAPS], preferred_element_type=F32)
    begin = LTAPS + PAD
    grad = pick_groups(edge, 0, PAD, per) + skip * n_ref[0:PAD].astype(F32)
    fg[1, tokens : tokens + PAD] = grad * n_ref[begin + PAD : begin + 2 * PAD].astype(F32)
    fg[2, tokens : tokens + PAD] = grad * n_ref[begin : begin + PAD].astype(F32)
    fg[0, tokens : tokens + PAD] = n_ref[begin + 2 * PAD : begin + 3 * PAD].astype(F32)
    for i in range(3):
        sums = [jnp.zeros((8, LANES), F32) for _ in range(SHORT)]
        for b in range(count):
            low = b * LTAPS
            inputs = x_ref[b, i].astype(F32)
            total = None
            for j in range(SHORT):
                later = fg[i, low + j : low + j + LTAPS]
                term = taps_ref[i, j : j + 1] * later
                total = term if total is None else total + term
                sums[j] = sums[j] + jnp.sum((later * inputs).reshape(LTAPS // 8, 8, LANES), axis=0)
            grad_ref[b, i] = total.astype(BF16)
        for j in range(SHORT):
            short_ref[i, j : j + 1] = jnp.sum(sums[j], axis=0, keepdims=True)
        short_ref[i, SHORT : SHORT + 1] = jnp.sum(gain, axis=0, keepdims=True)
    wide[...] = lax.dot_general(left[...], right[...], (((1,), (1,)), ((), ())), preferred_element_type=F32)
    for g in range(per):
        gram = wide[g * LTAPS : (g + 1) * LTAPS]
        long_ref[g : g + 1] = sum_by_lag(gram)


def backward(mixed_own, mixed_rest, feats, filt, x, later, short_taps, skip, table, chunk, chunks):
    blocks, _, rows, cols = x.shape
    cols //= chunks
    tokens = blocks * rows
    tiles = cols // LANES
    first = chunk * tiles
    tab_rows = table.shape[0] * LANES // skip.shape[1]
    per = tab_rows // LTAPS
    tok = pl.BlockSpec((tokens, LANES), lambda c: (0, first + c))
    return pl.pallas_call(
        backward_kernel,
        grid=(tiles,),
        in_specs=[
            tok,
            tok,
            pl.BlockSpec((3, tokens, LANES), lambda c: (0, 0, c)),
            pl.BlockSpec((tokens, LANES), lambda c: (0, c)),
            pl.BlockSpec((blocks, 3, rows, LANES), lambda c: (0, 0, 0, first + c)),
            pl.BlockSpec((later.shape[0], LANES), lambda c: (0, first + c)),
            pl.BlockSpec((3, SHORT, LANES), lambda c: (0, 0, first + c)),
            pl.BlockSpec((1, LANES), lambda c: (0, first + c)),
            pl.BlockSpec((tab_rows, 2 * LTAPS), lambda c: (first + c, 0)),
        ],
        out_specs=[
            pl.BlockSpec((blocks, 3, rows, LANES), lambda c: (0, 0, 0, c)),
            pl.BlockSpec((3, SHORT + 1, LANES), lambda c: (0, 0, c)),
            pl.BlockSpec((per, LTAPS), lambda c: (c, 0)),
        ],
        out_shape=[
            jax.ShapeDtypeStruct((blocks, 3, rows, cols), BF16),
            jax.ShapeDtypeStruct((3, SHORT + 1, cols), F32),
            jax.ShapeDtypeStruct((tiles * per, LTAPS), F32),
        ],
        scratch_shapes=[
            pltpu.VMEM((tokens + 2 * LTAPS, LANES), BF16),
            pltpu.VMEM((3, tokens + PAD, LANES), F32),
            pltpu.VMEM((tab_rows, 2 * LTAPS), F32),
            pltpu.VMEM((tab_rows, tokens), BF16),
            pltpu.VMEM((2 * LTAPS, tokens), BF16),
        ],
        compiler_params=params(),
        cost_estimate=pl.CostEstimate(flops=10**11, bytes_accessed=36 * tokens * cols, transcendentals=0),
        name="backward",
    )(mixed_own, mixed_rest, feats, filt, x, later, short_taps, skip, table)


def pack_kernel(*refs):
    out_ref = refs[-1]
    for i, ref in enumerate(refs[:3]):
        out_ref[0, i] = ref[...]


def pack(arrays, seq):
    rows, width = arrays[0].shape
    cols = width // seq
    return pl.pallas_call(
        pack_kernel,
        grid=(seq,),
        in_specs=[pl.BlockSpec((rows, cols), lambda s: (0, s))] * 3,
        out_specs=pl.BlockSpec((1, 3, rows, cols), lambda s: (s, 0, 0, 0)),
        out_shape=jax.ShapeDtypeStruct((seq, 3, rows, cols), BF16),
        compiler_params=params(),
        name="pack",
    )(*arrays)


def unpack_kernel(*refs):
    parts, outs = refs[:-3], refs[-3:]
    cols = parts[0].shape[3]
    for n, part in enumerate(parts):
        for i, out in enumerate(outs):
            out[:, n * cols : (n + 1) * cols] = part[0, i]


def unpack(parts):
    seq, _, rows, cols = parts[0].shape
    wide = cols * len(parts)
    shape = jax.ShapeDtypeStruct((rows, seq * wide), BF16)
    return pl.pallas_call(
        unpack_kernel,
        grid=(seq,),
        in_specs=[pl.BlockSpec((1, 3, rows, cols), lambda s: (s, 0, 0, 0))] * len(parts),
        out_specs=[pl.BlockSpec((rows, wide), lambda s: (0, s))] * 3,
        out_shape=[shape] * 3,
        compiler_params=params(),
        name="unpack",
    )(*parts)


def along(block, axis, distance):
    size = lax.axis_size(axis)
    return lax.ppermute(block, axis, [(i, i + distance) for i in range(size) if 0 <= i + distance < size])


def around(block, axis, distance):
    size = lax.axis_size(axis)
    return lax.ppermute(block, axis, [(i, (i + distance) % size) for i in range(size)])


def across(block, axis, bit):
    return lax.ppermute(block, axis, [(i, i ^ bit) for i in range(lax.axis_size(axis))])


def bits_of(axis):
    size = lax.axis_size(axis)
    return [1 << n for n in range(size.bit_length() - 1)]


def sum_over(value, axes):
    for axis in axes:
        for bit in bits_of(axis):
            value = value + across(value, axis, bit)
    return value


def split_kernel(y_ref, *refs):
    count = (len(refs) - 1) // 2
    for n in range(count):
        refs[count + 1 + n][...] = refs[n][...]


def split_cotangent(cotangent, y, ys, col_part, after):
    rows, width = cotangent.shape

    def source(step):
        return pl.BlockSpec((rows, col_part), lambda z, y_ref: (0, z * ys + (y_ref[0] + step) % ys))

    return pl.pallas_call(
        split_kernel,
        grid_spec=pltpu.PrefetchScalarGridSpec(
            num_scalar_prefetch=1,
            grid=(Z,),
            in_specs=[source(step) for step in range(ys)] + [pl.BlockSpec(memory_space=pl.ANY)],
            out_specs=[pl.BlockSpec((rows, col_part), lambda z, _: (0, z))] * ys,
        ),
        out_shape=[jax.ShapeDtypeStruct((rows, width // ys), BF16)] * ys,
        compiler_params=params(),
        name="split",
    )(y.reshape(1), *([cotangent] * ys), after)


def join_kernel(axis, count, *refs):
    out = refs[-1]
    for n in range(count):
        size = refs[n].shape[axis]
        here = slice(n * size, (n + 1) * size)
        if axis == 0:
            out[here] = refs[n][...]
        else:
            out[:, here] = refs[n][...]


def join(parts, axis, after=()):
    shape = list(parts[0].shape)
    tile = shape[-1] // Z
    block = pl.BlockSpec((*shape[:-1], tile), lambda i: (0, 0, 0, i))
    shape[axis] *= len(parts)
    return pl.pallas_call(
        functools.partial(join_kernel, axis, len(parts)),
        grid=(Z,),
        in_specs=[block] * len(parts) + [pl.BlockSpec(memory_space=pl.ANY)] * len(after),
        out_specs=pl.BlockSpec((*shape[:-1], tile), lambda i: (0, 0, 0, i)),
        out_shape=jax.ShapeDtypeStruct(tuple(shape), BF16),
        compiler_params=params(),
        name="join",
    )(*parts, *after)


def own_cotangent(cotangent, col_part, after):
    ys, y = lax.axis_size("y"), lax.axis_index("y")
    held = split_cotangent(cotangent, y, ys, col_part, after)
    held = [around(part, "y", step) if step else part for step, part in enumerate(held)]
    return join([part[None, None] for part in held], 0)


def gather_cotangent(held, after):
    bits = bits_of("seq")
    for bit in reversed(bits[1:]):
        held = join([held, across(held, "seq", bit)], 1, after)
    return held, across(held, "seq", bits[0])


def mixed_grad_kernel(waits, place_ref, a_ref, b_ref, w_ref, *refs):
    out_ref, head_ref = refs[waits : waits + 2]
    found = refs[-1]
    _, count, rows, _ = a_ref.shape
    tokens = count * rows
    pieces = jnp.concatenate([ref[...].reshape(tokens, -1) for ref in (a_ref, b_ref)], axis=0)
    found[...] = contract(pieces, w_ref[...], 1)
    for block in range(2 * count):
        there = pl.multiple_of(place_ref[block] * rows, rows)
        out_ref[block * rows : (block + 1) * rows] = found[pl.ds(there, rows)].astype(out_ref.dtype)
    head_ref[...] = out_ref[0 : LTAPS + PAD]


def mixed_grad(cots, weights, place, step, dtype, after, passed=False):
    _, count, rows, width = cots[0].shape
    tokens = 2 * count * rows
    cols = weights.shape[0]
    tile = min(cols, 2 * LANES)
    piece = pl.BlockSpec((1, count, rows, width), lambda i, _: (step, 0, 0, 0))
    return pl.pallas_call(
        functools.partial(mixed_grad_kernel, len(after)),
        grid_spec=pltpu.PrefetchScalarGridSpec(
            num_scalar_prefetch=1,
            grid=(cols // tile,),
            in_specs=[
                piece,
                piece,
                pl.BlockSpec((tile, width), lambda i, _: (i, 0)),
            ]
            + [pl.BlockSpec(memory_space=pl.ANY)] * len(after),
            out_specs=[
                pl.BlockSpec((tokens, tile), lambda i, _: (0, i)),
                pl.BlockSpec((LTAPS + PAD, tile), lambda i, _: (0, i)),
            ]
            + [pl.BlockSpec(memory_space=pl.ANY)] * passed,
            scratch_shapes=[pltpu.VMEM((tokens, tile), F32)],
        ),
        input_output_aliases={4: 2} if passed else {},
        out_shape=[
            jax.ShapeDtypeStruct((tokens, cols), dtype),
            jax.ShapeDtypeStruct((LTAPS + PAD, cols), dtype),
        ]
        + [jax.ShapeDtypeStruct(after[0].shape, after[0].dtype)] * passed,
        compiler_params=params(),
        name="mixed_grad",
    )(place, *cots, weights, *after)


def weight_grad_kernel(scale, a_ref, b_ref, *refs):
    steps, count, rows, tile = a_ref.shape
    tokens = count * rows
    mixed, out = refs[:steps], refs[-1]
    total = None
    for step in range(steps):
        for n, ref in enumerate((a_ref, b_ref)):
            left = mixed[step][:, n * tokens : (n + 1) * tokens]
            term = jnp.dot(left, ref[step].reshape(tokens, tile), preferred_element_type=F32)
            total = term if total is None else total + term
    out[...] = (total * scale).astype(BF16)


def weight_grad(cots, mixed, chunk, chunks, scale, target, after):
    steps, count, rows, width = cots[0].shape
    part, tokens = mixed[0].shape
    tile = width // Z
    piece = pl.BlockSpec((steps, count, rows, tile), lambda i: (0, 0, 0, i))
    extra = [*after] + ([] if target is None else [target])
    return pl.pallas_call(
        functools.partial(weight_grad_kernel, scale),
        grid=(Z,),
        in_specs=[piece, piece]
        + [pl.BlockSpec((part, tokens), lambda i: (0, 0))] * len(mixed)
        + [pl.BlockSpec(memory_space=pl.ANY)] * len(extra),
        out_specs=pl.BlockSpec((part, tile), lambda i: (chunk, i)),
        out_shape=jax.ShapeDtypeStruct((part * chunks, width), BF16),
        input_output_aliases={} if target is None else {2 + len(mixed) + len(after): 0},
        compiler_params=params(),
        name="weight_grad",
    )(*cots, *mixed, *extra)


def tail_kernel(x_ref, before_ref, taps_ref, *refs):
    out_ref, xf = refs[-2:]
    rows = x_ref.shape[2]
    for i in range(3):
        out_ref[i * PAD : (i + 1) * PAD] = x_ref[0, i, rows - PAD :]
    for tile in range(x_ref.shape[3] // LANES):
        cols = slice(tile * LANES, (tile + 1) * LANES)
        taps = taps_ref[:, :, cols]
        prod = None
        for i in (1, 2):
            xf[tile, i - 1, 0:PAD] = before_ref[0, i, :, cols].astype(F32)
            xf[tile, i - 1, PAD:] = x_ref[0, i, :, cols].astype(F32)
            feature = taps[i, 0:1] * xf[tile, i - 1, PAD : PAD + rows]
            for j in range(1, SHORT):
                feature = feature + taps[i, j : j + 1] * xf[tile, i - 1, PAD - j : PAD - j + rows]
            prod = feature if prod is None else prod * feature
        out_ref[3 * PAD :, cols] = prod.astype(BF16)


def tail_of(x, short_taps, after):
    seq, _, rows, cols = x.shape
    wide = min(cols, 4 * LANES)
    out_rows = 3 * PAD + rows
    return pl.pallas_call(
        tail_kernel,
        grid=(cols // wide,),
        in_specs=[
            pl.BlockSpec((1, 3, rows, wide), lambda c: (seq - 1, 0, 0, c)),
            pl.BlockSpec((1, 3, PAD, wide), lambda c: (seq - 2, 0, rows // PAD - 1, c)),
            pl.BlockSpec((3, SHORT, wide), lambda c: (0, 0, c)),
        ]
        + [pl.BlockSpec(memory_space=pl.ANY)] * len(after),
        out_specs=pl.BlockSpec((out_rows, wide), lambda c: (0, c)),
        out_shape=jax.ShapeDtypeStruct((out_rows, cols), BF16),
        scratch_shapes=[pltpu.VMEM((wide // LANES, 2, PAD + rows, LANES), F32)],
        compiler_params=params(),
        name="tail",
    )(x, x, short_taps, *after)


def head_kernel(chunks, mo_ref, mr_ref, *refs):
    out_ref = refs[-1]
    edge = LTAPS + PAD
    part = out_ref.shape[1] // chunks
    for h in range(chunks):
        own = slice(h * part, (h + 1) * part)
        f_ref, filt_ref = refs[2 * h : 2 * h + 2]
        mixed = mo_ref[:, own] + mr_ref[:, own].astype(F32)
        out_ref[0:edge, own] = (mixed * f_ref[0]).astype(BF16)
        out_ref[edge : edge + PAD, own] = f_ref[1, 0:PAD].astype(BF16)
        out_ref[edge + PAD : edge + 2 * PAD, own] = f_ref[2, 0:PAD].astype(BF16)
        out_ref[edge + 2 * PAD :, own] = (mixed[0:PAD] * filt_ref[0:PAD]).astype(BF16)


def head_of(mixed_own, mixed_rest, mixers, after):
    edge, cols = LTAPS + PAD, mixed_own.shape[1]
    part = cols // len(mixers)
    whole = pl.BlockSpec((edge, cols), lambda i: (0, 0))
    feat_specs = [
        pl.BlockSpec((3, edge, part), lambda i: (0, 0, 0)),
        pl.BlockSpec((edge, part), lambda i: (0, 0)),
    ]
    return pl.pallas_call(
        functools.partial(head_kernel, len(mixers)),
        grid=(1,),
        in_specs=[whole, whole] + feat_specs * len(mixers) + [pl.BlockSpec(memory_space=pl.ANY)] * len(after),
        out_specs=pl.BlockSpec((edge + 3 * PAD, cols), lambda i: (0, 0)),
        out_shape=jax.ShapeDtypeStruct((edge + 3 * PAD, cols), BF16),
        compiler_params=params(),
        name="head",
    )(mixed_own, mixed_rest, *[array for mixer in mixers for array in mixer[1:]], *after)


def contract(a, b, dim):
    return lax.dot_general(a, b, (((dim,), (dim,)), ((), ())), preferred_element_type=F32)


def places(seq):
    bits = bits_of("seq")
    source = lax.iota(jnp.int32, seq) ^ lax.axis_index("seq")
    return sum(((source >> n) & 1) << (len(bits) - 1 - n) for n in range(len(bits)))


def body(queries, keys, values, cotangent, out_weight, short_taps, long_taps, skip_gain):
    rows, width = queries.shape
    col_part = out_weight.shape[1]
    seq, ys = lax.axis_size("seq"), lax.axis_size("y")
    cols = width // seq
    chunks = 2 if cols % (2 * LANES) == 0 else 1
    groups = long_taps.shape[1]
    fsdp = ("z", "y")
    grad_scale = float(rows * seq * ys * Z) ** (-0.5)

    weights = lax.all_gather(out_weight, "z", axis=1, tiled=True)
    fwd_table, bwd_table = make_tables(long_taps)
    skip = skip_gain.reshape(1, cols)
    place = places(seq)
    by_owner = pack((queries, keys, values), seq)
    x = lax.all_to_all(by_owner, "seq", split_axis=0, concat_axis=0, tiled=True)
    held = own_cotangent(cotangent, col_part, by_owner)
    tail = tail_of(x, short_taps, [fwd_table, held])
    halo = along(tail, fsdp, 1)
    cots = gather_cotangent(held, [halo])
    mixers = []
    for h in range(chunks):
        after = mixers[-1][0] if mixers else cots[0]
        mixers.append(forward(x, halo, short_taps, skip, fwd_table, place, h, chunks, after))

    mixed_all = [
        [around(mixed, "y", step) if step else mixed for step in range(ys)] for mixed, _, _ in mixers
    ]

    parts, heads = [], []
    for step in range(1, ys):
        part, head = mixed_grad(cots, weights, place, step, BF16, [parts[-1] if parts else mixers[-1][0]])
        parts.append(part)
        heads.append(around(head, "y", -step))
    mixed_own, own_head, parts[-1] = mixed_grad(
        cots, weights, place, 0, F32, [parts[-1], *mixed_all[0][1:]], True
    )
    rest = [around(parts[step - 1], "y", -step) for step in range(1, ys)]
    mixed_rest = rest[0] if len(rest) == 1 else sum(piece.astype(F32) for piece in rest)
    head_rest = heads[0] if len(heads) == 1 else sum(piece.astype(F32) for piece in heads)
    head = head_of(own_head, head_rest, mixers, mixed_all[-1][1:])
    later = along(head, fsdp, -1)

    weight_sum = None
    for h in range(chunks):
        after = [later] if h == chunks - 1 else [head]
        weight_sum = weight_grad(cots, mixed_all[h], h, chunks, grad_scale, weight_sum, after)
    weight_part = lax.psum_scatter(weight_sum, "z", scatter_dimension=1, tiled=True)

    grads, short_parts, long_parts = [], [], []
    for h in range(chunks):
        _, feats, filt = mixers[h]
        grad, short_part, long_part = backward(
            mixed_own, mixed_rest, feats, filt, x, later, short_taps, skip, bwd_table, h, chunks
        )
        grads.append(lax.all_to_all(grad, "seq", split_axis=0, concat_axis=0, tiled=True))
        short_parts.append(short_part)
        long_parts.append(long_part)

    query_grad, key_grad, value_grad = unpack(grads)
    packed = jnp.concatenate(
        [
            jnp.concatenate(short_parts, axis=2).reshape(3 * (SHORT + 1), cols),
            jnp.concatenate(long_parts, axis=0).reshape(-1, cols),
        ],
        axis=0,
    )
    packed = sum_over(packed, ("y", "z")) * grad_scale
    short_sum = packed[: 3 * (SHORT + 1)].reshape(3, SHORT + 1, cols)
    long_sum = packed[3 * (SHORT + 1) :].reshape(groups, LTAPS).T
    return (
        query_grad,
        key_grad,
        value_grad,
        weight_part.astype(F32),
        short_sum[:, :SHORT],
        long_sum,
        short_sum[0, SHORT],
    )


def solution(mesh):
    fsdp, seq = mesh.shape["fsdp"], mesh.shape["seq"]
    split = Mesh(mesh.devices.reshape(Z, fsdp // Z, seq), ("z", "y", "seq"))
    tokens = P(("z", "y", "seq"), None)
    specs = (P("seq", ("z", "y")), P(None, None, "seq"), P(None, "seq"), P("seq"))
    return jax.shard_map(
        body,
        mesh=split,
        in_specs=(tokens,) * 4 + specs,
        out_specs=(tokens,) * 3 + specs,
        check_vma=False,
    )
```

```python
import functools

import jax
import jax.numpy as jnp
from jax import lax
from jax.experimental import pallas as pl
from jax.experimental.pallas import tpu as pltpu
from jax.sharding import Mesh
from jax.sharding import PartitionSpec as P

SHORT = 7
LTAPS = 128
LANES = 128
PAD = 16
Z = 4
F32 = jnp.float32
BF16 = jnp.bfloat16


def params():
    return pltpu.CompilerParams(vmem_limit_bytes=60 * 2**20)


def tables_kernel(fwd_ref, bwd_ref, tf_ref, tb_ref):
    for g in range(fwd_ref.shape[0]):
        rows = slice(g * LTAPS, (g + 1) * LTAPS)
        for src, dst in ((fwd_ref, tf_ref), (bwd_ref, tb_ref)):
            wide = jnp.broadcast_to(src[g : g + 1, :], (LTAPS, 2 * LTAPS))
            dst[rows, :] = pltpu.roll(wide, 0, 1, stride=1, stride_axis=0).astype(BF16)


def make_tables(long_taps):
    by_group = long_taps.T
    groups = by_group.shape[0]
    fwd = jnp.pad(by_group[:, ::-1], ((0, 0), (1, LTAPS - 1)))
    bwd = jnp.pad(by_group, ((0, 0), (0, LTAPS)))
    per = 8
    row_spec = pl.BlockSpec((per, 2 * LTAPS), lambda i: (i, 0))
    tab_spec = pl.BlockSpec((per * LTAPS, 2 * LTAPS), lambda i: (i, 0))
    shape = jax.ShapeDtypeStruct((groups * LTAPS, 2 * LTAPS), BF16)
    return pl.pallas_call(
        tables_kernel,
        grid=(groups // per,),
        in_specs=[row_spec, row_spec],
        out_specs=[tab_spec, tab_spec],
        out_shape=[shape, shape],
        compiler_params=params(),
        name="tables",
    )(fwd, bwd)


def pick_groups(wide, col, rows, per):
    lane_group = lax.broadcasted_iota(jnp.int32, (rows, LANES), 1) // (LANES // per)
    cols = slice(col * LANES, (col + 1) * LANES)
    out = wide[0:rows, cols]
    for g in range(1, per):
        out = jnp.where(lane_group == g, wide[g * rows : (g + 1) * rows, cols], out)
    return out


def features_of(taps_ref, row, xf, i, begin):
    total = taps_ref[row, 0:1] * xf[i, PAD + begin : PAD + begin + LTAPS]
    for j in range(1, SHORT):
        total = total + taps_ref[row, j : j + 1] * xf[i, PAD + begin - j : PAD + begin - j + LTAPS]
    return total


def forward_kernel(
    place_ref, x_ref, h_ref, taps_ref, skip_ref, tab_ref, _, mixed_ref, f_ref, filt_ref, xf, pf, pb, wide
):
    blocks, _, rows, _ = x_ref.shape
    tokens = blocks * rows
    per = tab_ref.shape[0] // LTAPS
    for i in range(3):
        xf[i, 0:PAD] = h_ref[i * PAD : (i + 1) * PAD].astype(F32)
        for b in range(blocks):
            begin = PAD + b * rows
            xf[i, begin : begin + rows] = x_ref[b, i].astype(F32)
    pb[0:LTAPS] = h_ref[3 * PAD : 3 * PAD + LTAPS]
    for begin in range(0, tokens, LTAPS):
        own = slice(begin, begin + LTAPS)
        f1 = features_of(taps_ref, 1, xf, 1, begin)
        f2 = features_of(taps_ref, 2, xf, 2, begin)
        prod = f1 * f2
        f_ref[1, own] = f1
        f_ref[2, own] = f2
        f_ref[0, own] = features_of(taps_ref, 0, xf, 0, begin)
        pf[own] = prod
        pb[LTAPS + begin : 2 * LTAPS + begin] = prod.astype(BF16)
    skip = skip_ref[...]
    for b in range(0, tokens // LTAPS, 2):
        low = b * LTAPS
        windows = jnp.concatenate([pb[low : low + 2 * LTAPS], pb[low + LTAPS : low + 3 * LTAPS]], axis=1)
        wide[...] = jnp.dot(tab_ref[...], windows, preferred_element_type=F32)
        for n in range(2):
            own = slice(low + n * LTAPS, low + (n + 1) * LTAPS)
            filtered = pick_groups(wide, n, LTAPS, per) + skip * pf[own]
            filt_ref[own] = filtered
            mixed = f_ref[0, own] * filtered
            there = pl.multiple_of(place_ref[b + n] * LTAPS, LTAPS)
            mixed_ref[:, pl.ds(there, LTAPS)] = mixed.T.astype(BF16)


def forward(x, halo, short_taps, skip, table, place, chunk, chunks, after):
    blocks, _, rows, cols = x.shape
    cols //= chunks
    tokens = blocks * rows
    tiles = cols // LANES
    first = chunk * tiles
    tab_rows = table.shape[0] * LANES // skip.shape[1]
    return pl.pallas_call(
        forward_kernel,
        grid_spec=pltpu.PrefetchScalarGridSpec(
            num_scalar_prefetch=1,
            grid=(tiles,),
            in_specs=[
                pl.BlockSpec((blocks, 3, rows, LANES), lambda c, _: (0, 0, 0, first + c)),
                pl.BlockSpec((halo.shape[0], LANES), lambda c, _: (0, first + c)),
                pl.BlockSpec((3, SHORT, LANES), lambda c, _: (0, 0, first + c)),
                pl.BlockSpec((1, LANES), lambda c, _: (0, first + c)),
                pl.BlockSpec((tab_rows, 2 * LTAPS), lambda c, _: (first + c, 0)),
                pl.BlockSpec(memory_space=pl.ANY),
            ],
            out_specs=[
                pl.BlockSpec((LANES, tokens), lambda c, _: (c, 0)),
                pl.BlockSpec((3, tokens, LANES), lambda c, _: (0, 0, c)),
                pl.BlockSpec((tokens, LANES), lambda c, _: (0, c)),
            ],
            scratch_shapes=[
                pltpu.VMEM((3, PAD + tokens, LANES), F32),
                pltpu.VMEM((tokens, LANES), F32),
                pltpu.VMEM((LTAPS + tokens, LANES), BF16),
                pltpu.VMEM((tab_rows, 2 * LTAPS), F32),
            ],
        ),
        out_shape=[
            jax.ShapeDtypeStruct((cols, tokens), BF16),
            jax.ShapeDtypeStruct((3, tokens, cols), F32),
            jax.ShapeDtypeStruct((tokens, cols), F32),
        ],
        compiler_params=params(),
        name="forward",
    )(place, x, halo, short_taps, skip, table, after)


def sum_by_lag(gram):
    wide = gram.shape[1]
    parts = [gram[i : i + 8] for i in range(0, gram.shape[0], 8)]
    step = 8
    while len(parts) > 1:
        parts = [
            parts[k] + pltpu.roll(parts[k + 1], wide - step, 1) for k in range(0, len(parts), 2)
        ]
        step *= 2
    total = parts[0]
    row = lax.broadcasted_iota(jnp.int32, total.shape, 0)
    for bit in (1, 2, 4):
        total = jnp.where((row & bit) != 0, pltpu.roll(total, wide - bit, 1), total)
    return jnp.sum(total[:, :LTAPS], axis=0, keepdims=True)


def backward_kernel(
    mo_ref, mr_ref, f_ref, filt_ref, x_ref, n_ref, taps_ref, skip_ref, tab_ref,
    grad_ref, short_ref, long_ref, db, fg, wide, left, right,
):
    blocks, _, rows, _ = x_ref.shape
    tokens = blocks * rows
    per = tab_ref.shape[0] // LTAPS
    count = tokens // LTAPS
    skip = skip_ref[...]
    lane_group = lax.broadcasted_iota(jnp.int32, (1, LANES), 1) // (LANES // per)
    gain = jnp.zeros((8, LANES), F32)
    for b in range(count):
        own = slice(b * LTAPS, (b + 1) * LTAPS)
        mixed_grad = mo_ref[own] + mr_ref[own].astype(F32)
        slope = mixed_grad * f_ref[0, own]
        db[own] = slope.astype(BF16)
        fg[0, own] = mixed_grad * filt_ref[own]
        fg[1, own] = skip * slope
        prod = f_ref[1, own] * f_ref[2, own]
        gain = gain + jnp.sum((prod * slope).reshape(LTAPS // 8, 8, LANES), axis=0)
        prod_b = prod.astype(BF16)
        for g in range(per):
            keep = (lane_group == g).astype(F32).astype(BF16)
            left[g * LTAPS : (g + 1) * LTAPS, b * LANES : (b + 1) * LANES] = prod_b * keep
    db[tokens : tokens + LTAPS + PAD] = n_ref[0 : LTAPS + PAD]
    db[tokens + LTAPS + PAD :] = jnp.zeros((LTAPS - PAD, LANES), BF16)
    for b in range(count):
        right[:, b * LANES : (b + 1) * LANES] = db[b * LTAPS : (b + 2) * LTAPS]
    for b in range(0, count, 2):
        wide[...] = jnp.dot(
            tab_ref[...], right[:, b * LANES : (b + 2) * LANES], preferred_element_type=F32
        )
        for n in range(2):
            own = slice((b + n) * LTAPS, (b + n + 1) * LTAPS)
            grad = pick_groups(wide, n, LTAPS, per) + fg[1, own]
            fg[1, own] = grad * f_ref[2, own]
            fg[2, own] = grad * f_ref[1, own]
    few = jnp.concatenate([tab_ref[g * LTAPS : g * LTAPS + PAD] for g in range(per)], axis=0)
    edge = jnp.dot(few, db[tokens : tokens + 2 * LTAPS], preferred_element_type=F32)
    begin = LTAPS + PAD
    grad = pick_groups(edge, 0, PAD, per) + skip * n_ref[0:PAD].astype(F32)
    fg[1, tokens : tokens + PAD] = grad * n_ref[begin + PAD : begin + 2 * PAD].astype(F32)
    fg[2, tokens : tokens + PAD] = grad * n_ref[begin : begin + PAD].astype(F32)
    fg[0, tokens : tokens + PAD] = n_ref[begin + 2 * PAD : begin + 3 * PAD].astype(F32)
    for i in range(3):
        sums = [jnp.zeros((8, LANES), F32) for _ in range(SHORT)]
        for b in range(count):
            low = b * LTAPS
            inputs = x_ref[b, i].astype(F32)
            total = None
            for j in range(SHORT):
                later = fg[i, low + j : low + j + LTAPS]
                term = taps_ref[i, j : j + 1] * later
                total = term if total is None else total + term
                sums[j] = sums[j] + jnp.sum((later * inputs).reshape(LTAPS // 8, 8, LANES), axis=0)
            grad_ref[b, i] = total.astype(BF16)
        for j in range(SHORT):
            short_ref[i, j : j + 1] = jnp.sum(sums[j], axis=0, keepdims=True)
        short_ref[i, SHORT : SHORT + 1] = jnp.sum(gain, axis=0, keepdims=True)
    wide[...] = lax.dot_general(left[...], right[...], (((1,), (1,)), ((), ())), preferred_element_type=F32)
    for g in range(per):
        gram = wide[g * LTAPS : (g + 1) * LTAPS]
        long_ref[g : g + 1] = sum_by_lag(gram)


def backward(mixed_own, mixed_rest, feats, filt, x, later, short_taps, skip, table, chunk, chunks):
    blocks, _, rows, cols = x.shape
    cols //= chunks
    tokens = blocks * rows
    tiles = cols // LANES
    first = chunk * tiles
    tab_rows = table.shape[0] * LANES // skip.shape[1]
    per = tab_rows // LTAPS
    tok = pl.BlockSpec((tokens, LANES), lambda c: (0, first + c))
    return pl.pallas_call(
        backward_kernel,
        grid=(tiles,),
        in_specs=[
            tok,
            tok,
            pl.BlockSpec((3, tokens, LANES), lambda c: (0, 0, c)),
            pl.BlockSpec((tokens, LANES), lambda c: (0, c)),
            pl.BlockSpec((blocks, 3, rows, LANES), lambda c: (0, 0, 0, first + c)),
            pl.BlockSpec((later.shape[0], LANES), lambda c: (0, first + c)),
            pl.BlockSpec((3, SHORT, LANES), lambda c: (0, 0, first + c)),
            pl.BlockSpec((1, LANES), lambda c: (0, first + c)),
            pl.BlockSpec((tab_rows, 2 * LTAPS), lambda c: (first + c, 0)),
        ],
        out_specs=[
            pl.BlockSpec((blocks, 3, rows, LANES), lambda c: (0, 0, 0, c)),
            pl.BlockSpec((3, SHORT + 1, LANES), lambda c: (0, 0, c)),
            pl.BlockSpec((per, LTAPS), lambda c: (c, 0)),
        ],
        out_shape=[
            jax.ShapeDtypeStruct((blocks, 3, rows, cols), BF16),
            jax.ShapeDtypeStruct((3, SHORT + 1, cols), F32),
            jax.ShapeDtypeStruct((tiles * per, LTAPS), F32),
        ],
        scratch_shapes=[
            pltpu.VMEM((tokens + 2 * LTAPS, LANES), BF16),
            pltpu.VMEM((3, tokens + PAD, LANES), F32),
            pltpu.VMEM((tab_rows, 2 * LTAPS), F32),
            pltpu.VMEM((tab_rows, tokens), BF16),
            pltpu.VMEM((2 * LTAPS, tokens), BF16),
        ],
        compiler_params=params(),
        cost_estimate=pl.CostEstimate(flops=10**11, bytes_accessed=36 * tokens * cols, transcendentals=0),
        name="backward",
    )(mixed_own, mixed_rest, feats, filt, x, later, short_taps, skip, table)


def pack_kernel(*refs):
    out_ref = refs[-1]
    for i, ref in enumerate(refs[:3]):
        out_ref[0, i] = ref[...]


def pack(arrays, seq):
    rows, width = arrays[0].shape
    cols = width // seq
    return pl.pallas_call(
        pack_kernel,
        grid=(seq,),
        in_specs=[pl.BlockSpec((rows, cols), lambda s: (0, s))] * 3,
        out_specs=pl.BlockSpec((1, 3, rows, cols), lambda s: (s, 0, 0, 0)),
        out_shape=jax.ShapeDtypeStruct((seq, 3, rows, cols), BF16),
        compiler_params=params(),
        name="pack",
    )(*arrays)


def unpack_kernel(*refs):
    parts, outs = refs[:-3], refs[-3:]
    cols = parts[0].shape[3]
    for n, part in enumerate(parts):
        for i, out in enumerate(outs):
            out[:, n * cols : (n + 1) * cols] = part[0, i]


def unpack(parts):
    seq, _, rows, cols = parts[0].shape
    wide = cols * len(parts)
    shape = jax.ShapeDtypeStruct((rows, seq * wide), BF16)
    return pl.pallas_call(
        unpack_kernel,
        grid=(seq,),
        in_specs=[pl.BlockSpec((1, 3, rows, cols), lambda s: (s, 0, 0, 0))] * len(parts),
        out_specs=[pl.BlockSpec((rows, wide), lambda s: (0, s))] * 3,
        out_shape=[shape] * 3,
        compiler_params=params(),
        name="unpack",
    )(*parts)


def along(block, axis, distance):
    size = lax.axis_size(axis)
    return lax.ppermute(block, axis, [(i, i + distance) for i in range(size) if 0 <= i + distance < size])


def around(block, axis, distance):
    size = lax.axis_size(axis)
    return lax.ppermute(block, axis, [(i, (i + distance) % size) for i in range(size)])


def across(block, axis, bit):
    return lax.ppermute(block, axis, [(i, i ^ bit) for i in range(lax.axis_size(axis))])


def bits_of(axis):
    size = lax.axis_size(axis)
    return [1 << n for n in range(size.bit_length() - 1)]


def sum_over(value, axes):
    for axis in axes:
        for bit in bits_of(axis):
            value = value + across(value, axis, bit)
    return value


def split_kernel(y_ref, *refs):
    count = (len(refs) - 1) // 2
    for n in range(count):
        refs[count + 1 + n][...] = refs[n][...]


def split_cotangent(cotangent, y, ys, col_part, after):
    rows, width = cotangent.shape

    def source(step):
        return pl.BlockSpec((rows, col_part), lambda z, y_ref: (0, z * ys + (y_ref[0] + step) % ys))

    return pl.pallas_call(
        split_kernel,
        grid_spec=pltpu.PrefetchScalarGridSpec(
            num_scalar_prefetch=1,
            grid=(Z,),
            in_specs=[source(step) for step in range(ys)] + [pl.BlockSpec(memory_space=pl.ANY)],
            out_specs=[pl.BlockSpec((rows, col_part), lambda z, _: (0, z))] * ys,
        ),
        out_shape=[jax.ShapeDtypeStruct((rows, width // ys), BF16)] * ys,
        compiler_params=params(),
        name="split",
    )(y.reshape(1), *([cotangent] * ys), after)


def join_kernel(axis, count, *refs):
    out = refs[-1]
    for n in range(count):
        size = refs[n].shape[axis]
        here = slice(n * size, (n + 1) * size)
        if axis == 0:
            out[here] = refs[n][...]
        else:
            out[:, here] = refs[n][...]


def join(parts, axis, after=()):
    shape = list(parts[0].shape)
    tile = shape[-1] // Z
    block = pl.BlockSpec((*shape[:-1], tile), lambda i: (0, 0, 0, i))
    shape[axis] *= len(parts)
    return pl.pallas_call(
        functools.partial(join_kernel, axis, len(parts)),
        grid=(Z,),
        in_specs=[block] * len(parts) + [pl.BlockSpec(memory_space=pl.ANY)] * len(after),
        out_specs=pl.BlockSpec((*shape[:-1], tile), lambda i: (0, 0, 0, i)),
        out_shape=jax.ShapeDtypeStruct(tuple(shape), BF16),
        compiler_params=params(),
        name="join",
    )(*parts, *after)


def own_cotangent(cotangent, col_part, after):
    ys, y = lax.axis_size("y"), lax.axis_index("y")
    held = split_cotangent(cotangent, y, ys, col_part, after)
    held = [around(part, "y", step) if step else part for step, part in enumerate(held)]
    return join([part[None, None] for part in held], 0)


def gather_cotangent(held, after):
    bits = bits_of("seq")
    for bit in reversed(bits[1:]):
        held = join([held, across(held, "seq", bit)], 1, after)
    return held, across(held, "seq", bits[0])


def mixed_grad_kernel(waits, place_ref, a_ref, b_ref, w_ref, *refs):
    out_ref, head_ref = refs[waits : waits + 2]
    found = refs[-1]
    _, count, rows, _ = a_ref.shape
    tokens = count * rows
    pieces = jnp.concatenate([ref[...].reshape(tokens, -1) for ref in (a_ref, b_ref)], axis=0)
    found[...] = contract(pieces, w_ref[...], 1)
    for block in range(2 * count):
        there = pl.multiple_of(place_ref[block] * rows, rows)
        out_ref[block * rows : (block + 1) * rows] = found[pl.ds(there, rows)].astype(out_ref.dtype)
    head_ref[...] = out_ref[0 : LTAPS + PAD]


def mixed_grad(cots, weights, place, step, dtype, after, passed=False):
    _, count, rows, width = cots[0].shape
    tokens = 2 * count * rows
    cols = weights.shape[0]
    tile = min(cols, 2 * LANES)
    piece = pl.BlockSpec((1, count, rows, width), lambda i, _: (step, 0, 0, 0))
    return pl.pallas_call(
        functools.partial(mixed_grad_kernel, len(after)),
        grid_spec=pltpu.PrefetchScalarGridSpec(
            num_scalar_prefetch=1,
            grid=(cols // tile,),
            in_specs=[
                piece,
                piece,
                pl.BlockSpec((tile, width), lambda i, _: (i, 0)),
            ]
            + [pl.BlockSpec(memory_space=pl.ANY)] * len(after),
            out_specs=[
                pl.BlockSpec((tokens, tile), lambda i, _: (0, i)),
                pl.BlockSpec((LTAPS + PAD, tile), lambda i, _: (0, i)),
            ]
            + [pl.BlockSpec(memory_space=pl.ANY)] * passed,
            scratch_shapes=[pltpu.VMEM((tokens, tile), F32)],
        ),
        input_output_aliases={4: 2} if passed else {},
        out_shape=[
            jax.ShapeDtypeStruct((tokens, cols), dtype),
            jax.ShapeDtypeStruct((LTAPS + PAD, cols), dtype),
        ]
        + [jax.ShapeDtypeStruct(after[0].shape, after[0].dtype)] * passed,
        compiler_params=params(),
        name="mixed_grad",
    )(place, *cots, weights, *after)


def weight_grad_kernel(scale, a_ref, b_ref, *refs):
    steps, count, rows, tile = a_ref.shape
    tokens = count * rows
    mixed, out = refs[:steps], refs[-1]
    total = None
    for step in range(steps):
        for n, ref in enumerate((a_ref, b_ref)):
            left = mixed[step][:, n * tokens : (n + 1) * tokens]
            term = jnp.dot(left, ref[step].reshape(tokens, tile), preferred_element_type=F32)
            total = term if total is None else total + term
    out[...] = (total * scale).astype(BF16)


def weight_grad(cots, mixed, chunk, chunks, scale, target, after):
    steps, count, rows, width = cots[0].shape
    part, tokens = mixed[0].shape
    tile = width // Z
    piece = pl.BlockSpec((steps, count, rows, tile), lambda i: (0, 0, 0, i))
    extra = [*after] + ([] if target is None else [target])
    return pl.pallas_call(
        functools.partial(weight_grad_kernel, scale),
        grid=(Z,),
        in_specs=[piece, piece]
        + [pl.BlockSpec((part, tokens), lambda i: (0, 0))] * len(mixed)
        + [pl.BlockSpec(memory_space=pl.ANY)] * len(extra),
        out_specs=pl.BlockSpec((part, tile), lambda i: (chunk, i)),
        out_shape=jax.ShapeDtypeStruct((part * chunks, width), BF16),
        input_output_aliases={} if target is None else {2 + len(mixed) + len(after): 0},
        compiler_params=params(),
        name="weight_grad",
    )(*cots, *mixed, *extra)


def tail_kernel(x_ref, before_ref, taps_ref, *refs):
    out_ref, xf = refs[-2:]
    rows = x_ref.shape[2]
    for i in range(3):
        out_ref[i * PAD : (i + 1) * PAD] = x_ref[0, i, rows - PAD :]
    for tile in range(x_ref.shape[3] // LANES):
        cols = slice(tile * LANES, (tile + 1) * LANES)
        taps = taps_ref[:, :, cols]
        prod = None
        for i in (1, 2):
            xf[tile, i - 1, 0:PAD] = before_ref[0, i, :, cols].astype(F32)
            xf[tile, i - 1, PAD:] = x_ref[0, i, :, cols].astype(F32)
            feature = taps[i, 0:1] * xf[tile, i - 1, PAD : PAD + rows]
            for j in range(1, SHORT):
                feature = feature + taps[i, j : j + 1] * xf[tile, i - 1, PAD - j : PAD - j + rows]
            prod = feature if prod is None else prod * feature
        out_ref[3 * PAD :, cols] = prod.astype(BF16)


def tail_of(x, short_taps, after):
    seq, _, rows, cols = x.shape
    wide = min(cols, 4 * LANES)
    out_rows = 3 * PAD + rows
    return pl.pallas_call(
        tail_kernel,
        grid=(cols // wide,),
        in_specs=[
            pl.BlockSpec((1, 3, rows, wide), lambda c: (seq - 1, 0, 0, c)),
            pl.BlockSpec((1, 3, PAD, wide), lambda c: (seq - 2, 0, rows // PAD - 1, c)),
            pl.BlockSpec((3, SHORT, wide), lambda c: (0, 0, c)),
        ]
        + [pl.BlockSpec(memory_space=pl.ANY)] * len(after),
        out_specs=pl.BlockSpec((out_rows, wide), lambda c: (0, c)),
        out_shape=jax.ShapeDtypeStruct((out_rows, cols), BF16),
        scratch_shapes=[pltpu.VMEM((wide // LANES, 2, PAD + rows, LANES), F32)],
        compiler_params=params(),
        name="tail",
    )(x, x, short_taps, *after)


def head_kernel(chunks, mo_ref, mr_ref, *refs):
    out_ref = refs[-1]
    edge = LTAPS + PAD
    part = out_ref.shape[1] // chunks
    for h in range(chunks):
        own = slice(h * part, (h + 1) * part)
        f_ref, filt_ref = refs[2 * h : 2 * h + 2]
        mixed = mo_ref[:, own] + mr_ref[:, own].astype(F32)
        out_ref[0:edge, own] = (mixed * f_ref[0]).astype(BF16)
        out_ref[edge : edge + PAD, own] = f_ref[1, 0:PAD].astype(BF16)
        out_ref[edge + PAD : edge + 2 * PAD, own] = f_ref[2, 0:PAD].astype(BF16)
        out_ref[edge + 2 * PAD :, own] = (mixed[0:PAD] * filt_ref[0:PAD]).astype(BF16)


def head_of(mixed_own, mixed_rest, mixers, after):
    edge, cols = LTAPS + PAD, mixed_own.shape[1]
    part = cols // len(mixers)
    whole = pl.BlockSpec((edge, cols), lambda i: (0, 0))
    feat_specs = [
        pl.BlockSpec((3, edge, part), lambda i: (0, 0, 0)),
        pl.BlockSpec((edge, part), lambda i: (0, 0)),
    ]
    return pl.pallas_call(
        functools.partial(head_kernel, len(mixers)),
        grid=(1,),
        in_specs=[whole, whole] + feat_specs * len(mixers) + [pl.BlockSpec(memory_space=pl.ANY)] * len(after),
        out_specs=pl.BlockSpec((edge + 3 * PAD, cols), lambda i: (0, 0)),
        out_shape=jax.ShapeDtypeStruct((edge + 3 * PAD, cols), BF16),
        compiler_params=params(),
        name="head",
    )(mixed_own, mixed_rest, *[array for mixer in mixers for array in mixer[1:]], *after)


def contract(a, b, dim):
    return lax.dot_general(a, b, (((dim,), (dim,)), ((), ())), preferred_element_type=F32)


def places(seq):
    bits = bits_of("seq")
    source = lax.iota(jnp.int32, seq) ^ lax.axis_index("seq")
    return sum(((source >> n) & 1) << (len(bits) - 1 - n) for n in range(len(bits)))


def body(queries, keys, values, cotangent, out_weight, short_taps, long_taps, skip_gain):
    rows, width = queries.shape
    col_part = out_weight.shape[1]
    seq, ys = lax.axis_size("seq"), lax.axis_size("y")
    cols = width // seq
    chunks = 2 if cols % (2 * LANES) == 0 else 1
    groups = long_taps.shape[1]
    fsdp = ("z", "y")
    grad_scale = float(rows * seq * ys * Z) ** (-0.5)

    weights = lax.all_gather(out_weight, "z", axis=1, tiled=True)
    fwd_table, bwd_table = make_tables(long_taps)
    skip = skip_gain.reshape(1, cols)
    place = places(seq)
    by_owner = pack((queries, keys, values), seq)
    x = lax.all_to_all(by_owner, "seq", split_axis=0, concat_axis=0, tiled=True)
    held = own_cotangent(cotangent, col_part, by_owner)
    tail = tail_of(x, short_taps, [fwd_table, held])
    halo = along(tail, fsdp, 1)
    cots = gather_cotangent(held, [halo])
    mixers = []
    for h in range(chunks):
        after = mixers[-1][0] if mixers else cots[0]
        mixers.append(forward(x, halo, short_taps, skip, fwd_table, place, h, chunks, after))

    mixed_all = [
        [around(mixed, "y", step) if step else mixed for step in range(ys)] for mixed, _, _ in mixers
    ]

    parts, heads = [], []
    for step in range(1, ys):
        part, head = mixed_grad(cots, weights, place, step, BF16, [parts[-1] if parts else mixers[-1][0]])
        parts.append(part)
        heads.append(around(head, "y", -step))
    mixed_own, own_head, parts[-1] = mixed_grad(
        cots, weights, place, 0, F32, [parts[-1], *[piece for pieces in mixed_all for piece in pieces[1:]]], True
    )
    rest = [around(parts[step - 1], "y", -step) for step in range(1, ys)]
    mixed_rest = rest[0] if len(rest) == 1 else sum(piece.astype(F32) for piece in rest)
    head_rest = heads[0] if len(heads) == 1 else sum(piece.astype(F32) for piece in heads)
    head = head_of(own_head, head_rest, mixers, [])
    later = along(head, fsdp, -1)

    weight_sum = None
    for h in range(chunks):
        after = [later] if h == chunks - 1 else [head]
        weight_sum = weight_grad(cots, mixed_all[h], h, chunks, grad_scale, weight_sum, after)
    weight_part = lax.psum_scatter(weight_sum, "z", scatter_dimension=1, tiled=True)

    grads, short_parts, long_parts = [], [], []
    for h in range(chunks):
        _, feats, filt = mixers[h]
        grad, short_part, long_part = backward(
            mixed_own, mixed_rest, feats, filt, x, later, short_taps, skip, bwd_table, h, chunks
        )
        grads.append(lax.all_to_all(grad, "seq", split_axis=0, concat_axis=0, tiled=True))
        short_parts.append(short_part)
        long_parts.append(long_part)

    query_grad, key_grad, value_grad = unpack(grads)
    packed = jnp.concatenate(
        [
            jnp.concatenate(short_parts, axis=2).reshape(3 * (SHORT + 1), cols),
            jnp.concatenate(long_parts, axis=0).reshape(-1, cols),
        ],
        axis=0,
    )
    packed = sum_over(packed, ("y", "z")) * grad_scale
    short_sum = packed[: 3 * (SHORT + 1)].reshape(3, SHORT + 1, cols)
    long_sum = packed[3 * (SHORT + 1) :].reshape(groups, LTAPS).T
    return (
        query_grad,
        key_grad,
        value_grad,
        weight_part.astype(F32),
        short_sum[:, :SHORT],
        long_sum,
        short_sum[0, SHORT],
    )


def solution(mesh):
    fsdp, seq = mesh.shape["fsdp"], mesh.shape["seq"]
    split = Mesh(mesh.devices.reshape(Z, fsdp // Z, seq), ("z", "y", "seq"))
    tokens = P(("z", "y", "seq"), None)
    specs = (P("seq", ("z", "y")), P(None, None, "seq"), P(None, "seq"), P("seq"))
    return jax.shard_map(
        body,
        mesh=split,
        in_specs=(tokens,) * 4 + specs,
        out_specs=(tokens,) * 3 + specs,
        check_vma=False,
    )
```

```python
import functools

import jax
import jax.numpy as jnp
from jax import lax
from jax.experimental import pallas as pl
from jax.experimental.pallas import tpu as pltpu
from jax.sharding import Mesh
from jax.sharding import PartitionSpec as P

SHORT = 7
LTAPS = 128
LANES = 128
PAD = 16
Z = 4
F32 = jnp.float32
BF16 = jnp.bfloat16


def params():
    return pltpu.CompilerParams(vmem_limit_bytes=60 * 2**20)


def tables_kernel(fwd_ref, bwd_ref, tf_ref, tb_ref):
    for g in range(fwd_ref.shape[0]):
        rows = slice(g * LTAPS, (g + 1) * LTAPS)
        for src, dst in ((fwd_ref, tf_ref), (bwd_ref, tb_ref)):
            wide = jnp.broadcast_to(src[g : g + 1, :], (LTAPS, 2 * LTAPS))
            dst[rows, :] = pltpu.roll(wide, 0, 1, stride=1, stride_axis=0).astype(BF16)


def make_tables(long_taps):
    by_group = long_taps.T
    groups = by_group.shape[0]
    fwd = jnp.pad(by_group[:, ::-1], ((0, 0), (1, LTAPS - 1)))
    bwd = jnp.pad(by_group, ((0, 0), (0, LTAPS)))
    per = 8
    row_spec = pl.BlockSpec((per, 2 * LTAPS), lambda i: (i, 0))
    tab_spec = pl.BlockSpec((per * LTAPS, 2 * LTAPS), lambda i: (i, 0))
    shape = jax.ShapeDtypeStruct((groups * LTAPS, 2 * LTAPS), BF16)
    return pl.pallas_call(
        tables_kernel,
        grid=(groups // per,),
        in_specs=[row_spec, row_spec],
        out_specs=[tab_spec, tab_spec],
        out_shape=[shape, shape],
        compiler_params=params(),
        name="tables",
    )(fwd, bwd)


def pick_groups(wide, col, rows, per):
    lane_group = lax.broadcasted_iota(jnp.int32, (rows, LANES), 1) // (LANES // per)
    cols = slice(col * LANES, (col + 1) * LANES)
    out = wide[0:rows, cols]
    for g in range(1, per):
        out = jnp.where(lane_group == g, wide[g * rows : (g + 1) * rows, cols], out)
    return out


def features_of(taps_ref, row, xf, i, begin):
    total = taps_ref[row, 0:1] * xf[i, PAD + begin : PAD + begin + LTAPS]
    for j in range(1, SHORT):
        total = total + taps_ref[row, j : j + 1] * xf[i, PAD + begin - j : PAD + begin - j + LTAPS]
    return total


def forward_kernel(
    place_ref, x_ref, h_ref, taps_ref, skip_ref, tab_ref, _, mixed_ref, f_ref, filt_ref, xf, pf, pb, wide
):
    blocks, _, rows, _ = x_ref.shape
    tokens = blocks * rows
    per = tab_ref.shape[0] // LTAPS
    for i in range(3):
        xf[i, 0:PAD] = h_ref[i * PAD : (i + 1) * PAD].astype(F32)
        for b in range(blocks):
            begin = PAD + b * rows
            xf[i, begin : begin + rows] = x_ref[b, i].astype(F32)
    pb[0:LTAPS] = h_ref[3 * PAD : 3 * PAD + LTAPS]
    for begin in range(0, tokens, LTAPS):
        own = slice(begin, begin + LTAPS)
        f1 = features_of(taps_ref, 1, xf, 1, begin)
        f2 = features_of(taps_ref, 2, xf, 2, begin)
        prod = f1 * f2
        f_ref[1, own] = f1
        f_ref[2, own] = f2
        f_ref[0, own] = features_of(taps_ref, 0, xf, 0, begin)
        pf[own] = prod
        pb[LTAPS + begin : 2 * LTAPS + begin] = prod.astype(BF16)
    skip = skip_ref[...]
    for b in range(0, tokens // LTAPS, 2):
        low = b * LTAPS
        windows = jnp.concatenate([pb[low : low + 2 * LTAPS], pb[low + LTAPS : low + 3 * LTAPS]], axis=1)
        wide[...] = jnp.dot(tab_ref[...], windows, preferred_element_type=F32)
        for n in range(2):
            own = slice(low + n * LTAPS, low + (n + 1) * LTAPS)
            filtered = pick_groups(wide, n, LTAPS, per) + skip * pf[own]
            filt_ref[own] = filtered
            mixed = f_ref[0, own] * filtered
            there = pl.multiple_of(place_ref[b + n] * LTAPS, LTAPS)
            mixed_ref[:, pl.ds(there, LTAPS)] = mixed.T.astype(BF16)


def forward(x, halo, short_taps, skip, table, place, chunk, chunks, after):
    blocks, _, rows, cols = x.shape
    cols //= chunks
    tokens = blocks * rows
    tiles = cols // LANES
    first = chunk * tiles
    tab_rows = table.shape[0] * LANES // skip.shape[1]
    return pl.pallas_call(
        forward_kernel,
        grid_spec=pltpu.PrefetchScalarGridSpec(
            num_scalar_prefetch=1,
            grid=(tiles,),
            in_specs=[
                pl.BlockSpec((blocks, 3, rows, LANES), lambda c, _: (0, 0, 0, first + c)),
                pl.BlockSpec((halo.shape[0], LANES), lambda c, _: (0, first + c)),
                pl.BlockSpec((3, SHORT, LANES), lambda c, _: (0, 0, first + c)),
                pl.BlockSpec((1, LANES), lambda c, _: (0, first + c)),
                pl.BlockSpec((tab_rows, 2 * LTAPS), lambda c, _: (first + c, 0)),
                pl.BlockSpec(memory_space=pl.ANY),
            ],
            out_specs=[
                pl.BlockSpec((LANES, tokens), lambda c, _: (c, 0)),
                pl.BlockSpec((3, tokens, LANES), lambda c, _: (0, 0, c)),
                pl.BlockSpec((tokens, LANES), lambda c, _: (0, c)),
            ],
            scratch_shapes=[
                pltpu.VMEM((3, PAD + tokens, LANES), F32),
                pltpu.VMEM((tokens, LANES), F32),
                pltpu.VMEM((LTAPS + tokens, LANES), BF16),
                pltpu.VMEM((tab_rows, 2 * LTAPS), F32),
            ],
        ),
        out_shape=[
            jax.ShapeDtypeStruct((cols, tokens), BF16),
            jax.ShapeDtypeStruct((3, tokens, cols), F32),
            jax.ShapeDtypeStruct((tokens, cols), F32),
        ],
        compiler_params=params(),
        name="forward",
    )(place, x, halo, short_taps, skip, table, after)


def sum_by_lag(gram):
    wide = gram.shape[1]
    parts = [gram[i : i + 8] for i in range(0, gram.shape[0], 8)]
    step = 8
    while len(parts) > 1:
        parts = [
            parts[k] + pltpu.roll(parts[k + 1], wide - step, 1) for k in range(0, len(parts), 2)
        ]
        step *= 2
    total = parts[0]
    row = lax.broadcasted_iota(jnp.int32, total.shape, 0)
    for bit in (1, 2, 4):
        total = jnp.where((row & bit) != 0, pltpu.roll(total, wide - bit, 1), total)
    return jnp.sum(total[:, :LTAPS], axis=0, keepdims=True)


def backward_kernel(
    mo_ref, mr_ref, f_ref, filt_ref, x_ref, n_ref, taps_ref, skip_ref, tab_ref,
    grad_ref, short_ref, long_ref, db, fg, wide, left, right,
):
    blocks, _, rows, _ = x_ref.shape
    tokens = blocks * rows
    per = tab_ref.shape[0] // LTAPS
    count = tokens // LTAPS
    skip = skip_ref[...]
    lane_group = lax.broadcasted_iota(jnp.int32, (1, LANES), 1) // (LANES // per)
    gain = jnp.zeros((8, LANES), F32)
    for b in range(count):
        own = slice(b * LTAPS, (b + 1) * LTAPS)
        mixed_grad = mo_ref[own] + mr_ref[own].astype(F32)
        slope = mixed_grad * f_ref[0, own]
        db[own] = slope.astype(BF16)
        fg[0, own] = mixed_grad * filt_ref[own]
        fg[1, own] = skip * slope
        prod = f_ref[1, own] * f_ref[2, own]
        gain = gain + jnp.sum((prod * slope).reshape(LTAPS // 8, 8, LANES), axis=0)
        prod_b = prod.astype(BF16)
        for g in range(per):
            keep = (lane_group == g).astype(F32).astype(BF16)
            left[g * LTAPS : (g + 1) * LTAPS, b * LANES : (b + 1) * LANES] = prod_b * keep
    db[tokens : tokens + LTAPS + PAD] = n_ref[0 : LTAPS + PAD]
    db[tokens + LTAPS + PAD :] = jnp.zeros((LTAPS - PAD, LANES), BF16)
    for b in range(count):
        right[:, b * LANES : (b + 1) * LANES] = db[b * LTAPS : (b + 2) * LTAPS]
    for b in range(0, count, 2):
        wide[...] = jnp.dot(
            tab_ref[...], right[:, b * LANES : (b + 2) * LANES], preferred_element_type=F32
        )
        for n in range(2):
            own = slice((b + n) * LTAPS, (b + n + 1) * LTAPS)
            grad = pick_groups(wide, n, LTAPS, per) + fg[1, own]
            fg[1, own] = grad * f_ref[2, own]
            fg[2, own] = grad * f_ref[1, own]
    few = jnp.concatenate([tab_ref[g * LTAPS : g * LTAPS + PAD] for g in range(per)], axis=0)
    edge = jnp.dot(few, db[tokens : tokens + 2 * LTAPS], preferred_element_type=F32)
    begin = LTAPS + PAD
    grad = pick_groups(edge, 0, PAD, per) + skip * n_ref[0:PAD].astype(F32)
    fg[1, tokens : tokens + PAD] = grad * n_ref[begin + PAD : begin + 2 * PAD].astype(F32)
    fg[2, tokens : tokens + PAD] = grad * n_ref[begin : begin + PAD].astype(F32)
    fg[0, tokens : tokens + PAD] = n_ref[begin + 2 * PAD : begin + 3 * PAD].astype(F32)
    for i in range(3):
        sums = [jnp.zeros((8, LANES), F32) for _ in range(SHORT)]
        for b in range(count):
            low = b * LTAPS
            inputs = x_ref[b, i].astype(F32)
            total = None
            for j in range(SHORT):
                later = fg[i, low + j : low + j + LTAPS]
                term = taps_ref[i, j : j + 1] * later
                total = term if total is None else total + term
                sums[j] = sums[j] + jnp.sum((later * inputs).reshape(LTAPS // 8, 8, LANES), axis=0)
            grad_ref[b, i] = total.astype(BF16)
        for j in range(SHORT):
            short_ref[i, j : j + 1] = jnp.sum(sums[j], axis=0, keepdims=True)
        short_ref[i, SHORT : SHORT + 1] = jnp.sum(gain, axis=0, keepdims=True)
    wide[...] = lax.dot_general(left[...], right[...], (((1,), (1,)), ((), ())), preferred_element_type=F32)
    for g in range(per):
        gram = wide[g * LTAPS : (g + 1) * LTAPS]
        long_ref[g : g + 1] = sum_by_lag(gram)


def backward(mixed_own, mixed_rest, feats, filt, x, later, short_taps, skip, table, chunk, chunks):
    blocks, _, rows, cols = x.shape
    cols //= chunks
    tokens = blocks * rows
    tiles = cols // LANES
    first = chunk * tiles
    tab_rows = table.shape[0] * LANES // skip.shape[1]
    per = tab_rows // LTAPS
    tok = pl.BlockSpec((tokens, LANES), lambda c: (0, first + c))
    return pl.pallas_call(
        backward_kernel,
        grid=(tiles,),
        in_specs=[
            tok,
            tok,
            pl.BlockSpec((3, tokens, LANES), lambda c: (0, 0, c)),
            pl.BlockSpec((tokens, LANES), lambda c: (0, c)),
            pl.BlockSpec((blocks, 3, rows, LANES), lambda c: (0, 0, 0, first + c)),
            pl.BlockSpec((later.shape[0], LANES), lambda c: (0, first + c)),
            pl.BlockSpec((3, SHORT, LANES), lambda c: (0, 0, first + c)),
            pl.BlockSpec((1, LANES), lambda c: (0, first + c)),
            pl.BlockSpec((tab_rows, 2 * LTAPS), lambda c: (first + c, 0)),
        ],
        out_specs=[
            pl.BlockSpec((blocks, 3, rows, LANES), lambda c: (0, 0, 0, c)),
            pl.BlockSpec((3, SHORT + 1, LANES), lambda c: (0, 0, c)),
            pl.BlockSpec((per, LTAPS), lambda c: (c, 0)),
        ],
        out_shape=[
            jax.ShapeDtypeStruct((blocks, 3, rows, cols), BF16),
            jax.ShapeDtypeStruct((3, SHORT + 1, cols), F32),
            jax.ShapeDtypeStruct((tiles * per, LTAPS), F32),
        ],
        scratch_shapes=[
            pltpu.VMEM((tokens + 2 * LTAPS, LANES), BF16),
            pltpu.VMEM((3, tokens + PAD, LANES), F32),
            pltpu.VMEM((tab_rows, 2 * LTAPS), F32),
            pltpu.VMEM((tab_rows, tokens), BF16),
            pltpu.VMEM((2 * LTAPS, tokens), BF16),
        ],
        compiler_params=params(),
        cost_estimate=pl.CostEstimate(flops=10**11, bytes_accessed=36 * tokens * cols, transcendentals=0),
        name="backward",
    )(mixed_own, mixed_rest, feats, filt, x, later, short_taps, skip, table)


def pack_kernel(*refs):
    out_ref = refs[-1]
    for i, ref in enumerate(refs[:3]):
        out_ref[0, i] = ref[...]


def pack(arrays, seq):
    rows, width = arrays[0].shape
    cols = width // seq
    return pl.pallas_call(
        pack_kernel,
        grid=(seq,),
        in_specs=[pl.BlockSpec((rows, cols), lambda s: (0, s))] * 3,
        out_specs=pl.BlockSpec((1, 3, rows, cols), lambda s: (s, 0, 0, 0)),
        out_shape=jax.ShapeDtypeStruct((seq, 3, rows, cols), BF16),
        compiler_params=params(),
        name="pack",
    )(*arrays)


def unpack_kernel(*refs):
    parts, outs = refs[:-3], refs[-3:]
    cols = parts[0].shape[3]
    for n, part in enumerate(parts):
        for i, out in enumerate(outs):
            out[:, n * cols : (n + 1) * cols] = part[0, i]


def unpack(parts):
    seq, _, rows, cols = parts[0].shape
    wide = cols * len(parts)
    shape = jax.ShapeDtypeStruct((rows, seq * wide), BF16)
    return pl.pallas_call(
        unpack_kernel,
        grid=(seq,),
        in_specs=[pl.BlockSpec((1, 3, rows, cols), lambda s: (s, 0, 0, 0))] * len(parts),
        out_specs=[pl.BlockSpec((rows, wide), lambda s: (0, s))] * 3,
        out_shape=[shape] * 3,
        compiler_params=params(),
        name="unpack",
    )(*parts)


def along(block, axis, distance):
    size = lax.axis_size(axis)
    return lax.ppermute(block, axis, [(i, i + distance) for i in range(size) if 0 <= i + distance < size])


def around(block, axis, distance):
    size = lax.axis_size(axis)
    return lax.ppermute(block, axis, [(i, (i + distance) % size) for i in range(size)])


def across(block, axis, bit):
    return lax.ppermute(block, axis, [(i, i ^ bit) for i in range(lax.axis_size(axis))])


def bits_of(axis):
    size = lax.axis_size(axis)
    return [1 << n for n in range(size.bit_length() - 1)]


def sum_over(value, axes):
    for axis in axes:
        for bit in bits_of(axis):
            value = value + across(value, axis, bit)
    return value


def split_kernel(y_ref, *refs):
    count = (len(refs) - 1) // 2
    for n in range(count):
        refs[count + 1 + n][...] = refs[n][...]


def split_cotangent(cotangent, y, ys, col_part, after):
    rows, width = cotangent.shape

    def source(step):
        return pl.BlockSpec((rows, col_part), lambda z, y_ref: (0, z * ys + (y_ref[0] + step) % ys))

    return pl.pallas_call(
        split_kernel,
        grid_spec=pltpu.PrefetchScalarGridSpec(
            num_scalar_prefetch=1,
            grid=(Z,),
            in_specs=[source(step) for step in range(ys)] + [pl.BlockSpec(memory_space=pl.ANY)],
            out_specs=[pl.BlockSpec((rows, col_part), lambda z, _: (0, z))] * ys,
        ),
        out_shape=[jax.ShapeDtypeStruct((rows, width // ys), BF16)] * ys,
        compiler_params=params(),
        name="split",
    )(y.reshape(1), *([cotangent] * ys), after)


def join_kernel(axis, count, *refs):
    out = refs[-1]
    for n in range(count):
        size = refs[n].shape[axis]
        here = slice(n * size, (n + 1) * size)
        if axis == 0:
            out[here] = refs[n][...]
        else:
            out[:, here] = refs[n][...]


def join(parts, axis, after=()):
    shape = list(parts[0].shape)
    tile = shape[-1] // Z
    block = pl.BlockSpec((*shape[:-1], tile), lambda i: (0, 0, 0, i))
    shape[axis] *= len(parts)
    return pl.pallas_call(
        functools.partial(join_kernel, axis, len(parts)),
        grid=(Z,),
        in_specs=[block] * len(parts) + [pl.BlockSpec(memory_space=pl.ANY)] * len(after),
        out_specs=pl.BlockSpec((*shape[:-1], tile), lambda i: (0, 0, 0, i)),
        out_shape=jax.ShapeDtypeStruct(tuple(shape), BF16),
        compiler_params=params(),
        name="join",
    )(*parts, *after)


def own_cotangent(cotangent, col_part, after):
    ys, y = lax.axis_size("y"), lax.axis_index("y")
    held = split_cotangent(cotangent, y, ys, col_part, after)
    held = [around(part, "y", step) if step else part for step, part in enumerate(held)]
    return join([part[None, None] for part in held], 0)


def gather_cotangent(held, after):
    bits = bits_of("seq")
    for bit in reversed(bits[1:]):
        held = join([held, across(held, "seq", bit)], 1, after)
    return held, across(held, "seq", bits[0])


def mixed_grad_kernel(waits, place_ref, a_ref, b_ref, w_ref, *refs):
    out_ref, head_ref = refs[waits : waits + 2]
    found = refs[-1]
    _, count, rows, _ = a_ref.shape
    tokens = count * rows
    pieces = jnp.concatenate([ref[...].reshape(tokens, -1) for ref in (a_ref, b_ref)], axis=0)
    found[...] = contract(pieces, w_ref[...], 1)
    for block in range(2 * count):
        there = pl.multiple_of(place_ref[block] * rows, rows)
        out_ref[block * rows : (block + 1) * rows] = found[pl.ds(there, rows)].astype(out_ref.dtype)
    head_ref[...] = out_ref[0 : LTAPS + PAD]


def mixed_grad(cots, weights, place, step, dtype, after):
    _, count, rows, width = cots[0].shape
    tokens = 2 * count * rows
    cols = weights.shape[0]
    tile = min(cols, 2 * LANES)
    piece = pl.BlockSpec((1, count, rows, width), lambda i, _: (step, 0, 0, 0))
    return pl.pallas_call(
        functools.partial(mixed_grad_kernel, len(after)),
        grid_spec=pltpu.PrefetchScalarGridSpec(
            num_scalar_prefetch=1,
            grid=(cols // tile,),
            in_specs=[
                piece,
                piece,
                pl.BlockSpec((tile, width), lambda i, _: (i, 0)),
            ]
            + [pl.BlockSpec(memory_space=pl.ANY)] * len(after),
            out_specs=[
                pl.BlockSpec((tokens, tile), lambda i, _: (0, i)),
                pl.BlockSpec((LTAPS + PAD, tile), lambda i, _: (0, i)),
            ],
            scratch_shapes=[pltpu.VMEM((tokens, tile), F32)],
        ),
        out_shape=[
            jax.ShapeDtypeStruct((tokens, cols), dtype),
            jax.ShapeDtypeStruct((LTAPS + PAD, cols), dtype),
        ],
        compiler_params=params(),
        name="mixed_grad",
    )(place, *cots, weights, *after)


def weight_grad_kernel(scale, a_ref, b_ref, *refs):
    steps, count, rows, tile = a_ref.shape
    tokens = count * rows
    mixed, out = refs[:steps], refs[-1]
    total = None
    for step in range(steps):
        for n, ref in enumerate((a_ref, b_ref)):
            left = mixed[step][:, n * tokens : (n + 1) * tokens]
            term = jnp.dot(left, ref[step].reshape(tokens, tile), preferred_element_type=F32)
            total = term if total is None else total + term
    out[...] = (total * scale).astype(BF16)


def weight_grad(cots, mixed, chunk, chunks, scale, target, after):
    steps, count, rows, width = cots[0].shape
    part, tokens = mixed[0].shape
    tile = width // Z
    piece = pl.BlockSpec((steps, count, rows, tile), lambda i: (0, 0, 0, i))
    extra = [*after] + ([] if target is None else [target])
    return pl.pallas_call(
        functools.partial(weight_grad_kernel, scale),
        grid=(Z,),
        in_specs=[piece, piece]
        + [pl.BlockSpec((part, tokens), lambda i: (0, 0))] * len(mixed)
        + [pl.BlockSpec(memory_space=pl.ANY)] * len(extra),
        out_specs=pl.BlockSpec((part, tile), lambda i: (chunk, i)),
        out_shape=jax.ShapeDtypeStruct((part * chunks, width), BF16),
        input_output_aliases={} if target is None else {2 + len(mixed) + len(after): 0},
        compiler_params=params(),
        name="weight_grad",
    )(*cots, *mixed, *extra)


def tail_kernel(x_ref, before_ref, taps_ref, *refs):
    out_ref, xf = refs[-2:]
    rows = x_ref.shape[2]
    for i in range(3):
        out_ref[i * PAD : (i + 1) * PAD] = x_ref[0, i, rows - PAD :]
    for tile in range(x_ref.shape[3] // LANES):
        cols = slice(tile * LANES, (tile + 1) * LANES)
        taps = taps_ref[:, :, cols]
        prod = None
        for i in (1, 2):
            xf[tile, i - 1, 0:PAD] = before_ref[0, i, :, cols].astype(F32)
            xf[tile, i - 1, PAD:] = x_ref[0, i, :, cols].astype(F32)
            feature = taps[i, 0:1] * xf[tile, i - 1, PAD : PAD + rows]
            for j in range(1, SHORT):
                feature = feature + taps[i, j : j + 1] * xf[tile, i - 1, PAD - j : PAD - j + rows]
            prod = feature if prod is None else prod * feature
        out_ref[3 * PAD :, cols] = prod.astype(BF16)


def tail_of(x, short_taps, after):
    seq, _, rows, cols = x.shape
    wide = min(cols, 4 * LANES)
    out_rows = 3 * PAD + rows
    return pl.pallas_call(
        tail_kernel,
        grid=(cols // wide,),
        in_specs=[
            pl.BlockSpec((1, 3, rows, wide), lambda c: (seq - 1, 0, 0, c)),
            pl.BlockSpec((1, 3, PAD, wide), lambda c: (seq - 2, 0, rows // PAD - 1, c)),
            pl.BlockSpec((3, SHORT, wide), lambda c: (0, 0, c)),
        ]
        + [pl.BlockSpec(memory_space=pl.ANY)] * len(after),
        out_specs=pl.BlockSpec((out_rows, wide), lambda c: (0, c)),
        out_shape=jax.ShapeDtypeStruct((out_rows, cols), BF16),
        scratch_shapes=[pltpu.VMEM((wide // LANES, 2, PAD + rows, LANES), F32)],
        compiler_params=params(),
        name="tail",
    )(x, x, short_taps, *after)


def head_kernel(chunks, mo_ref, mr_ref, *refs):
    out_ref = refs[-2]
    edge = LTAPS + PAD
    part = out_ref.shape[1] // chunks
    for h in range(chunks):
        own = slice(h * part, (h + 1) * part)
        f_ref, filt_ref = refs[2 * h : 2 * h + 2]
        mixed = mo_ref[:, own] + mr_ref[:, own].astype(F32)
        out_ref[0:edge, own] = (mixed * f_ref[0]).astype(BF16)
        out_ref[edge : edge + PAD, own] = f_ref[1, 0:PAD].astype(BF16)
        out_ref[edge + PAD : edge + 2 * PAD, own] = f_ref[2, 0:PAD].astype(BF16)
        out_ref[edge + 2 * PAD :, own] = (mixed[0:PAD] * filt_ref[0:PAD]).astype(BF16)


def head_of(mixed_own, mixed_rest, mixers, passed):
    edge, cols = LTAPS + PAD, mixed_own.shape[1]
    part = cols // len(mixers)
    whole = pl.BlockSpec((edge, cols), lambda i: (0, 0))
    feat_specs = [
        pl.BlockSpec((3, edge, part), lambda i: (0, 0, 0)),
        pl.BlockSpec((edge, part), lambda i: (0, 0)),
    ]
    return pl.pallas_call(
        functools.partial(head_kernel, len(mixers)),
        grid=(1,),
        in_specs=[whole, whole] + feat_specs * len(mixers) + [pl.BlockSpec(memory_space=pl.ANY)],
        out_specs=[pl.BlockSpec((edge + 3 * PAD, cols), lambda i: (0, 0)), pl.BlockSpec(memory_space=pl.ANY)],
        out_shape=[
            jax.ShapeDtypeStruct((edge + 3 * PAD, cols), BF16),
            jax.ShapeDtypeStruct(passed.shape, passed.dtype),
        ],
        input_output_aliases={2 + 2 * len(mixers): 1},
        compiler_params=params(),
        name="head",
    )(mixed_own, mixed_rest, *[array for mixer in mixers for array in mixer[1:]], passed)


def contract(a, b, dim):
    return lax.dot_general(a, b, (((dim,), (dim,)), ((), ())), preferred_element_type=F32)


def places(seq):
    bits = bits_of("seq")
    source = lax.iota(jnp.int32, seq) ^ lax.axis_index("seq")
    return sum(((source >> n) & 1) << (len(bits) - 1 - n) for n in range(len(bits)))


def body(queries, keys, values, cotangent, out_weight, short_taps, long_taps, skip_gain):
    rows, width = queries.shape
    col_part = out_weight.shape[1]
    seq, ys = lax.axis_size("seq"), lax.axis_size("y")
    cols = width // seq
    chunks = 2 if cols % (2 * LANES) == 0 else 1
    groups = long_taps.shape[1]
    fsdp = ("z", "y")
    grad_scale = float(rows * seq * ys * Z) ** (-0.5)

    weights = lax.all_gather(out_weight, "z", axis=1, tiled=True)
    fwd_table, bwd_table = make_tables(long_taps)
    skip = skip_gain.reshape(1, cols)
    place = places(seq)
    by_owner = pack((queries, keys, values), seq)
    x = lax.all_to_all(by_owner, "seq", split_axis=0, concat_axis=0, tiled=True)
    held = own_cotangent(cotangent, col_part, by_owner)
    tail = tail_of(x, short_taps, [fwd_table, held])
    halo = along(tail, fsdp, 1)
    cots = gather_cotangent(held, [halo])
    mixers = []
    for h in range(chunks):
        after = mixers[-1][0] if mixers else cots[0]
        mixers.append(forward(x, halo, short_taps, skip, fwd_table, place, h, chunks, after))

    mixed_all = [
        [around(mixed, "y", step) if step else mixed for step in range(ys)] for mixed, _, _ in mixers
    ]

    parts, heads = [], []
    for step in range(1, ys):
        part, head = mixed_grad(cots, weights, place, step, BF16, [parts[-1] if parts else mixers[-1][0]])
        parts.append(part)
        heads.append(around(head, "y", -step))
    mixed_own, own_head = mixed_grad(cots, weights, place, 0, F32, [parts[-1], *mixed_all[0][1:]])
    head_rest = heads[0] if len(heads) == 1 else sum(piece.astype(F32) for piece in heads)
    head, parts[-1] = head_of(own_head, head_rest, mixers, parts[-1])
    rest = [around(parts[step - 1], "y", -step) for step in range(1, ys)]
    mixed_rest = rest[0] if len(rest) == 1 else sum(piece.astype(F32) for piece in rest)
    later = along(head, fsdp, -1)

    weight_sum = None
    for h in range(chunks):
        after = [later] if h == chunks - 1 else [head]
        weight_sum = weight_grad(cots, mixed_all[h], h, chunks, grad_scale, weight_sum, after)
    weight_part = lax.psum_scatter(weight_sum, "z", scatter_dimension=1, tiled=True)

    grads, short_parts, long_parts = [], [], []
    for h in range(chunks):
        _, feats, filt = mixers[h]
        grad, short_part, long_part = backward(
            mixed_own, mixed_rest, feats, filt, x, later, short_taps, skip, bwd_table, h, chunks
        )
        grads.append(lax.all_to_all(grad, "seq", split_axis=0, concat_axis=0, tiled=True))
        short_parts.append(short_part)
        long_parts.append(long_part)

    query_grad, key_grad, value_grad = unpack(grads)
    packed = jnp.concatenate(
        [
            jnp.concatenate(short_parts, axis=2).reshape(3 * (SHORT + 1), cols),
            jnp.concatenate(long_parts, axis=0).reshape(-1, cols),
        ],
        axis=0,
    )
    packed = sum_over(packed, ("y", "z")) * grad_scale
    short_sum = packed[: 3 * (SHORT + 1)].reshape(3, SHORT + 1, cols)
    long_sum = packed[3 * (SHORT + 1) :].reshape(groups, LTAPS).T
    return (
        query_grad,
        key_grad,
        value_grad,
        weight_part.astype(F32),
        short_sum[:, :SHORT],
        long_sum,
        short_sum[0, SHORT],
    )


def solution(mesh):
    fsdp, seq = mesh.shape["fsdp"], mesh.shape["seq"]
    split = Mesh(mesh.devices.reshape(Z, fsdp // Z, seq), ("z", "y", "seq"))
    tokens = P(("z", "y", "seq"), None)
    specs = (P("seq", ("z", "y")), P(None, None, "seq"), P(None, "seq"), P("seq"))
    return jax.shard_map(
        body,
        mesh=split,
        in_specs=(tokens,) * 4 + specs,
        out_specs=(tokens,) * 3 + specs,
        check_vma=False,
    )
```

```python
import functools

import jax
import jax.numpy as jnp
from jax import lax
from jax.experimental import pallas as pl
from jax.experimental.pallas import tpu as pltpu
from jax.sharding import Mesh
from jax.sharding import PartitionSpec as P

SHORT = 7
LTAPS = 128
LANES = 128
PAD = 16
Z = 4
F32 = jnp.float32
BF16 = jnp.bfloat16


def params():
    return pltpu.CompilerParams(vmem_limit_bytes=60 * 2**20)


def tables_kernel(fwd_ref, bwd_ref, tf_ref, tb_ref):
    for g in range(fwd_ref.shape[0]):
        rows = slice(g * LTAPS, (g + 1) * LTAPS)
        for src, dst in ((fwd_ref, tf_ref), (bwd_ref, tb_ref)):
            wide = jnp.broadcast_to(src[g : g + 1, :], (LTAPS, 2 * LTAPS))
            dst[rows, :] = pltpu.roll(wide, 0, 1, stride=1, stride_axis=0).astype(BF16)


def make_tables(long_taps):
    by_group = long_taps.T
    groups = by_group.shape[0]
    fwd = jnp.pad(by_group[:, ::-1], ((0, 0), (1, LTAPS - 1)))
    bwd = jnp.pad(by_group, ((0, 0), (0, LTAPS)))
    per = 8
    row_spec = pl.BlockSpec((per, 2 * LTAPS), lambda i: (i, 0))
    tab_spec = pl.BlockSpec((per * LTAPS, 2 * LTAPS), lambda i: (i, 0))
    shape = jax.ShapeDtypeStruct((groups * LTAPS, 2 * LTAPS), BF16)
    return pl.pallas_call(
        tables_kernel,
        grid=(groups // per,),
        in_specs=[row_spec, row_spec],
        out_specs=[tab_spec, tab_spec],
        out_shape=[shape, shape],
        compiler_params=params(),
        name="tables",
    )(fwd, bwd)


def pick_groups(wide, col, rows, per):
    lane_group = lax.broadcasted_iota(jnp.int32, (rows, LANES), 1) // (LANES // per)
    cols = slice(col * LANES, (col + 1) * LANES)
    out = wide[0:rows, cols]
    for g in range(1, per):
        out = jnp.where(lane_group == g, wide[g * rows : (g + 1) * rows, cols], out)
    return out


def features_of(taps_ref, row, xf, i, begin):
    total = taps_ref[row, 0:1] * xf[i, PAD + begin : PAD + begin + LTAPS]
    for j in range(1, SHORT):
        total = total + taps_ref[row, j : j + 1] * xf[i, PAD + begin - j : PAD + begin - j + LTAPS]
    return total


def forward_kernel(
    place_ref, x_ref, h_ref, taps_ref, skip_ref, tab_ref, _, mixed_ref, f_ref, filt_ref, xf, pf, pb, wide
):
    blocks, _, rows, _ = x_ref.shape
    tokens = blocks * rows
    per = tab_ref.shape[0] // LTAPS
    for i in range(3):
        xf[i, 0:PAD] = h_ref[i * PAD : (i + 1) * PAD].astype(F32)
        for b in range(blocks):
            begin = PAD + b * rows
            xf[i, begin : begin + rows] = x_ref[b, i].astype(F32)
    pb[0:LTAPS] = h_ref[3 * PAD : 3 * PAD + LTAPS]
    for begin in range(0, tokens, LTAPS):
        own = slice(begin, begin + LTAPS)
        f1 = features_of(taps_ref, 1, xf, 1, begin)
        f2 = features_of(taps_ref, 2, xf, 2, begin)
        prod = f1 * f2
        f_ref[1, own] = f1
        f_ref[2, own] = f2
        f_ref[0, own] = features_of(taps_ref, 0, xf, 0, begin)
        pf[own] = prod
        pb[LTAPS + begin : 2 * LTAPS + begin] = prod.astype(BF16)
    skip = skip_ref[...]
    for b in range(0, tokens // LTAPS, 2):
        low = b * LTAPS
        windows = jnp.concatenate([pb[low : low + 2 * LTAPS], pb[low + LTAPS : low + 3 * LTAPS]], axis=1)
        wide[...] = jnp.dot(tab_ref[...], windows, preferred_element_type=F32)
        for n in range(2):
            own = slice(low + n * LTAPS, low + (n + 1) * LTAPS)
            filtered = pick_groups(wide, n, LTAPS, per) + skip * pf[own]
            filt_ref[own] = filtered
            mixed = f_ref[0, own] * filtered
            there = pl.multiple_of(place_ref[b + n] * LTAPS, LTAPS)
            mixed_ref[:, pl.ds(there, LTAPS)] = mixed.T.astype(BF16)


def forward(x, halo, short_taps, skip, table, place, chunk, chunks, after):
    blocks, _, rows, cols = x.shape
    cols //= chunks
    tokens = blocks * rows
    tiles = cols // LANES
    first = chunk * tiles
    tab_rows = table.shape[0] * LANES // skip.shape[1]
    return pl.pallas_call(
        forward_kernel,
        grid_spec=pltpu.PrefetchScalarGridSpec(
            num_scalar_prefetch=1,
            grid=(tiles,),
            in_specs=[
                pl.BlockSpec((blocks, 3, rows, LANES), lambda c, _: (0, 0, 0, first + c)),
                pl.BlockSpec((halo.shape[0], LANES), lambda c, _: (0, first + c)),
                pl.BlockSpec((3, SHORT, LANES), lambda c, _: (0, 0, first + c)),
                pl.BlockSpec((1, LANES), lambda c, _: (0, first + c)),
                pl.BlockSpec((tab_rows, 2 * LTAPS), lambda c, _: (first + c, 0)),
                pl.BlockSpec(memory_space=pl.ANY),
            ],
            out_specs=[
                pl.BlockSpec((LANES, tokens), lambda c, _: (c, 0)),
                pl.BlockSpec((3, tokens, LANES), lambda c, _: (0, 0, c)),
                pl.BlockSpec((tokens, LANES), lambda c, _: (0, c)),
            ],
            scratch_shapes=[
                pltpu.VMEM((3, PAD + tokens, LANES), F32),
                pltpu.VMEM((tokens, LANES), F32),
                pltpu.VMEM((LTAPS + tokens, LANES), BF16),
                pltpu.VMEM((tab_rows, 2 * LTAPS), F32),
            ],
        ),
        out_shape=[
            jax.ShapeDtypeStruct((cols, tokens), BF16),
            jax.ShapeDtypeStruct((3, tokens, cols), F32),
            jax.ShapeDtypeStruct((tokens, cols), F32),
        ],
        compiler_params=params(),
        name="forward",
    )(place, x, halo, short_taps, skip, table, after)


def sum_by_lag(gram):
    wide = gram.shape[1]
    parts = [gram[i : i + 8] for i in range(0, gram.shape[0], 8)]
    step = 8
    while len(parts) > 1:
        parts = [
            parts[k] + pltpu.roll(parts[k + 1], wide - step, 1) for k in range(0, len(parts), 2)
        ]
        step *= 2
    total = parts[0]
    row = lax.broadcasted_iota(jnp.int32, total.shape, 0)
    for bit in (1, 2, 4):
        total = jnp.where((row & bit) != 0, pltpu.roll(total, wide - bit, 1), total)
    return jnp.sum(total[:, :LTAPS], axis=0, keepdims=True)


def backward_kernel(
    mo_ref, mr_ref, f_ref, filt_ref, x_ref, n_ref, taps_ref, skip_ref, tab_ref,
    grad_ref, short_ref, long_ref, db, fg, wide, left, right,
):
    blocks, _, rows, _ = x_ref.shape
    tokens = blocks * rows
    per = tab_ref.shape[0] // LTAPS
    count = tokens // LTAPS
    skip = skip_ref[...]
    lane_group = lax.broadcasted_iota(jnp.int32, (1, LANES), 1) // (LANES // per)
    gain = jnp.zeros((8, LANES), F32)
    for b in range(count):
        own = slice(b * LTAPS, (b + 1) * LTAPS)
        mixed_grad = mo_ref[own] + mr_ref[own].astype(F32)
        slope = mixed_grad * f_ref[0, own]
        db[own] = slope.astype(BF16)
        fg[0, own] = mixed_grad * filt_ref[own]
        fg[1, own] = skip * slope
        prod = f_ref[1, own] * f_ref[2, own]
        gain = gain + jnp.sum((prod * slope).reshape(LTAPS // 8, 8, LANES), axis=0)
        prod_b = prod.astype(BF16)
        for g in range(per):
            keep = (lane_group == g).astype(F32).astype(BF16)
            left[g * LTAPS : (g + 1) * LTAPS, b * LANES : (b + 1) * LANES] = prod_b * keep
    db[tokens : tokens + LTAPS + PAD] = n_ref[0 : LTAPS + PAD]
    db[tokens + LTAPS + PAD :] = jnp.zeros((LTAPS - PAD, LANES), BF16)
    for b in range(count):
        right[:, b * LANES : (b + 1) * LANES] = db[b * LTAPS : (b + 2) * LTAPS]
    for b in range(0, count, 2):
        wide[...] = jnp.dot(
            tab_ref[...], right[:, b * LANES : (b + 2) * LANES], preferred_element_type=F32
        )
        for n in range(2):
            own = slice((b + n) * LTAPS, (b + n + 1) * LTAPS)
            grad = pick_groups(wide, n, LTAPS, per) + fg[1, own]
            fg[1, own] = grad * f_ref[2, own]
            fg[2, own] = grad * f_ref[1, own]
    few = jnp.concatenate([tab_ref[g * LTAPS : g * LTAPS + PAD] for g in range(per)], axis=0)
    edge = jnp.dot(few, db[tokens : tokens + 2 * LTAPS], preferred_element_type=F32)
    begin = LTAPS + PAD
    grad = pick_groups(edge, 0, PAD, per) + skip * n_ref[0:PAD].astype(F32)
    fg[1, tokens : tokens + PAD] = grad * n_ref[begin + PAD : begin + 2 * PAD].astype(F32)
    fg[2, tokens : tokens + PAD] = grad * n_ref[begin : begin + PAD].astype(F32)
    fg[0, tokens : tokens + PAD] = n_ref[begin + 2 * PAD : begin + 3 * PAD].astype(F32)
    for i in range(3):
        sums = [jnp.zeros((8, LANES), F32) for _ in range(SHORT)]
        for b in range(count):
            low = b * LTAPS
            inputs = x_ref[b, i].astype(F32)
            total = None
            for j in range(SHORT):
                later = fg[i, low + j : low + j + LTAPS]
                term = taps_ref[i, j : j + 1] * later
                total = term if total is None else total + term
                sums[j] = sums[j] + jnp.sum((later * inputs).reshape(LTAPS // 8, 8, LANES), axis=0)
            grad_ref[b, i] = total.astype(BF16)
        for j in range(SHORT):
            short_ref[i, j : j + 1] = jnp.sum(sums[j], axis=0, keepdims=True)
        short_ref[i, SHORT : SHORT + 1] = jnp.sum(gain, axis=0, keepdims=True)
    wide[...] = lax.dot_general(left[...], right[...], (((1,), (1,)), ((), ())), preferred_element_type=F32)
    for g in range(per):
        gram = wide[g * LTAPS : (g + 1) * LTAPS]
        long_ref[g : g + 1] = sum_by_lag(gram)


def backward(mixed_own, mixed_rest, feats, filt, x, later, short_taps, skip, table, chunk, chunks):
    blocks, _, rows, cols = x.shape
    cols //= chunks
    tokens = blocks * rows
    tiles = cols // LANES
    first = chunk * tiles
    tab_rows = table.shape[0] * LANES // skip.shape[1]
    per = tab_rows // LTAPS
    tok = pl.BlockSpec((tokens, LANES), lambda c: (0, first + c))
    return pl.pallas_call(
        backward_kernel,
        grid=(tiles,),
        in_specs=[
            tok,
            tok,
            pl.BlockSpec((3, tokens, LANES), lambda c: (0, 0, c)),
            pl.BlockSpec((tokens, LANES), lambda c: (0, c)),
            pl.BlockSpec((blocks, 3, rows, LANES), lambda c: (0, 0, 0, first + c)),
            pl.BlockSpec((later.shape[0], LANES), lambda c: (0, first + c)),
            pl.BlockSpec((3, SHORT, LANES), lambda c: (0, 0, first + c)),
            pl.BlockSpec((1, LANES), lambda c: (0, first + c)),
            pl.BlockSpec((tab_rows, 2 * LTAPS), lambda c: (first + c, 0)),
        ],
        out_specs=[
            pl.BlockSpec((blocks, 3, rows, LANES), lambda c: (0, 0, 0, c)),
            pl.BlockSpec((3, SHORT + 1, LANES), lambda c: (0, 0, c)),
            pl.BlockSpec((per, LTAPS), lambda c: (c, 0)),
        ],
        out_shape=[
            jax.ShapeDtypeStruct((blocks, 3, rows, cols), BF16),
            jax.ShapeDtypeStruct((3, SHORT + 1, cols), F32),
            jax.ShapeDtypeStruct((tiles * per, LTAPS), F32),
        ],
        scratch_shapes=[
            pltpu.VMEM((tokens + 2 * LTAPS, LANES), BF16),
            pltpu.VMEM((3, tokens + PAD, LANES), F32),
            pltpu.VMEM((tab_rows, 2 * LTAPS), F32),
            pltpu.VMEM((tab_rows, tokens), BF16),
            pltpu.VMEM((2 * LTAPS, tokens), BF16),
        ],
        compiler_params=params(),
        cost_estimate=pl.CostEstimate(flops=10**11, bytes_accessed=36 * tokens * cols, transcendentals=0),
        name="backward",
    )(mixed_own, mixed_rest, feats, filt, x, later, short_taps, skip, table)


def pack_kernel(*refs):
    out_ref = refs[-1]
    for i, ref in enumerate(refs[:3]):
        out_ref[0, i] = ref[...]


def pack(arrays, seq):
    rows, width = arrays[0].shape
    cols = width // seq
    return pl.pallas_call(
        pack_kernel,
        grid=(seq,),
        in_specs=[pl.BlockSpec((rows, cols), lambda s: (0, s))] * 3,
        out_specs=pl.BlockSpec((1, 3, rows, cols), lambda s: (s, 0, 0, 0)),
        out_shape=jax.ShapeDtypeStruct((seq, 3, rows, cols), BF16),
        compiler_params=params(),
        name="pack",
    )(*arrays)


def unpack_kernel(*refs):
    parts, outs = refs[:-3], refs[-3:]
    cols = parts[0].shape[3]
    for n, part in enumerate(parts):
        for i, out in enumerate(outs):
            out[:, n * cols : (n + 1) * cols] = part[0, i]


def unpack(parts):
    seq, _, rows, cols = parts[0].shape
    wide = cols * len(parts)
    shape = jax.ShapeDtypeStruct((rows, seq * wide), BF16)
    return pl.pallas_call(
        unpack_kernel,
        grid=(seq,),
        in_specs=[pl.BlockSpec((1, 3, rows, cols), lambda s: (s, 0, 0, 0))] * len(parts),
        out_specs=[pl.BlockSpec((rows, wide), lambda s: (0, s))] * 3,
        out_shape=[shape] * 3,
        compiler_params=params(),
        name="unpack",
    )(*parts)


def along(block, axis, distance):
    size = lax.axis_size(axis)
    return lax.ppermute(block, axis, [(i, i + distance) for i in range(size) if 0 <= i + distance < size])


def around(block, axis, distance):
    size = lax.axis_size(axis)
    return lax.ppermute(block, axis, [(i, (i + distance) % size) for i in range(size)])


def across(block, axis, bit):
    return lax.ppermute(block, axis, [(i, i ^ bit) for i in range(lax.axis_size(axis))])


def bits_of(axis):
    size = lax.axis_size(axis)
    return [1 << n for n in range(size.bit_length() - 1)]


def sum_over(value, axes):
    for axis in axes:
        for bit in bits_of(axis):
            value = value + across(value, axis, bit)
    return value


def split_kernel(y_ref, *refs):
    count = (len(refs) - 1) // 2
    for n in range(count):
        refs[count + 1 + n][...] = refs[n][...]


def split_cotangent(cotangent, y, ys, col_part, after):
    rows, width = cotangent.shape

    def source(step):
        return pl.BlockSpec((rows, col_part), lambda z, y_ref: (0, z * ys + (y_ref[0] + step) % ys))

    return pl.pallas_call(
        split_kernel,
        grid_spec=pltpu.PrefetchScalarGridSpec(
            num_scalar_prefetch=1,
            grid=(Z,),
            in_specs=[source(step) for step in range(ys)] + [pl.BlockSpec(memory_space=pl.ANY)],
            out_specs=[pl.BlockSpec((rows, col_part), lambda z, _: (0, z))] * ys,
        ),
        out_shape=[jax.ShapeDtypeStruct((rows, width // ys), BF16)] * ys,
        compiler_params=params(),
        name="split",
    )(y.reshape(1), *([cotangent] * ys), after)


def join_kernel(axis, count, *refs):
    out = refs[-1]
    for n in range(count):
        size = refs[n].shape[axis]
        here = slice(n * size, (n + 1) * size)
        if axis == 0:
            out[here] = refs[n][...]
        else:
            out[:, here] = refs[n][...]


def join(parts, axis, after=()):
    shape = list(parts[0].shape)
    tile = shape[-1] // Z
    block = pl.BlockSpec((*shape[:-1], tile), lambda i: (0, 0, 0, i))
    shape[axis] *= len(parts)
    return pl.pallas_call(
        functools.partial(join_kernel, axis, len(parts)),
        grid=(Z,),
        in_specs=[block] * len(parts) + [pl.BlockSpec(memory_space=pl.ANY)] * len(after),
        out_specs=pl.BlockSpec((*shape[:-1], tile), lambda i: (0, 0, 0, i)),
        out_shape=jax.ShapeDtypeStruct(tuple(shape), BF16),
        compiler_params=params(),
        name="join",
    )(*parts, *after)


def own_cotangent(cotangent, col_part, after):
    ys, y = lax.axis_size("y"), lax.axis_index("y")
    held = split_cotangent(cotangent, y, ys, col_part, after)
    held = [around(part, "y", step) if step else part for step, part in enumerate(held)]
    return join([part[None, None] for part in held], 0)


def gather_cotangent(held, after):
    bits = bits_of("seq")
    for bit in reversed(bits[1:]):
        held = join([held, across(held, "seq", bit)], 1, after)
    return held, across(held, "seq", bits[0])


def mixed_grad_kernel(waits, place_ref, a_ref, b_ref, w_ref, *refs):
    out_ref, head_ref = refs[waits : waits + 2]
    found = refs[-1]
    _, count, rows, _ = a_ref.shape
    tokens = count * rows
    pieces = jnp.concatenate([ref[...].reshape(tokens, -1) for ref in (a_ref, b_ref)], axis=0)
    found[...] = contract(pieces, w_ref[...], 1)
    for block in range(2 * count):
        there = pl.multiple_of(place_ref[block] * rows, rows)
        out_ref[block * rows : (block + 1) * rows] = found[pl.ds(there, rows)].astype(out_ref.dtype)
    head_ref[...] = out_ref[0 : LTAPS + PAD]


def mixed_grad(cots, weights, place, step, dtype, after):
    _, count, rows, width = cots[0].shape
    tokens = 2 * count * rows
    cols = weights.shape[0]
    tile = min(cols, 2 * LANES)
    piece = pl.BlockSpec((1, count, rows, width), lambda i, _: (step, 0, 0, 0))
    return pl.pallas_call(
        functools.partial(mixed_grad_kernel, len(after)),
        grid_spec=pltpu.PrefetchScalarGridSpec(
            num_scalar_prefetch=1,
            grid=(cols // tile,),
            in_specs=[
                piece,
                piece,
                pl.BlockSpec((tile, width), lambda i, _: (i, 0)),
            ]
            + [pl.BlockSpec(memory_space=pl.ANY)] * len(after),
            out_specs=[
                pl.BlockSpec((tokens, tile), lambda i, _: (0, i)),
                pl.BlockSpec((LTAPS + PAD, tile), lambda i, _: (0, i)),
            ],
            scratch_shapes=[pltpu.VMEM((tokens, tile), F32)],
        ),
        out_shape=[
            jax.ShapeDtypeStruct((tokens, cols), dtype),
            jax.ShapeDtypeStruct((LTAPS + PAD, cols), dtype),
        ],
        compiler_params=params(),
        name="mixed_grad",
    )(place, *cots, weights, *after)


def weight_grad_kernel(scale, a_ref, b_ref, *refs):
    steps, count, rows, tile = a_ref.shape
    tokens = count * rows
    mixed, out = refs[:steps], refs[-1]
    total = None
    for step in range(steps):
        for n, ref in enumerate((a_ref, b_ref)):
            left = mixed[step][:, n * tokens : (n + 1) * tokens]
            term = jnp.dot(left, ref[step].reshape(tokens, tile), preferred_element_type=F32)
            total = term if total is None else total + term
    out[...] = (total * scale).astype(BF16)


def weight_grad(cots, mixed, chunk, chunks, scale, target, after):
    steps, count, rows, width = cots[0].shape
    part, tokens = mixed[0].shape
    tile = width // Z
    piece = pl.BlockSpec((steps, count, rows, tile), lambda i: (0, 0, 0, i))
    extra = [*after] + ([] if target is None else [target])
    return pl.pallas_call(
        functools.partial(weight_grad_kernel, scale),
        grid=(Z,),
        in_specs=[piece, piece]
        + [pl.BlockSpec((part, tokens), lambda i: (0, 0))] * len(mixed)
        + [pl.BlockSpec(memory_space=pl.ANY)] * len(extra),
        out_specs=pl.BlockSpec((part, tile), lambda i: (chunk, i)),
        out_shape=jax.ShapeDtypeStruct((part * chunks, width), BF16),
        input_output_aliases={} if target is None else {2 + len(mixed) + len(after): 0},
        compiler_params=params(),
        name="weight_grad",
    )(*cots, *mixed, *extra)


def tail_kernel(x_ref, before_ref, taps_ref, *refs):
    out_ref, xf = refs[-2:]
    rows = x_ref.shape[2]
    for i in range(3):
        out_ref[i * PAD : (i + 1) * PAD] = x_ref[0, i, rows - PAD :]
    for tile in range(x_ref.shape[3] // LANES):
        cols = slice(tile * LANES, (tile + 1) * LANES)
        taps = taps_ref[:, :, cols]
        prod = None
        for i in (1, 2):
            xf[tile, i - 1, 0:PAD] = before_ref[0, i, :, cols].astype(F32)
            xf[tile, i - 1, PAD:] = x_ref[0, i, :, cols].astype(F32)
            feature = taps[i, 0:1] * xf[tile, i - 1, PAD : PAD + rows]
            for j in range(1, SHORT):
                feature = feature + taps[i, j : j + 1] * xf[tile, i - 1, PAD - j : PAD - j + rows]
            prod = feature if prod is None else prod * feature
        out_ref[3 * PAD :, cols] = prod.astype(BF16)


def tail_of(x, short_taps, after):
    seq, _, rows, cols = x.shape
    wide = min(cols, 4 * LANES)
    out_rows = 3 * PAD + rows
    return pl.pallas_call(
        tail_kernel,
        grid=(cols // wide,),
        in_specs=[
            pl.BlockSpec((1, 3, rows, wide), lambda c: (seq - 1, 0, 0, c)),
            pl.BlockSpec((1, 3, PAD, wide), lambda c: (seq - 2, 0, rows // PAD - 1, c)),
            pl.BlockSpec((3, SHORT, wide), lambda c: (0, 0, c)),
        ]
        + [pl.BlockSpec(memory_space=pl.ANY)] * len(after),
        out_specs=pl.BlockSpec((out_rows, wide), lambda c: (0, c)),
        out_shape=jax.ShapeDtypeStruct((out_rows, cols), BF16),
        scratch_shapes=[pltpu.VMEM((wide // LANES, 2, PAD + rows, LANES), F32)],
        compiler_params=params(),
        name="tail",
    )(x, x, short_taps, *after)


def head_kernel(chunks, mo_ref, mr_ref, *refs):
    out_ref = refs[-2]
    edge = LTAPS + PAD
    part = out_ref.shape[1] // chunks
    for h in range(chunks):
        own = slice(h * part, (h + 1) * part)
        f_ref, filt_ref = refs[2 * h : 2 * h + 2]
        mixed = mo_ref[:, own] + mr_ref[:, own].astype(F32)
        out_ref[0:edge, own] = (mixed * f_ref[0]).astype(BF16)
        out_ref[edge : edge + PAD, own] = f_ref[1, 0:PAD].astype(BF16)
        out_ref[edge + PAD : edge + 2 * PAD, own] = f_ref[2, 0:PAD].astype(BF16)
        out_ref[edge + 2 * PAD :, own] = (mixed[0:PAD] * filt_ref[0:PAD]).astype(BF16)


def head_of(mixed_own, mixed_rest, mixers, passed):
    edge, cols = LTAPS + PAD, mixed_own.shape[1]
    part = cols // len(mixers)
    whole = pl.BlockSpec((edge, cols), lambda i: (0, 0))
    feat_specs = [
        pl.BlockSpec((3, edge, part), lambda i: (0, 0, 0)),
        pl.BlockSpec((edge, part), lambda i: (0, 0)),
    ]
    return pl.pallas_call(
        functools.partial(head_kernel, len(mixers)),
        grid=(1,),
        in_specs=[whole, whole] + feat_specs * len(mixers) + [pl.BlockSpec(memory_space=pl.ANY)],
        out_specs=[pl.BlockSpec((edge + 3 * PAD, cols), lambda i: (0, 0)), pl.BlockSpec(memory_space=pl.ANY)],
        out_shape=[
            jax.ShapeDtypeStruct((edge + 3 * PAD, cols), BF16),
            jax.ShapeDtypeStruct(passed.shape, passed.dtype),
        ],
        input_output_aliases={2 + 2 * len(mixers): 1},
        compiler_params=params(),
        name="head",
    )(mixed_own, mixed_rest, *[array for mixer in mixers for array in mixer[1:]], passed)


def contract(a, b, dim):
    return lax.dot_general(a, b, (((dim,), (dim,)), ((), ())), preferred_element_type=F32)


def places(seq):
    bits = bits_of("seq")
    source = lax.iota(jnp.int32, seq) ^ lax.axis_index("seq")
    return sum(((source >> n) & 1) << (len(bits) - 1 - n) for n in range(len(bits)))


def body(queries, keys, values, cotangent, out_weight, short_taps, long_taps, skip_gain):
    rows, width = queries.shape
    col_part = out_weight.shape[1]
    seq, ys = lax.axis_size("seq"), lax.axis_size("y")
    cols = width // seq
    chunks = 2 if cols % (2 * LANES) == 0 else 1
    groups = long_taps.shape[1]
    fsdp = ("z", "y")
    grad_scale = float(rows * seq * ys * Z) ** (-0.5)

    weights = lax.all_gather(out_weight, "z", axis=1, tiled=True)
    fwd_table, bwd_table = make_tables(long_taps)
    skip = skip_gain.reshape(1, cols)
    place = places(seq)
    by_owner = pack((queries, keys, values), seq)
    x = lax.all_to_all(by_owner, "seq", split_axis=0, concat_axis=0, tiled=True)
    held = own_cotangent(cotangent, col_part, by_owner)
    tail = tail_of(x, short_taps, [fwd_table, held])
    halo = along(tail, fsdp, 1)
    cots = gather_cotangent(held, [halo])
    mixers = []
    for h in range(chunks):
        after = mixers[-1][0] if mixers else cots[0]
        mixers.append(forward(x, halo, short_taps, skip, fwd_table, place, h, chunks, after))

    mixed_all = [
        [around(mixed, "y", step) if step else mixed for step in range(ys)] for mixed, _, _ in mixers
    ]

    parts, heads = [], []
    for step in range(1, ys):
        part, head = mixed_grad(
            cots, weights, place, step, BF16, [parts[-1] if parts else mixers[-1][0], *mixed_all[0][1:]]
        )
        parts.append(part)
        heads.append(around(head, "y", -step))
    mixed_own, own_head = mixed_grad(cots, weights, place, 0, F32, [parts[-1], *mixed_all[-1][1:]])
    head_rest = heads[0] if len(heads) == 1 else sum(piece.astype(F32) for piece in heads)
    head, parts[-1] = head_of(own_head, head_rest, mixers, parts[-1])
    rest = [around(parts[step - 1], "y", -step) for step in range(1, ys)]
    mixed_rest = rest[0] if len(rest) == 1 else sum(piece.astype(F32) for piece in rest)
    later = along(head, fsdp, -1)

    weight_sum = None
    for h in range(chunks):
        after = [later] if h == chunks - 1 else [head]
        weight_sum = weight_grad(cots, mixed_all[h], h, chunks, grad_scale, weight_sum, after)
    weight_part = lax.psum_scatter(weight_sum, "z", scatter_dimension=1, tiled=True)

    grads, short_parts, long_parts = [], [], []
    for h in range(chunks):
        _, feats, filt = mixers[h]
        grad, short_part, long_part = backward(
            mixed_own, mixed_rest, feats, filt, x, later, short_taps, skip, bwd_table, h, chunks
        )
        grads.append(lax.all_to_all(grad, "seq", split_axis=0, concat_axis=0, tiled=True))
        short_parts.append(short_part)
        long_parts.append(long_part)

    query_grad, key_grad, value_grad = unpack(grads)
    packed = jnp.concatenate(
        [
            jnp.concatenate(short_parts, axis=2).reshape(3 * (SHORT + 1), cols),
            jnp.concatenate(long_parts, axis=0).reshape(-1, cols),
        ],
        axis=0,
    )
    packed = sum_over(packed, ("y", "z")) * grad_scale
    short_sum = packed[: 3 * (SHORT + 1)].reshape(3, SHORT + 1, cols)
    long_sum = packed[3 * (SHORT + 1) :].reshape(groups, LTAPS).T
    return (
        query_grad,
        key_grad,
        value_grad,
        weight_part.astype(F32),
        short_sum[:, :SHORT],
        long_sum,
        short_sum[0, SHORT],
    )


def solution(mesh):
    fsdp, seq = mesh.shape["fsdp"], mesh.shape["seq"]
    split = Mesh(mesh.devices.reshape(Z, fsdp // Z, seq), ("z", "y", "seq"))
    tokens = P(("z", "y", "seq"), None)
    specs = (P("seq", ("z", "y")), P(None, None, "seq"), P(None, "seq"), P("seq"))
    return jax.shard_map(
        body,
        mesh=split,
        in_specs=(tokens,) * 4 + specs,
        out_specs=(tokens,) * 3 + specs,
        check_vma=False,
    )
```

```python
import functools

import jax
import jax.numpy as jnp
from jax import lax
from jax.experimental import pallas as pl
from jax.experimental.pallas import tpu as pltpu
from jax.sharding import Mesh
from jax.sharding import PartitionSpec as P

SHORT = 7
LTAPS = 128
LANES = 128
PAD = 16
Z = 4
F32 = jnp.float32
BF16 = jnp.bfloat16


def params():
    return pltpu.CompilerParams(vmem_limit_bytes=60 * 2**20)


def tables_kernel(fwd_ref, bwd_ref, tf_ref, tb_ref):
    for g in range(fwd_ref.shape[0]):
        rows = slice(g * LTAPS, (g + 1) * LTAPS)
        for src, dst in ((fwd_ref, tf_ref), (bwd_ref, tb_ref)):
            wide = jnp.broadcast_to(src[g : g + 1, :], (LTAPS, 2 * LTAPS))
            dst[rows, :] = pltpu.roll(wide, 0, 1, stride=1, stride_axis=0).astype(BF16)


def make_tables(long_taps):
    by_group = long_taps.T
    groups = by_group.shape[0]
    fwd = jnp.pad(by_group[:, ::-1], ((0, 0), (1, LTAPS - 1)))
    bwd = jnp.pad(by_group, ((0, 0), (0, LTAPS)))
    per = 8
    row_spec = pl.BlockSpec((per, 2 * LTAPS), lambda i: (i, 0))
    tab_spec = pl.BlockSpec((per * LTAPS, 2 * LTAPS), lambda i: (i, 0))
    shape = jax.ShapeDtypeStruct((groups * LTAPS, 2 * LTAPS), BF16)
    return pl.pallas_call(
        tables_kernel,
        grid=(groups // per,),
        in_specs=[row_spec, row_spec],
        out_specs=[tab_spec, tab_spec],
        out_shape=[shape, shape],
        compiler_params=params(),
        name="tables",
    )(fwd, bwd)


def pick_groups(wide, col, rows, per):
    lane_group = lax.broadcasted_iota(jnp.int32, (rows, LANES), 1) // (LANES // per)
    cols = slice(col * LANES, (col + 1) * LANES)
    out = wide[0:rows, cols]
    for g in range(1, per):
        out = jnp.where(lane_group == g, wide[g * rows : (g + 1) * rows, cols], out)
    return out


def features_of(taps_ref, row, xf, i, begin):
    total = taps_ref[row, 0:1] * xf[i, PAD + begin : PAD + begin + LTAPS]
    for j in range(1, SHORT):
        total = total + taps_ref[row, j : j + 1] * xf[i, PAD + begin - j : PAD + begin - j + LTAPS]
    return total


def forward_kernel(
    place_ref, x_ref, h_ref, taps_ref, skip_ref, tab_ref, _, mixed_ref, f_ref, filt_ref, xf, pf, pb, wide
):
    blocks, _, rows, _ = x_ref.shape
    tokens = blocks * rows
    per = tab_ref.shape[0] // LTAPS
    for i in range(3):
        xf[i, 0:PAD] = h_ref[i * PAD : (i + 1) * PAD].astype(F32)
        for b in range(blocks):
            begin = PAD + b * rows
            xf[i, begin : begin + rows] = x_ref[b, i].astype(F32)
    pb[0:LTAPS] = h_ref[3 * PAD : 3 * PAD + LTAPS]
    for begin in range(0, tokens, LTAPS):
        own = slice(begin, begin + LTAPS)
        f1 = features_of(taps_ref, 1, xf, 1, begin)
        f2 = features_of(taps_ref, 2, xf, 2, begin)
        prod = f1 * f2
        f_ref[1, own] = f1
        f_ref[2, own] = f2
        f_ref[0, own] = features_of(taps_ref, 0, xf, 0, begin)
        pf[own] = prod
        pb[LTAPS + begin : 2 * LTAPS + begin] = prod.astype(BF16)
    skip = skip_ref[...]
    for b in range(0, tokens // LTAPS, 2):
        low = b * LTAPS
        windows = jnp.concatenate([pb[low : low + 2 * LTAPS], pb[low + LTAPS : low + 3 * LTAPS]], axis=1)
        wide[...] = jnp.dot(tab_ref[...], windows, preferred_element_type=F32)
        for n in range(2):
            own = slice(low + n * LTAPS, low + (n + 1) * LTAPS)
            filtered = pick_groups(wide, n, LTAPS, per) + skip * pf[own]
            filt_ref[own] = filtered
            mixed = f_ref[0, own] * filtered
            there = pl.multiple_of(place_ref[b + n] * LTAPS, LTAPS)
            mixed_ref[:, pl.ds(there, LTAPS)] = mixed.T.astype(BF16)


def forward(x, halo, short_taps, skip, table, place, chunk, chunks, after):
    blocks, _, rows, cols = x.shape
    cols //= chunks
    tokens = blocks * rows
    tiles = cols // LANES
    first = chunk * tiles
    tab_rows = table.shape[0] * LANES // skip.shape[1]
    return pl.pallas_call(
        forward_kernel,
        grid_spec=pltpu.PrefetchScalarGridSpec(
            num_scalar_prefetch=1,
            grid=(tiles,),
            in_specs=[
                pl.BlockSpec((blocks, 3, rows, LANES), lambda c, _: (0, 0, 0, first + c)),
                pl.BlockSpec((halo.shape[0], LANES), lambda c, _: (0, first + c)),
                pl.BlockSpec((3, SHORT, LANES), lambda c, _: (0, 0, first + c)),
                pl.BlockSpec((1, LANES), lambda c, _: (0, first + c)),
                pl.BlockSpec((tab_rows, 2 * LTAPS), lambda c, _: (first + c, 0)),
                pl.BlockSpec(memory_space=pl.ANY),
            ],
            out_specs=[
                pl.BlockSpec((LANES, tokens), lambda c, _: (c, 0)),
                pl.BlockSpec((3, tokens, LANES), lambda c, _: (0, 0, c)),
                pl.BlockSpec((tokens, LANES), lambda c, _: (0, c)),
            ],
            scratch_shapes=[
                pltpu.VMEM((3, PAD + tokens, LANES), F32),
                pltpu.VMEM((tokens, LANES), F32),
                pltpu.VMEM((LTAPS + tokens, LANES), BF16),
                pltpu.VMEM((tab_rows, 2 * LTAPS), F32),
            ],
        ),
        out_shape=[
            jax.ShapeDtypeStruct((cols, tokens), BF16),
            jax.ShapeDtypeStruct((3, tokens, cols), F32),
            jax.ShapeDtypeStruct((tokens, cols), F32),
        ],
        compiler_params=params(),
        name="forward",
    )(place, x, halo, short_taps, skip, table, after)


def sum_by_lag(gram):
    wide = gram.shape[1]
    parts = [gram[i : i + 8] for i in range(0, gram.shape[0], 8)]
    step = 8
    while len(parts) > 1:
        parts = [
            parts[k] + pltpu.roll(parts[k + 1], wide - step, 1) for k in range(0, len(parts), 2)
        ]
        step *= 2
    total = parts[0]
    row = lax.broadcasted_iota(jnp.int32, total.shape, 0)
    for bit in (1, 2, 4):
        total = jnp.where((row & bit) != 0, pltpu.roll(total, wide - bit, 1), total)
    return jnp.sum(total[:, :LTAPS], axis=0, keepdims=True)


def backward_kernel(
    mo_ref, mr_ref, f_ref, filt_ref, x_ref, n_ref, taps_ref, skip_ref, tab_ref,
    grad_ref, short_ref, long_ref, db, fg, wide, left, right,
):
    blocks, _, rows, _ = x_ref.shape
    tokens = blocks * rows
    per = tab_ref.shape[0] // LTAPS
    count = tokens // LTAPS
    skip = skip_ref[...]
    lane_group = lax.broadcasted_iota(jnp.int32, (1, LANES), 1) // (LANES // per)
    gain = jnp.zeros((8, LANES), F32)
    for b in range(count):
        own = slice(b * LTAPS, (b + 1) * LTAPS)
        mixed_grad = mo_ref[own] + mr_ref[own].astype(F32)
        slope = mixed_grad * f_ref[0, own]
        db[own] = slope.astype(BF16)
        fg[0, own] = mixed_grad * filt_ref[own]
        fg[1, own] = skip * slope
        prod = f_ref[1, own] * f_ref[2, own]
        gain = gain + jnp.sum((prod * slope).reshape(LTAPS // 8, 8, LANES), axis=0)
        prod_b = prod.astype(BF16)
        for g in range(per):
            keep = (lane_group == g).astype(F32).astype(BF16)
            left[g * LTAPS : (g + 1) * LTAPS, b * LANES : (b + 1) * LANES] = prod_b * keep
    db[tokens : tokens + LTAPS + PAD] = n_ref[0 : LTAPS + PAD]
    db[tokens + LTAPS + PAD :] = jnp.zeros((LTAPS - PAD, LANES), BF16)
    for b in range(count):
        right[:, b * LANES : (b + 1) * LANES] = db[b * LTAPS : (b + 2) * LTAPS]
    for b in range(0, count, 2):
        wide[...] = jnp.dot(
            tab_ref[...], right[:, b * LANES : (b + 2) * LANES], preferred_element_type=F32
        )
        for n in range(2):
            own = slice((b + n) * LTAPS, (b + n + 1) * LTAPS)
            grad = pick_groups(wide, n, LTAPS, per) + fg[1, own]
            fg[1, own] = grad * f_ref[2, own]
            fg[2, own] = grad * f_ref[1, own]
    few = jnp.concatenate([tab_ref[g * LTAPS : g * LTAPS + PAD] for g in range(per)], axis=0)
    edge = jnp.dot(few, db[tokens : tokens + 2 * LTAPS], preferred_element_type=F32)
    begin = LTAPS + PAD
    grad = pick_groups(edge, 0, PAD, per) + skip * n_ref[0:PAD].astype(F32)
    fg[1, tokens : tokens + PAD] = grad * n_ref[begin + PAD : begin + 2 * PAD].astype(F32)
    fg[2, tokens : tokens + PAD] = grad * n_ref[begin : begin + PAD].astype(F32)
    fg[0, tokens : tokens + PAD] = n_ref[begin + 2 * PAD : begin + 3 * PAD].astype(F32)
    for i in range(3):
        sums = [jnp.zeros((8, LANES), F32) for _ in range(SHORT)]
        for b in range(count):
            low = b * LTAPS
            inputs = x_ref[b, i].astype(F32)
            total = None
            for j in range(SHORT):
                later = fg[i, low + j : low + j + LTAPS]
                term = taps_ref[i, j : j + 1] * later
                total = term if total is None else total + term
                sums[j] = sums[j] + jnp.sum((later * inputs).reshape(LTAPS // 8, 8, LANES), axis=0)
            grad_ref[b, i] = total.astype(BF16)
        for j in range(SHORT):
            short_ref[i, j : j + 1] = jnp.sum(sums[j], axis=0, keepdims=True)
        short_ref[i, SHORT : SHORT + 1] = jnp.sum(gain, axis=0, keepdims=True)
    wide[...] = lax.dot_general(left[...], right[...], (((1,), (1,)), ((), ())), preferred_element_type=F32)
    for g in range(per):
        gram = wide[g * LTAPS : (g + 1) * LTAPS]
        long_ref[g : g + 1] = sum_by_lag(gram)


def backward(mixed_own, mixed_rest, feats, filt, x, later, short_taps, skip, table, chunk, chunks):
    blocks, _, rows, cols = x.shape
    cols //= chunks
    tokens = blocks * rows
    tiles = cols // LANES
    first = chunk * tiles
    tab_rows = table.shape[0] * LANES // skip.shape[1]
    per = tab_rows // LTAPS
    tok = pl.BlockSpec((tokens, LANES), lambda c: (0, first + c))
    return pl.pallas_call(
        backward_kernel,
        grid=(tiles,),
        in_specs=[
            tok,
            tok,
            pl.BlockSpec((3, tokens, LANES), lambda c: (0, 0, c)),
            pl.BlockSpec((tokens, LANES), lambda c: (0, c)),
            pl.BlockSpec((blocks, 3, rows, LANES), lambda c: (0, 0, 0, first + c)),
            pl.BlockSpec((later.shape[0], LANES), lambda c: (0, first + c)),
            pl.BlockSpec((3, SHORT, LANES), lambda c: (0, 0, first + c)),
            pl.BlockSpec((1, LANES), lambda c: (0, first + c)),
            pl.BlockSpec((tab_rows, 2 * LTAPS), lambda c: (first + c, 0)),
        ],
        out_specs=[
            pl.BlockSpec((blocks, 3, rows, LANES), lambda c: (0, 0, 0, c)),
            pl.BlockSpec((3, SHORT + 1, LANES), lambda c: (0, 0, c)),
            pl.BlockSpec((per, LTAPS), lambda c: (c, 0)),
        ],
        out_shape=[
            jax.ShapeDtypeStruct((blocks, 3, rows, cols), BF16),
            jax.ShapeDtypeStruct((3, SHORT + 1, cols), F32),
            jax.ShapeDtypeStruct((tiles * per, LTAPS), F32),
        ],
        scratch_shapes=[
            pltpu.VMEM((tokens + 2 * LTAPS, LANES), BF16),
            pltpu.VMEM((3, tokens + PAD, LANES), F32),
            pltpu.VMEM((tab_rows, 2 * LTAPS), F32),
            pltpu.VMEM((tab_rows, tokens), BF16),
            pltpu.VMEM((2 * LTAPS, tokens), BF16),
        ],
        compiler_params=params(),
        cost_estimate=pl.CostEstimate(flops=10**11, bytes_accessed=36 * tokens * cols, transcendentals=0),
        name="backward",
    )(mixed_own, mixed_rest, feats, filt, x, later, short_taps, skip, table)


def pack_kernel(*refs):
    out_ref = refs[-1]
    for i, ref in enumerate(refs[:3]):
        out_ref[0, i] = ref[...]


def pack(arrays, seq):
    rows, width = arrays[0].shape
    cols = width // seq
    return pl.pallas_call(
        pack_kernel,
        grid=(seq,),
        in_specs=[pl.BlockSpec((rows, cols), lambda s: (0, s))] * 3,
        out_specs=pl.BlockSpec((1, 3, rows, cols), lambda s: (s, 0, 0, 0)),
        out_shape=jax.ShapeDtypeStruct((seq, 3, rows, cols), BF16),
        compiler_params=params(),
        name="pack",
    )(*arrays)


def unpack_kernel(*refs):
    parts, outs = refs[:-3], refs[-3:]
    cols = parts[0].shape[3]
    for n, part in enumerate(parts):
        for i, out in enumerate(outs):
            out[:, n * cols : (n + 1) * cols] = part[0, i]


def unpack(parts):
    seq, _, rows, cols = parts[0].shape
    wide = cols * len(parts)
    shape = jax.ShapeDtypeStruct((rows, seq * wide), BF16)
    return pl.pallas_call(
        unpack_kernel,
        grid=(seq,),
        in_specs=[pl.BlockSpec((1, 3, rows, cols), lambda s: (s, 0, 0, 0))] * len(parts),
        out_specs=[pl.BlockSpec((rows, wide), lambda s: (0, s))] * 3,
        out_shape=[shape] * 3,
        compiler_params=params(),
        name="unpack",
    )(*parts)


def along(block, axis, distance):
    size = lax.axis_size(axis)
    return lax.ppermute(block, axis, [(i, i + distance) for i in range(size) if 0 <= i + distance < size])


def around(block, axis, distance):
    size = lax.axis_size(axis)
    return lax.ppermute(block, axis, [(i, (i + distance) % size) for i in range(size)])


def across(block, axis, bit):
    return lax.ppermute(block, axis, [(i, i ^ bit) for i in range(lax.axis_size(axis))])


def bits_of(axis):
    size = lax.axis_size(axis)
    return [1 << n for n in range(size.bit_length() - 1)]


def sum_over(value, axes):
    for axis in axes:
        for bit in bits_of(axis):
            value = value + across(value, axis, bit)
    return value


def split_kernel(y_ref, *refs):
    count = (len(refs) - 1) // 2
    for n in range(count):
        refs[count + 1 + n][...] = refs[n][...]


def split_cotangent(cotangent, y, ys, col_part, after):
    rows, width = cotangent.shape

    def source(step):
        return pl.BlockSpec((rows, col_part), lambda z, y_ref: (0, z * ys + (y_ref[0] + step) % ys))

    return pl.pallas_call(
        split_kernel,
        grid_spec=pltpu.PrefetchScalarGridSpec(
            num_scalar_prefetch=1,
            grid=(Z,),
            in_specs=[source(step) for step in range(ys)] + [pl.BlockSpec(memory_space=pl.ANY)],
            out_specs=[pl.BlockSpec((rows, col_part), lambda z, _: (0, z))] * ys,
        ),
        out_shape=[jax.ShapeDtypeStruct((rows, width // ys), BF16)] * ys,
        compiler_params=params(),
        name="split",
    )(y.reshape(1), *([cotangent] * ys), after)


def join_kernel(axis, count, *refs):
    out = refs[-1]
    for n in range(count):
        size = refs[n].shape[axis]
        here = slice(n * size, (n + 1) * size)
        if axis == 0:
            out[here] = refs[n][...]
        else:
            out[:, here] = refs[n][...]


def join(parts, axis, after=()):
    shape = list(parts[0].shape)
    tile = shape[-1] // Z
    block = pl.BlockSpec((*shape[:-1], tile), lambda i: (0, 0, 0, i))
    shape[axis] *= len(parts)
    return pl.pallas_call(
        functools.partial(join_kernel, axis, len(parts)),
        grid=(Z,),
        in_specs=[block] * len(parts) + [pl.BlockSpec(memory_space=pl.ANY)] * len(after),
        out_specs=pl.BlockSpec((*shape[:-1], tile), lambda i: (0, 0, 0, i)),
        out_shape=jax.ShapeDtypeStruct(tuple(shape), BF16),
        compiler_params=params(),
        name="join",
    )(*parts, *after)


def own_cotangent(cotangent, col_part, after):
    ys, y = lax.axis_size("y"), lax.axis_index("y")
    held = split_cotangent(cotangent, y, ys, col_part, after)
    held = [around(part, "y", step) if step else part for step, part in enumerate(held)]
    return join([part[None, None] for part in held], 0)


def gather_cotangent(held, after):
    bits = bits_of("seq")
    for bit in reversed(bits[1:]):
        held = join([held, across(held, "seq", bit)], 1, after)
    return held, across(held, "seq", bits[0])


def mixed_grad_kernel(waits, place_ref, a_ref, b_ref, w_ref, *refs):
    out_ref, head_ref = refs[waits : waits + 2]
    found = refs[-1]
    _, count, rows, _ = a_ref.shape
    tokens = count * rows
    pieces = jnp.concatenate([ref[...].reshape(tokens, -1) for ref in (a_ref, b_ref)], axis=0)
    found[...] = contract(pieces, w_ref[...], 1)
    for block in range(2 * count):
        there = pl.multiple_of(place_ref[block] * rows, rows)
        out_ref[block * rows : (block + 1) * rows] = found[pl.ds(there, rows)].astype(out_ref.dtype)
    head_ref[...] = out_ref[0 : LTAPS + PAD]


def mixed_grad(cots, weights, place, step, dtype, after):
    _, count, rows, width = cots[0].shape
    tokens = 2 * count * rows
    cols = weights.shape[0]
    tile = min(cols, 2 * LANES)
    piece = pl.BlockSpec((1, count, rows, width), lambda i, _: (step, 0, 0, 0))
    return pl.pallas_call(
        functools.partial(mixed_grad_kernel, len(after)),
        grid_spec=pltpu.PrefetchScalarGridSpec(
            num_scalar_prefetch=1,
            grid=(cols // tile,),
            in_specs=[
                piece,
                piece,
                pl.BlockSpec((tile, width), lambda i, _: (i, 0)),
            ]
            + [pl.BlockSpec(memory_space=pl.ANY)] * len(after),
            out_specs=[
                pl.BlockSpec((tokens, tile), lambda i, _: (0, i)),
                pl.BlockSpec((LTAPS + PAD, tile), lambda i, _: (0, i)),
            ],
            scratch_shapes=[pltpu.VMEM((tokens, tile), F32)],
        ),
        out_shape=[
            jax.ShapeDtypeStruct((tokens, cols), dtype),
            jax.ShapeDtypeStruct((LTAPS + PAD, cols), dtype),
        ],
        compiler_params=params(),
        name="mixed_grad",
    )(place, *cots, weights, *after)


def weight_grad_kernel(scale, a_ref, b_ref, *refs):
    steps, count, rows, tile = a_ref.shape
    tokens = count * rows
    mixed, out = refs[:steps], refs[-1]
    total = None
    for step in range(steps):
        for n, ref in enumerate((a_ref, b_ref)):
            left = mixed[step][:, n * tokens : (n + 1) * tokens]
            term = jnp.dot(left, ref[step].reshape(tokens, tile), preferred_element_type=F32)
            total = term if total is None else total + term
    out[...] = (total * scale).astype(BF16)


def weight_grad(cots, mixed, chunk, chunks, scale, target, after):
    steps, count, rows, width = cots[0].shape
    part, tokens = mixed[0].shape
    tile = width // Z
    piece = pl.BlockSpec((steps, count, rows, tile), lambda i: (0, 0, 0, i))
    extra = [*after] + ([] if target is None else [target])
    return pl.pallas_call(
        functools.partial(weight_grad_kernel, scale),
        grid=(Z,),
        in_specs=[piece, piece]
        + [pl.BlockSpec((part, tokens), lambda i: (0, 0))] * len(mixed)
        + [pl.BlockSpec(memory_space=pl.ANY)] * len(extra),
        out_specs=pl.BlockSpec((part, tile), lambda i: (chunk, i)),
        out_shape=jax.ShapeDtypeStruct((part * chunks, width), BF16),
        input_output_aliases={} if target is None else {2 + len(mixed) + len(after): 0},
        compiler_params=params(),
        name="weight_grad",
    )(*cots, *mixed, *extra)


def tail_kernel(x_ref, before_ref, taps_ref, *refs):
    out_ref, xf = refs[-2:]
    rows = x_ref.shape[2]
    for i in range(3):
        out_ref[i * PAD : (i + 1) * PAD] = x_ref[0, i, rows - PAD :]
    for tile in range(x_ref.shape[3] // LANES):
        cols = slice(tile * LANES, (tile + 1) * LANES)
        taps = taps_ref[:, :, cols]
        prod = None
        for i in (1, 2):
            xf[tile, i - 1, 0:PAD] = before_ref[0, i, :, cols].astype(F32)
            xf[tile, i - 1, PAD:] = x_ref[0, i, :, cols].astype(F32)
            feature = taps[i, 0:1] * xf[tile, i - 1, PAD : PAD + rows]
            for j in range(1, SHORT):
                feature = feature + taps[i, j : j + 1] * xf[tile, i - 1, PAD - j : PAD - j + rows]
            prod = feature if prod is None else prod * feature
        out_ref[3 * PAD :, cols] = prod.astype(BF16)


def tail_of(x, short_taps, after):
    seq, _, rows, cols = x.shape
    wide = min(cols, 4 * LANES)
    out_rows = 3 * PAD + rows
    return pl.pallas_call(
        tail_kernel,
        grid=(cols // wide,),
        in_specs=[
            pl.BlockSpec((1, 3, rows, wide), lambda c: (seq - 1, 0, 0, c)),
            pl.BlockSpec((1, 3, PAD, wide), lambda c: (seq - 2, 0, rows // PAD - 1, c)),
            pl.BlockSpec((3, SHORT, wide), lambda c: (0, 0, c)),
        ]
        + [pl.BlockSpec(memory_space=pl.ANY)] * len(after),
        out_specs=pl.BlockSpec((out_rows, wide), lambda c: (0, c)),
        out_shape=jax.ShapeDtypeStruct((out_rows, cols), BF16),
        scratch_shapes=[pltpu.VMEM((wide // LANES, 2, PAD + rows, LANES), F32)],
        compiler_params=params(),
        name="tail",
    )(x, x, short_taps, *after)


def head_kernel(chunks, mo_ref, mr_ref, *refs):
    out_ref = refs[-1]
    edge = LTAPS + PAD
    part = out_ref.shape[1] // chunks
    for h in range(chunks):
        own = slice(h * part, (h + 1) * part)
        f_ref, filt_ref = refs[2 * h : 2 * h + 2]
        mixed = mo_ref[:, own] + mr_ref[:, own].astype(F32)
        out_ref[0:edge, own] = (mixed * f_ref[0]).astype(BF16)
        out_ref[edge : edge + PAD, own] = f_ref[1, 0:PAD].astype(BF16)
        out_ref[edge + PAD : edge + 2 * PAD, own] = f_ref[2, 0:PAD].astype(BF16)
        out_ref[edge + 2 * PAD :, own] = (mixed[0:PAD] * filt_ref[0:PAD]).astype(BF16)


def head_of(mixed_own, mixed_rest, mixers):
    edge, cols = LTAPS + PAD, mixed_own.shape[1]
    part = cols // len(mixers)
    whole = pl.BlockSpec((edge, cols), lambda i: (0, 0))
    feat_specs = [
        pl.BlockSpec((3, edge, part), lambda i: (0, 0, 0)),
        pl.BlockSpec((edge, part), lambda i: (0, 0)),
    ]
    return pl.pallas_call(
        functools.partial(head_kernel, len(mixers)),
        grid=(1,),
        in_specs=[whole, whole] + feat_specs * len(mixers),
        out_specs=pl.BlockSpec((edge + 3 * PAD, cols), lambda i: (0, 0)),
        out_shape=jax.ShapeDtypeStruct((edge + 3 * PAD, cols), BF16),
        compiler_params=params(),
        name="head",
    )(mixed_own, mixed_rest, *[array for mixer in mixers for array in mixer[1:]])


def pass_kernel(*_):
    pass


def pass_after(value, after):
    return pl.pallas_call(
        pass_kernel,
        in_specs=[pl.BlockSpec(memory_space=pl.ANY)] * 2,
        out_specs=pl.BlockSpec(memory_space=pl.ANY),
        out_shape=jax.ShapeDtypeStruct(value.shape, value.dtype),
        input_output_aliases={0: 0},
        name="pass_after",
    )(value, after)


def contract(a, b, dim):
    return lax.dot_general(a, b, (((dim,), (dim,)), ((), ())), preferred_element_type=F32)


def places(seq):
    bits = bits_of("seq")
    source = lax.iota(jnp.int32, seq) ^ lax.axis_index("seq")
    return sum(((source >> n) & 1) << (len(bits) - 1 - n) for n in range(len(bits)))


def body(queries, keys, values, cotangent, out_weight, short_taps, long_taps, skip_gain):
    rows, width = queries.shape
    col_part = out_weight.shape[1]
    seq, ys = lax.axis_size("seq"), lax.axis_size("y")
    cols = width // seq
    chunks = 2 if cols % (2 * LANES) == 0 else 1
    groups = long_taps.shape[1]
    fsdp = ("z", "y")
    grad_scale = float(rows * seq * ys * Z) ** (-0.5)

    weights = lax.all_gather(out_weight, "z", axis=1, tiled=True)
    fwd_table, bwd_table = make_tables(long_taps)
    skip = skip_gain.reshape(1, cols)
    place = places(seq)
    by_owner = pack((queries, keys, values), seq)
    x = lax.all_to_all(by_owner, "seq", split_axis=0, concat_axis=0, tiled=True)
    held = own_cotangent(cotangent, col_part, by_owner)
    tail = tail_of(x, short_taps, [fwd_table, held])
    halo = along(tail, fsdp, 1)
    cots = gather_cotangent(held, [halo])
    mixers = []
    for h in range(chunks):
        after = mixers[-1][0] if mixers else cots[0]
        mixers.append(forward(x, halo, short_taps, skip, fwd_table, place, h, chunks, after))

    mixed_all = [
        [around(mixed, "y", step) if step else mixed for step in range(ys)] for mixed, _, _ in mixers
    ]

    parts, heads = [], []
    for step in range(1, ys):
        part, head = mixed_grad(
            cots, weights, place, step, BF16, [parts[-1] if parts else mixers[-1][0], *mixed_all[0][1:]]
        )
        parts.append(part)
        heads.append(around(head, "y", -step))
    mixed_own, own_head = mixed_grad(cots, weights, place, 0, F32, [parts[-1], *mixed_all[-1][1:]])
    head_rest = heads[0] if len(heads) == 1 else sum(piece.astype(F32) for piece in heads)
    head = head_of(own_head, head_rest, mixers)
    later = along(head, fsdp, -1)
    parts[-1] = pass_after(parts[-1], later)
    rest = [around(parts[step - 1], "y", -step) for step in range(1, ys)]
    mixed_rest = rest[0] if len(rest) == 1 else sum(piece.astype(F32) for piece in rest)

    weight_sum = None
    for h in range(chunks):
        after = [later] if h == chunks - 1 else [head]
        weight_sum = weight_grad(cots, mixed_all[h], h, chunks, grad_scale, weight_sum, after)
    weight_part = lax.psum_scatter(weight_sum, "z", scatter_dimension=1, tiled=True)

    grads, short_parts, long_parts = [], [], []
    for h in range(chunks):
        _, feats, filt = mixers[h]
        grad, short_part, long_part = backward(
            mixed_own, mixed_rest, feats, filt, x, later, short_taps, skip, bwd_table, h, chunks
        )
        grads.append(lax.all_to_all(grad, "seq", split_axis=0, concat_axis=0, tiled=True))
        short_parts.append(short_part)
        long_parts.append(long_part)

    query_grad, key_grad, value_grad = unpack(grads)
    packed = jnp.concatenate(
        [
            jnp.concatenate(short_parts, axis=2).reshape(3 * (SHORT + 1), cols),
            jnp.concatenate(long_parts, axis=0).reshape(-1, cols),
        ],
        axis=0,
    )
    packed = sum_over(packed, ("y", "z")) * grad_scale
    short_sum = packed[: 3 * (SHORT + 1)].reshape(3, SHORT + 1, cols)
    long_sum = packed[3 * (SHORT + 1) :].reshape(groups, LTAPS).T
    return (
        query_grad,
        key_grad,
        value_grad,
        weight_part.astype(F32),
        short_sum[:, :SHORT],
        long_sum,
        short_sum[0, SHORT],
    )


def solution(mesh):
    fsdp, seq = mesh.shape["fsdp"], mesh.shape["seq"]
    split = Mesh(mesh.devices.reshape(Z, fsdp // Z, seq), ("z", "y", "seq"))
    tokens = P(("z", "y", "seq"), None)
    specs = (P("seq", ("z", "y")), P(None, None, "seq"), P(None, "seq"), P("seq"))
    return jax.shard_map(
        body,
        mesh=split,
        in_specs=(tokens,) * 4 + specs,
        out_specs=(tokens,) * 3 + specs,
        check_vma=False,
    )
```
